32 devices in a mesh: fsdp: 4 (over x, core), heads: 2 (over y), tensor: 4 (over z).
Axes of the slice: x: 2, y: 2, z: 4, core: 2. Of those that a mesh axis runs over, the one named last changes fastest.
Arguments:
- tokens: bfloat16 [32768, 2048], P(('fsdp', 'heads', 'tensor')), may hold values from -6 to 6
- cotangent: bfloat16 [32768, 2048], P(('fsdp', 'heads', 'tensor')), may hold values from -6 to 6
- seq_lens: int32 [16, 3], P(('fsdp', 'tensor')), may hold values from 129 to 1024, as said below
- block_pos: int32 [16, 16], P(('fsdp', 'tensor')), may hold values from 0 to 15, as said below
- norm1_gain: float32 [2048], replicated, may hold values from 0.5 to 1.5
- w_query: bfloat16 [2048, 2048], P(None, ('heads', 'fsdp', 'tensor')), may hold values from -0.125 to 0.125
- key_matrix: bfloat16 [2048, 1024], P(None, ('heads', 'fsdp', 'tensor')), may hold values from -0.125 to 0.125
- value_matrix: bfloat16 [2048, 1024], P(None, ('heads', 'fsdp', 'tensor')), may hold values from -0.125 to 0.125
- query_gain: float32 [128], replicated, may hold values from 0.5 to 1.5
- key_gain: float32 [128], replicated, may hold values from 0.5 to 1.5
- w_out: bfloat16 [2048, 2048], P(('heads', 'fsdp', 'tensor')), may hold values from -0.75 to 0.75
- norm2_gain: float32 [2048], replicated, may hold values from 0.5 to 1.5
- w_gate: bfloat16 [2048, 6144], P(('fsdp', 'heads'), 'tensor'), may hold values from -0.125 to 0.125
- w_up: bfloat16 [2048, 6144], P(('fsdp', 'heads'), 'tensor'), may hold values from -0.125 to 0.125
- w_down: bfloat16 [6144, 2048], P('tensor', ('fsdp', 'heads')), may hold values from -0.078125 to 0.078125
Outputs:
- output: bfloat16 [32768, 2048], P(('fsdp', 'heads', 'tensor'))
- tokens_grad: float32 [32768, 2048], P(('fsdp', 'heads', 'tensor'))
- norm1_gain_grad: float32 [2048], replicated
- w_query_grad: float32 [2048, 2048], P(None, ('heads', 'fsdp', 'tensor'))
- w_key_grad: float32 [2048, 1024], P(None, ('heads', 'fsdp', 'tensor'))
- w_value_grad: float32 [2048, 1024], P(None, ('heads', 'fsdp', 'tensor'))
- query_gain_grad: float32 [128], replicated
- key_gain_grad: float32 [128], replicated
- w_out_grad: float32 [2048, 2048], P(('heads', 'fsdp', 'tensor'))
- norm2_gain_grad: float32 [2048], replicated
- w_gate_grad: float32 [2048, 6144], P(('fsdp', 'heads'), 'tensor')
- w_up_grad: float32 [2048, 6144], P(('fsdp', 'heads'), 'tensor')
- w_down_grad: float32 [6144, 2048], P('tensor', ('fsdp', 'heads'))
The draws below stay inside these ranges and needn't reach their ends.
Inputs may be any that keep to these rules, and one draw needn't show every extreme that they name: `seq_lens`: in each row one sequence, at a place drawn from the seed, has exactly 1024 tokens; every other one has at most (8) // 2 * 128, so that all sequences of a group, padded to whole blocks, fit in its 16 blocks. `block_pos`: each row is a permutation: the block at position p lies on heads index (p + c) mod 2 as its local block p // 2, with c drawn for each row; entry h * 8 + j is the position of local block j of heads index h.
All inputs are finite; a program needn't handle non-finite values.
Results may differ from the reference program's by a relative error of at most 0.017.
Values may be sent and summed in bfloat16 or wider, within the bound.
A program may use at most 384 MiB of HBM per device.

```python
import math
import jax
import jax.numpy as jnp
from jax import lax

MODEL_WIDTH = 2048
QUERY_HEADS = 16
KEY_VALUE_HEADS = 8
HEAD_SIZE = 128
FF = 6144
BLK = 128
SEQ_BLOCKS = 8
GROUP_BLOCKS = 16
DEV_BLOCKS = 8
ROWS_DEV = 1024
SEQS = 3
GROUPS = 16
TOKENS = 32768
N_FSDP = 4
N_HEADS = 2
N_TENSOR = 4


def draw_seq_lens(key, part):
    key = jax.random.fold_in(key, 11)
    key_short, key_long = jax.random.split(key)
    ceiling = (GROUP_BLOCKS - SEQ_BLOCKS) // (SEQS - 1) * BLK
    shorter = jax.random.randint(key_short, (GROUPS, SEQS), BLK + 1, ceiling + 1)
    longest = jax.random.randint(key_long, (GROUPS, 1), 0, SEQS)
    column = jnp.arange(SEQS)[None, :]
    return jnp.where(column == longest, SEQ_BLOCKS * BLK, shorter).astype(jnp.int32)


def draw_block_pos(key, part):
    key = jax.random.fold_in(key, 23)
    rotation = jax.random.randint(key, (GROUPS, 1), 0, N_HEADS)
    slot = jnp.arange(GROUP_BLOCKS)[None, :]
    device_of = slot // DEV_BLOCKS
    local_of = slot % DEV_BLOCKS
    return (local_of * N_HEADS + (device_of - rotation) % N_HEADS).astype(jnp.int32)


def levels(key, shape, cuts, low, high):
    def one(dim, parts):
        draws = jax.random.uniform(jax.random.fold_in(jax.random.fold_in(key, 6), dim), (parts,), jnp.float32, low / len(cuts), high / len(cuts))
        return jnp.repeat(jnp.exp(draws), shape[dim] // parts).reshape((-1,) + (1,) * (len(shape) - dim - 1))

    gain = one(*cuts[0])
    for cut in cuts[1:]:
        gain = gain * one(*cut)
    return gain


def scatter_about(key, extent, spread, most, pieces=(), kind=jnp.bfloat16):
    drawn = spread * jax.random.normal(key, extent, jnp.float32)
    if pieces:
        drawn = drawn * levels(key, extent, pieces, -0.22, 0.18)
    return jnp.clip(drawn, -most, most).astype(kind)


def setup_inputs(seed: int = 0) -> dict:
    arg_keys = jax.random.split(jax.random.key(seed), 16)
    tokens = scatter_about(arg_keys[0], (TOKENS, MODEL_WIDTH), 1.0, 6.0, ((0, 32),))
    cotangent = scatter_about(arg_keys[1], (TOKENS, MODEL_WIDTH), 1.0, 6.0, ((0, 32),))
    seq_lens = draw_seq_lens(jax.random.fold_in(arg_keys[15], 71), 0)
    block_pos = draw_block_pos(jax.random.fold_in(arg_keys[15], 71), 0)
    norm1_gain = jnp.clip(1.0 + 0.1 * jax.random.normal(arg_keys[4], (MODEL_WIDTH,), jnp.float32), 0.5, 1.5)
    w_query = scatter_about(arg_keys[5], (MODEL_WIDTH, QUERY_HEADS * HEAD_SIZE), MODEL_WIDTH ** -0.5, 0.125, ((1, 32),))
    key_matrix = scatter_about(arg_keys[6], (MODEL_WIDTH, KEY_VALUE_HEADS * HEAD_SIZE), MODEL_WIDTH ** -0.5, 0.125, ((1, 32),))
    value_matrix = scatter_about(arg_keys[7], (MODEL_WIDTH, KEY_VALUE_HEADS * HEAD_SIZE), MODEL_WIDTH ** -0.5, 0.125, ((1, 32),))
    query_gain = jnp.clip(1.0 + 0.1 * jax.random.normal(arg_keys[8], (HEAD_SIZE,), jnp.float32), 0.5, 1.5)
    key_gain = jnp.clip(1.0 + 0.1 * jax.random.normal(arg_keys[9], (HEAD_SIZE,), jnp.float32), 0.5, 1.5)
    w_out = scatter_about(arg_keys[10], (QUERY_HEADS * HEAD_SIZE, MODEL_WIDTH), (QUERY_HEADS * HEAD_SIZE // 32) ** -0.5, 0.75, ((0, 32),))
    norm2_gain = jnp.clip(1.0 + 0.1 * jax.random.normal(arg_keys[11], (MODEL_WIDTH,), jnp.float32), 0.5, 1.5)
    w_gate = scatter_about(arg_keys[12], (MODEL_WIDTH, FF), MODEL_WIDTH ** -0.5, 0.125, ((0, 8), (1, 4)))
    w_up = scatter_about(arg_keys[13], (MODEL_WIDTH, FF), MODEL_WIDTH ** -0.5, 0.125, ((0, 8), (1, 4)))
    w_down = scatter_about(arg_keys[14], (FF, MODEL_WIDTH), FF ** -0.5, 0.078125, ((0, 4), (1, 8)))
    return dict(tokens=tokens, cotangent=cotangent, seq_lens=seq_lens, block_pos=block_pos, norm1_gain=norm1_gain, w_query=w_query, key_matrix=key_matrix, value_matrix=value_matrix, query_gain=query_gain, key_gain=key_gain, w_out=w_out, norm2_gain=norm2_gain, w_gate=w_gate, w_up=w_up, w_down=w_down)


EPS_NORM = 1e-06
ROPE_BASE = 1000000.0
NEG_FILL = -1e+30
PRECISE = lax.Precision.HIGHEST

@jax.custom_vjp
def lower_precision(v):
    return lax.optimization_barrier(v.astype(jnp.bfloat16)).astype(jnp.float32)

@jax.custom_vjp
def lower_precision_grad(v):
    return v

def low_keep(v):
    return (lower_precision(v), None)

def low_pass(kept, grad):
    return (grad,)

def back_keep(v):
    return (v, None)

def back_low(kept, grad):
    return (lower_precision(grad),)
lower_precision.defvjp(low_keep, low_pass)
lower_precision_grad.defvjp(back_keep, back_low)

def row_info(lengths, positions):
    block_count = ((lengths + BLK - 1) // BLK).astype(jnp.int32)
    ends = jnp.cumsum(block_count).astype(jnp.int32)
    starts = (ends - block_count).astype(jnp.int32)
    used = ends[-1]
    column = positions[:, None]
    inside = (column >= starts[None, :]) & (column < ends[None, :])
    past = positions >= used
    seq_block = lax.optimization_barrier(jnp.sum((column >= ends[None, :]).astype(jnp.int32), axis=1)).astype(jnp.int32)
    first_block = (lax.optimization_barrier(jnp.sum(jnp.where(inside, starts[None, :], 0), axis=1)) + jnp.where(past, used, 0)).astype(jnp.int32)
    limit = lax.optimization_barrier(jnp.sum(jnp.where(inside, lengths[None, :], 0), axis=1)).astype(jnp.int32)
    offsets = jnp.arange(BLK, dtype=jnp.int32)[None, :]
    pos_rows = ((positions - first_block)[:, None] * BLK + offsets).astype(jnp.int32)
    seq_rows = jnp.broadcast_to(seq_block[:, None], pos_rows.shape)
    valid_rows = jnp.logical_not(past)[:, None] & (pos_rows < limit[:, None])
    return (seq_rows.reshape(-1), pos_rows.reshape(-1), valid_rows.reshape(-1))

def rope_tables(pos_rows):
    half_dim = HEAD_SIZE // 2
    freq = jnp.exp(jnp.arange(half_dim, dtype=jnp.float32) * (-2.0 * math.log(ROPE_BASE) / HEAD_SIZE))
    angles = pos_rows.astype(jnp.float32)[:, None] * freq[None, :]
    return (jnp.cos(angles), jnp.sin(angles))

def rotate(value_rows, cos_tab, sin_tab):
    half_dim = value_rows.shape[-1] // 2
    first_half, second_half = (value_rows[..., :half_dim], value_rows[..., half_dim:])
    return jnp.concatenate([first_half * cos_tab - second_half * sin_tab, second_half * cos_tab + first_half * sin_tab], axis=-1)

def rms_norm(value_rows, gain_vec):
    return value_rows * lax.rsqrt(lax.optimization_barrier(jnp.mean(value_rows * value_rows, axis=-1, keepdims=True)) + EPS_NORM) * gain_vec

def matrix_product(left, right):
    return jnp.dot(left, right, precision=PRECISE)

def to_groups(array):
    array = array.reshape((N_FSDP, N_HEADS, N_TENSOR, ROWS_DEV) + array.shape[1:])
    array = jnp.swapaxes(array, 1, 2)
    return array.reshape((N_FSDP * N_TENSOR, N_HEADS * ROWS_DEV) + array.shape[4:])

def from_groups(array):
    array = array.reshape((N_FSDP, N_TENSOR, N_HEADS, ROWS_DEV) + array.shape[2:])
    array = jnp.swapaxes(array, 1, 2)
    return array.reshape((N_FSDP * N_HEADS * N_TENSOR * ROWS_DEV,) + array.shape[4:])

def group_forward(weights, group_x, lengths, positions):
    norm1_gain, w_query, key_matrix, value_matrix, query_gain, key_gain, w_out, norm2_gain, w_gate, w_up, w_down = weights
    seq_rows, pos_rows, valid_rows = row_info(lengths, positions)
    total_rows = group_x.shape[0]
    group_factor = QUERY_HEADS // KEY_VALUE_HEADS
    scale = HEAD_SIZE ** (-0.5)
    first_normed = lower_precision(rms_norm(group_x, norm1_gain))
    q_raw = lower_precision_grad(matrix_product(first_normed, w_query)).reshape(total_rows, QUERY_HEADS, HEAD_SIZE)
    key_unnormed = lower_precision_grad(matrix_product(first_normed, key_matrix)).reshape(total_rows, KEY_VALUE_HEADS, HEAD_SIZE)
    value_rows = lower_precision_grad(lower_precision(matrix_product(first_normed, value_matrix))).reshape(total_rows, KEY_VALUE_HEADS, HEAD_SIZE)
    cos_tab, sin_tab = rope_tables(pos_rows)
    cos_tab, sin_tab = (cos_tab[:, None, :], sin_tab[:, None, :])
    query_rows = lower_precision_grad(lower_precision(rotate(rms_norm(q_raw, query_gain), cos_tab, sin_tab)))
    key = lower_precision_grad(lower_precision(rotate(rms_norm(key_unnormed, key_gain), cos_tab, sin_tab)))
    allowed = (seq_rows[:, None] == seq_rows[None, :]) & (pos_rows[None, :] <= pos_rows[:, None])
    query_head_rows = query_rows.reshape(total_rows, KEY_VALUE_HEADS, group_factor, HEAD_SIZE).transpose(1, 2, 0, 3)
    key_heads = key.transpose(1, 0, 2)
    value_heads = value_rows.transpose(1, 0, 2)

    def one_head(operands):
        q_part, k_part, v_part = operands
        scores = lower_precision_grad(jnp.einsum('gqd,kd->gqk', q_part, k_part, precision=PRECISE) * scale)
        scores = jnp.where(allowed[None], scores, NEG_FILL)
        probs = jax.nn.softmax(scores, axis=-1)
        return jnp.einsum('gqk,kd->gqd', lower_precision(probs), v_part, precision=PRECISE)
    attended = lax.map(jax.checkpoint(one_head), (query_head_rows, key_heads, value_heads))
    attended = lower_precision_grad(lower_precision(attended.transpose(2, 0, 1, 3).reshape(total_rows, QUERY_HEADS * HEAD_SIZE)))
    resid = group_x + lower_precision_grad(matrix_product(attended, w_out))
    normed2 = lower_precision(rms_norm(resid, norm2_gain))
    gate = lower_precision_grad(matrix_product(normed2, w_gate))
    upper = lower_precision_grad(matrix_product(normed2, w_up))
    act = lower_precision(jax.nn.silu(gate) * upper)
    mixed = lower_precision_grad(matrix_product(act, w_down))
    return jnp.where(valid_rows[:, None], resid + mixed, 0.0)

def reference(tokens, cotangent, seq_lens, block_pos, norm1_gain, w_query, key_matrix, value_matrix, query_gain, key_gain, w_out, norm2_gain, w_gate, w_up, w_down):
    weights = tuple((item.astype(jnp.float32) for item in (norm1_gain, w_query, key_matrix, value_matrix, query_gain, key_gain, w_out, norm2_gain, w_gate, w_up, w_down)))
    group_x = to_groups(tokens.astype(jnp.float32))
    group_cot = to_groups(cotangent.astype(jnp.float32))

    def forward(inputs, params):

        def single(operands):
            return group_forward(params, operands[0], operands[1], operands[2])
        return lax.map(jax.checkpoint(single), (inputs, seq_lens, block_pos))
    outputs, pullback = jax.vjp(forward, group_x, weights)
    input_grad, weight_grads = pullback(group_cot)
    return (from_groups(outputs).astype(jnp.bfloat16), from_groups(input_grad), weight_grads[0], weight_grads[1], weight_grads[2], weight_grads[3], weight_grads[4], weight_grads[5], weight_grads[6], weight_grads[7], weight_grads[8], weight_grads[9], weight_grads[10])
```

```python
import functools
import math

import jax
import jax.numpy as jnp
from jax import lax
from jax.experimental import pallas as pl
from jax.experimental.pallas import tpu as pltpu
from jax.sharding import Mesh
from jax.sharding import PartitionSpec as P

QUERY_HEADS = 16
KEY_VALUE_HEADS = 8
HEAD_SIZE = 128
BLK = 128


EPS_NORM = 1e-06
ROPE_BASE = 1000000.0
NEG_FILL = -1e30


def row_info(lengths, positions):
    block_count = (lengths + BLK - 1) // BLK
    ends = jnp.cumsum(block_count)
    starts = ends - block_count
    used = ends[-1]
    column = positions[:, None]
    inside = (column >= starts[None, :]) & (column < ends[None, :])
    past = positions >= used
    seq_block = jnp.sum((column >= ends[None, :]).astype(jnp.int32), axis=1)
    first_block = jnp.sum(jnp.where(inside, starts[None, :], 0), axis=1) + jnp.where(past, used, 0)
    limit = jnp.sum(jnp.where(inside, lengths[None, :], 0), axis=1)
    offsets = jnp.arange(BLK, dtype=jnp.int32)[None, :]
    pos_rows = (positions - first_block)[:, None] * BLK + offsets
    seq_rows = jnp.broadcast_to(seq_block[:, None], pos_rows.shape)
    valid_rows = jnp.logical_not(past)[:, None] & (pos_rows < limit[:, None])
    return (seq_rows.reshape(-1), pos_rows.reshape(-1), valid_rows.reshape(-1))


def rope_tables(pos_rows):
    half_dim = HEAD_SIZE // 2
    freq = jnp.exp(
        jnp.arange(half_dim, dtype=jnp.float32) * (-2.0 * math.log(ROPE_BASE) / HEAD_SIZE)
    )
    angles = pos_rows.astype(jnp.float32)[:, None] * freq[None, :]
    return (jnp.cos(angles)[:, None, :], jnp.sin(angles)[:, None, :])


def rotate(value_rows, cos_tab, sin_tab):
    half_dim = value_rows.shape[-1] // 2
    first_half, second_half = (value_rows[..., :half_dim], value_rows[..., half_dim:])
    return jnp.concatenate(
        [
            first_half * cos_tab - second_half * sin_tab,
            second_half * cos_tab + first_half * sin_tab,
        ],
        axis=-1,
    )


def unrotate(upstream, cos_tab, sin_tab):
    half_dim = upstream.shape[-1] // 2
    first_half, second_half = (upstream[..., :half_dim], upstream[..., half_dim:])
    return jnp.concatenate(
        [
            first_half * cos_tab + second_half * sin_tab,
            second_half * cos_tab - first_half * sin_tab,
        ],
        axis=-1,
    )


def rms_parts(value_rows, gain_vec):
    scales = lax.rsqrt(jnp.mean(value_rows * value_rows, axis=-1, keepdims=True) + EPS_NORM)
    return (value_rows * scales * gain_vec, scales)


def norm_back(value_rows, scales, gain_vec, upstream):
    weighted = upstream * gain_vec
    inner = jnp.sum(value_rows * weighted, axis=-1, keepdims=True) / value_rows.shape[-1]
    return scales * weighted - value_rows * scales * scales * scales * inner


def matrix_product(left, right):
    return jnp.dot(left, right, preferred_element_type=jnp.float32)


def dot_rows(left, right):
    return lax.dot_general(
        left, right, (((0,), (0,)), ((), ())), preferred_element_type=jnp.float32
    )


def dot_cols(left, right):
    return lax.dot_general(
        left, right, (((1,), (1,)), ((), ())), preferred_element_type=jnp.float32
    )


def swap_cols(array, outer, inner):
    lead = array.shape[0]
    return jnp.swapaxes(array.reshape(lead, outer, inner, -1), 1, 2).reshape(lead, -1)


def swap_rows(array, outer, inner):
    width = array.shape[1]
    return jnp.swapaxes(array.reshape(outer, inner, -1, width), 0, 1).reshape(-1, width)


def spread_rows(local_rows):
    return lax.all_gather(local_rows, "tensor", axis=0, tiled=True)


def to_heads(packed):
    return lax.all_to_all(packed, "heads", split_axis=1, concat_axis=0, tiled=True)


def to_rows(packed):
    return lax.all_to_all(packed, "heads", split_axis=0, concat_axis=1, tiled=True)


def tensor_sum(term, row_count):
    total = lax.psum(
        term(0, row_count * lax.axis_size("tensor")).astype(jnp.bfloat16), "tensor"
    ).astype(jnp.float32)
    return lax.dynamic_slice_in_dim(total, lax.axis_index("tensor") * row_count, row_count)


def block_scores(query_blk, key_all, seq_blk, pos_blk, seq_all, pos_all):
    scores = jnp.einsum(
        "qkgd,pkd->kgqp", query_blk, key_all, preferred_element_type=jnp.float32
    ) * HEAD_SIZE ** (-0.5)
    allowed = (seq_blk[:, None] == seq_all[None, :]) & (pos_all[None, :] <= pos_blk[:, None])
    return jnp.where(allowed[None, None], scores, NEG_FILL)


def attend_forward(query_grp, key_grp, value_grp, seq_all, pos_all):
    group_factor = QUERY_HEADS // KEY_VALUE_HEADS
    group_len = query_grp.shape[0]
    kv_local = key_grp.shape[1] // HEAD_SIZE
    query_four = query_grp.reshape(group_len, kv_local, group_factor, HEAD_SIZE)
    key_three = key_grp.reshape(group_len, kv_local, HEAD_SIZE)
    value_three = value_grp.reshape(group_len, kv_local, HEAD_SIZE)
    block_rows = min(512, group_len)

    def forward_block(block_idx):
        first_row = block_idx * block_rows
        query_blk = lax.dynamic_slice_in_dim(query_four, first_row, block_rows)
        seq_blk = lax.dynamic_slice_in_dim(seq_all, first_row, block_rows)
        pos_blk = lax.dynamic_slice_in_dim(pos_all, first_row, block_rows)
        scores = block_scores(query_blk, key_three, seq_blk, pos_blk, seq_all, pos_all)
        peak = jnp.max(scores, axis=-1, keepdims=True)
        expo = jnp.exp(scores - peak)
        total = jnp.sum(expo, axis=-1, keepdims=True)
        probs_b = (expo / total).astype(jnp.bfloat16)
        attended = jnp.einsum(
            "kgqp,pkd->qkgd", probs_b, value_three, preferred_element_type=jnp.float32
        )
        return (attended, (peak + jnp.log(total))[..., 0])

    attended, log_sums = lax.map(forward_block, jnp.arange(group_len // block_rows))
    return (
        attended.reshape(group_len, kv_local * group_factor * HEAD_SIZE).astype(jnp.bfloat16),
        log_sums,
    )


def attend_backward(query_grp, key_grp, value_grp, grad_grp, log_sums, seq_all, pos_all):
    group_factor = QUERY_HEADS // KEY_VALUE_HEADS
    scale = HEAD_SIZE ** (-0.5)
    group_len = query_grp.shape[0]
    kv_local = key_grp.shape[1] // HEAD_SIZE
    query_four = query_grp.reshape(group_len, kv_local, group_factor, HEAD_SIZE)
    key_three = key_grp.reshape(group_len, kv_local, HEAD_SIZE)
    value_three = value_grp.reshape(group_len, kv_local, HEAD_SIZE)
    grad_four = grad_grp.reshape(group_len, kv_local, group_factor, HEAD_SIZE)
    block_rows = min(512, group_len)

    def backward_block(carry, block_idx):
        key_acc, value_acc = carry
        first_row = block_idx * block_rows
        query_blk = lax.dynamic_slice_in_dim(query_four, first_row, block_rows)
        grad_blk = lax.dynamic_slice_in_dim(grad_four, first_row, block_rows)
        seq_blk = lax.dynamic_slice_in_dim(seq_all, first_row, block_rows)
        pos_blk = lax.dynamic_slice_in_dim(pos_all, first_row, block_rows)
        scores = block_scores(query_blk, key_three, seq_blk, pos_blk, seq_all, pos_all)
        probs = jnp.exp(scores - log_sums[block_idx][..., None])
        probs_b = probs.astype(jnp.bfloat16)
        prob_grad = jnp.einsum(
            "qkgd,pkd->kgqp", grad_blk, value_three, preferred_element_type=jnp.float32
        )
        score_grad_b = (
            probs * (prob_grad - jnp.sum(probs * prob_grad, axis=-1, keepdims=True))
        ).astype(jnp.bfloat16)
        query_grad = (
            jnp.einsum(
                "kgqp,pkd->qkgd", score_grad_b, key_three, preferred_element_type=jnp.float32
            )
            * scale
        )
        key_acc = (
            key_acc
            + jnp.einsum(
                "kgqp,qkgd->pkd", score_grad_b, query_blk, preferred_element_type=jnp.float32
            )
            * scale
        )
        value_acc = value_acc + jnp.einsum(
            "kgqp,qkgd->pkd", probs_b, grad_blk, preferred_element_type=jnp.float32
        )
        return ((key_acc, value_acc), query_grad)

    empty = jnp.zeros((group_len, kv_local, HEAD_SIZE), jnp.float32)
    (key_acc, value_acc), query_blocks = lax.scan(
        backward_block, (empty, empty), jnp.arange(group_len // block_rows)
    )
    query_grad_b = query_blocks.reshape(group_len, kv_local * group_factor * HEAD_SIZE).astype(
        jnp.bfloat16
    )
    key_grad_b = key_acc.reshape(group_len, kv_local * HEAD_SIZE).astype(jnp.bfloat16)
    value_grad_b = value_acc.reshape(group_len, kv_local * HEAD_SIZE).astype(jnp.bfloat16)
    return (query_grad_b, key_grad_b, value_grad_b)


def project_heads(normed_b, query_w, key_w, value_w, query_gain, key_gain, pos_rows):
    lines = normed_b.shape[0]
    q_raw = matrix_product(normed_b, query_w).reshape(lines, -1, HEAD_SIZE)
    key_unnormed = matrix_product(normed_b, key_w).reshape(lines, -1, HEAD_SIZE)
    value_b = matrix_product(normed_b, value_w).astype(jnp.bfloat16)
    cos_tab, sin_tab = rope_tables(pos_rows)
    q_normed, q_scale = rms_parts(q_raw, query_gain)
    k_normed, k_scale = rms_parts(key_unnormed, key_gain)
    query_b = rotate(q_normed, cos_tab, sin_tab).astype(jnp.bfloat16).reshape(lines, -1)
    key_b = rotate(k_normed, cos_tab, sin_tab).astype(jnp.bfloat16).reshape(lines, -1)
    return (query_b, key_b, value_b, (q_raw, q_scale, key_unnormed, k_scale, cos_tab, sin_tab))


def heads_back(query_back, key_back, kept, query_gain, key_gain):
    q_raw, q_scale, key_unnormed, k_scale, cos_tab, sin_tab = kept
    lines = q_raw.shape[0]
    q_turned = unrotate(query_back.astype(jnp.float32).reshape(q_raw.shape), cos_tab, sin_tab)
    k_turned = unrotate(key_back.astype(jnp.float32).reshape(key_unnormed.shape), cos_tab, sin_tab)
    q_raw_grad = (
        norm_back(q_raw, q_scale, query_gain, q_turned).reshape(lines, -1).astype(jnp.bfloat16)
    )
    k_raw_grad = (
        norm_back(key_unnormed, k_scale, key_gain, k_turned).reshape(lines, -1).astype(jnp.bfloat16)
    )
    qgain_part = jnp.sum(q_turned * q_raw * q_scale, axis=(0, 1))
    kgain_part = jnp.sum(k_turned * key_unnormed * k_scale, axis=(0, 1))
    return (q_raw_grad, k_raw_grad, qgain_part, kgain_part)


def plain_layer(
    tokens,
    cotangent,
    seq_lens,
    block_pos,
    norm1_gain,
    w_query,
    key_matrix,
    value_matrix,
    query_gain,
    key_gain,
    w_out,
    norm2_gain,
    w_gate,
    w_up,
    w_down,
):
    row_count = tokens.shape[0]
    fsdp_count = lax.axis_size("fsdp")
    heads_count = lax.axis_size("heads")
    gate_full, up_full, down_full = (
        lax.all_gather(w_gate, ("fsdp", "heads"), axis=0, tiled=True),
        lax.all_gather(w_up, ("fsdp", "heads"), axis=0, tiled=True),
        lax.all_gather(w_down, ("fsdp", "heads"), axis=1, tiled=True),
    )
    seq_all, pos_all, valid_all = row_info(seq_lens[0], block_pos[0])
    own_first = lax.axis_index("heads") * row_count
    pos_own = lax.dynamic_slice_in_dim(pos_all, own_first, row_count)
    valid_own = lax.dynamic_slice_in_dim(valid_all, own_first, row_count).astype(jnp.float32)[
        :, None
    ]
    inputs = tokens.astype(jnp.float32)
    first_normed, scale1 = rms_parts(inputs, norm1_gain)
    normed1_b = first_normed.astype(jnp.bfloat16)
    query_all, key_all, value_all, out_all = (
        lax.all_gather(w_query, ("fsdp", "heads", "tensor"), axis=1, tiled=True),
        lax.all_gather(key_matrix, ("fsdp", "heads", "tensor"), axis=1, tiled=True),
        lax.all_gather(value_matrix, ("fsdp", "heads", "tensor"), axis=1, tiled=True),
        lax.all_gather(w_out, ("fsdp", "heads", "tensor"), axis=0, tiled=True),
    )
    query_full = swap_cols(query_all, fsdp_count, heads_count)
    key_full = swap_cols(key_all, fsdp_count, heads_count)
    value_full = swap_cols(value_all, fsdp_count, heads_count)
    out_full = swap_rows(out_all, fsdp_count, heads_count)
    query_b, key_b, value_b, kept = project_heads(
        normed1_b, query_full, key_full, value_full, query_gain, key_gain, pos_own
    )
    q_width = query_b.shape[1] // heads_count
    k_width = key_b.shape[1] // heads_count
    packed = jnp.concatenate(
        [
            query_b.reshape(row_count, heads_count, q_width),
            key_b.reshape(row_count, heads_count, k_width),
            value_b.reshape(row_count, heads_count, k_width),
        ],
        axis=2,
    )
    grouped = to_heads(packed.reshape(row_count, -1))
    query_grp = grouped[:, :q_width]
    key_grp = grouped[:, q_width : q_width + k_width]
    value_grp = grouped[:, q_width + k_width :]
    attended_b, log_sums = attend_forward(query_grp, key_grp, value_grp, seq_all, pos_all)
    attn_tok = to_rows(attended_b)
    resid = inputs + matrix_product(attn_tok, out_full)
    normed2, scale2 = rms_parts(resid, norm2_gain)
    normed2_b = normed2.astype(jnp.bfloat16)
    wide_in = spread_rows(normed2_b)
    gate_pre = matrix_product(wide_in, gate_full)
    up_pre = matrix_product(wide_in, up_full)
    sigmoid_gate = jax.nn.sigmoid(gate_pre)
    silu_gate = gate_pre * sigmoid_gate
    act_b = (silu_gate * up_pre).astype(jnp.bfloat16)

    def forward_term(first_row, span):
        return matrix_product(act_b, down_full)

    mixed = tensor_sum(forward_term, row_count)
    output = (valid_own * (resid + mixed)).astype(jnp.bfloat16)
    grad_out = valid_own * cotangent.astype(jnp.float32)
    wide_grad = spread_rows(grad_out.astype(jnp.bfloat16))
    act_grad = dot_cols(wide_grad, down_full)
    down_grad = dot_rows(act_b, wide_grad)
    gate_grad_b = (
        act_grad * up_pre * sigmoid_gate * (1.0 + gate_pre * (1.0 - sigmoid_gate))
    ).astype(jnp.bfloat16)
    up_grad_b = (act_grad * silu_gate).astype(jnp.bfloat16)
    gate_wgrad = dot_rows(wide_in, gate_grad_b)
    up_wgrad = dot_rows(wide_in, up_grad_b)

    def backward_term(first_row, span):
        return dot_cols(gate_grad_b, gate_full) + dot_cols(up_grad_b, up_full)

    normed2_grad = tensor_sum(backward_term, row_count)
    gate_sum, up_sum, down_sum = (
        lax.psum_scatter(
            gate_wgrad.astype(jnp.bfloat16), ("fsdp", "heads"), scatter_dimension=0, tiled=True
        ).astype(jnp.float32),
        lax.psum_scatter(
            up_wgrad.astype(jnp.bfloat16), ("fsdp", "heads"), scatter_dimension=0, tiled=True
        ).astype(jnp.float32),
        lax.psum_scatter(
            down_grad.astype(jnp.bfloat16), ("fsdp", "heads"), scatter_dimension=1, tiled=True
        ).astype(jnp.float32),
    )
    resid_grad = grad_out + norm_back(resid, scale2, norm2_gain, normed2_grad)
    gain2_part = jnp.sum(normed2_grad * resid * scale2, axis=0)
    resid_grad_b = resid_grad.astype(jnp.bfloat16)
    out_wgrad = dot_rows(attn_tok, resid_grad_b)
    attn_grad_b = dot_cols(resid_grad_b, out_full).astype(jnp.bfloat16)
    attn_grad_grp = to_heads(attn_grad_b)
    query_grad_b, key_grad_b, value_grad_b = attend_backward(
        query_grp, key_grp, value_grp, attn_grad_grp, log_sums, seq_all, pos_all
    )
    back_packed = to_rows(jnp.concatenate([query_grad_b, key_grad_b, value_grad_b], axis=1))
    back_three = back_packed.reshape(row_count, heads_count, -1)
    query_back = back_three[:, :, :q_width].reshape(row_count, -1)
    key_back = back_three[:, :, q_width : q_width + k_width].reshape(row_count, -1)
    value_back = back_three[:, :, q_width + k_width :].reshape(row_count, -1)
    q_raw_grad, k_raw_grad, qgain_part, kgain_part = heads_back(
        query_back, key_back, kept, query_gain, key_gain
    )
    query_wgrad = swap_cols(dot_rows(normed1_b, q_raw_grad), heads_count, fsdp_count)
    key_wgrad = swap_cols(dot_rows(normed1_b, k_raw_grad), heads_count, fsdp_count)
    value_wgrad = swap_cols(dot_rows(normed1_b, value_back), heads_count, fsdp_count)
    out_wgrad = swap_rows(out_wgrad, heads_count, fsdp_count)
    normed1_grad = (
        dot_cols(q_raw_grad, query_full)
        + dot_cols(k_raw_grad, key_full)
        + dot_cols(value_back, value_full)
    )
    query_sum, key_sum, value_sum, out_sum = (
        lax.psum_scatter(query_wgrad, ("fsdp", "heads", "tensor"), scatter_dimension=1, tiled=True),
        lax.psum_scatter(key_wgrad, ("fsdp", "heads", "tensor"), scatter_dimension=1, tiled=True),
        lax.psum_scatter(value_wgrad, ("fsdp", "heads", "tensor"), scatter_dimension=1, tiled=True),
        lax.psum_scatter(out_wgrad, ("fsdp", "heads", "tensor"), scatter_dimension=0, tiled=True),
    )
    tokens_grad = resid_grad + norm_back(inputs, scale1, norm1_gain, normed1_grad)
    gain1_part = jnp.sum(normed1_grad * inputs * scale1, axis=0)
    gain1_sum, qgain_sum, kgain_sum, gain2_sum = lax.psum(
        (gain1_part, qgain_part, kgain_part, gain2_part), ("fsdp", "heads", "tensor")
    )
    return (
        output,
        tokens_grad,
        gain1_sum,
        query_sum,
        key_sum,
        value_sum,
        qgain_sum,
        kgain_sum,
        out_sum,
        gain2_sum,
        gate_sum,
        up_sum,
        down_sum,
    )


def plain_solution(mesh):
    return jax.shard_map(
        plain_layer,
        mesh=mesh,
        in_specs=(
            P(("fsdp", "heads", "tensor"), None),
            P(("fsdp", "heads", "tensor"), None),
            P(("fsdp", "tensor"), None),
            P(("fsdp", "tensor"), None),
            P(),
            P(None, ("heads", "fsdp", "tensor")),
            P(None, ("heads", "fsdp", "tensor")),
            P(None, ("heads", "fsdp", "tensor")),
            P(),
            P(),
            P(("heads", "fsdp", "tensor"), None),
            P(),
            P(("fsdp", "heads"), "tensor"),
            P(("fsdp", "heads"), "tensor"),
            P("tensor", ("fsdp", "heads")),
        ),
        out_specs=(
            P(("fsdp", "heads", "tensor"), None),
            P(("fsdp", "heads", "tensor"), None),
            P(),
            P(None, ("heads", "fsdp", "tensor")),
            P(None, ("heads", "fsdp", "tensor")),
            P(None, ("heads", "fsdp", "tensor")),
            P(),
            P(),
            P(("heads", "fsdp", "tensor"), None),
            P(),
            P(("fsdp", "heads"), "tensor"),
            P(("fsdp", "heads"), "tensor"),
            P("tensor", ("fsdp", "heads")),
        ),
        check_vma=False,
    )


VMEM_LIMIT = 56 * 1024 * 1024
SWAP = ((0, 1), (1, 0))
ROW_TILE = 256
SCALE = HEAD_SIZE ** (-0.5)


def dot_t(left, right):
    return lax.dot_general(
        left, right, (((1,), (1,)), ((), ())), preferred_element_type=jnp.float32
    )


def swap(array, axis):
    return lax.ppermute(array, axis, SWAP)


def pick(first, second, index):
    return jnp.where(index == 0, first, second)


def join(mine, other, index, axis):
    return pick(
        jnp.concatenate([mine, other], axis=axis),
        jnp.concatenate([other, mine], axis=axis),
        index,
    )


def gather_z(array):
    return lax.all_gather(array, "z", axis=0, tiled=True)


def scatter_z(array):
    return lax.psum_scatter(array, "z", scatter_dimension=0, tiled=True)


def four_pieces(own, via):
    along_x, along_y = swap(own, "x"), swap(own, "y")
    corner = swap(along_y, "x") if via == "x" else swap(along_x, "y")
    return [own, along_x, along_y, corner]


def add_pieces(pieces, via):
    own, along_x, along_y, corner = pieces
    if via == "x":
        along_y = along_y + swap(corner, "x")
    else:
        along_x = along_x + swap(corner, "y")
    return own + swap(along_x, "x") + swap(along_y, "y")


def to_core(array, core):
    half = array.shape[0] // 2
    first, second = array[:half], array[half:]
    other = swap(pick(second, first, core), "c")
    return join(pick(first, second, core), other, core, 1)


def from_core(array, core):
    half = array.shape[1] // 2
    first, second = array[:, :half], array[:, half:]
    other = swap(pick(second, first, core), "c")
    return join(pick(first, second, core), other, core, 0)


def params(flops, bytes_accessed):
    return dict(
        compiler_params=pltpu.CompilerParams(vmem_limit_bytes=VMEM_LIMIT),
        cost_estimate=pl.CostEstimate(
            flops=flops, bytes_accessed=bytes_accessed, transcendentals=0
        ),
    )


def reorder_kernel(order_ref, in_ref, out_ref):
    out_ref[...] = in_ref[...]


def reorder(array, order):
    rows, width = array.shape
    parts = order.shape[0]
    return pl.pallas_call(
        reorder_kernel,
        grid_spec=pltpu.PrefetchScalarGridSpec(
            num_scalar_prefetch=1,
            grid=(parts,),
            in_specs=[pl.BlockSpec((rows, width // parts), lambda i, o: (0, o[i]))],
            out_specs=pl.BlockSpec((rows, width // parts), lambda i, o: (0, i)),
        ),
        out_shape=jax.ShapeDtypeStruct(array.shape, array.dtype),
        name="reorder",
        **params(0, 2 * array.size * array.dtype.itemsize),
    )(order, array)


def head_norm(raw, gain):
    scale = lax.rsqrt(jnp.mean(raw * raw, axis=-1, keepdims=True) + EPS_NORM)
    return raw * scale * gain


def turn(value, cos_tab, sin_tab):
    return value * cos_tab + pltpu.roll(value, HEAD_SIZE // 2, 1) * sin_tab


def heads_kernel(raw_ref, cos_ref, sin_ref, qgain_ref, kgain_ref, q_ref, k_ref, v_ref):
    raw = raw_ref[...]
    cos_tab, sin_tab = cos_ref[...], sin_ref[...]
    for head in range(2):
        at = slice(head * HEAD_SIZE, (head + 1) * HEAD_SIZE)
        q_ref[:, at] = turn(head_norm(raw[:, at], qgain_ref[...]), cos_tab, sin_tab).astype(
            jnp.bfloat16
        )
    k_raw = raw[:, 2 * HEAD_SIZE : 3 * HEAD_SIZE]
    k_ref[...] = turn(head_norm(k_raw, kgain_ref[...]), cos_tab, sin_tab).astype(jnp.bfloat16)
    v_ref[...] = raw[:, 3 * HEAD_SIZE :].astype(jnp.bfloat16)


def make_heads(raw, cos_tab, sin_tab, query_gain, key_gain):
    rows, width = raw.shape
    count = width // (4 * HEAD_SIZE)
    table = pl.BlockSpec((ROW_TILE, HEAD_SIZE), lambda i, r: (i, 0))
    gain = pl.BlockSpec((1, HEAD_SIZE), lambda i, r: (0, 0))
    one = pl.BlockSpec((ROW_TILE, HEAD_SIZE), lambda i, r: (i, r))
    return pl.pallas_call(
        heads_kernel,
        grid=(rows // ROW_TILE, count),
        in_specs=[
            pl.BlockSpec((ROW_TILE, 4 * HEAD_SIZE), lambda i, r: (i, r)),
            table,
            table,
            gain,
            gain,
        ],
        out_specs=[pl.BlockSpec((ROW_TILE, 2 * HEAD_SIZE), lambda i, r: (i, r)), one, one],
        out_shape=[
            jax.ShapeDtypeStruct((rows, count * 2 * HEAD_SIZE), jnp.bfloat16),
            jax.ShapeDtypeStruct((rows, count * HEAD_SIZE), jnp.bfloat16),
            jax.ShapeDtypeStruct((rows, count * HEAD_SIZE), jnp.bfloat16),
        ],
        name="make_heads",
        **params(0, raw.size * 6),
    )(raw, cos_tab, sin_tab, query_gain[None, :], key_gain[None, :])


def heads_back_kernel(
    raw_ref,
    dq_ref,
    dk_ref,
    dk_far_ref,
    dv_ref,
    dv_far_ref,
    cos_ref,
    sin_ref,
    qgain_ref,
    kgain_ref,
    out_ref,
    gain_ref,
):
    raw = raw_ref[...]
    cos_tab, sin_tab = cos_ref[...], sin_ref[...]

    @pl.when((pl.program_id(0) == 0) & (pl.program_id(1) == 0))
    def _():
        gain_ref[...] = jnp.zeros_like(gain_ref)

    def back(value, upstream, gain):
        turned = upstream * cos_tab - pltpu.roll(upstream, HEAD_SIZE // 2, 1) * sin_tab
        scale = lax.rsqrt(jnp.mean(value * value, axis=-1, keepdims=True) + EPS_NORM)
        hat = value * scale
        weighted = turned * gain
        inner = jnp.mean(hat * weighted, axis=-1, keepdims=True)
        grad = scale * (weighted - hat * inner)
        return grad.astype(jnp.bfloat16), jnp.sum(turned * hat, axis=0, keepdims=True)

    q_sum = jnp.zeros((1, HEAD_SIZE), jnp.float32)
    for head in range(2):
        at = slice(head * HEAD_SIZE, (head + 1) * HEAD_SIZE)
        grad, part = back(raw[:, at], dq_ref[:, at].astype(jnp.float32), qgain_ref[...])
        out_ref[:, at] = grad
        q_sum = q_sum + part
    key_up = dk_ref[...].astype(jnp.float32) + dk_far_ref[...].astype(jnp.float32)
    grad, k_sum = back(raw[:, 2 * HEAD_SIZE : 3 * HEAD_SIZE], key_up, kgain_ref[...])
    out_ref[:, 2 * HEAD_SIZE : 3 * HEAD_SIZE] = grad
    out_ref[:, 3 * HEAD_SIZE :] = (
        dv_ref[...].astype(jnp.float32) + dv_far_ref[...].astype(jnp.float32)
    ).astype(jnp.bfloat16)
    gain_ref[0:1, :] += q_sum
    gain_ref[1:2, :] += k_sum


def heads_return(raw, dq, dk, dk_far, dv, dv_far, cos_tab, sin_tab, query_gain, key_gain):
    rows, width = raw.shape
    count = width // (4 * HEAD_SIZE)
    table = pl.BlockSpec((ROW_TILE, HEAD_SIZE), lambda i, r: (i, 0))
    gain = pl.BlockSpec((1, HEAD_SIZE), lambda i, r: (0, 0))
    one = pl.BlockSpec((ROW_TILE, HEAD_SIZE), lambda i, r: (i, r))
    far = pl.BlockSpec((ROW_TILE, HEAD_SIZE), lambda i, r: (i, (r + 2) % 4))
    full = pl.BlockSpec((ROW_TILE, 4 * HEAD_SIZE), lambda i, r: (i, r))
    return pl.pallas_call(
        heads_back_kernel,
        grid=(rows // ROW_TILE, count),
        in_specs=[
            full,
            pl.BlockSpec((ROW_TILE, 2 * HEAD_SIZE), lambda i, r: (i, r)),
            one,
            far,
            one,
            far,
            table,
            table,
            gain,
            gain,
        ],
        out_specs=[full, pl.BlockSpec((8, HEAD_SIZE), lambda i, r: (0, 0))],
        out_shape=[
            jax.ShapeDtypeStruct((rows, width), jnp.bfloat16),
            jax.ShapeDtypeStruct((8, HEAD_SIZE), jnp.float32),
        ],
        name="heads_return",
        **params(0, raw.size * 8),
    )(raw, dq, dk, dk_far, dv, dv_far, cos_tab, sin_tab, query_gain[None, :], key_gain[None, :])


def stack_heads(block):
    return jnp.concatenate([block[:, :HEAD_SIZE], block[:, HEAD_SIZE:]], axis=0)


def pair_mask(first_key, row_block, pair, parity):
    rows = lax.broadcasted_iota(jnp.int32, (2 * BLK, 2 * BLK), 0)
    cols = lax.broadcasted_iota(jnp.int32, (2 * BLK, 2 * BLK), 1)
    row_at = row_block * BLK + lax.rem(rows, BLK)
    key_block = 2 * pair + jnp.where(cols < BLK, parity, 1 - parity)
    key_at = key_block * BLK + lax.rem(cols, BLK)
    return (key_at <= row_at) & (key_at >= first_key * BLK)


def attend_kernel(info_ref, q_ref, ko_ref, vo_ref, kf_ref, vf_ref, o_ref, l_ref):
    group = pl.program_id(0)
    blocks = q_ref.shape[0] // BLK
    parity = info_ref[group, blocks]

    def one_block(j, _):
        first_key = info_ref[group, j]
        rows = pl.ds(pl.multiple_of(j * BLK, BLK), BLK)
        query = stack_heads(q_ref[rows, :])

        def one_pair(m, carry):
            total, acc = carry
            at = pl.ds(pl.multiple_of(m * BLK, BLK), BLK)
            key = jnp.concatenate([ko_ref[at, :], kf_ref[at, :]], axis=0)
            value = jnp.concatenate([vo_ref[at, :], vf_ref[at, :]], axis=0)
            score = dot_t(query, key) * SCALE
            expo = jnp.where(
                pair_mask(first_key, 2 * j + parity, m, parity), jnp.exp(score), 0.0
            )
            total = total + jnp.sum(expo, axis=1, keepdims=True)
            acc = acc + matrix_product(expo.astype(jnp.bfloat16), value)
            return total, acc

        total, acc = lax.fori_loop(
            lax.div(first_key, 2),
            j + 1,
            one_pair,
            (jnp.zeros((2 * BLK, 1), jnp.float32), jnp.zeros((2 * BLK, HEAD_SIZE), jnp.float32)),
        )
        out = (acc / total).astype(jnp.bfloat16)
        o_ref[rows, :HEAD_SIZE] = out[:BLK]
        o_ref[rows, HEAD_SIZE:] = out[BLK:]
        lane = lax.broadcasted_iota(jnp.int32, (BLK, HEAD_SIZE), 1)
        l_ref[rows, :] = jnp.where(lane == 0, total[:BLK], total[BLK:])
        return 0

    lax.fori_loop(0, blocks, one_block, 0)


def attend(info, query, key, value, key_far, value_far):
    groups = 2
    rows = query.shape[0] // groups
    count = key.shape[1] // HEAD_SIZE
    own = pl.BlockSpec((rows, HEAD_SIZE), lambda g, r, s: (g, r))
    far = pl.BlockSpec((rows, HEAD_SIZE), lambda g, r, s: (g, (r + 2) % 4))
    wide = pl.BlockSpec((rows, 2 * HEAD_SIZE), lambda g, r, s: (g, r))
    return pl.pallas_call(
        attend_kernel,
        grid_spec=pltpu.PrefetchScalarGridSpec(
            num_scalar_prefetch=1,
            grid=(groups, count),
            in_specs=[wide, own, own, far, far],
            out_specs=[wide, own],
        ),
        out_shape=[
            jax.ShapeDtypeStruct(query.shape, jnp.bfloat16),
            jax.ShapeDtypeStruct(key.shape, jnp.float32),
        ],
        name="attend",
        **params(20_000_000_000, 40_000_000),
    )(info, query, key, value, key_far, value_far)


def attend_back_kernel(
    info_ref,
    q_ref,
    do_ref,
    o_ref,
    l_ref,
    ko_ref,
    vo_ref,
    kf_ref,
    vf_ref,
    dq_ref,
    dko_ref,
    dvo_ref,
    dkf_ref,
    dvf_ref,
    kacc_ref,
    vacc_ref,
):
    group = pl.program_id(0)
    blocks = q_ref.shape[0] // BLK
    parity = info_ref[group, blocks]
    kacc_ref[...] = jnp.zeros_like(kacc_ref)
    vacc_ref[...] = jnp.zeros_like(vacc_ref)

    def one_block(j, _):
        first_key = info_ref[group, j]
        rows = pl.ds(pl.multiple_of(j * BLK, BLK), BLK)
        query = stack_heads(q_ref[rows, :])
        attn = stack_heads(o_ref[rows, :]).astype(jnp.float32)
        grad = stack_heads(do_ref[rows, :]).astype(jnp.float32)
        total = jnp.concatenate([l_ref[rows, 0:1], l_ref[rows, 1:2]], axis=0)
        grad_b = (grad / total).astype(jnp.bfloat16)
        inner = jnp.sum(grad_b.astype(jnp.float32) * attn, axis=1, keepdims=True)

        def one_pair(m, dq):
            at = pl.ds(pl.multiple_of(m * BLK, BLK), BLK)
            key = jnp.concatenate([ko_ref[at, :], kf_ref[at, :]], axis=0)
            value = jnp.concatenate([vo_ref[at, :], vf_ref[at, :]], axis=0)
            score = dot_t(query, key) * SCALE
            expo = jnp.where(
                pair_mask(first_key, 2 * j + parity, m, parity), jnp.exp(score), 0.0
            )
            d_score = (expo * (dot_t(grad_b, value) - inner)).astype(jnp.bfloat16)
            d_key = dot_rows(d_score, query)
            d_value = dot_rows(expo.astype(jnp.bfloat16), grad_b)
            kacc_ref[0, at, :] += d_key[:BLK]
            kacc_ref[1, at, :] += d_key[BLK:]
            vacc_ref[0, at, :] += d_value[:BLK]
            vacc_ref[1, at, :] += d_value[BLK:]
            return dq + matrix_product(d_score, key)

        dq = lax.fori_loop(
            lax.div(first_key, 2), j + 1, one_pair, jnp.zeros((2 * BLK, HEAD_SIZE), jnp.float32)
        )
        dq = (dq * SCALE).astype(jnp.bfloat16)
        dq_ref[rows, :HEAD_SIZE] = dq[:BLK]
        dq_ref[rows, HEAD_SIZE:] = dq[BLK:]
        return 0

    lax.fori_loop(0, blocks, one_block, 0)
    dko_ref[...] = (kacc_ref[0] * SCALE).astype(jnp.bfloat16)
    dkf_ref[...] = (kacc_ref[1] * SCALE).astype(jnp.bfloat16)
    dvo_ref[...] = vacc_ref[0].astype(jnp.bfloat16)
    dvf_ref[...] = vacc_ref[1].astype(jnp.bfloat16)


def attend_back(info, query, d_attn, attn, total, key, value, key_far, value_far):
    groups = 2
    rows = query.shape[0] // groups
    count = key.shape[1] // HEAD_SIZE
    own = pl.BlockSpec((rows, HEAD_SIZE), lambda g, r, s: (g, r))
    far = pl.BlockSpec((rows, HEAD_SIZE), lambda g, r, s: (g, (r + 2) % 4))
    wide = pl.BlockSpec((rows, 2 * HEAD_SIZE), lambda g, r, s: (g, r))
    narrow = jax.ShapeDtypeStruct(key.shape, jnp.bfloat16)
    return pl.pallas_call(
        attend_back_kernel,
        grid_spec=pltpu.PrefetchScalarGridSpec(
            num_scalar_prefetch=1,
            grid=(groups, count),
            in_specs=[wide, wide, wide, own, own, own, far, far],
            out_specs=[wide, own, own, own, own],
            scratch_shapes=[
                pltpu.VMEM((2, rows, HEAD_SIZE), jnp.float32),
                pltpu.VMEM((2, rows, HEAD_SIZE), jnp.float32),
            ],
        ),
        out_shape=[
            jax.ShapeDtypeStruct(query.shape, jnp.bfloat16),
            narrow,
            narrow,
            narrow,
            narrow,
        ],
        name="attend_back",
        **params(50_000_000_000, 60_000_000),
    )(info, query, d_attn, attn, total, key, value, key_far, value_far)


HIDDEN_TILE = 256
ROW_STEP = 512


def ffn_up_kernel(x_ref, g0, g1, g2, g3, u0, u1, u2, u3, act_ref, dgate_ref, silu_ref):
    depth = g0.shape[1]
    for first in range(0, x_ref.shape[0], ROW_STEP):
        rows = slice(first, first + ROW_STEP)
        gate = jnp.zeros((ROW_STEP, HIDDEN_TILE), jnp.float32)
        upper = jnp.zeros((ROW_STEP, HIDDEN_TILE), jnp.float32)
        for i, (g, u) in enumerate(((g0, u0), (g1, u1), (g2, u2), (g3, u3))):
            x = x_ref[rows, i * depth : (i + 1) * depth]
            gate = gate + dot_t(x, g[...])
            upper = upper + dot_t(x, u[...])
        sig = 1.0 / (1.0 + jnp.exp(-gate))
        silu = gate * sig
        act_ref[rows, :] = (silu * upper).astype(jnp.bfloat16)
        silu_ref[rows, :] = silu.astype(jnp.bfloat16)
        dgate_ref[rows, :] = (upper * sig * (1.0 + gate * (1.0 - sig))).astype(jnp.bfloat16)


def ffn_up(x, gates, ups):
    rows, width = x.shape
    hidden, depth = gates[0].shape
    weight = pl.BlockSpec((HIDDEN_TILE, depth), lambda j: (j, 0))
    out = pl.BlockSpec((rows, HIDDEN_TILE), lambda j: (0, j))
    shape = jax.ShapeDtypeStruct((rows, hidden), jnp.bfloat16)
    return pl.pallas_call(
        ffn_up_kernel,
        grid=(hidden // HIDDEN_TILE,),
        in_specs=[pl.BlockSpec((rows, width), lambda j: (0, 0))] + [weight] * 8,
        out_specs=[out] * 3,
        out_shape=[shape] * 3,
        name="ffn_up",
        **params(4 * rows * width * hidden, 70_000_000),
    )(x, *gates, *ups)


def ffn_back_kernel(dy_ref, w_ref, dgate_ref, silu_ref, gate_ref, up_ref):
    for first in range(0, dy_ref.shape[0], ROW_STEP):
        rows = slice(first, first + ROW_STEP)
        d_act = dot_t(dy_ref[rows, :], w_ref[...])
        gate_ref[rows, :] = (d_act * dgate_ref[rows, :].astype(jnp.float32)).astype(jnp.bfloat16)
        up_ref[rows, :] = (d_act * silu_ref[rows, :].astype(jnp.float32)).astype(jnp.bfloat16)


def ffn_back(dy, w_down, dgate, silu):
    rows, width = dy.shape
    hidden = w_down.shape[0]
    out = pl.BlockSpec((rows, HIDDEN_TILE), lambda j: (0, j))
    shape = jax.ShapeDtypeStruct((rows, hidden), jnp.bfloat16)
    return pl.pallas_call(
        ffn_back_kernel,
        grid=(hidden // HIDDEN_TILE,),
        in_specs=[
            pl.BlockSpec((rows, width), lambda j: (0, 0)),
            pl.BlockSpec((HIDDEN_TILE, width), lambda j: (j, 0)),
            out,
            out,
        ],
        out_specs=[out] * 2,
        out_shape=[shape] * 2,
        name="ffn_back",
        **params(2 * rows * width * hidden, 70_000_000),
    )(dy, w_down, dgate, silu)


def block_info(lengths, positions, first):
    count = (lengths + BLK - 1) // BLK
    ends = jnp.cumsum(count)
    starts = jnp.concatenate([jnp.zeros((1,), jnp.int32), ends])
    own = lax.dynamic_slice_in_dim(positions, first, 8)
    first_keys = jnp.max(jnp.where(starts[None, :] <= own[:, None], starts[None, :], 0), axis=1)
    limits = jnp.concatenate([lengths, jnp.zeros((1,), jnp.int32)])
    seq = jnp.sum((own[:, None] >= ends[None, :]).astype(jnp.int32), axis=1)
    limit = jnp.sum(jnp.where(seq[:, None] == jnp.arange(4)[None, :], limits[None, :], 0), axis=1)
    pos = ((own - first_keys)[:, None] * BLK + jnp.arange(BLK)[None, :]).astype(jnp.int32)
    valid = pos < limit[:, None]
    return first_keys, own, pos.reshape(-1), valid.reshape(-1)


def chip_layer(
    tokens,
    cotangent,
    seq_lens,
    block_pos,
    norm1_gain,
    w_query,
    key_matrix,
    value_matrix,
    query_gain,
    key_gain,
    w_out,
    norm2_gain,
    w_gate,
    w_up,
    w_down,
):
    xi, core, yi = lax.axis_index("x"), lax.axis_index("c"), lax.axis_index("y")
    rows, width = tokens.shape
    bf16, f32 = jnp.bfloat16, jnp.float32

    q_in, k_in = w_query.shape[1], key_matrix.shape[1]
    attn_shard = jnp.concatenate([w_query.T, key_matrix.T, value_matrix.T, w_out], axis=0)
    attn_w = four_pieces(gather_z(attn_shard), "x")
    attn_w = [a.reshape(4, attn_shard.shape[0], width) for a in attn_w]

    def part(first, last):
        return [a[:, first:last].reshape(-1, width) for a in attn_w]

    q_w, k_w = part(0, q_in), part(q_in, q_in + k_in)
    v_w, o_w = part(q_in + k_in, q_in + 2 * k_in), part(q_in + 2 * k_in, attn_shard.shape[0])
    qkv_w = jnp.concatenate([w for trio in zip(q_w, k_w, v_w) for w in trio], axis=0)
    out_w = jnp.concatenate(o_w, axis=0)
    gate_w = four_pieces(gather_z(to_core(w_gate.T, core)), "y")
    up_w = four_pieces(gather_z(to_core(w_up.T, core)), "x")
    down_w = gather_z(jnp.concatenate(four_pieces(to_core(w_down, core), "y"), axis=1))

    lengths_here = jnp.concatenate([seq_lens[0], block_pos[0]]).astype(f32)
    lengths_there = swap(lengths_here[None, :], "c")[0].astype(jnp.int32)
    first_own = yi * 8
    keys_here, at_here, pos_here, valid_here = block_info(seq_lens[0], block_pos[0], first_own)
    keys_there, at_there, pos_there, _ = block_info(
        lengths_there[:3], lengths_there[3:], first_own
    )
    info = jnp.stack(
        [
            jnp.concatenate([keys_here, at_here[:1]]),
            jnp.concatenate([keys_there, at_there[:1]]),
        ]
    ).astype(jnp.int32)
    freq = jnp.exp(
        jnp.arange(HEAD_SIZE // 2, dtype=f32) * (-2.0 * math.log(ROPE_BASE) / HEAD_SIZE)
    )
    angles = jnp.concatenate([pos_here, pos_there]).astype(f32)[:, None] * freq[None, :]
    cos_half, sin_half = jnp.cos(angles), jnp.sin(angles)
    cos_tab = jnp.concatenate([cos_half, cos_half], axis=1)
    sin_tab = jnp.concatenate([-sin_half, sin_half], axis=1)
    valid = valid_here.astype(f32)[:, None]

    blocks = jnp.arange(8)
    ry, rx, rc = blocks // 4, (blocks // 2) % 2, blocks % 2
    order = ((rx ^ xi) * 4 + rc * 2 + (ry ^ yi)).astype(jnp.int32)
    nx, nc, ny = blocks // 4, (blocks // 2) % 2, blocks % 2
    order_back = ((ny ^ yi) * 4 + (nx ^ xi) * 2 + nc).astype(jnp.int32)

    def both(own):
        return jnp.concatenate([own, swap(own, "c")], axis=0)

    inputs = tokens.astype(f32)
    first_normed, scale1 = rms_parts(inputs, norm1_gain)
    normed1 = both(first_normed.astype(bf16))
    grad_out = valid * cotangent.astype(f32)
    dy = both(reorder(grad_out.astype(bf16), order))

    raw = dot_t(normed1, qkv_w)
    query, key, value = make_heads(raw, cos_tab, sin_tab, query_gain, key_gain)
    key_far, value_far = swap(key, "y"), swap(value, "y")
    attn, totals = attend(info, query, key, value, key_far, value_far)
    out_there = swap(matrix_product(attn[rows:], out_w).astype(bf16), "c")
    resid = inputs + matrix_product(attn[:rows], out_w) + out_there.astype(f32)
    normed2, scale2 = rms_parts(resid, norm2_gain)
    normed2_b = both(reorder(normed2.astype(bf16), order))

    act, dgate, silu = ffn_up(normed2_b, gate_w, up_w)
    mixed_there = swap(matrix_product(act[rows:], down_w).astype(bf16), "c")
    mixed = (matrix_product(act[:rows], down_w) + mixed_there.astype(f32)).astype(bf16)
    output = (valid * (resid + reorder(mixed, order_back).astype(f32))).astype(bf16)

    down_sum = scatter_z(dot_rows(act, dy).astype(bf16))
    fourth = width // 4
    down_sum = add_pieces([down_sum[:, i * fourth : (i + 1) * fourth] for i in range(4)], "x")
    gate_grad, up_grad = ffn_back(dy, down_w, dgate, silu)
    pieces = [normed2_b[:, i * fourth : (i + 1) * fourth] for i in range(4)]
    gate_sum = scatter_z(add_pieces([dot_rows(gate_grad, p).astype(bf16) for p in pieces], "y"))
    up_sum = scatter_z(add_pieces([dot_rows(up_grad, p).astype(bf16) for p in pieces], "x"))

    def back_term(first):
        g, u = gate_grad[first : first + rows], up_grad[first : first + rows]
        return jnp.concatenate(
            [(matrix_product(g, a) + matrix_product(u, b)).astype(bf16) for a, b in zip(gate_w, up_w)],
            axis=1,
        )

    normed2_there = swap(back_term(rows), "c")
    normed2_grad = reorder(
        (back_term(0).astype(f32) + normed2_there.astype(f32)).astype(bf16), order_back
    ).astype(f32)
    resid_grad = grad_out + norm_back(resid, scale2, norm2_gain, normed2_grad)
    gain2_part = jnp.sum(normed2_grad * resid * scale2, axis=0)
    resid_grad_b = both(resid_grad.astype(bf16))
    d_attn = dot_t(resid_grad_b, out_w).astype(bf16)
    dq, dk, dv, dk_far, dv_far = attend_back(
        info, query, d_attn, attn, totals, key, value, key_far, value_far
    )
    dk_back, dv_back = swap(dk_far, "y"), swap(dv_far, "y")
    raw_grad, head_gains = heads_return(
        raw, dq, dk, dk_back, dv, dv_back, cos_tab, sin_tab, query_gain, key_gain
    )

    out_span, qkv_span = out_w.shape[0] // 4, qkv_w.shape[0] // 4
    out_sum = scatter_z(
        add_pieces(
            [
                dot_rows(attn[:, i * out_span : (i + 1) * out_span], resid_grad_b).astype(bf16)
                for i in range(4)
            ],
            "y",
        )
    )
    qkv_sum = add_pieces(
        [
            dot_rows(raw_grad[:, i * qkv_span : (i + 1) * qkv_span], normed1).astype(bf16)
            for i in range(4)
        ],
        "x",
    )
    q_rows, k_rows = 4 * q_in, 4 * k_in
    qkv_sum = scatter_z(
        jnp.concatenate(
            [
                qkv_sum[:q_rows].reshape(4, q_in, width),
                qkv_sum[q_rows : q_rows + k_rows].reshape(4, k_in, width),
                qkv_sum[q_rows + k_rows :].reshape(4, k_in, width),
            ],
            axis=1,
        ).reshape(-1, width)
    ).astype(f32)

    normed1_there = swap(matrix_product(raw_grad[rows:], qkv_w).astype(bf16), "c")
    normed1_grad = matrix_product(raw_grad[:rows], qkv_w) + normed1_there.astype(f32)
    tokens_grad = resid_grad + norm_back(inputs, scale1, norm1_gain, normed1_grad)
    gain1_part = jnp.sum(normed1_grad * inputs * scale1, axis=0)
    gains = jnp.concatenate([gain1_part, gain2_part, head_gains[0], head_gains[1]])[None, :]
    for axis in ("c", "x", "y"):
        gains = gains + swap(gains, axis)
    for step in (1, 2):
        gains = gains + lax.ppermute(gains, "z", [(i, i ^ step) for i in range(4)])
    gains = gains[0]

    return (
        output,
        tokens_grad,
        gains[:width],
        qkv_sum[:q_in].T,
        qkv_sum[q_in : q_in + k_in].T,
        qkv_sum[q_in + k_in :].T,
        gains[2 * width : 2 * width + HEAD_SIZE],
        gains[2 * width + HEAD_SIZE :],
        out_sum.astype(f32),
        gains[width : 2 * width],
        from_core(gate_sum, core).astype(f32).T,
        from_core(up_sum, core).astype(f32).T,
        from_core(down_sum, core).astype(f32),
    )


def chip_solution(mesh):
    fine = Mesh(mesh.devices.reshape(2, 2, 2, 4), ("x", "c", "y", "z"))
    row_spec = P(("x", "c", "y", "z"), None)
    group_spec = P(("x", "c", "z"), None)
    head_cols = P(None, ("y", "x", "c", "z"))
    head_rows = P(("y", "x", "c", "z"), None)
    up_spec, down_spec = P(("x", "c", "y"), "z"), P("z", ("x", "c", "y"))
    return jax.shard_map(
        chip_layer,
        mesh=fine,
        in_specs=(
            row_spec,
            row_spec,
            group_spec,
            group_spec,
            P(),
            head_cols,
            head_cols,
            head_cols,
            P(),
            P(),
            head_rows,
            P(),
            up_spec,
            up_spec,
            down_spec,
        ),
        out_specs=(
            row_spec,
            row_spec,
            P(),
            head_cols,
            head_cols,
            head_cols,
            P(),
            P(),
            head_rows,
            P(),
            up_spec,
            up_spec,
            down_spec,
        ),
        check_vma=False,
    )


def solution(mesh):
    sizes = dict(mesh.shape)
    if sizes == {"fsdp": 4, "heads": 2, "tensor": 4}:
        return chip_solution(mesh)
    return plain_solution(mesh)
```

```python
import functools
import math

import jax
import jax.numpy as jnp
from jax import lax
from jax.experimental import pallas as pl
from jax.experimental.pallas import tpu as pltpu
from jax.sharding import Mesh
from jax.sharding import PartitionSpec as P

QUERY_HEADS = 16
KEY_VALUE_HEADS = 8
HEAD_SIZE = 128
BLK = 128


EPS_NORM = 1e-06
ROPE_BASE = 1000000.0
NEG_FILL = -1e30


def row_info(lengths, positions):
    block_count = (lengths + BLK - 1) // BLK
    ends = jnp.cumsum(block_count)
    starts = ends - block_count
    used = ends[-1]
    column = positions[:, None]
    inside = (column >= starts[None, :]) & (column < ends[None, :])
    past = positions >= used
    seq_block = jnp.sum((column >= ends[None, :]).astype(jnp.int32), axis=1)
    first_block = jnp.sum(jnp.where(inside, starts[None, :], 0), axis=1) + jnp.where(past, used, 0)
    limit = jnp.sum(jnp.where(inside, lengths[None, :], 0), axis=1)
    offsets = jnp.arange(BLK, dtype=jnp.int32)[None, :]
    pos_rows = (positions - first_block)[:, None] * BLK + offsets
    seq_rows = jnp.broadcast_to(seq_block[:, None], pos_rows.shape)
    valid_rows = jnp.logical_not(past)[:, None] & (pos_rows < limit[:, None])
    return (seq_rows.reshape(-1), pos_rows.reshape(-1), valid_rows.reshape(-1))


def rope_tables(pos_rows):
    half_dim = HEAD_SIZE // 2
    freq = jnp.exp(
        jnp.arange(half_dim, dtype=jnp.float32) * (-2.0 * math.log(ROPE_BASE) / HEAD_SIZE)
    )
    angles = pos_rows.astype(jnp.float32)[:, None] * freq[None, :]
    return (jnp.cos(angles)[:, None, :], jnp.sin(angles)[:, None, :])


def rotate(value_rows, cos_tab, sin_tab):
    half_dim = value_rows.shape[-1] // 2
    first_half, second_half = (value_rows[..., :half_dim], value_rows[..., half_dim:])
    return jnp.concatenate(
        [
            first_half * cos_tab - second_half * sin_tab,
            second_half * cos_tab + first_half * sin_tab,
        ],
        axis=-1,
    )


def unrotate(upstream, cos_tab, sin_tab):
    half_dim = upstream.shape[-1] // 2
    first_half, second_half = (upstream[..., :half_dim], upstream[..., half_dim:])
    return jnp.concatenate(
        [
            first_half * cos_tab + second_half * sin_tab,
            second_half * cos_tab - first_half * sin_tab,
        ],
        axis=-1,
    )


def rms_parts(value_rows, gain_vec):
    scales = lax.rsqrt(jnp.mean(value_rows * value_rows, axis=-1, keepdims=True) + EPS_NORM)
    return (value_rows * scales * gain_vec, scales)


def norm_back(value_rows, scales, gain_vec, upstream):
    weighted = upstream * gain_vec
    inner = jnp.sum(value_rows * weighted, axis=-1, keepdims=True) / value_rows.shape[-1]
    return scales * weighted - value_rows * scales * scales * scales * inner


def matrix_product(left, right):
    return jnp.dot(left, right, preferred_element_type=jnp.float32)


def dot_rows(left, right):
    return lax.dot_general(
        left, right, (((0,), (0,)), ((), ())), preferred_element_type=jnp.float32
    )


def dot_cols(left, right):
    return lax.dot_general(
        left, right, (((1,), (1,)), ((), ())), preferred_element_type=jnp.float32
    )


def swap_cols(array, outer, inner):
    lead = array.shape[0]
    return jnp.swapaxes(array.reshape(lead, outer, inner, -1), 1, 2).reshape(lead, -1)


def swap_rows(array, outer, inner):
    width = array.shape[1]
    return jnp.swapaxes(array.reshape(outer, inner, -1, width), 0, 1).reshape(-1, width)


def spread_rows(local_rows):
    return lax.all_gather(local_rows, "tensor", axis=0, tiled=True)


def to_heads(packed):
    return lax.all_to_all(packed, "heads", split_axis=1, concat_axis=0, tiled=True)


def to_rows(packed):
    return lax.all_to_all(packed, "heads", split_axis=0, concat_axis=1, tiled=True)


def tensor_sum(term, row_count):
    total = lax.psum(
        term(0, row_count * lax.axis_size("tensor")).astype(jnp.bfloat16), "tensor"
    ).astype(jnp.float32)
    return lax.dynamic_slice_in_dim(total, lax.axis_index("tensor") * row_count, row_count)


def block_scores(query_blk, key_all, seq_blk, pos_blk, seq_all, pos_all):
    scores = jnp.einsum(
        "qkgd,pkd->kgqp", query_blk, key_all, preferred_element_type=jnp.float32
    ) * HEAD_SIZE ** (-0.5)
    allowed = (seq_blk[:, None] == seq_all[None, :]) & (pos_all[None, :] <= pos_blk[:, None])
    return jnp.where(allowed[None, None], scores, NEG_FILL)


def attend_forward(query_grp, key_grp, value_grp, seq_all, pos_all):
    group_factor = QUERY_HEADS // KEY_VALUE_HEADS
    group_len = query_grp.shape[0]
    kv_local = key_grp.shape[1] // HEAD_SIZE
    query_four = query_grp.reshape(group_len, kv_local, group_factor, HEAD_SIZE)
    key_three = key_grp.reshape(group_len, kv_local, HEAD_SIZE)
    value_three = value_grp.reshape(group_len, kv_local, HEAD_SIZE)
    block_rows = min(512, group_len)

    def forward_block(block_idx):
        first_row = block_idx * block_rows
        query_blk = lax.dynamic_slice_in_dim(query_four, first_row, block_rows)
        seq_blk = lax.dynamic_slice_in_dim(seq_all, first_row, block_rows)
        pos_blk = lax.dynamic_slice_in_dim(pos_all, first_row, block_rows)
        scores = block_scores(query_blk, key_three, seq_blk, pos_blk, seq_all, pos_all)
        peak = jnp.max(scores, axis=-1, keepdims=True)
        expo = jnp.exp(scores - peak)
        total = jnp.sum(expo, axis=-1, keepdims=True)
        probs_b = (expo / total).astype(jnp.bfloat16)
        attended = jnp.einsum(
            "kgqp,pkd->qkgd", probs_b, value_three, preferred_element_type=jnp.float32
        )
        return (attended, (peak + jnp.log(total))[..., 0])

    attended, log_sums = lax.map(forward_block, jnp.arange(group_len // block_rows))
    return (
        attended.reshape(group_len, kv_local * group_factor * HEAD_SIZE).astype(jnp.bfloat16),
        log_sums,
    )


def attend_backward(query_grp, key_grp, value_grp, grad_grp, log_sums, seq_all, pos_all):
    group_factor = QUERY_HEADS // KEY_VALUE_HEADS
    scale = HEAD_SIZE ** (-0.5)
    group_len = query_grp.shape[0]
    kv_local = key_grp.shape[1] // HEAD_SIZE
    query_four = query_grp.reshape(group_len, kv_local, group_factor, HEAD_SIZE)
    key_three = key_grp.reshape(group_len, kv_local, HEAD_SIZE)
    value_three = value_grp.reshape(group_len, kv_local, HEAD_SIZE)
    grad_four = grad_grp.reshape(group_len, kv_local, group_factor, HEAD_SIZE)
    block_rows = min(512, group_len)

    def backward_block(carry, block_idx):
        key_acc, value_acc = carry
        first_row = block_idx * block_rows
        query_blk = lax.dynamic_slice_in_dim(query_four, first_row, block_rows)
        grad_blk = lax.dynamic_slice_in_dim(grad_four, first_row, block_rows)
        seq_blk = lax.dynamic_slice_in_dim(seq_all, first_row, block_rows)
        pos_blk = lax.dynamic_slice_in_dim(pos_all, first_row, block_rows)
        scores = block_scores(query_blk, key_three, seq_blk, pos_blk, seq_all, pos_all)
        probs = jnp.exp(scores - log_sums[block_idx][..., None])
        probs_b = probs.astype(jnp.bfloat16)
        prob_grad = jnp.einsum(
            "qkgd,pkd->kgqp", grad_blk, value_three, preferred_element_type=jnp.float32
        )
        score_grad_b = (
            probs * (prob_grad - jnp.sum(probs * prob_grad, axis=-1, keepdims=True))
        ).astype(jnp.bfloat16)
        query_grad = (
            jnp.einsum(
                "kgqp,pkd->qkgd", score_grad_b, key_three, preferred_element_type=jnp.float32
            )
            * scale
        )
        key_acc = (
            key_acc
            + jnp.einsum(
                "kgqp,qkgd->pkd", score_grad_b, query_blk, preferred_element_type=jnp.float32
            )
            * scale
        )
        value_acc = value_acc + jnp.einsum(
            "kgqp,qkgd->pkd", probs_b, grad_blk, preferred_element_type=jnp.float32
        )
        return ((key_acc, value_acc), query_grad)

    empty = jnp.zeros((group_len, kv_local, HEAD_SIZE), jnp.float32)
    (key_acc, value_acc), query_blocks = lax.scan(
        backward_block, (empty, empty), jnp.arange(group_len // block_rows)
    )
    query_grad_b = query_blocks.reshape(group_len, kv_local * group_factor * HEAD_SIZE).astype(
        jnp.bfloat16
    )
    key_grad_b = key_acc.reshape(group_len, kv_local * HEAD_SIZE).astype(jnp.bfloat16)
    value_grad_b = value_acc.reshape(group_len, kv_local * HEAD_SIZE).astype(jnp.bfloat16)
    return (query_grad_b, key_grad_b, value_grad_b)


def project_heads(normed_b, query_w, key_w, value_w, query_gain, key_gain, pos_rows):
    lines = normed_b.shape[0]
    q_raw = matrix_product(normed_b, query_w).reshape(lines, -1, HEAD_SIZE)
    key_unnormed = matrix_product(normed_b, key_w).reshape(lines, -1, HEAD_SIZE)
    value_b = matrix_product(normed_b, value_w).astype(jnp.bfloat16)
    cos_tab, sin_tab = rope_tables(pos_rows)
    q_normed, q_scale = rms_parts(q_raw, query_gain)
    k_normed, k_scale = rms_parts(key_unnormed, key_gain)
    query_b = rotate(q_normed, cos_tab, sin_tab).astype(jnp.bfloat16).reshape(lines, -1)
    key_b = rotate(k_normed, cos_tab, sin_tab).astype(jnp.bfloat16).reshape(lines, -1)
    return (query_b, key_b, value_b, (q_raw, q_scale, key_unnormed, k_scale, cos_tab, sin_tab))


def heads_back(query_back, key_back, kept, query_gain, key_gain):
    q_raw, q_scale, key_unnormed, k_scale, cos_tab, sin_tab = kept
    lines = q_raw.shape[0]
    q_turned = unrotate(query_back.astype(jnp.float32).reshape(q_raw.shape), cos_tab, sin_tab)
    k_turned = unrotate(key_back.astype(jnp.float32).reshape(key_unnormed.shape), cos_tab, sin_tab)
    q_raw_grad = (
        norm_back(q_raw, q_scale, query_gain, q_turned).reshape(lines, -1).astype(jnp.bfloat16)
    )
    k_raw_grad = (
        norm_back(key_unnormed, k_scale, key_gain, k_turned).reshape(lines, -1).astype(jnp.bfloat16)
    )
    qgain_part = jnp.sum(q_turned * q_raw * q_scale, axis=(0, 1))
    kgain_part = jnp.sum(k_turned * key_unnormed * k_scale, axis=(0, 1))
    return (q_raw_grad, k_raw_grad, qgain_part, kgain_part)


def plain_layer(
    tokens,
    cotangent,
    seq_lens,
    block_pos,
    norm1_gain,
    w_query,
    key_matrix,
    value_matrix,
    query_gain,
    key_gain,
    w_out,
    norm2_gain,
    w_gate,
    w_up,
    w_down,
):
    row_count = tokens.shape[0]
    fsdp_count = lax.axis_size("fsdp")
    heads_count = lax.axis_size("heads")
    gate_full, up_full, down_full = (
        lax.all_gather(w_gate, ("fsdp", "heads"), axis=0, tiled=True),
        lax.all_gather(w_up, ("fsdp", "heads"), axis=0, tiled=True),
        lax.all_gather(w_down, ("fsdp", "heads"), axis=1, tiled=True),
    )
    seq_all, pos_all, valid_all = row_info(seq_lens[0], block_pos[0])
    own_first = lax.axis_index("heads") * row_count
    pos_own = lax.dynamic_slice_in_dim(pos_all, own_first, row_count)
    valid_own = lax.dynamic_slice_in_dim(valid_all, own_first, row_count).astype(jnp.float32)[
        :, None
    ]
    inputs = tokens.astype(jnp.float32)
    first_normed, scale1 = rms_parts(inputs, norm1_gain)
    normed1_b = first_normed.astype(jnp.bfloat16)
    query_all, key_all, value_all, out_all = (
        lax.all_gather(w_query, ("fsdp", "heads", "tensor"), axis=1, tiled=True),
        lax.all_gather(key_matrix, ("fsdp", "heads", "tensor"), axis=1, tiled=True),
        lax.all_gather(value_matrix, ("fsdp", "heads", "tensor"), axis=1, tiled=True),
        lax.all_gather(w_out, ("fsdp", "heads", "tensor"), axis=0, tiled=True),
    )
    query_full = swap_cols(query_all, fsdp_count, heads_count)
    key_full = swap_cols(key_all, fsdp_count, heads_count)
    value_full = swap_cols(value_all, fsdp_count, heads_count)
    out_full = swap_rows(out_all, fsdp_count, heads_count)
    query_b, key_b, value_b, kept = project_heads(
        normed1_b, query_full, key_full, value_full, query_gain, key_gain, pos_own
    )
    q_width = query_b.shape[1] // heads_count
    k_width = key_b.shape[1] // heads_count
    packed = jnp.concatenate(
        [
            query_b.reshape(row_count, heads_count, q_width),
            key_b.reshape(row_count, heads_count, k_width),
            value_b.reshape(row_count, heads_count, k_width),
        ],
        axis=2,
    )
    grouped = to_heads(packed.reshape(row_count, -1))
    query_grp = grouped[:, :q_width]
    key_grp = grouped[:, q_width : q_width + k_width]
    value_grp = grouped[:, q_width + k_width :]
    attended_b, log_sums = attend_forward(query_grp, key_grp, value_grp, seq_all, pos_all)
    attn_tok = to_rows(attended_b)
    resid = inputs + matrix_product(attn_tok, out_full)
    normed2, scale2 = rms_parts(resid, norm2_gain)
    normed2_b = normed2.astype(jnp.bfloat16)
    wide_in = spread_rows(normed2_b)
    gate_pre = matrix_product(wide_in, gate_full)
    up_pre = matrix_product(wide_in, up_full)
    sigmoid_gate = jax.nn.sigmoid(gate_pre)
    silu_gate = gate_pre * sigmoid_gate
    act_b = (silu_gate * up_pre).astype(jnp.bfloat16)

    def forward_term(first_row, span):
        return matrix_product(act_b, down_full)

    mixed = tensor_sum(forward_term, row_count)
    output = (valid_own * (resid + mixed)).astype(jnp.bfloat16)
    grad_out = valid_own * cotangent.astype(jnp.float32)
    wide_grad = spread_rows(grad_out.astype(jnp.bfloat16))
    act_grad = dot_cols(wide_grad, down_full)
    down_grad = dot_rows(act_b, wide_grad)
    gate_grad_b = (
        act_grad * up_pre * sigmoid_gate * (1.0 + gate_pre * (1.0 - sigmoid_gate))
    ).astype(jnp.bfloat16)
    up_grad_b = (act_grad * silu_gate).astype(jnp.bfloat16)
    gate_wgrad = dot_rows(wide_in, gate_grad_b)
    up_wgrad = dot_rows(wide_in, up_grad_b)

    def backward_term(first_row, span):
        return dot_cols(gate_grad_b, gate_full) + dot_cols(up_grad_b, up_full)

    normed2_grad = tensor_sum(backward_term, row_count)
    gate_sum, up_sum, down_sum = (
        lax.psum_scatter(
            gate_wgrad.astype(jnp.bfloat16), ("fsdp", "heads"), scatter_dimension=0, tiled=True
        ).astype(jnp.float32),
        lax.psum_scatter(
            up_wgrad.astype(jnp.bfloat16), ("fsdp", "heads"), scatter_dimension=0, tiled=True
        ).astype(jnp.float32),
        lax.psum_scatter(
            down_grad.astype(jnp.bfloat16), ("fsdp", "heads"), scatter_dimension=1, tiled=True
        ).astype(jnp.float32),
    )
    resid_grad = grad_out + norm_back(resid, scale2, norm2_gain, normed2_grad)
    gain2_part = jnp.sum(normed2_grad * resid * scale2, axis=0)
    resid_grad_b = resid_grad.astype(jnp.bfloat16)
    out_wgrad = dot_rows(attn_tok, resid_grad_b)
    attn_grad_b = dot_cols(resid_grad_b, out_full).astype(jnp.bfloat16)
    attn_grad_grp = to_heads(attn_grad_b)
    query_grad_b, key_grad_b, value_grad_b = attend_backward(
        query_grp, key_grp, value_grp, attn_grad_grp, log_sums, seq_all, pos_all
    )
    back_packed = to_rows(jnp.concatenate([query_grad_b, key_grad_b, value_grad_b], axis=1))
    back_three = back_packed.reshape(row_count, heads_count, -1)
    query_back = back_three[:, :, :q_width].reshape(row_count, -1)
    key_back = back_three[:, :, q_width : q_width + k_width].reshape(row_count, -1)
    value_back = back_three[:, :, q_width + k_width :].reshape(row_count, -1)
    q_raw_grad, k_raw_grad, qgain_part, kgain_part = heads_back(
        query_back, key_back, kept, query_gain, key_gain
    )
    query_wgrad = swap_cols(dot_rows(normed1_b, q_raw_grad), heads_count, fsdp_count)
    key_wgrad = swap_cols(dot_rows(normed1_b, k_raw_grad), heads_count, fsdp_count)
    value_wgrad = swap_cols(dot_rows(normed1_b, value_back), heads_count, fsdp_count)
    out_wgrad = swap_rows(out_wgrad, heads_count, fsdp_count)
    normed1_grad = (
        dot_cols(q_raw_grad, query_full)
        + dot_cols(k_raw_grad, key_full)
        + dot_cols(value_back, value_full)
    )
    query_sum, key_sum, value_sum, out_sum = (
        lax.psum_scatter(query_wgrad, ("fsdp", "heads", "tensor"), scatter_dimension=1, tiled=True),
        lax.psum_scatter(key_wgrad, ("fsdp", "heads", "tensor"), scatter_dimension=1, tiled=True),
        lax.psum_scatter(value_wgrad, ("fsdp", "heads", "tensor"), scatter_dimension=1, tiled=True),
        lax.psum_scatter(out_wgrad, ("fsdp", "heads", "tensor"), scatter_dimension=0, tiled=True),
    )
    tokens_grad = resid_grad + norm_back(inputs, scale1, norm1_gain, normed1_grad)
    gain1_part = jnp.sum(normed1_grad * inputs * scale1, axis=0)
    gain1_sum, qgain_sum, kgain_sum, gain2_sum = lax.psum(
        (gain1_part, qgain_part, kgain_part, gain2_part), ("fsdp", "heads", "tensor")
    )
    return (
        output,
        tokens_grad,
        gain1_sum,
        query_sum,
        key_sum,
        value_sum,
        qgain_sum,
        kgain_sum,
        out_sum,
        gain2_sum,
        gate_sum,
        up_sum,
        down_sum,
    )


def plain_solution(mesh):
    return jax.shard_map(
        plain_layer,
        mesh=mesh,
        in_specs=(
            P(("fsdp", "heads", "tensor"), None),
            P(("fsdp", "heads", "tensor"), None),
            P(("fsdp", "tensor"), None),
            P(("fsdp", "tensor"), None),
            P(),
            P(None, ("heads", "fsdp", "tensor")),
            P(None, ("heads", "fsdp", "tensor")),
            P(None, ("heads", "fsdp", "tensor")),
            P(),
            P(),
            P(("heads", "fsdp", "tensor"), None),
            P(),
            P(("fsdp", "heads"), "tensor"),
            P(("fsdp", "heads"), "tensor"),
            P("tensor", ("fsdp", "heads")),
        ),
        out_specs=(
            P(("fsdp", "heads", "tensor"), None),
            P(("fsdp", "heads", "tensor"), None),
            P(),
            P(None, ("heads", "fsdp", "tensor")),
            P(None, ("heads", "fsdp", "tensor")),
            P(None, ("heads", "fsdp", "tensor")),
            P(),
            P(),
            P(("heads", "fsdp", "tensor"), None),
            P(),
            P(("fsdp", "heads"), "tensor"),
            P(("fsdp", "heads"), "tensor"),
            P("tensor", ("fsdp", "heads")),
        ),
        check_vma=False,
    )


VMEM_LIMIT = 56 * 1024 * 1024
LOG2_E = 1.4426950408889634
SWAP = ((0, 1), (1, 0))
ROW_TILE = 1024
SCALE = HEAD_SIZE ** (-0.5)


def dot_t(left, right):
    return lax.dot_general(
        left, right, (((1,), (1,)), ((), ())), preferred_element_type=jnp.float32
    )


def swap(array, axis):
    return lax.ppermute(array, axis, SWAP)


def pick(first, second, index):
    return jnp.where(index == 0, first, second)


def join(mine, other, index, axis):
    return pick(
        jnp.concatenate([mine, other], axis=axis),
        jnp.concatenate([other, mine], axis=axis),
        index,
    )


def gather_z(array):
    return lax.all_gather(array, "z", axis=0, tiled=True)


def scatter_z(array):
    return lax.psum_scatter(array, "z", scatter_dimension=0, tiled=True)


def after(array, *done):
    return lax.optimization_barrier((array, *done))[0]


def sync(*arrays):
    return lax.optimization_barrier(arrays)


def to_core(array, core):
    half = array.shape[0] // 2
    first, second = array[:half], array[half:]
    other = swap(pick(second, first, core), "c")
    return join(pick(first, second, core), other, core, 1)


def from_core(array, core, count):
    half = array.shape[1] // 2
    span = array.shape[0] // count
    first, second = array[:, :half], array[:, half:]
    other = swap(pick(second, first, core), "c").reshape(count, span, half)
    mine = pick(first, second, core).reshape(count, span, half)
    return join(mine, other, core, 1).reshape(-1, half)


def call(kernel, inputs, in_specs, out_specs, out_shape, grid, after=(), prefetch=None, **more):
    lead = 0 if prefetch is None else 1
    count, extra = lead + len(inputs), len(after)

    def body(*refs):
        kernel(*refs[:count], *refs[count + extra :])

    if prefetch is not None:
        prefetched, inputs = [prefetch], list(inputs)
    else:
        prefetched, inputs = [], list(inputs)
    scratch = more.pop("scratch_shapes", ())
    return pl.pallas_call(
        body,
        grid_spec=pltpu.PrefetchScalarGridSpec(
            num_scalar_prefetch=lead,
            grid=grid,
            in_specs=list(in_specs) + [pl.BlockSpec(memory_space=pl.ANY)] * extra,
            out_specs=out_specs,
            scratch_shapes=scratch,
        ),
        out_shape=out_shape,
        compiler_params=pltpu.CompilerParams(vmem_limit_bytes=VMEM_LIMIT),
        cost_estimate=pl.CostEstimate(flops=1000, bytes_accessed=1000, transcendentals=0),
        **more,
    )(*prefetched, *inputs, *after)


def reorder_kernel(order_ref, in_ref, out_ref):
    out_ref[...] = in_ref[...]


def reorder(array, order, after=()):
    rows, width = array.shape
    parts = order.shape[0]
    return call(
        reorder_kernel,
        [array],
        [pl.BlockSpec((rows, width // parts), lambda i, o: (0, o[i]))],
        pl.BlockSpec((rows, width // parts), lambda i, o: (0, i)),
        jax.ShapeDtypeStruct(array.shape, array.dtype),
        (parts,),
        after,
        order,
        name="reorder",
    )


def lane_mean(value):
    ones = jnp.full((HEAD_SIZE, HEAD_SIZE), 1.0 / HEAD_SIZE, jnp.bfloat16)
    high = value.astype(jnp.bfloat16)
    low = (value - high.astype(jnp.float32)).astype(jnp.bfloat16)
    return matrix_product(high, ones) + matrix_product(low, ones)


def heads_kernel(count, raw_ref, cos_ref, sin_ref, gain_ref, out_ref):
    raw = raw_ref[:, :HEAD_SIZE]
    value = raw * lax.rsqrt(lane_mean(raw * raw) + EPS_NORM) * gain_ref[...]
    out_ref[:, :HEAD_SIZE] = (
        value * cos_ref[...] + pltpu.roll(value, HEAD_SIZE // 2, 1) * sin_ref[...]
    ).astype(jnp.bfloat16)
    if count == 2:
        out_ref[:, HEAD_SIZE:] = raw_ref[:, HEAD_SIZE:].astype(jnp.bfloat16)


def make_heads(raw, cos_tab, sin_tab, gain, count, first, rows, after=()):
    width = raw.shape[1]
    skip = first // ROW_TILE
    table = pl.BlockSpec((ROW_TILE, HEAD_SIZE), lambda i, r: (i + skip, 0))
    return call(
        functools.partial(heads_kernel, count),
        [raw, cos_tab, sin_tab, gain[None, :]],
        [
            pl.BlockSpec((ROW_TILE, count * HEAD_SIZE), lambda i, r: (i + skip, r)),
            table,
            table,
            pl.BlockSpec((1, HEAD_SIZE), lambda i, r: (0, 0)),
        ],
        pl.BlockSpec((ROW_TILE, count * HEAD_SIZE), lambda i, r: (i, r)),
        jax.ShapeDtypeStruct((rows, width), jnp.bfloat16),
        (rows // ROW_TILE, width // (count * HEAD_SIZE)),
        after,
        name="make_heads",
    )


def heads_back_kernel(count, raw_ref, cos_ref, sin_ref, gain_ref, *rest):
    *up_refs, out_ref, sum_ref = rest

    @pl.when((pl.program_id(0) == 0) & (pl.program_id(1) == 0))
    def _():
        sum_ref[...] = jnp.zeros_like(sum_ref)

    raw = raw_ref[:, :HEAD_SIZE]
    upstream = up_refs[0][...].astype(jnp.float32)
    for ref in up_refs[1:]:
        upstream = upstream + ref[...].astype(jnp.float32)
    if count == 2:
        out_ref[:, HEAD_SIZE:] = upstream[:, HEAD_SIZE:].astype(jnp.bfloat16)
        upstream = upstream[:, :HEAD_SIZE]
    turned = upstream * cos_ref[...] - pltpu.roll(upstream, HEAD_SIZE // 2, 1) * sin_ref[...]
    scale = lax.rsqrt(lane_mean(raw * raw) + EPS_NORM)
    hat = raw * scale
    weighted = turned * gain_ref[...]
    out_ref[:, :HEAD_SIZE] = (scale * (weighted - hat * lane_mean(hat * weighted))).astype(
        jnp.bfloat16
    )
    sum_ref[0:1, :] += jnp.sum(turned * hat, axis=0, keepdims=True)


def heads_return(raw, upstream, far, cos_tab, sin_tab, gain, count, after=()):
    rows, width = raw.shape
    heads = width // (count * HEAD_SIZE)
    table = pl.BlockSpec((ROW_TILE, HEAD_SIZE), lambda i, r: (i, 0))
    one = pl.BlockSpec((ROW_TILE, count * HEAD_SIZE), lambda i, r: (i, r))
    across = pl.BlockSpec(
        (ROW_TILE, count * HEAD_SIZE), lambda i, r: (i, (r + heads // 2) % heads)
    )
    return call(
        functools.partial(heads_back_kernel, count),
        [raw, cos_tab, sin_tab, gain[None, :], upstream] + far,
        [one, table, table, pl.BlockSpec((1, HEAD_SIZE), lambda i, r: (0, 0)), one]
        + [across] * len(far),
        [one, pl.BlockSpec((8, HEAD_SIZE), lambda i, r: (0, 0))],
        [
            jax.ShapeDtypeStruct((rows, width), jnp.bfloat16),
            jax.ShapeDtypeStruct((8, HEAD_SIZE), jnp.float32),
        ],
        (rows // ROW_TILE, heads),
        after,
        name="heads_return",
    )


def stack_heads(block):
    return jnp.concatenate([block[:, :HEAD_SIZE], block[:, HEAD_SIZE:]], axis=0)


def key_bias(first_key, pair, parity):
    cols = lax.broadcasted_iota(jnp.int32, (1, 2 * BLK), 1)
    block = 2 * pair + jnp.where(cols < BLK, parity, 1 - parity)
    return jnp.where(block >= first_key, 0.0, NEG_FILL)


def last_bias(first_key, pair, parity):
    rows = lax.broadcasted_iota(jnp.int32, (2 * BLK, 2 * BLK), 0)
    cols = lax.broadcasted_iota(jnp.int32, (2 * BLK, 2 * BLK), 1)
    far = (parity == 1) & (2 * pair >= first_key)
    own = lax.rem(cols, BLK) <= lax.rem(rows, BLK)
    far_bias = jnp.where(far, 0.0, NEG_FILL)
    return jnp.where(cols < BLK, jnp.where(own, 0.0, NEG_FILL), far_bias)


def pair_of(own_ref, far_ref, m, first):
    at = pl.ds(pl.multiple_of(m * BLK, BLK), BLK)
    lanes = slice(first, first + HEAD_SIZE)
    return jnp.concatenate([own_ref[at, lanes], far_ref[at, lanes]], axis=0)


def attend_kernel(group, info_ref, q_ref, own_ref, far_ref, o_ref, l_ref):
    blocks = q_ref.shape[0] // BLK
    parity = info_ref[group, blocks]

    def one_block(j, _):
        first_key = info_ref[group, j]
        rows = pl.ds(pl.multiple_of(j * BLK, BLK), BLK)
        query = stack_heads(q_ref[rows, :])

        def step(m, bias, carry):
            total, acc = carry
            score = dot_t(query, pair_of(own_ref, far_ref, m, 0))
            expo = jnp.exp2(score * (SCALE * LOG2_E) + bias)
            total = total + jnp.sum(expo, axis=1, keepdims=True)
            value = pair_of(own_ref, far_ref, m, HEAD_SIZE)
            acc = acc + matrix_product(expo.astype(jnp.bfloat16), value)
            return total, acc

        carry = step(
            j,
            last_bias(first_key, j, parity),
            (jnp.zeros((2 * BLK, 1), jnp.float32), jnp.zeros((2 * BLK, HEAD_SIZE), jnp.float32)),
        )
        total, acc = lax.fori_loop(
            lax.div(first_key, 2),
            j,
            lambda m, c: step(m, key_bias(first_key, m, parity), c),
            carry,
        )
        out = (acc / total).astype(jnp.bfloat16)
        o_ref[rows, :HEAD_SIZE] = out[:BLK]
        o_ref[rows, HEAD_SIZE:] = out[BLK:]
        lane = lax.broadcasted_iota(jnp.int32, (BLK, HEAD_SIZE), 1)
        l_ref[rows, :] = jnp.where(lane == 0, total[:BLK], total[BLK:])
        return 0

    lax.fori_loop(0, blocks, one_block, 0)


def attend(group, info, query, own, far, after=()):
    rows = query.shape[0] // 2
    count = query.shape[1] // (2 * HEAD_SIZE)
    wide = pl.BlockSpec((rows, 2 * HEAD_SIZE), lambda r, s: (group, r))
    here = pl.BlockSpec((rows, 2 * HEAD_SIZE), lambda r, s: (0, r))
    return call(
        functools.partial(attend_kernel, group),
        [query, own, far],
        [wide, here, pl.BlockSpec((rows, 2 * HEAD_SIZE), lambda r, s: (0, (r + 2) % 4))],
        [here, pl.BlockSpec((rows, HEAD_SIZE), lambda r, s: (0, r))],
        [
            jax.ShapeDtypeStruct((rows, query.shape[1]), jnp.bfloat16),
            jax.ShapeDtypeStruct((rows, count * HEAD_SIZE), jnp.float32),
        ],
        (count,),
        after,
        info,
        name="attend",
    )


def attend_back_kernel(
    group,
    info_ref,
    q_ref,
    do_ref,
    o_ref,
    l_ref,
    own_ref,
    far_ref,
    dq_ref,
    down_ref,
    dfar_ref,
    kacc_ref,
    vacc_ref,
):
    blocks = q_ref.shape[0] // BLK
    parity = info_ref[group, blocks]
    kacc_ref[...] = jnp.zeros_like(kacc_ref)
    vacc_ref[...] = jnp.zeros_like(vacc_ref)

    def one_block(j, _):
        first_key = info_ref[group, j]
        rows = pl.ds(pl.multiple_of(j * BLK, BLK), BLK)
        query = stack_heads(q_ref[rows, :])
        attn = stack_heads(o_ref[rows, :]).astype(jnp.float32)
        grad = stack_heads(do_ref[rows, :]).astype(jnp.float32)
        total = jnp.concatenate([l_ref[rows, 0:1], l_ref[rows, 1:2]], axis=0)
        grad_b = (grad / total).astype(jnp.bfloat16)
        inner = jnp.sum(grad_b.astype(jnp.float32) * attn, axis=1, keepdims=True)

        def step(m, bias, dq):
            at = pl.ds(pl.multiple_of(m * BLK, BLK), BLK)
            key = pair_of(own_ref, far_ref, m, 0)
            expo = jnp.exp2(dot_t(query, key) * (SCALE * LOG2_E) + bias)
            d_prob = dot_t(grad_b, pair_of(own_ref, far_ref, m, HEAD_SIZE))
            d_score = (expo * (d_prob - inner)).astype(jnp.bfloat16)
            d_key = dot_rows(d_score, query)
            d_value = dot_rows(expo.astype(jnp.bfloat16), grad_b)
            kacc_ref[0, at, :] += d_key[:BLK]
            kacc_ref[1, at, :] += d_key[BLK:]
            vacc_ref[0, at, :] += d_value[:BLK]
            vacc_ref[1, at, :] += d_value[BLK:]
            return dq + matrix_product(d_score, key)

        dq = step(
            j, last_bias(first_key, j, parity), jnp.zeros((2 * BLK, HEAD_SIZE), jnp.float32)
        )
        dq = lax.fori_loop(
            lax.div(first_key, 2),
            j,
            lambda m, c: step(m, key_bias(first_key, m, parity), c),
            dq,
        )
        dq = (dq * SCALE).astype(jnp.bfloat16)
        dq_ref[rows, :HEAD_SIZE] = dq[:BLK]
        dq_ref[rows, HEAD_SIZE:] = dq[BLK:]
        return 0

    lax.fori_loop(0, blocks, one_block, 0)
    for half, ref in enumerate((down_ref, dfar_ref)):
        ref[:, :HEAD_SIZE] = (kacc_ref[half] * SCALE).astype(jnp.bfloat16)
        ref[:, HEAD_SIZE:] = vacc_ref[half].astype(jnp.bfloat16)


def attend_back(group, info, query, d_attn, attn, total, own, far, after=()):
    rows = query.shape[0] // 2
    count = query.shape[1] // (2 * HEAD_SIZE)
    wide = pl.BlockSpec((rows, 2 * HEAD_SIZE), lambda r, s: (group, r))
    here = pl.BlockSpec((rows, 2 * HEAD_SIZE), lambda r, s: (0, r))
    shape = jax.ShapeDtypeStruct((rows, query.shape[1]), jnp.bfloat16)
    return call(
        functools.partial(attend_back_kernel, group),
        [query, d_attn, attn, total, own, far],
        [
            wide,
            here,
            here,
            pl.BlockSpec((rows, HEAD_SIZE), lambda r, s: (0, r)),
            here,
            pl.BlockSpec((rows, 2 * HEAD_SIZE), lambda r, s: (0, (r + 2) % 4)),
        ],
        [here] * 3,
        [shape] * 3,
        (count,),
        after,
        info,
        scratch_shapes=[
            pltpu.VMEM((2, rows, HEAD_SIZE), jnp.float32),
            pltpu.VMEM((2, rows, HEAD_SIZE), jnp.float32),
        ],
        name="attend_back",
    )


HIDDEN_TILE = 512
ROW_STEP = 512


def ffn_up_kernel(x_ref, g0, g1, g2, g3, u0, u1, u2, u3, act_ref, dgate_ref, silu_ref):
    gate_w = jnp.concatenate([g0[...], g1[...], g2[...], g3[...]], axis=1).T
    up_w = jnp.concatenate([u0[...], u1[...], u2[...], u3[...]], axis=1).T
    for first in range(0, x_ref.shape[0], ROW_STEP):
        rows = slice(first, first + ROW_STEP)
        gate = matrix_product(x_ref[rows, :], gate_w)
        upper = matrix_product(x_ref[rows, :], up_w)
        sig = 0.5 * jnp.tanh(0.5 * gate) + 0.5
        silu = gate * sig
        act_ref[rows, :] = (silu * upper).astype(jnp.bfloat16)
        silu_ref[rows, :] = silu.astype(jnp.bfloat16)
        dgate_ref[rows, :] = (upper * (sig + silu * (1.0 - sig))).astype(jnp.bfloat16)


def ffn_up(x, gates, ups, after=()):
    rows, width = x.shape
    hidden, depth = gates[0].shape
    weight = pl.BlockSpec((HIDDEN_TILE, depth), lambda j: (j, 0))
    out = pl.BlockSpec((rows, HIDDEN_TILE), lambda j: (0, j))
    shape = jax.ShapeDtypeStruct((rows, hidden), jnp.bfloat16)
    return call(
        ffn_up_kernel,
        [x, *gates, *ups],
        [pl.BlockSpec((rows, width), lambda j: (0, 0))] + [weight] * 8,
        [out] * 3,
        [shape] * 3,
        (hidden // HIDDEN_TILE,),
        after,
        name="ffn_up",
    )


def ffn_back_kernel(dy_ref, wa_ref, wb_ref, dgate_ref, silu_ref, gate_ref, up_ref):
    weight = jnp.concatenate([wa_ref[...], wb_ref[...]], axis=1).T
    for first in range(0, dy_ref.shape[0], ROW_STEP):
        rows = slice(first, first + ROW_STEP)
        d_act = matrix_product(dy_ref[rows, :], weight)
        gate_ref[rows, :] = (d_act * dgate_ref[rows, :].astype(jnp.float32)).astype(jnp.bfloat16)
        up_ref[rows, :] = (d_act * silu_ref[rows, :].astype(jnp.float32)).astype(jnp.bfloat16)


def ffn_back(dy, downs, dgate, silu, after=()):
    rows, width = dy.shape
    hidden = downs[0].shape[0]
    out = pl.BlockSpec((rows, HIDDEN_TILE), lambda j: (0, j))
    shape = jax.ShapeDtypeStruct((rows, hidden), jnp.bfloat16)
    return call(
        ffn_back_kernel,
        [dy, *downs, dgate, silu],
        [
            pl.BlockSpec((rows, width), lambda j: (0, 0)),
            pl.BlockSpec((HIDDEN_TILE, width // 2), lambda j: (j, 0)),
            pl.BlockSpec((HIDDEN_TILE, width // 2), lambda j: (j, 0)),
            out,
            out,
        ],
        [out] * 2,
        [shape] * 2,
        (hidden // HIDDEN_TILE,),
        after,
        name="ffn_back",
    )


def weight_grad_kernel(left_ref, right_ref, *out_refs):
    left = left_ref[...].T
    span = out_refs[0].shape[1]
    for i, out_ref in enumerate(out_refs):
        right = right_ref[:, i * span : (i + 1) * span]
        out_ref[...] = matrix_product(left, right).astype(jnp.bfloat16)


def weight_grad(left, right, first, last, count, after=()):
    rows, hidden = left.shape
    width = last - first
    shape = jax.ShapeDtypeStruct((hidden, width // count), jnp.bfloat16)
    return call(
        weight_grad_kernel,
        [left, right],
        [
            pl.BlockSpec((rows, HIDDEN_TILE), lambda j: (0, j)),
            pl.BlockSpec((rows, width), lambda j: (0, first // width)),
        ],
        [pl.BlockSpec((HIDDEN_TILE, width // count), lambda j: (j, 0))] * count,
        [shape] * count,
        (hidden // HIDDEN_TILE,),
        after,
        name="weight_grad",
    )


def to_model_kernel(terms, order_ref, *refs):
    left_refs, weight_refs = refs[:terms], refs[terms:-2]
    out_ref, acc_ref = refs[-2:]
    pieces = len(weight_refs) // terms
    span = weight_refs[0].shape[1]

    @pl.when(pl.program_id(0) == 0)
    def _():
        acc_ref[...] = jnp.zeros_like(acc_ref)

    left = jnp.concatenate([ref[...] for ref in left_refs], axis=1)
    for i in range(pieces):
        weight = jnp.concatenate([weight_refs[t * pieces + i][...] for t in range(terms)], axis=0)
        acc_ref[:, i * span : (i + 1) * span] += matrix_product(left, weight)

    @pl.when(pl.program_id(0) == pl.num_programs(0) - 1)
    def _():
        block = acc_ref.shape[1] // order_ref.shape[0]
        for i in range(order_ref.shape[0]):
            at = pl.ds(pl.multiple_of(order_ref[i] * block, block), block)
            out_ref[:, at] = acc_ref[:, i * block : (i + 1) * block].astype(jnp.bfloat16)


def to_model(lefts, weights, order, half, rows, after=()):
    hidden = lefts[0].shape[1]
    span, pieces = weights[0][0].shape[1], len(weights[0])
    return call(
        functools.partial(to_model_kernel, len(lefts)),
        [*lefts, *(w for group in weights for w in group)],
        [pl.BlockSpec((rows, HIDDEN_TILE), lambda j, o: (half, j))] * len(lefts)
        + [pl.BlockSpec((HIDDEN_TILE, span), lambda j, o: (j, 0))] * (len(lefts) * pieces),
        pl.BlockSpec((rows, span * pieces), lambda j, o: (0, 0)),
        jax.ShapeDtypeStruct((rows, span * pieces), jnp.bfloat16),
        (hidden // HIDDEN_TILE,),
        after,
        order,
        scratch_shapes=[pltpu.VMEM((rows, span * pieces), jnp.float32)],
        name="to_model",
    )


def to_hidden_kernel(x_ref, weight_ref, out_ref):
    out_ref[...] = matrix_product(x_ref[...], weight_ref[...].T).astype(jnp.bfloat16)


def to_hidden(x, weight, after=()):
    rows, width = x.shape
    hidden = weight.shape[0]
    return call(
        to_hidden_kernel,
        [x, weight],
        [
            pl.BlockSpec((rows, width), lambda j: (0, 0)),
            pl.BlockSpec((HIDDEN_TILE, width), lambda j: (j, 0)),
        ],
        pl.BlockSpec((rows, HIDDEN_TILE), lambda j: (0, j)),
        jax.ShapeDtypeStruct((rows, hidden), jnp.bfloat16),
        (hidden // HIDDEN_TILE,),
        after,
        name="to_hidden",
    )


NORM_TILE = 128


def resid_kernel(order_ref, tokens_ref, own_ref, there_ref, gain_ref, resid_ref, normed_ref):
    resid = (
        tokens_ref[...].astype(jnp.float32)
        + own_ref[...].astype(jnp.float32)
        + there_ref[...].astype(jnp.float32)
    )
    resid_ref[...] = resid
    scale = lax.rsqrt(jnp.mean(resid * resid, axis=-1, keepdims=True) + EPS_NORM)
    normed = (resid * scale * gain_ref[...]).astype(jnp.bfloat16)
    block = normed.shape[1] // order_ref.shape[0]
    for i in range(order_ref.shape[0]):
        at = pl.ds(pl.multiple_of(order_ref[i] * block, block), block)
        normed_ref[:, at] = normed[:, i * block : (i + 1) * block]


def resid_norm(tokens, own, there, gain, order, after=()):
    rows, width = tokens.shape
    tile = pl.BlockSpec((NORM_TILE, width), lambda i, o: (i, 0))
    return call(
        resid_kernel,
        [tokens, own, there, gain[None, :]],
        [tile, tile, tile, pl.BlockSpec((1, width), lambda i, o: (0, 0))],
        [tile, tile],
        [
            jax.ShapeDtypeStruct((rows, width), jnp.float32),
            jax.ShapeDtypeStruct((rows, width), jnp.bfloat16),
        ],
        (rows // NORM_TILE,),
        after,
        order,
        name="resid_norm",
    )


def norm_back_kernel(value_ref, base_ref, own_ref, there_ref, gain_ref, *out_refs):
    *grad_refs, sum_ref = out_refs

    @pl.when(pl.program_id(0) == 0)
    def _():
        sum_ref[...] = jnp.zeros_like(sum_ref)

    value = value_ref[...].astype(jnp.float32)
    upstream = own_ref[...].astype(jnp.float32) + there_ref[...].astype(jnp.float32)
    scale = lax.rsqrt(jnp.mean(value * value, axis=-1, keepdims=True) + EPS_NORM)
    hat = value * scale
    weighted = upstream * gain_ref[...]
    inner = jnp.mean(hat * weighted, axis=-1, keepdims=True)
    grad = base_ref[...].astype(jnp.float32) + scale * (weighted - hat * inner)
    for ref in grad_refs:
        ref[...] = grad.astype(ref.dtype)
    sum_ref[0:1, :] += jnp.sum(upstream * hat, axis=0, keepdims=True)


def norm_return(value, base, own, there, gain, dtypes, after=()):
    rows, width = value.shape
    tile = pl.BlockSpec((NORM_TILE, width), lambda i: (i, 0))
    return call(
        norm_back_kernel,
        [value, base, own, there, gain[None, :]],
        [tile, tile, tile, tile, pl.BlockSpec((1, width), lambda i: (0, 0))],
        [tile] * len(dtypes) + [pl.BlockSpec((8, width), lambda i: (0, 0))],
        [jax.ShapeDtypeStruct((rows, width), d) for d in dtypes]
        + [jax.ShapeDtypeStruct((8, width), jnp.float32)],
        (rows // NORM_TILE,),
        after,
        name="norm_return",
    )


def block_info(lengths, positions, first):
    count = (lengths + BLK - 1) // BLK
    ends = jnp.cumsum(count)
    starts = jnp.concatenate([jnp.zeros((1,), jnp.int32), ends])
    own = lax.dynamic_slice_in_dim(positions, first, 8)
    first_keys = jnp.max(jnp.where(starts[None, :] <= own[:, None], starts[None, :], 0), axis=1)
    limits = jnp.concatenate([lengths, jnp.zeros((1,), jnp.int32)])
    seq = jnp.sum((own[:, None] >= ends[None, :]).astype(jnp.int32), axis=1)
    limit = jnp.sum(jnp.where(seq[:, None] == jnp.arange(4)[None, :], limits[None, :], 0), axis=1)
    pos = ((own - first_keys)[:, None] * BLK + jnp.arange(BLK)[None, :]).astype(jnp.int32)
    valid = pos < limit[:, None]
    return first_keys, own, pos.reshape(-1), valid.reshape(-1)


def chip_layer(
    tokens,
    cotangent,
    seq_lens,
    block_pos,
    norm1_gain,
    w_query,
    key_matrix,
    value_matrix,
    query_gain,
    key_gain,
    w_out,
    norm2_gain,
    w_gate,
    w_up,
    w_down,
):
    xi, core, yi = lax.axis_index("x"), lax.axis_index("c"), lax.axis_index("y")
    rows, width = tokens.shape
    bf16, f32 = jnp.bfloat16, jnp.float32
    half, fourth = width // 2, width // 4

    q_in, k_in = w_query.shape[1], key_matrix.shape[1]
    down_0 = to_core(w_down, core)
    down_x, down_y = swap(down_0, "x"), swap(down_0, "y")
    down_c = swap(down_x, "y")
    qkv_0 = gather_z(jnp.concatenate([w_query.T, key_matrix.T, value_matrix.T], axis=0))
    gate_0 = gather_z(to_core(after(w_gate, down_0).T, core))
    out_0 = gather_z(w_out)
    up_0 = gather_z(to_core(after(w_up, down_0).T, core))
    down_w = [
        gather_z(jnp.concatenate([down_0, down_x], axis=1)),
        gather_z(jnp.concatenate([down_y, down_c], axis=1)),
    ]
    qkv_start = after(qkv_0, down_x, down_y, down_c)
    qkv_x, qkv_y = swap(qkv_start, "x"), swap(qkv_start, "y")
    middle = qkv_0.shape[0] // 2
    qkv_y_top, qkv_x_low, _, _ = lax.optimization_barrier(
        (qkv_y[:middle], qkv_x[middle:], qkv_x, qkv_y)
    )
    qkv_c = jnp.concatenate([swap(qkv_y_top, "x"), swap(qkv_x_low, "y")], axis=0)
    qkv_p = [
        a.reshape(4, q_in + 2 * k_in, width) for a in (qkv_0, qkv_x, qkv_y, qkv_c)
    ]
    q_w = jnp.concatenate([a[:, :q_in].reshape(-1, width) for a in qkv_p], axis=0)
    kv_w = jnp.concatenate(
        [
            part.reshape(-1, width)
            for a in qkv_p
            for part in (a[:, q_in : q_in + k_in], a[:, q_in + k_in :])
        ],
        axis=0,
    )
    split = gate_0.shape[0] // 2
    gate_send = after(gate_0, qkv_c)
    gate_x, gate_y = swap(gate_send, "x"), swap(gate_send, "y")
    out_send = after(out_0, qkv_c)
    out_x, out_y = swap(out_send, "x"), swap(out_send, "y")

    lengths_here = jnp.concatenate([seq_lens[0], block_pos[0]]).astype(f32)
    lengths_there = swap(lengths_here[None, :], "c")[0].astype(jnp.int32)
    first_own = yi * 8
    keys_here, at_here, pos_here, valid_here = block_info(seq_lens[0], block_pos[0], first_own)
    keys_there, at_there, pos_there, _ = block_info(
        lengths_there[:3], lengths_there[3:], first_own
    )
    info = jnp.stack(
        [
            jnp.concatenate([keys_here, at_here[:1]]),
            jnp.concatenate([keys_there, at_there[:1]]),
        ]
    ).astype(jnp.int32)
    freq = jnp.exp(
        jnp.arange(HEAD_SIZE // 2, dtype=f32) * (-2.0 * math.log(ROPE_BASE) / HEAD_SIZE)
    )
    angles = jnp.concatenate([pos_here, pos_there]).astype(f32)[:, None] * freq[None, :]
    cos_half, sin_half = jnp.cos(angles), jnp.sin(angles)
    cos_tab = jnp.concatenate([cos_half, cos_half], axis=1)
    sin_tab = jnp.concatenate([-sin_half, sin_half], axis=1)
    valid = valid_here.astype(f32)[:, None]

    blocks = jnp.arange(8)
    ry, rx, rc = blocks // 4, (blocks // 2) % 2, blocks % 2
    order = ((rx ^ xi) * 4 + rc * 2 + (ry ^ yi)).astype(jnp.int32)
    nx, nc, ny = blocks // 4, (blocks // 2) % 2, blocks % 2
    order_back = ((ny ^ yi) * 4 + (nx ^ xi) * 2 + nc).astype(jnp.int32)

    def both(own):
        return jnp.concatenate([own, swap(own, "c")], axis=0)

    inputs = tokens.astype(f32)
    first_normed, scale1 = rms_parts(inputs, norm1_gain)
    normed1 = both(first_normed.astype(bf16))
    dy_own = (valid * cotangent.astype(f32)).astype(bf16)
    dy = both(reorder(dy_own, order))

    q_raw = dot_t(normed1, q_w)
    query = make_heads(q_raw, cos_tab, sin_tab, query_gain, 1, 0, 2 * rows)
    kv_raw = dot_t(after(normed1, query), kv_w)
    kv0 = make_heads(kv_raw, cos_tab, sin_tab, key_gain, 2, 0, rows)
    kv1 = make_heads(kv_raw, cos_tab, sin_tab, key_gain, 2, rows, rows, [kv0])
    kv0, kv1, gate_x, gate_y, out_x, out_y, up_0 = sync(
        kv0, kv1, gate_x, gate_y, out_x, out_y, up_0
    )
    kv_far0 = swap(kv0, "y")
    kv_far1 = swap(after(kv1, kv_far0), "y")
    out_c = swap(out_y, "x")
    up_x = swap(up_0, "x")
    attn0, totals0 = attend(0, info, query, kv0, kv_far0, [dy])
    kv_far1, attn0, up_0, up_x, gate_y, out_c = sync(kv_far1, attn0, up_0, up_x, gate_y, out_c)
    out_w = jnp.concatenate([out_0, out_x, out_y, out_c], axis=0)
    up_y, gate_c = swap(up_0, "y"), swap(gate_y, "x")
    attn1, totals1 = attend(1, info, query, kv1, kv_far1)
    same = jnp.arange(8, dtype=jnp.int32)
    out_term = to_model([attn1], [[out_w]], same, 0, rows)
    out_there = swap(out_term, "c")
    out_here = to_model([attn0], [[out_w]], same, 0, rows, [out_term])
    resid, normed2_own = resid_norm(
        tokens, out_here, out_there, norm2_gain, order_back, [down_w[0]]
    )
    normed2_b = both(normed2_own)
    up_y_top, up_x_low, *_ = sync(up_y[:split], up_x[split:], up_y, gate_c, normed2_own)
    up_c = jnp.concatenate([swap(up_y_top, "x"), swap(up_x_low, "y")], axis=0)
    gate_w, up_w = [gate_0, gate_x, gate_y, gate_c], [up_0, up_x, up_y, up_c]
    act, dgate, silu = ffn_up(normed2_b, gate_w, up_w, [dy])

    def stacked(first, second):
        return jnp.concatenate([first, second], axis=0)

    def corner_start(corner):
        span = corner.shape[0] // 2
        return swap(corner[:span], "x"), swap(corner[span:], "y")

    def corner_add(along_x, along_y, from_x, from_y):
        span = from_x.shape[0]
        return (
            stacked(along_x[:span], along_x[span:] + from_y),
            stacked(along_y[:span] + from_x, along_y[span:]),
        )

    (down_first,) = weight_grad(act, dy, 0, half, 1)
    (down_second,) = weight_grad(act, dy, half, width, 1, [down_first])
    down_a, down_b = scatter_z(down_first), scatter_z(down_second)
    gate_grad, up_grad = ffn_back(dy, down_w, dgate, silu, [down_second])
    g_own, g_x, g_y, g_c = weight_grad(gate_grad, normed2_b, 0, width, 4)
    g_from = corner_start(g_c)
    u_own, u_x, u_y, u_c = weight_grad(up_grad, normed2_b, 0, width, 4, [g_own])
    g_x, g_y, _ = sync(*corner_add(g_x, g_y, *g_from), u_own)
    got_gx, got_gy = swap(g_x, "x"), swap(g_y, "y")
    there = to_model([gate_grad, up_grad], [gate_w, up_w], order, 1, rows, [g_x, g_y, down_a])
    normed2_there = swap(there, "c")
    normed2_own = to_model([gate_grad, up_grad], [gate_w, up_w], order, 0, rows, [there])
    g_own, got_gx, got_gy, normed2_own, u_c = sync(g_own, got_gx, got_gy, normed2_own, u_c)
    gate_sum = scatter_z(g_own + got_gx + got_gy)
    u_from = corner_start(u_c)
    resid_grad, resid_here, gain2_sum = norm_return(
        resid, dy_own, normed2_own, normed2_there, norm2_gain, (f32, bf16)
    )
    resid_there = swap(resid_here, "c")
    mixed_term = to_model([act], [down_w], order, 1, rows, [resid_here])
    mixed_there = swap(mixed_term, "c")
    resid_here, mixed_term, down_b, *u_from = sync(resid_here, mixed_term, down_b, *u_from)
    u_x, u_y = corner_add(u_x, u_y, *u_from)
    d_own, d_x = down_a[:, :fourth], down_a[:, fourth:]
    d_y, d_c = down_b[:, :fourth], down_b[:, fourth:]
    resid_here, u_x, u_y, d_c = sync(resid_here, u_x, u_y, d_c)
    got_ux, got_uy = swap(u_x, "x"), swap(u_y, "y")
    got_dc = swap(d_c, "x")

    d_attn0 = to_hidden(resid_here, out_w)
    dq0, dkv0, dkv0_far = attend_back(0, info, query, d_attn0, attn0, totals0, kv0, kv_far0)
    dkv0_back = swap(dkv0_far, "y")
    mixed_own = to_model([act], [down_w], order, 0, rows, [dkv0_far])
    mixed_own, resid_there, u_own, got_ux, got_uy, got_dc = sync(
        mixed_own, resid_there, u_own, got_ux, got_uy, got_dc
    )
    up_sum = scatter_z(u_own + got_ux + got_uy)
    d_y = d_y + got_dc
    d_x, d_y, resid_there = sync(d_x, d_y, resid_there)
    got_dx, got_dy = swap(d_x, "x"), swap(d_y, "y")
    d_attn1 = to_hidden(resid_there, out_w)
    dq1, dkv1, dkv1_far = attend_back(1, info, query, d_attn1, attn1, totals1, kv1, kv_far1)
    dkv1_far, dkv0_back, d_own, got_dx, got_dy, dq1 = sync(
        dkv1_far, dkv0_back, d_own, got_dx, got_dy, dq1
    )
    dkv1_back = swap(dkv1_far, "y")
    q_grad, q_gains = heads_return(
        q_raw, stacked(dq0, dq1), [], cos_tab, sin_tab, query_gain, 1
    )
    (o_grad,) = weight_grad(
        stacked(attn0, attn1), stacked(after(resid_here, q_grad), resid_there), 0, width, 1
    )
    (w_grad,) = weight_grad(q_grad, normed1, 0, width, 1)
    a_own, a_x, a_y, a_c = (
        stacked(*pair) for pair in zip(jnp.split(w_grad, 4), jnp.split(o_grad, 4))
    )
    dkv1_back, a_own, a_x, a_y, a_c = sync(dkv1_back, a_own, a_x, a_y, a_c)
    a_from = corner_start(a_c)
    kv_grad, k_gains = heads_return(
        kv_raw,
        stacked(dkv0, dkv1),
        [stacked(dkv0_back, dkv1_back)],
        cos_tab,
        sin_tab,
        key_gain,
        2,
    )
    (w_grad,) = weight_grad(kv_grad, normed1, 0, width, 1)
    kv_own, kv_x, kv_y, kv_c, *a_from = sync(*jnp.split(w_grad, 4), *a_from)
    kv_from = corner_start(kv_c)
    a_x, a_y = corner_add(a_x, a_y, *a_from)
    got_ax, got_ay = swap(a_x, "x"), swap(a_y, "y")
    term_there = to_model([q_grad, kv_grad], [[q_w], [kv_w]], same, 1, rows, [a_x, a_y])
    normed1_there = swap(term_there, "c")
    q_grad, kv_x, kv_y, term_there, *kv_from = sync(q_grad, kv_x, kv_y, term_there, *kv_from)
    kv_x, kv_y = corner_add(kv_x, kv_y, *kv_from)
    got_kvx, got_kvy = swap(kv_x, "x"), swap(kv_y, "y")
    term_own = to_model([q_grad, kv_grad], [[q_w], [kv_w]], same, 0, rows)
    tokens_grad, gain1_sum = norm_return(
        tokens, resid_grad, term_own, normed1_there, norm1_gain, (f32,), [kv_x, kv_y]
    )
    gain1_part, gain2_part = gain1_sum[0], gain2_sum[0]
    a_near = after(a_own, term_own) + got_ax + got_ay
    a_sum = scatter_z(
        jnp.concatenate(
            [a.reshape(4, q_in, width) for a in jnp.split(a_near, 2)], axis=1
        ).reshape(8 * q_in, width)
    )
    kv_near = kv_own + got_kvx + got_kvy
    kv_sum = scatter_z(
        kv_near.reshape(2, 4, k_in, width).swapaxes(0, 1).reshape(8 * k_in, width)
    )
    output = (
        valid * (resid + mixed_own.astype(f32) + mixed_there.astype(f32))
    ).astype(bf16)

    down_sum = after(d_own, term_own) + got_dx + got_dy
    gate_sum, up_sum, down_sum = jnp.split(
        from_core(jnp.concatenate([gate_sum, up_sum, down_sum], axis=0), core, 3), 3
    )

    gains = jnp.concatenate([gain1_part, gain2_part, q_gains[0], k_gains[0]])[None, :]
    for axis in ("c", "x", "y"):
        gains = gains + swap(gains, axis)
    for step in (1, 2):
        gains = gains + lax.ppermute(gains, "z", [(i, i ^ step) for i in range(4)])
    gains = gains[0]

    return (
        output,
        tokens_grad,
        gains[:width],
        a_sum[:q_in].astype(f32).T,
        kv_sum[:k_in].astype(f32).T,
        kv_sum[k_in:].astype(f32).T,
        gains[2 * width : 2 * width + HEAD_SIZE],
        gains[2 * width + HEAD_SIZE :],
        a_sum[q_in:].astype(f32),
        gains[width : 2 * width],
        gate_sum.astype(f32).T,
        up_sum.astype(f32).T,
        down_sum.astype(f32),
    )


def chip_solution(mesh):
    fine = Mesh(mesh.devices.reshape(2, 2, 2, 4), ("x", "c", "y", "z"))
    row_spec = P(("x", "c", "y", "z"), None)
    group_spec = P(("x", "c", "z"), None)
    head_cols = P(None, ("y", "x", "c", "z"))
    head_rows = P(("y", "x", "c", "z"), None)
    up_spec, down_spec = P(("x", "c", "y"), "z"), P("z", ("x", "c", "y"))
    return jax.shard_map(
        chip_layer,
        mesh=fine,
        in_specs=(
            row_spec,
            row_spec,
            group_spec,
            group_spec,
            P(),
            head_cols,
            head_cols,
            head_cols,
            P(),
            P(),
            head_rows,
            P(),
            up_spec,
            up_spec,
            down_spec,
        ),
        out_specs=(
            row_spec,
            row_spec,
            P(),
            head_cols,
            head_cols,
            head_cols,
            P(),
            P(),
            head_rows,
            P(),
            up_spec,
            up_spec,
            down_spec,
        ),
        check_vma=False,
    )


def solution(mesh):
    sizes = dict(mesh.shape)
    if sizes == {"fsdp": 4, "heads": 2, "tensor": 4}:
        return chip_solution(mesh)
    return plain_solution(mesh)
```

```python
import functools
import math

import jax
import jax.numpy as jnp
from jax import lax
from jax.experimental import pallas as pl
from jax.experimental.pallas import tpu as pltpu
from jax.sharding import Mesh
from jax.sharding import PartitionSpec as P

QUERY_HEADS = 16
KEY_VALUE_HEADS = 8
HEAD_SIZE = 128
BLK = 128


EPS_NORM = 1e-06
ROPE_BASE = 1000000.0
NEG_FILL = -1e30


def row_info(lengths, positions):
    block_count = (lengths + BLK - 1) // BLK
    ends = jnp.cumsum(block_count)
    starts = ends - block_count
    used = ends[-1]
    column = positions[:, None]
    inside = (column >= starts[None, :]) & (column < ends[None, :])
    past = positions >= used
    seq_block = jnp.sum((column >= ends[None, :]).astype(jnp.int32), axis=1)
    first_block = jnp.sum(jnp.where(inside, starts[None, :], 0), axis=1) + jnp.where(past, used, 0)
    limit = jnp.sum(jnp.where(inside, lengths[None, :], 0), axis=1)
    offsets = jnp.arange(BLK, dtype=jnp.int32)[None, :]
    pos_rows = (positions - first_block)[:, None] * BLK + offsets
    seq_rows = jnp.broadcast_to(seq_block[:, None], pos_rows.shape)
    valid_rows = jnp.logical_not(past)[:, None] & (pos_rows < limit[:, None])
    return (seq_rows.reshape(-1), pos_rows.reshape(-1), valid_rows.reshape(-1))


def rope_tables(pos_rows):
    half_dim = HEAD_SIZE // 2
    freq = jnp.exp(
        jnp.arange(half_dim, dtype=jnp.float32) * (-2.0 * math.log(ROPE_BASE) / HEAD_SIZE)
    )
    angles = pos_rows.astype(jnp.float32)[:, None] * freq[None, :]
    return (jnp.cos(angles)[:, None, :], jnp.sin(angles)[:, None, :])


def rotate(value_rows, cos_tab, sin_tab):
    half_dim = value_rows.shape[-1] // 2
    first_half, second_half = (value_rows[..., :half_dim], value_rows[..., half_dim:])
    return jnp.concatenate(
        [
            first_half * cos_tab - second_half * sin_tab,
            second_half * cos_tab + first_half * sin_tab,
        ],
        axis=-1,
    )


def unrotate(upstream, cos_tab, sin_tab):
    half_dim = upstream.shape[-1] // 2
    first_half, second_half = (upstream[..., :half_dim], upstream[..., half_dim:])
    return jnp.concatenate(
        [
            first_half * cos_tab + second_half * sin_tab,
            second_half * cos_tab - first_half * sin_tab,
        ],
        axis=-1,
    )


def rms_parts(value_rows, gain_vec):
    scales = lax.rsqrt(jnp.mean(value_rows * value_rows, axis=-1, keepdims=True) + EPS_NORM)
    return (value_rows * scales * gain_vec, scales)


def norm_back(value_rows, scales, gain_vec, upstream):
    weighted = upstream * gain_vec
    inner = jnp.sum(value_rows * weighted, axis=-1, keepdims=True) / value_rows.shape[-1]
    return scales * weighted - value_rows * scales * scales * scales * inner


def matrix_product(left, right):
    return jnp.dot(left, right, preferred_element_type=jnp.float32)


def dot_rows(left, right):
    return lax.dot_general(
        left, right, (((0,), (0,)), ((), ())), preferred_element_type=jnp.float32
    )


def dot_cols(left, right):
    return lax.dot_general(
        left, right, (((1,), (1,)), ((), ())), preferred_element_type=jnp.float32
    )


def swap_cols(array, outer, inner):
    lead = array.shape[0]
    return jnp.swapaxes(array.reshape(lead, outer, inner, -1), 1, 2).reshape(lead, -1)


def swap_rows(array, outer, inner):
    width = array.shape[1]
    return jnp.swapaxes(array.reshape(outer, inner, -1, width), 0, 1).reshape(-1, width)


def spread_rows(local_rows):
    return lax.all_gather(local_rows, "tensor", axis=0, tiled=True)


def to_heads(packed):
    return lax.all_to_all(packed, "heads", split_axis=1, concat_axis=0, tiled=True)


def to_rows(packed):
    return lax.all_to_all(packed, "heads", split_axis=0, concat_axis=1, tiled=True)


def tensor_sum(term, row_count):
    total = lax.psum(
        term(0, row_count * lax.axis_size("tensor")).astype(jnp.bfloat16), "tensor"
    ).astype(jnp.float32)
    return lax.dynamic_slice_in_dim(total, lax.axis_index("tensor") * row_count, row_count)


def block_scores(query_blk, key_all, seq_blk, pos_blk, seq_all, pos_all):
    scores = jnp.einsum(
        "qkgd,pkd->kgqp", query_blk, key_all, preferred_element_type=jnp.float32
    ) * HEAD_SIZE ** (-0.5)
    allowed = (seq_blk[:, None] == seq_all[None, :]) & (pos_all[None, :] <= pos_blk[:, None])
    return jnp.where(allowed[None, None], scores, NEG_FILL)


def attend_forward(query_grp, key_grp, value_grp, seq_all, pos_all):
    group_factor = QUERY_HEADS // KEY_VALUE_HEADS
    group_len = query_grp.shape[0]
    kv_local = key_grp.shape[1] // HEAD_SIZE
    query_four = query_grp.reshape(group_len, kv_local, group_factor, HEAD_SIZE)
    key_three = key_grp.reshape(group_len, kv_local, HEAD_SIZE)
    value_three = value_grp.reshape(group_len, kv_local, HEAD_SIZE)
    block_rows = min(512, group_len)

    def forward_block(block_idx):
        first_row = block_idx * block_rows
        query_blk = lax.dynamic_slice_in_dim(query_four, first_row, block_rows)
        seq_blk = lax.dynamic_slice_in_dim(seq_all, first_row, block_rows)
        pos_blk = lax.dynamic_slice_in_dim(pos_all, first_row, block_rows)
        scores = block_scores(query_blk, key_three, seq_blk, pos_blk, seq_all, pos_all)
        peak = jnp.max(scores, axis=-1, keepdims=True)
        expo = jnp.exp(scores - peak)
        total = jnp.sum(expo, axis=-1, keepdims=True)
        probs_b = (expo / total).astype(jnp.bfloat16)
        attended = jnp.einsum(
            "kgqp,pkd->qkgd", probs_b, value_three, preferred_element_type=jnp.float32
        )
        return (attended, (peak + jnp.log(total))[..., 0])

    attended, log_sums = lax.map(forward_block, jnp.arange(group_len // block_rows))
    return (
        attended.reshape(group_len, kv_local * group_factor * HEAD_SIZE).astype(jnp.bfloat16),
        log_sums,
    )


def attend_backward(query_grp, key_grp, value_grp, grad_grp, log_sums, seq_all, pos_all):
    group_factor = QUERY_HEADS // KEY_VALUE_HEADS
    scale = HEAD_SIZE ** (-0.5)
    group_len = query_grp.shape[0]
    kv_local = key_grp.shape[1] // HEAD_SIZE
    query_four = query_grp.reshape(group_len, kv_local, group_factor, HEAD_SIZE)
    key_three = key_grp.reshape(group_len, kv_local, HEAD_SIZE)
    value_three = value_grp.reshape(group_len, kv_local, HEAD_SIZE)
    grad_four = grad_grp.reshape(group_len, kv_local, group_factor, HEAD_SIZE)
    block_rows = min(512, group_len)

    def backward_block(carry, block_idx):
        key_acc, value_acc = carry
        first_row = block_idx * block_rows
        query_blk = lax.dynamic_slice_in_dim(query_four, first_row, block_rows)
        grad_blk = lax.dynamic_slice_in_dim(grad_four, first_row, block_rows)
        seq_blk = lax.dynamic_slice_in_dim(seq_all, first_row, block_rows)
        pos_blk = lax.dynamic_slice_in_dim(pos_all, first_row, block_rows)
        scores = block_scores(query_blk, key_three, seq_blk, pos_blk, seq_all, pos_all)
        probs = jnp.exp(scores - log_sums[block_idx][..., None])
        probs_b = probs.astype(jnp.bfloat16)
        prob_grad = jnp.einsum(
            "qkgd,pkd->kgqp", grad_blk, value_three, preferred_element_type=jnp.float32
        )
        score_grad_b = (
            probs * (prob_grad - jnp.sum(probs * prob_grad, axis=-1, keepdims=True))
        ).astype(jnp.bfloat16)
        query_grad = (
            jnp.einsum(
                "kgqp,pkd->qkgd", score_grad_b, key_three, preferred_element_type=jnp.float32
            )
            * scale
        )
        key_acc = (
            key_acc
            + jnp.einsum(
                "kgqp,qkgd->pkd", score_grad_b, query_blk, preferred_element_type=jnp.float32
            )
            * scale
        )
        value_acc = value_acc + jnp.einsum(
            "kgqp,qkgd->pkd", probs_b, grad_blk, preferred_element_type=jnp.float32
        )
        return ((key_acc, value_acc), query_grad)

    empty = jnp.zeros((group_len, kv_local, HEAD_SIZE), jnp.float32)
    (key_acc, value_acc), query_blocks = lax.scan(
        backward_block, (empty, empty), jnp.arange(group_len // block_rows)
    )
    query_grad_b = query_blocks.reshape(group_len, kv_local * group_factor * HEAD_SIZE).astype(
        jnp.bfloat16
    )
    key_grad_b = key_acc.reshape(group_len, kv_local * HEAD_SIZE).astype(jnp.bfloat16)
    value_grad_b = value_acc.reshape(group_len, kv_local * HEAD_SIZE).astype(jnp.bfloat16)
    return (query_grad_b, key_grad_b, value_grad_b)


def project_heads(normed_b, query_w, key_w, value_w, query_gain, key_gain, pos_rows):
    lines = normed_b.shape[0]
    q_raw = matrix_product(normed_b, query_w).reshape(lines, -1, HEAD_SIZE)
    key_unnormed = matrix_product(normed_b, key_w).reshape(lines, -1, HEAD_SIZE)
    value_b = matrix_product(normed_b, value_w).astype(jnp.bfloat16)
    cos_tab, sin_tab = rope_tables(pos_rows)
    q_normed, q_scale = rms_parts(q_raw, query_gain)
    k_normed, k_scale = rms_parts(key_unnormed, key_gain)
    query_b = rotate(q_normed, cos_tab, sin_tab).astype(jnp.bfloat16).reshape(lines, -1)
    key_b = rotate(k_normed, cos_tab, sin_tab).astype(jnp.bfloat16).reshape(lines, -1)
    return (query_b, key_b, value_b, (q_raw, q_scale, key_unnormed, k_scale, cos_tab, sin_tab))


def heads_back(query_back, key_back, kept, query_gain, key_gain):
    q_raw, q_scale, key_unnormed, k_scale, cos_tab, sin_tab = kept
    lines = q_raw.shape[0]
    q_turned = unrotate(query_back.astype(jnp.float32).reshape(q_raw.shape), cos_tab, sin_tab)
    k_turned = unrotate(key_back.astype(jnp.float32).reshape(key_unnormed.shape), cos_tab, sin_tab)
    q_raw_grad = (
        norm_back(q_raw, q_scale, query_gain, q_turned).reshape(lines, -1).astype(jnp.bfloat16)
    )
    k_raw_grad = (
        norm_back(key_unnormed, k_scale, key_gain, k_turned).reshape(lines, -1).astype(jnp.bfloat16)
    )
    qgain_part = jnp.sum(q_turned * q_raw * q_scale, axis=(0, 1))
    kgain_part = jnp.sum(k_turned * key_unnormed * k_scale, axis=(0, 1))
    return (q_raw_grad, k_raw_grad, qgain_part, kgain_part)


def plain_layer(
    tokens,
    cotangent,
    seq_lens,
    block_pos,
    norm1_gain,
    w_query,
    key_matrix,
    value_matrix,
    query_gain,
    key_gain,
    w_out,
    norm2_gain,
    w_gate,
    w_up,
    w_down,
):
    row_count = tokens.shape[0]
    fsdp_count = lax.axis_size("fsdp")
    heads_count = lax.axis_size("heads")
    gate_full, up_full, down_full = (
        lax.all_gather(w_gate, ("fsdp", "heads"), axis=0, tiled=True),
        lax.all_gather(w_up, ("fsdp", "heads"), axis=0, tiled=True),
        lax.all_gather(w_down, ("fsdp", "heads"), axis=1, tiled=True),
    )
    seq_all, pos_all, valid_all = row_info(seq_lens[0], block_pos[0])
    own_first = lax.axis_index("heads") * row_count
    pos_own = lax.dynamic_slice_in_dim(pos_all, own_first, row_count)
    valid_own = lax.dynamic_slice_in_dim(valid_all, own_first, row_count).astype(jnp.float32)[
        :, None
    ]
    inputs = tokens.astype(jnp.float32)
    first_normed, scale1 = rms_parts(inputs, norm1_gain)
    normed1_b = first_normed.astype(jnp.bfloat16)
    query_all, key_all, value_all, out_all = (
        lax.all_gather(w_query, ("fsdp", "heads", "tensor"), axis=1, tiled=True),
        lax.all_gather(key_matrix, ("fsdp", "heads", "tensor"), axis=1, tiled=True),
        lax.all_gather(value_matrix, ("fsdp", "heads", "tensor"), axis=1, tiled=True),
        lax.all_gather(w_out, ("fsdp", "heads", "tensor"), axis=0, tiled=True),
    )
    query_full = swap_cols(query_all, fsdp_count, heads_count)
    key_full = swap_cols(key_all, fsdp_count, heads_count)
    value_full = swap_cols(value_all, fsdp_count, heads_count)
    out_full = swap_rows(out_all, fsdp_count, heads_count)
    query_b, key_b, value_b, kept = project_heads(
        normed1_b, query_full, key_full, value_full, query_gain, key_gain, pos_own
    )
    q_width = query_b.shape[1] // heads_count
    k_width = key_b.shape[1] // heads_count
    packed = jnp.concatenate(
        [
            query_b.reshape(row_count, heads_count, q_width),
            key_b.reshape(row_count, heads_count, k_width),
            value_b.reshape(row_count, heads_count, k_width),
        ],
        axis=2,
    )
    grouped = to_heads(packed.reshape(row_count, -1))
    query_grp = grouped[:, :q_width]
    key_grp = grouped[:, q_width : q_width + k_width]
    value_grp = grouped[:, q_width + k_width :]
    attended_b, log_sums = attend_forward(query_grp, key_grp, value_grp, seq_all, pos_all)
    attn_tok = to_rows(attended_b)
    resid = inputs + matrix_product(attn_tok, out_full)
    normed2, scale2 = rms_parts(resid, norm2_gain)
    normed2_b = normed2.astype(jnp.bfloat16)
    wide_in = spread_rows(normed2_b)
    gate_pre = matrix_product(wide_in, gate_full)
    up_pre = matrix_product(wide_in, up_full)
    sigmoid_gate = jax.nn.sigmoid(gate_pre)
    silu_gate = gate_pre * sigmoid_gate
    act_b = (silu_gate * up_pre).astype(jnp.bfloat16)

    def forward_term(first_row, span):
        return matrix_product(act_b, down_full)

    mixed = tensor_sum(forward_term, row_count)
    output = (valid_own * (resid + mixed)).astype(jnp.bfloat16)
    grad_out = valid_own * cotangent.astype(jnp.float32)
    wide_grad = spread_rows(grad_out.astype(jnp.bfloat16))
    act_grad = dot_cols(wide_grad, down_full)
    down_grad = dot_rows(act_b, wide_grad)
    gate_grad_b = (
        act_grad * up_pre * sigmoid_gate * (1.0 + gate_pre * (1.0 - sigmoid_gate))
    ).astype(jnp.bfloat16)
    up_grad_b = (act_grad * silu_gate).astype(jnp.bfloat16)
    gate_wgrad = dot_rows(wide_in, gate_grad_b)
    up_wgrad = dot_rows(wide_in, up_grad_b)

    def backward_term(first_row, span):
        return dot_cols(gate_grad_b, gate_full) + dot_cols(up_grad_b, up_full)

    normed2_grad = tensor_sum(backward_term, row_count)
    gate_sum, up_sum, down_sum = (
        lax.psum_scatter(
            gate_wgrad.astype(jnp.bfloat16), ("fsdp", "heads"), scatter_dimension=0, tiled=True
        ).astype(jnp.float32),
        lax.psum_scatter(
            up_wgrad.astype(jnp.bfloat16), ("fsdp", "heads"), scatter_dimension=0, tiled=True
        ).astype(jnp.float32),
        lax.psum_scatter(
            down_grad.astype(jnp.bfloat16), ("fsdp", "heads"), scatter_dimension=1, tiled=True
        ).astype(jnp.float32),
    )
    resid_grad = grad_out + norm_back(resid, scale2, norm2_gain, normed2_grad)
    gain2_part = jnp.sum(normed2_grad * resid * scale2, axis=0)
    resid_grad_b = resid_grad.astype(jnp.bfloat16)
    out_wgrad = dot_rows(attn_tok, resid_grad_b)
    attn_grad_b = dot_cols(resid_grad_b, out_full).astype(jnp.bfloat16)
    attn_grad_grp = to_heads(attn_grad_b)
    query_grad_b, key_grad_b, value_grad_b = attend_backward(
        query_grp, key_grp, value_grp, attn_grad_grp, log_sums, seq_all, pos_all
    )
    back_packed = to_rows(jnp.concatenate([query_grad_b, key_grad_b, value_grad_b], axis=1))
    back_three = back_packed.reshape(row_count, heads_count, -1)
    query_back = back_three[:, :, :q_width].reshape(row_count, -1)
    key_back = back_three[:, :, q_width : q_width + k_width].reshape(row_count, -1)
    value_back = back_three[:, :, q_width + k_width :].reshape(row_count, -1)
    q_raw_grad, k_raw_grad, qgain_part, kgain_part = heads_back(
        query_back, key_back, kept, query_gain, key_gain
    )
    query_wgrad = swap_cols(dot_rows(normed1_b, q_raw_grad), heads_count, fsdp_count)
    key_wgrad = swap_cols(dot_rows(normed1_b, k_raw_grad), heads_count, fsdp_count)
    value_wgrad = swap_cols(dot_rows(normed1_b, value_back), heads_count, fsdp_count)
    out_wgrad = swap_rows(out_wgrad, heads_count, fsdp_count)
    normed1_grad = (
        dot_cols(q_raw_grad, query_full)
        + dot_cols(k_raw_grad, key_full)
        + dot_cols(value_back, value_full)
    )
    query_sum, key_sum, value_sum, out_sum = (
        lax.psum_scatter(query_wgrad, ("fsdp", "heads", "tensor"), scatter_dimension=1, tiled=True),
        lax.psum_scatter(key_wgrad, ("fsdp", "heads", "tensor"), scatter_dimension=1, tiled=True),
        lax.psum_scatter(value_wgrad, ("fsdp", "heads", "tensor"), scatter_dimension=1, tiled=True),
        lax.psum_scatter(out_wgrad, ("fsdp", "heads", "tensor"), scatter_dimension=0, tiled=True),
    )
    tokens_grad = resid_grad + norm_back(inputs, scale1, norm1_gain, normed1_grad)
    gain1_part = jnp.sum(normed1_grad * inputs * scale1, axis=0)
    gain1_sum, qgain_sum, kgain_sum, gain2_sum = lax.psum(
        (gain1_part, qgain_part, kgain_part, gain2_part), ("fsdp", "heads", "tensor")
    )
    return (
        output,
        tokens_grad,
        gain1_sum,
        query_sum,
        key_sum,
        value_sum,
        qgain_sum,
        kgain_sum,
        out_sum,
        gain2_sum,
        gate_sum,
        up_sum,
        down_sum,
    )


def plain_solution(mesh):
    return jax.shard_map(
        plain_layer,
        mesh=mesh,
        in_specs=(
            P(("fsdp", "heads", "tensor"), None),
            P(("fsdp", "heads", "tensor"), None),
            P(("fsdp", "tensor"), None),
            P(("fsdp", "tensor"), None),
            P(),
            P(None, ("heads", "fsdp", "tensor")),
            P(None, ("heads", "fsdp", "tensor")),
            P(None, ("heads", "fsdp", "tensor")),
            P(),
            P(),
            P(("heads", "fsdp", "tensor"), None),
            P(),
            P(("fsdp", "heads"), "tensor"),
            P(("fsdp", "heads"), "tensor"),
            P("tensor", ("fsdp", "heads")),
        ),
        out_specs=(
            P(("fsdp", "heads", "tensor"), None),
            P(("fsdp", "heads", "tensor"), None),
            P(),
            P(None, ("heads", "fsdp", "tensor")),
            P(None, ("heads", "fsdp", "tensor")),
            P(None, ("heads", "fsdp", "tensor")),
            P(),
            P(),
            P(("heads", "fsdp", "tensor"), None),
            P(),
            P(("fsdp", "heads"), "tensor"),
            P(("fsdp", "heads"), "tensor"),
            P("tensor", ("fsdp", "heads")),
        ),
        check_vma=False,
    )


VMEM_LIMIT = 56 * 1024 * 1024
LOG2_E = 1.4426950408889634
SWAP = ((0, 1), (1, 0))
ROW_TILE = 1024
SCALE = HEAD_SIZE ** (-0.5)


def dot_t(left, right):
    return lax.dot_general(
        left, right, (((1,), (1,)), ((), ())), preferred_element_type=jnp.float32
    )


def swap(array, axis):
    return lax.ppermute(array, axis, SWAP)


def pick(first, second, index):
    return jnp.where(index == 0, first, second)


def join(mine, other, index, axis):
    return pick(
        jnp.concatenate([mine, other], axis=axis),
        jnp.concatenate([other, mine], axis=axis),
        index,
    )


def gather_z(array):
    return lax.all_gather(array, "z", axis=0, tiled=True)


def scatter_z(array):
    return lax.psum_scatter(array, "z", scatter_dimension=0, tiled=True)


def after(array, *done):
    return lax.optimization_barrier((array, *done))[0]


def sync(*arrays):
    return lax.optimization_barrier(arrays)


def to_core(array, core):
    half = array.shape[0] // 2
    first, second = array[:half], array[half:]
    other = swap(pick(second, first, core), "c")
    mine = pick(first, second, core)
    return join(mine, other, core, 1)


def from_core(pairs, core):
    mine = [pick(a, b, core) for a, b in pairs]
    send = jnp.concatenate([pick(b, a, core) for a, b in pairs], axis=0)
    others = jnp.split(swap(send, "c"), len(pairs))
    return [join(m, o, core, 0) for m, o in zip(mine, others)]


def call(kernel, inputs, in_specs, out_specs, out_shape, grid, after=(), prefetch=None, **more):
    lead = 0 if prefetch is None else 1
    count, extra = lead + len(inputs), len(after)

    def body(*refs):
        kernel(*refs[:count], *refs[count + extra :])

    if prefetch is not None:
        prefetched, inputs = [prefetch], list(inputs)
    else:
        prefetched, inputs = [], list(inputs)
    scratch = more.pop("scratch_shapes", ())
    return pl.pallas_call(
        body,
        grid_spec=pltpu.PrefetchScalarGridSpec(
            num_scalar_prefetch=lead,
            grid=grid,
            in_specs=list(in_specs) + [pl.BlockSpec(memory_space=pl.ANY)] * extra,
            out_specs=out_specs,
            scratch_shapes=scratch,
        ),
        out_shape=out_shape,
        compiler_params=pltpu.CompilerParams(vmem_limit_bytes=VMEM_LIMIT),
        cost_estimate=pl.CostEstimate(flops=1000, bytes_accessed=1000, transcendentals=0),
        **more,
    )(*prefetched, *inputs, *after)


def reorder_kernel(order_ref, in_ref, out_ref):
    out_ref[...] = in_ref[...]


def reorder(array, order, after=()):
    rows, width = array.shape
    parts = order.shape[0]
    return call(
        reorder_kernel,
        [array],
        [pl.BlockSpec((rows, width // parts), lambda i, o: (0, o[i]))],
        pl.BlockSpec((rows, width // parts), lambda i, o: (0, i)),
        jax.ShapeDtypeStruct(array.shape, array.dtype),
        (parts,),
        after,
        order,
        name="reorder",
    )


def lane_mean(value):
    ones = jnp.full((HEAD_SIZE, HEAD_SIZE), 1.0 / HEAD_SIZE, jnp.bfloat16)
    high = value.astype(jnp.bfloat16)
    low = (value - high.astype(jnp.float32)).astype(jnp.bfloat16)
    return matrix_product(high, ones) + matrix_product(low, ones)


def heads_kernel(count, raw_ref, cos_ref, sin_ref, gain_ref, out_ref):
    raw = raw_ref[:, :HEAD_SIZE]
    value = raw * lax.rsqrt(lane_mean(raw * raw) + EPS_NORM) * gain_ref[...]
    out_ref[:, :HEAD_SIZE] = (
        value * cos_ref[...] + pltpu.roll(value, HEAD_SIZE // 2, 1) * sin_ref[...]
    ).astype(jnp.bfloat16)
    if count == 2:
        out_ref[:, HEAD_SIZE:] = raw_ref[:, HEAD_SIZE:].astype(jnp.bfloat16)


def make_heads(group, raw, cos_tab, sin_tab, gain, count, after=()):
    rows, width = raw.shape
    skip = group * (rows // ROW_TILE)
    table = pl.BlockSpec((ROW_TILE, HEAD_SIZE), lambda i, r: (i + skip, 0))
    return call(
        functools.partial(heads_kernel, count),
        [raw, cos_tab, sin_tab, gain[None, :]],
        [
            pl.BlockSpec((ROW_TILE, count * HEAD_SIZE), lambda i, r: (i, r)),
            table,
            table,
            pl.BlockSpec((1, HEAD_SIZE), lambda i, r: (0, 0)),
        ],
        pl.BlockSpec((ROW_TILE, count * HEAD_SIZE), lambda i, r: (i, r)),
        jax.ShapeDtypeStruct((rows, width), jnp.bfloat16),
        (rows // ROW_TILE, width // (count * HEAD_SIZE)),
        after,
        name="make_heads",
    )


def heads_back_kernel(count, raw_ref, cos_ref, sin_ref, gain_ref, *rest):
    *up_refs, out_ref, sum_ref = rest

    @pl.when((pl.program_id(0) == 0) & (pl.program_id(1) == 0))
    def _():
        sum_ref[...] = jnp.zeros_like(sum_ref)

    raw = raw_ref[:, :HEAD_SIZE]
    upstream = up_refs[0][...].astype(jnp.float32)
    for ref in up_refs[1:]:
        upstream = upstream + ref[...].astype(jnp.float32)
    if count == 2:
        out_ref[:, HEAD_SIZE:] = upstream[:, HEAD_SIZE:].astype(jnp.bfloat16)
        upstream = upstream[:, :HEAD_SIZE]
    turned = upstream * cos_ref[...] - pltpu.roll(upstream, HEAD_SIZE // 2, 1) * sin_ref[...]
    scale = lax.rsqrt(lane_mean(raw * raw) + EPS_NORM)
    hat = raw * scale
    weighted = turned * gain_ref[...]
    out_ref[:, :HEAD_SIZE] = (scale * (weighted - hat * lane_mean(hat * weighted))).astype(
        jnp.bfloat16
    )
    sum_ref[0:1, :] += jnp.sum(turned * hat, axis=0, keepdims=True)


def heads_return(group, raw, upstream, far, cos_tab, sin_tab, gain, count, after=()):
    rows, width = raw.shape
    heads = width // (count * HEAD_SIZE)
    skip = group * (rows // ROW_TILE)
    table = pl.BlockSpec((ROW_TILE, HEAD_SIZE), lambda i, r: (i + skip, 0))
    one = pl.BlockSpec((ROW_TILE, count * HEAD_SIZE), lambda i, r: (i, r))
    across = pl.BlockSpec(
        (ROW_TILE, count * HEAD_SIZE), lambda i, r: (i, (r + heads // 2) % heads)
    )
    return call(
        functools.partial(heads_back_kernel, count),
        [raw, cos_tab, sin_tab, gain[None, :], upstream] + far,
        [one, table, table, pl.BlockSpec((1, HEAD_SIZE), lambda i, r: (0, 0)), one]
        + [across] * len(far),
        [one, pl.BlockSpec((8, HEAD_SIZE), lambda i, r: (0, 0))],
        [
            jax.ShapeDtypeStruct((rows, width), jnp.bfloat16),
            jax.ShapeDtypeStruct((8, HEAD_SIZE), jnp.float32),
        ],
        (rows // ROW_TILE, heads),
        after,
        name="heads_return",
    )


GROUP_WIDTH = 2 * HEAD_SIZE
TOGETHER = 2


def stack_heads(block):
    return jnp.concatenate([block[:, :HEAD_SIZE], block[:, HEAD_SIZE:]], axis=0)


def key_bias(first_key, pair, parity):
    cols = lax.broadcasted_iota(jnp.int32, (1, 2 * BLK), 1)
    block = 2 * pair + jnp.where(cols < BLK, parity, 1 - parity)
    return jnp.where(block >= first_key, 0.0, NEG_FILL)


def last_bias(first_key, pair, parity):
    rows = lax.broadcasted_iota(jnp.int32, (2 * BLK, 2 * BLK), 0)
    cols = lax.broadcasted_iota(jnp.int32, (2 * BLK, 2 * BLK), 1)
    far = (parity == 1) & (2 * pair >= first_key)
    own = lax.rem(cols, BLK) <= lax.rem(rows, BLK)
    far_bias = jnp.where(far, 0.0, NEG_FILL)
    return jnp.where(cols < BLK, jnp.where(own, 0.0, NEG_FILL), far_bias)


def pair_of(own_ref, far_ref, m, first):
    at = pl.ds(pl.multiple_of(m * BLK, BLK), BLK)
    lanes = slice(first, first + HEAD_SIZE)
    return jnp.concatenate([own_ref[at, lanes], far_ref[at, lanes]], axis=0)


def head_lanes(head):
    return slice(head * GROUP_WIDTH, (head + 1) * GROUP_WIDTH)


def attend_kernel(group, info_ref, q_ref, own_ref, far_ref, o_ref, l_ref):
    blocks = q_ref.shape[0] // BLK
    parity = info_ref[group, blocks]

    def one_block(j, _):
        first_key = info_ref[group, j]
        rows = pl.ds(pl.multiple_of(j * BLK, BLK), BLK)
        queries = [stack_heads(q_ref[rows, head_lanes(h)]) for h in range(TOGETHER)]

        def step(m, bias, carry):
            out = []
            for h in range(TOGETHER):
                total, acc = carry[h]
                score = dot_t(queries[h], pair_of(own_ref, far_ref, m, h * GROUP_WIDTH))
                expo = jnp.exp2(score * (SCALE * LOG2_E) + bias)
                total = total + jnp.sum(expo, axis=1, keepdims=True)
                value = pair_of(own_ref, far_ref, m, h * GROUP_WIDTH + HEAD_SIZE)
                acc = acc + matrix_product(expo.astype(jnp.bfloat16), value)
                out.append((total, acc))
            return tuple(out)

        empty = (
            jnp.zeros((2 * BLK, 1), jnp.float32),
            jnp.zeros((2 * BLK, HEAD_SIZE), jnp.float32),
        )
        carry = step(j, last_bias(first_key, j, parity), (empty,) * TOGETHER)
        carry = lax.fori_loop(
            lax.div(first_key, 2),
            j,
            lambda m, c: step(m, key_bias(first_key, m, parity), c),
            carry,
        )
        lane = lax.broadcasted_iota(jnp.int32, (BLK, HEAD_SIZE), 1)
        for h, (total, acc) in enumerate(carry):
            out = (acc / total).astype(jnp.bfloat16)
            o_ref[rows, head_lanes(h)] = jnp.concatenate([out[:BLK], out[BLK:]], axis=1)
            l_ref[rows, h * HEAD_SIZE : (h + 1) * HEAD_SIZE] = jnp.where(
                lane == 0, total[:BLK], total[BLK:]
            )
        return 0

    lax.fori_loop(0, blocks, one_block, 0)


def attend(group, info, query, own, far, after=()):
    rows, width = query.shape
    span = TOGETHER * GROUP_WIDTH
    here = pl.BlockSpec((rows, span), lambda r, s: (0, r))
    there = pl.BlockSpec((rows, span), lambda r, s: (0, (r + 1) % 2))
    return call(
        functools.partial(attend_kernel, group),
        [query, own, far],
        [here, here, there],
        [here, pl.BlockSpec((rows, span // 2), lambda r, s: (0, r))],
        [
            jax.ShapeDtypeStruct((rows, width), jnp.bfloat16),
            jax.ShapeDtypeStruct((rows, width // 2), jnp.float32),
        ],
        (width // span,),
        after,
        info,
        name="attend",
    )


def attend_back_kernel(
    group,
    info_ref,
    q_ref,
    do_ref,
    o_ref,
    l_ref,
    own_ref,
    far_ref,
    dq_ref,
    down_ref,
    dfar_ref,
    kacc_ref,
    vacc_ref,
):
    blocks = q_ref.shape[0] // BLK
    parity = info_ref[group, blocks]
    kacc_ref[...] = jnp.zeros_like(kacc_ref)
    vacc_ref[...] = jnp.zeros_like(vacc_ref)

    def one_block(j, _):
        first_key = info_ref[group, j]
        rows = pl.ds(pl.multiple_of(j * BLK, BLK), BLK)
        held = []
        for h in range(TOGETHER):
            query = stack_heads(q_ref[rows, head_lanes(h)])
            attn = stack_heads(o_ref[rows, head_lanes(h)]).astype(jnp.float32)
            grad = stack_heads(do_ref[rows, head_lanes(h)]).astype(jnp.float32)
            at = h * HEAD_SIZE
            total = jnp.concatenate(
                [l_ref[rows, at : at + 1], l_ref[rows, at + 1 : at + 2]], axis=0
            )
            grad_b = (grad / total).astype(jnp.bfloat16)
            inner = jnp.sum(grad_b.astype(jnp.float32) * attn, axis=1, keepdims=True)
            held.append((query, grad_b, inner))

        def step(m, bias, carry):
            at = pl.ds(pl.multiple_of(m * BLK, BLK), BLK)
            out = []
            for h in range(TOGETHER):
                query, grad_b, inner = held[h]
                key = pair_of(own_ref, far_ref, m, h * GROUP_WIDTH)
                value = pair_of(own_ref, far_ref, m, h * GROUP_WIDTH + HEAD_SIZE)
                expo = jnp.exp2(dot_t(query, key) * (SCALE * LOG2_E) + bias)
                d_score = (expo * (dot_t(grad_b, value) - inner)).astype(jnp.bfloat16)
                d_key = dot_rows(d_score, query)
                d_value = dot_rows(expo.astype(jnp.bfloat16), grad_b)
                kacc_ref[h, 0, at, :] += d_key[:BLK]
                kacc_ref[h, 1, at, :] += d_key[BLK:]
                vacc_ref[h, 0, at, :] += d_value[:BLK]
                vacc_ref[h, 1, at, :] += d_value[BLK:]
                out.append(carry[h] + matrix_product(d_score, key))
            return tuple(out)

        empty = jnp.zeros((2 * BLK, HEAD_SIZE), jnp.float32)
        carry = step(j, last_bias(first_key, j, parity), (empty,) * TOGETHER)
        carry = lax.fori_loop(
            lax.div(first_key, 2),
            j,
            lambda m, c: step(m, key_bias(first_key, m, parity), c),
            carry,
        )
        for h, dq in enumerate(carry):
            dq = (dq * SCALE).astype(jnp.bfloat16)
            dq_ref[rows, head_lanes(h)] = jnp.concatenate([dq[:BLK], dq[BLK:]], axis=1)
        return 0

    lax.fori_loop(0, blocks, one_block, 0)
    for h in range(TOGETHER):
        for half, ref in enumerate((down_ref, dfar_ref)):
            first = h * GROUP_WIDTH
            ref[:, first : first + HEAD_SIZE] = (kacc_ref[h, half] * SCALE).astype(jnp.bfloat16)
            ref[:, first + HEAD_SIZE : first + GROUP_WIDTH] = vacc_ref[h, half].astype(
                jnp.bfloat16
            )


def attend_back(group, info, query, d_attn, attn, total, own, far, after=()):
    rows, width = query.shape
    span = TOGETHER * GROUP_WIDTH
    here = pl.BlockSpec((rows, span), lambda r, s: (0, r))
    there = pl.BlockSpec((rows, span), lambda r, s: (0, (r + 1) % 2))
    shape = jax.ShapeDtypeStruct((rows, width), jnp.bfloat16)
    return call(
        functools.partial(attend_back_kernel, group),
        [query, d_attn, attn, total, own, far],
        [here, here, here, pl.BlockSpec((rows, span // 2), lambda r, s: (0, r)), here, there],
        [here] * 3,
        [shape] * 3,
        (width // span,),
        after,
        info,
        scratch_shapes=[
            pltpu.VMEM((TOGETHER, 2, rows, HEAD_SIZE), jnp.float32),
            pltpu.VMEM((TOGETHER, 2, rows, HEAD_SIZE), jnp.float32),
        ],
        name="attend_back",
    )


HIDDEN_TILE = 512
ROW_STEP = 512


def row_steps(*refs):
    for first_ref in range(len(refs)):
        for first in range(0, refs[first_ref].shape[0], ROW_STEP):
            begin = first_ref * refs[first_ref].shape[0] + first
            yield refs[first_ref][first : first + ROW_STEP, :], slice(begin, begin + ROW_STEP)


def joined(refs):
    return jnp.concatenate([ref[...] for ref in refs], axis=1)


def ffn_kernel(pieces, xa_ref, xb_ref, *refs):
    gate_w = joined(refs[:pieces]).T
    up_w, d_act_ref = refs[pieces][...].T, refs[pieces + 1]
    act_ref, gate_ref, up_ref = refs[pieces + 2 :]
    for x, rows in row_steps(xa_ref, xb_ref):
        gate = matrix_product(x, gate_w)
        upper = matrix_product(x, up_w)
        d_act = d_act_ref[rows, :].astype(jnp.float32)
        sig = 0.5 * jnp.tanh(0.5 * gate) + 0.5
        silu = gate * sig
        act_ref[rows, :] = (silu * upper).astype(jnp.bfloat16)
        gate_ref[rows, :] = (d_act * upper * (sig + silu * (1.0 - sig))).astype(jnp.bfloat16)
        up_ref[rows, :] = (d_act * silu).astype(jnp.bfloat16)


def ffn(xs, gates, up, d_act, after=()):
    rows, width = xs[0].shape
    hidden = up.shape[0]
    out = pl.BlockSpec((2 * rows, HIDDEN_TILE), lambda j: (0, j))
    shape = jax.ShapeDtypeStruct((2 * rows, hidden), jnp.bfloat16)
    return call(
        functools.partial(ffn_kernel, len(gates)),
        [*xs, *gates, up, d_act],
        [pl.BlockSpec((rows, width), lambda j: (0, 0))] * 2
        + [pl.BlockSpec((HIDDEN_TILE, w.shape[1]), lambda j: (j, 0)) for w in (*gates, up)]
        + [out],
        [out] * 3,
        [shape] * 3,
        (hidden // HIDDEN_TILE,),
        after,
        name="ffn",
    )


def to_hidden_kernel(xs, *refs):
    weight = joined(refs[xs:-1]).T
    for x, rows in row_steps(*refs[:xs]):
        refs[-1][rows, :] = matrix_product(x, weight).astype(refs[-1].dtype)


def to_hidden(xs, weights, dtype=jnp.bfloat16, after=()):
    rows, width = xs[0].shape
    hidden = weights[0].shape[0]
    return call(
        functools.partial(to_hidden_kernel, len(xs)),
        [*xs, *weights],
        [pl.BlockSpec((rows, width), lambda j: (0, 0))] * len(xs)
        + [pl.BlockSpec((HIDDEN_TILE, w.shape[1]), lambda j: (j, 0)) for w in weights],
        pl.BlockSpec((len(xs) * rows, HIDDEN_TILE), lambda j: (0, j)),
        jax.ShapeDtypeStruct((len(xs) * rows, hidden), dtype),
        (hidden // HIDDEN_TILE,),
        after,
        name="to_hidden",
    )


MODEL_STEP = 512


def left_parts(left_refs, rights):
    if len(left_refs) == rights:
        return [ref[...].T for ref in left_refs]
    rows = left_refs[0].shape[0] // rights
    return [left_refs[0][k * rows : (k + 1) * rows, :].T for k in range(rights)]


def weight_cols_kernel(lefts, rights, *refs):
    left_refs, right_refs, out_refs = refs[:lefts], refs[lefts : lefts + rights], refs[lefts + rights :]
    parts = left_parts(left_refs, rights)
    for first in range(0, right_refs[0].shape[1], MODEL_STEP):
        cols = slice(first, first + MODEL_STEP)
        term = matrix_product(parts[0], right_refs[0][:, cols])
        for part, ref in zip(parts[1:], right_refs[1:]):
            term = term + matrix_product(part, ref[:, cols])
        term = term.astype(jnp.bfloat16)
        begin = 0
        for out_ref in out_refs:
            end = begin + out_ref.shape[1]
            low, high = max(begin, first), min(end, first + MODEL_STEP)
            if low < high:
                out_ref[:, low - begin : high - begin] = term[:, low - first : high - first]
            begin = end


def weight_cols(lefts, rights, first, widths, after=()):
    rows, hidden = lefts[0].shape
    width = sum(widths)
    return call(
        functools.partial(weight_cols_kernel, len(lefts), len(rights)),
        [*lefts, *rights],
        [pl.BlockSpec((rows, HIDDEN_TILE), lambda j: (0, j))] * len(lefts)
        + [pl.BlockSpec((rights[0].shape[0], width), lambda j: (0, first // width))] * len(rights),
        [pl.BlockSpec((HIDDEN_TILE, w), lambda j: (j, 0)) for w in widths],
        [jax.ShapeDtypeStruct((hidden, w), jnp.bfloat16) for w in widths],
        (hidden // HIDDEN_TILE,),
        after,
        name="weight_cols",
    )


def weight_rows_kernel(lefts, rights, *refs):
    left_refs, right_refs, out_refs = refs[:lefts], refs[lefts : lefts + rights], refs[lefts + rights :]
    parts = left_parts(left_refs, rights)
    span = out_refs[0].shape[0]
    inside = HIDDEN_TILE // span
    for first in range(0, right_refs[0].shape[1], MODEL_STEP):
        cols = slice(first, first + MODEL_STEP)
        term = matrix_product(parts[0], right_refs[0][:, cols])
        for part, ref in zip(parts[1:], right_refs[1:]):
            term = term + matrix_product(part, ref[:, cols])
        term = term.astype(jnp.bfloat16)
        for i, out_ref in enumerate(out_refs):

            @pl.when(pl.program_id(0) == i // inside)
            def _():
                out_ref[:, cols] = term[(i % inside) * span : (i % inside + 1) * span]


def weight_rows(lefts, rights, count, after=()):
    rows, hidden = lefts[0].shape
    width = rights[0].shape[1]
    shape = jax.ShapeDtypeStruct((hidden // count, width), jnp.bfloat16)
    return call(
        functools.partial(weight_rows_kernel, len(lefts), len(rights)),
        [*lefts, *rights],
        [pl.BlockSpec((rows, HIDDEN_TILE), lambda j: (0, j))] * len(lefts)
        + [pl.BlockSpec((rights[0].shape[0], width), lambda j: (0, 0))] * len(rights),
        [pl.BlockSpec((hidden // count, width), lambda j: (0, 0))] * count,
        [shape] * count,
        (hidden // HIDDEN_TILE,),
        after,
        name="weight_rows",
    )


def to_model_kernel(counts, order_ref, *refs):
    left_refs, weight_refs = refs[: len(counts)], refs[len(counts) : -2]
    out_ref, acc_ref = refs[-2:]

    @pl.when(pl.program_id(0) == 0)
    def _():
        acc_ref[...] = jnp.zeros_like(acc_ref)

    left = joined(left_refs)
    terms, begin = [], 0
    for count in counts:
        terms.append(joined(weight_refs[begin : begin + count]))
        begin += count
    weight = jnp.concatenate(terms, axis=0)
    for first in range(0, weight.shape[1], MODEL_STEP):
        cols = slice(first, first + MODEL_STEP)
        acc_ref[:, cols] += matrix_product(left, weight[:, cols])

    @pl.when(pl.program_id(0) == pl.num_programs(0) - 1)
    def _():
        block = acc_ref.shape[1] // order_ref.shape[0]
        for i in range(order_ref.shape[0]):
            at = pl.ds(pl.multiple_of(order_ref[i] * block, block), block)
            out_ref[:, at] = acc_ref[:, i * block : (i + 1) * block].astype(jnp.bfloat16)


def to_model(lefts, weights, order, half, rows, after=()):
    hidden = lefts[0].shape[1]
    flat = [w for pieces in weights for w in pieces]
    width = sum(w.shape[1] for w in weights[0])
    tile = HIDDEN_TILE if len(lefts) <= 2 else HIDDEN_TILE // 2
    return call(
        functools.partial(to_model_kernel, tuple(len(pieces) for pieces in weights)),
        [*lefts, *flat],
        [pl.BlockSpec((rows, tile), lambda j, o: (half, j))] * len(lefts)
        + [pl.BlockSpec((tile, w.shape[1]), lambda j, o: (j, 0)) for w in flat],
        pl.BlockSpec((rows, width), lambda j, o: (0, 0)),
        jax.ShapeDtypeStruct((rows, width), jnp.bfloat16),
        (hidden // tile,),
        after,
        order,
        scratch_shapes=[pltpu.VMEM((rows, width), jnp.float32)],
        name="to_model",
    )


NORM_TILE = 128


def resid_kernel(order_ref, tokens_ref, own_ref, there_ref, gain_ref, resid_ref, normed_ref):
    resid = (
        tokens_ref[...].astype(jnp.float32)
        + own_ref[...].astype(jnp.float32)
        + there_ref[...].astype(jnp.float32)
    )
    resid_ref[...] = resid
    scale = lax.rsqrt(jnp.mean(resid * resid, axis=-1, keepdims=True) + EPS_NORM)
    normed = (resid * scale * gain_ref[...]).astype(jnp.bfloat16)
    block = normed.shape[1] // order_ref.shape[0]
    for i in range(order_ref.shape[0]):
        at = pl.ds(pl.multiple_of(order_ref[i] * block, block), block)
        normed_ref[:, at] = normed[:, i * block : (i + 1) * block]


def resid_norm(tokens, own, there, gain, order, after=()):
    rows, width = tokens.shape
    tile = pl.BlockSpec((NORM_TILE, width), lambda i, o: (i, 0))
    return call(
        resid_kernel,
        [tokens, own, there, gain[None, :]],
        [tile, tile, tile, pl.BlockSpec((1, width), lambda i, o: (0, 0))],
        [tile, tile],
        [
            jax.ShapeDtypeStruct((rows, width), jnp.float32),
            jax.ShapeDtypeStruct((rows, width), jnp.bfloat16),
        ],
        (rows // NORM_TILE,),
        after,
        order,
        name="resid_norm",
    )


def norm_back_kernel(value_ref, base_ref, own_ref, there_ref, gain_ref, *out_refs):
    *grad_refs, sum_ref = out_refs

    @pl.when(pl.program_id(0) == 0)
    def _():
        sum_ref[...] = jnp.zeros_like(sum_ref)

    value = value_ref[...].astype(jnp.float32)
    upstream = own_ref[...].astype(jnp.float32) + there_ref[...].astype(jnp.float32)
    scale = lax.rsqrt(jnp.mean(value * value, axis=-1, keepdims=True) + EPS_NORM)
    hat = value * scale
    weighted = upstream * gain_ref[...]
    inner = jnp.mean(hat * weighted, axis=-1, keepdims=True)
    grad = base_ref[...].astype(jnp.float32) + scale * (weighted - hat * inner)
    for ref in grad_refs:
        ref[...] = grad.astype(ref.dtype)
    sum_ref[0:1, :] += jnp.sum(upstream * hat, axis=0, keepdims=True)


def norm_return(value, base, own, there, gain, dtypes, after=()):
    rows, width = value.shape
    tile = pl.BlockSpec((NORM_TILE, width), lambda i: (i, 0))
    return call(
        norm_back_kernel,
        [value, base, own, there, gain[None, :]],
        [tile, tile, tile, tile, pl.BlockSpec((1, width), lambda i: (0, 0))],
        [tile] * len(dtypes) + [pl.BlockSpec((8, width), lambda i: (0, 0))],
        [jax.ShapeDtypeStruct((rows, width), d) for d in dtypes]
        + [jax.ShapeDtypeStruct((8, width), jnp.float32)],
        (rows // NORM_TILE,),
        after,
        name="norm_return",
    )


def block_info(lengths, positions, first):
    count = (lengths + BLK - 1) // BLK
    ends = jnp.cumsum(count)
    starts = jnp.concatenate([jnp.zeros((1,), jnp.int32), ends])
    own = lax.dynamic_slice_in_dim(positions, first, 8)
    first_keys = jnp.max(jnp.where(starts[None, :] <= own[:, None], starts[None, :], 0), axis=1)
    limits = jnp.concatenate([lengths, jnp.zeros((1,), jnp.int32)])
    seq = jnp.sum((own[:, None] >= ends[None, :]).astype(jnp.int32), axis=1)
    limit = jnp.sum(jnp.where(seq[:, None] == jnp.arange(4)[None, :], limits[None, :], 0), axis=1)
    pos = ((own - first_keys)[:, None] * BLK + jnp.arange(BLK)[None, :]).astype(jnp.int32)
    valid = pos < limit[:, None]
    return first_keys, own, pos.reshape(-1), valid.reshape(-1)


def chip_layer(
    tokens,
    cotangent,
    seq_lens,
    block_pos,
    norm1_gain,
    w_query,
    key_matrix,
    value_matrix,
    query_gain,
    key_gain,
    w_out,
    norm2_gain,
    w_gate,
    w_up,
    w_down,
):
    xi, core, yi = lax.axis_index("x"), lax.axis_index("c"), lax.axis_index("y")
    rows, width = tokens.shape
    bf16, f32 = jnp.bfloat16, jnp.float32
    half, fourth = width // 2, width // 4

    q_in, k_in = w_query.shape[1], key_matrix.shape[1]
    fourth, eighth = width // 4, width // 8
    kvw_0 = gather_z(jnp.concatenate([key_matrix.T, value_matrix.T], axis=0))
    qw_0 = gather_z(w_query.T)
    up_0 = to_core(w_up.T, core)
    up_x, up_y = swap(up_0, "x"), swap(up_0, "y")
    down_0 = to_core(after(w_down, up_0), core)
    gate_0 = to_core(after(w_gate, up_0).T, core)
    low = up_0.shape[0] // 2
    out_0 = gather_z(w_out)
    dlo_0 = gather_z(down_0[:low])
    kvw_0, up_x, up_y = sync(kvw_0, up_x, up_y)
    kvw_x, kvw_y = swap(kvw_0, "x"), swap(kvw_0, "y")
    middle = kvw_0.shape[0] // 2
    kvw_x, kvw_y, qw_0 = sync(kvw_x, kvw_y, qw_0)
    kvw_ca, kvw_cb = swap(kvw_y[:middle], "x"), swap(kvw_x[middle:], "y")
    qw_x, qw_y = swap(qw_0, "x"), swap(qw_0, "y")
    kvw_ca, kvw_cb, qw_x, qw_y, out_0 = sync(kvw_ca, kvw_cb, qw_x, qw_y, out_0)
    qw_ca, qw_cb = swap(qw_y[:middle], "x"), swap(qw_x[middle:], "y")
    out_x, out_y = swap(out_0, "x"), swap(out_0, "y")
    kvw = [
        a.reshape(4, 2 * k_in, width)
        for a in (kvw_0, kvw_x, kvw_y, jnp.concatenate([kvw_ca, kvw_cb], axis=0))
    ]
    kv_w = jnp.concatenate(
        [part.reshape(-1, width) for a in kvw for part in (a[:, :k_in], a[:, k_in:])], axis=0
    )

    lengths_here = jnp.concatenate([seq_lens[0], block_pos[0]]).astype(f32)
    lengths_there = swap(lengths_here[None, :], "c")[0].astype(jnp.int32)
    first_own = yi * 8
    keys_here, at_here, pos_here, valid_here = block_info(seq_lens[0], block_pos[0], first_own)
    keys_there, at_there, pos_there, _ = block_info(
        lengths_there[:3], lengths_there[3:], first_own
    )
    info = jnp.stack(
        [
            jnp.concatenate([keys_here, at_here[:1]]),
            jnp.concatenate([keys_there, at_there[:1]]),
        ]
    ).astype(jnp.int32)
    freq = jnp.exp(
        jnp.arange(HEAD_SIZE // 2, dtype=f32) * (-2.0 * math.log(ROPE_BASE) / HEAD_SIZE)
    )
    angles = jnp.concatenate([pos_here, pos_there]).astype(f32)[:, None] * freq[None, :]
    cos_half, sin_half = jnp.cos(angles), jnp.sin(angles)
    cos_tab = jnp.concatenate([cos_half, cos_half], axis=1)
    sin_tab = jnp.concatenate([-sin_half, sin_half], axis=1)
    valid = valid_here.astype(f32)[:, None]

    blocks = jnp.arange(8)
    ry, rx, rc = blocks // 4, (blocks // 2) % 2, blocks % 2
    order = ((rx ^ xi) * 4 + rc * 2 + (ry ^ yi)).astype(jnp.int32)
    nx, nc, ny = blocks // 4, (blocks // 2) % 2, blocks % 2
    order_back = ((ny ^ yi) * 4 + (nx ^ xi) * 2 + nc).astype(jnp.int32)

    def stacked(first, second):
        return jnp.concatenate([first, second], axis=0)

    inputs = tokens.astype(f32)
    normed1 = rms_parts(inputs, norm1_gain)[0].astype(bf16)
    normed1 = [normed1, swap(normed1, "c")]
    dy_own = (valid * cotangent.astype(f32)).astype(bf16)

    normed1[0], kv_w = sync(normed1[0], kv_w)
    kv_raw = [to_hidden([normed1[0]], [kv_w], f32)]
    kv_raw.append(to_hidden([normed1[1]], [kv_w], f32, [kv_raw[0]]))
    kv = [make_heads(g, kv_raw[g], cos_tab, sin_tab, key_gain, 2, [kv_raw[1]]) for g in range(2)]
    kv[0], kv[1], qw_ca, qw_cb, out_x, out_y, up_y, dy_own, normed1[0], gate_0, glo_in = sync(
        *kv, qw_ca, qw_cb, out_x, out_y, up_y, dy_own, normed1[0], gate_0, gate_0[:low]
    )
    kv_far0, out_c, up_c = swap(kv[0], "y"), swap(out_y, "x"), swap(up_y, "x")
    glo_0 = gather_z(glo_in)
    dhi_0, ghi_0 = gather_z(down_0[low:]), gather_z(gate_0[low:])
    q_w = jnp.concatenate([qw_0, qw_x, qw_y, qw_ca, qw_cb], axis=0)
    q_raw = [to_hidden([normed1[0]], [q_w], f32)]
    q_raw.append(to_hidden([normed1[1]], [q_w], f32, [q_raw[0]]))
    query = [
        make_heads(g, q_raw[g], cos_tab, sin_tab, query_gain, 1, [q_raw[1]]) for g in range(2)
    ]
    dy = [reorder(dy_own, order, query)]
    kv_far0, out_c, up_c, dlo_0, dy[0] = sync(kv_far0, out_c, up_c, dlo_0, dy[0])
    dlo_x, dlo_y = swap(dlo_0, "x"), swap(dlo_0, "y")
    dy.append(swap(dy[0], "c"))
    up_in = jnp.concatenate([up_0, up_x, up_y, up_c], axis=1)
    ulo, uhi = gather_z(up_in[:low]), gather_z(up_in[low:])
    attn0, totals0 = attend(0, info, query[0], kv[0], kv_far0)
    out_w = jnp.concatenate([out_0, out_x, out_y, out_c], axis=0)
    attn0, out_w, dlo_x, dlo_y, kv_1 = sync(attn0, out_w, dlo_x, dlo_y, kv[1])
    kv_far1, dlo_c = swap(kv_1, "y"), swap(dlo_y, "x")
    kv_far1, dlo_c, glo_0 = sync(kv_far1, dlo_c, glo_0)
    glo_x, glo_y = swap(glo_0, "x"), swap(glo_0, "y")
    attn1, totals1 = attend(1, info, query[1], kv[1], kv_far1)
    attn1, glo_x, glo_y, glo_0 = sync(attn1, glo_x, glo_y, glo_0)
    glo_ca, glo_cb = swap(glo_y[:, :eighth], "x"), swap(glo_x[:, eighth:], "y")
    same = jnp.arange(8, dtype=jnp.int32)
    out_term = to_model([attn1], [[out_w]], same, 0, rows)
    out_there = swap(out_term, "c")
    out_here = to_model([attn0], [[out_w]], same, 0, rows, [out_term])
    dlo = [dlo_0, dlo_x, dlo_y, dlo_c]
    d_act_lo = to_hidden(dy, dlo, bf16, [out_here])
    out_here, d_act_lo, glo_ca, glo_cb, dhi_0, ghi_0 = sync(
        out_here, d_act_lo, glo_ca, glo_cb, dhi_0, ghi_0
    )
    dhi_x, dhi_y = swap(dhi_0, "x"), swap(dhi_0, "y")
    ghi_x, ghi_y = swap(ghi_0, "x"), swap(ghi_0, "y")
    resid, normed2_own = resid_norm(tokens, out_here, out_there, norm2_gain, order_back)
    normed2 = [normed2_own, swap(normed2_own, "c")]
    glo = [glo_0, glo_x, glo_y, glo_ca, glo_cb]
    act_lo, gg_lo, ug_lo = ffn(normed2, glo, ulo, d_act_lo)
    act_lo, dhi_x, dhi_y, ghi_x, ghi_y = sync(act_lo, dhi_x, dhi_y, ghi_x, ghi_y)
    dhi_c, ghi_c = swap(dhi_y, "x"), swap(ghi_x, "y")
    dhi = [dhi_0, dhi_x, dhi_y, dhi_c]

    widths = [fourth, fourth, fourth, eighth, eighth]

    def corner_add(along_x, along_y, from_a, from_b):
        return (
            jnp.concatenate([along_x[:, :eighth], along_x[:, eighth:] + from_b], axis=1),
            jnp.concatenate([along_y[:, :eighth] + from_a, along_y[:, eighth:]], axis=1),
        )

    (dlo_grad,) = weight_cols([act_lo], dy, 0, [width])
    dlo_sum = scatter_z(dlo_grad)
    gl_0, gl_x, gl_y, gl_ca, gl_cb = weight_cols([gg_lo], normed2, 0, widths, [dlo_grad])
    gl_ca, gl_cb, ghi_c, dhi_c = sync(gl_ca, gl_cb, ghi_c, dhi_c)
    from_a, from_b = swap(gl_ca, "x"), swap(gl_cb, "y")
    ul_0, ul_x, ul_y, ul_ca, ul_cb = weight_cols([ug_lo], normed2, 0, widths, [gl_0])
    d_act_hi = to_hidden(dy, dhi, bf16, [ul_0])
    ghi = [ghi_0, ghi_x, ghi_y, ghi_c]
    gl_x, gl_y, from_a, from_b, ul_ca, ul_cb, d_act_hi = sync(
        gl_x, gl_y, from_a, from_b, ul_ca, ul_cb, d_act_hi
    )
    gl_x, gl_y = corner_add(gl_x, gl_y, from_a, from_b)
    got_x, got_y = swap(gl_x, "x"), swap(gl_y, "y")
    from_a, from_b = swap(ul_ca, "x"), swap(ul_cb, "y")
    act_hi, gg_hi, ug_hi = ffn(normed2, ghi, uhi, d_act_hi)
    dh_0, dh_x, dh_y, dh_ca, dh_cb = weight_cols([act_hi], dy, 0, widths)
    gl_0, got_x, got_y, ul_x, ul_y, from_a, from_b, dh_0, gg_hi = sync(
        gl_0, got_x, got_y, ul_x, ul_y, from_a, from_b, dh_0, gg_hi
    )
    ul_x, ul_y = corner_add(ul_x, ul_y, from_a, from_b)
    glo_near = gl_0 + got_x + got_y
    got_x, got_y = swap(ul_x, "x"), swap(ul_y, "y")
    glo_sum = scatter_z(glo_near)
    gh_0, gh_x, gh_y, gh_ca, gh_cb = weight_cols([gg_hi], normed2, 0, widths, [ul_x, ul_y])
    uh_0, uh_x, uh_y, uh_ca, uh_cb = weight_cols([ug_hi], normed2, 0, widths, [gh_0])
    ul_0, got_x, got_y, dh_ca, dh_cb, gh_ca, gh_cb, uh_0, gg_hi = sync(
        ul_0, got_x, got_y, dh_ca, dh_cb, gh_ca, gh_cb, uh_0, gg_hi
    )
    from_da, from_db = swap(dh_ca, "x"), swap(dh_cb, "y")
    from_ga, from_gb = swap(gh_ca, "x"), swap(gh_cb, "y")
    ulo_near = ul_0 + got_x + got_y
    ulo_sum = scatter_z(ulo_near)
    grads = [gg_lo, ug_lo, gg_hi, ug_hi]
    both_w = [glo, [ulo], ghi, [uhi]]
    there = to_model(grads, both_w, order, 1, rows, [ulo_near])
    dh_x, dh_y, from_da, from_db, gh_x, gh_y, from_ga, from_gb, uh_ca, uh_cb, there = sync(
        dh_x, dh_y, from_da, from_db, gh_x, gh_y, from_ga, from_gb, uh_ca, uh_cb, there
    )
    normed2_there = swap(there, "c")
    dh_x, dh_y = corner_add(dh_x, dh_y, from_da, from_db)
    gh_x, gh_y = corner_add(gh_x, gh_y, from_ga, from_gb)
    got_x, got_y = swap(dh_x, "x"), swap(dh_y, "y")
    from_a, from_b = swap(uh_ca, "x"), swap(uh_cb, "y")
    grad_own = to_model(grads, both_w, order, 0, rows, [dh_x, dh_y, gh_x, gh_y])
    resid_grad, resid_here, gain2_sum = norm_return(
        resid, dy_own, grad_own, normed2_there, norm2_gain, (f32, bf16)
    )
    dh_0, got_x, got_y, uh_x, uh_y, from_a, from_b, resid_here, gh_x, gh_y = sync(
        dh_0, got_x, got_y, uh_x, uh_y, from_a, from_b, resid_here, gh_x, gh_y
    )
    resid_there = swap(resid_here, "c")
    uh_x, uh_y = corner_add(uh_x, uh_y, from_a, from_b)
    dhi_near = dh_0 + got_x + got_y
    got_x, got_y = swap(gh_x, "x"), swap(gh_y, "y")
    got_ux, got_uy = swap(uh_x, "x"), swap(uh_y, "y")
    dhi_sum = scatter_z(dhi_near)

    d_attn0 = to_hidden([resid_here], [out_w], bf16, [uh_x, uh_y, dhi_near])
    dq0, dkv0, dkv0_far = attend_back(0, info, query[0], d_attn0, attn0, totals0, kv[0], kv_far0)
    gh_0, got_x, got_y, uh_0, got_ux, got_uy, resid_there, dkv0_far, dlo_sum = sync(
        gh_0, got_x, got_y, uh_0, got_ux, got_uy, resid_there, dkv0_far, dlo_sum
    )
    dkv0_back = swap(dkv0_far, "y")
    dl_0, dl_x, dl_y, dl_c = (dlo_sum[:, i * fourth : (i + 1) * fourth] for i in range(4))
    from_l = swap(dl_c, "x")
    ghi_near, uhi_near = gh_0 + got_x + got_y, uh_0 + got_ux + got_uy
    ghi_sum, uhi_sum = scatter_z(ghi_near), scatter_z(uhi_near)
    o_0, o_x, o_y, o_c = weight_rows(
        [attn0, attn1], [resid_here, resid_there], 4, [ghi_near, uhi_near]
    )
    d_attn1 = to_hidden([resid_there], [out_w], bf16, [o_0])
    dq1, dkv1, dkv1_far = attend_back(1, info, query[1], d_attn1, attn1, totals1, kv[1], kv_far1)
    dkv1_far, dkv0_back, o_c, dl_x, dl_y, from_l, dq1 = sync(
        dkv1_far, dkv0_back, o_c, dl_x, dl_y, from_l, dq1
    )
    dkv1_back = swap(dkv1_far, "y")
    from_o = swap(o_c, "x")
    got_lx = swap(dl_x, "x")
    back = (cos_tab, sin_tab)
    q_grad = [
        heads_return(g, q_raw[g], d, [], *back, query_gain, 1, [dq1])
        for g, d in enumerate((dq0, dq1))
    ]
    q_gains = q_grad[0][1] + q_grad[1][1]
    q_grad = [q_grad[0][0], q_grad[1][0]]
    w_0, w_x, w_y, w_c = weight_rows(q_grad, normed1, 4)
    mixed_term = to_model([act_lo, act_hi], [dlo, dhi], order, 1, rows, [w_0])
    dkv1_back, from_o, w_c, mixed_term, o_x, o_y, dl_y = sync(
        dkv1_back, from_o, w_c, mixed_term, o_x, o_y, dl_y
    )

    def halves(array):
        span = array.shape[0] // 2
        return array[:span], array[span:]

    def corner_rows(along_x, along_y, from_a, from_b):
        (x_a, x_b), (y_a, y_b) = halves(along_x), halves(along_y)
        return stacked(x_a, x_b + from_b), stacked(y_a + from_a, y_b)

    w_a, w_b = halves(w_c)
    from_wa, from_wb = swap(w_a, "x"), swap(w_b, "y")
    got_ox, got_oy = swap(o_x, "x"), swap(o_y + from_o, "y")
    kv_grad = [
        heads_return(g, kv_raw[g], d, [e], *back, key_gain, 2)
        for g, (d, e) in enumerate(((dkv0, dkv0_back), (dkv1, dkv1_back)))
    ]
    k_gains = kv_grad[0][1] + kv_grad[1][1]
    kv_grad = [kv_grad[0][0], kv_grad[1][0]]
    kv_0, kv_x, kv_y, kv_c = weight_rows(kv_grad, normed1, 4)
    kv_c, from_wa, from_wb, got_ox, got_oy, w_x, w_y, kv_grad[1] = sync(
        kv_c, from_wa, from_wb, got_ox, got_oy, w_x, w_y, kv_grad[1]
    )
    kv_a, kv_b = halves(kv_c)
    from_a, from_b = swap(kv_a, "x"), swap(kv_b, "y")
    w_x, w_y = corner_rows(w_x, w_y, from_wa, from_wb)
    got_wx, got_wy = swap(w_x, "x"), swap(w_y, "y")
    term_there = to_model([q_grad[1], kv_grad[1]], [[q_w], [kv_w]], same, 0, rows)
    o_near = o_0 + got_ox + got_oy
    kv_x, kv_y, from_a, from_b, term_there, o_near = sync(
        kv_x, kv_y, from_a, from_b, term_there, o_near
    )
    o_sum = scatter_z(o_near)
    normed1_there = swap(term_there, "c")
    kv_x, kv_y = corner_rows(kv_x, kv_y, from_a, from_b)
    got_kx, got_ky = swap(kv_x, "x"), swap(kv_y, "y")
    term_own = to_model([q_grad[0], kv_grad[0]], [[q_w], [kv_w]], same, 0, rows, [kv_x, kv_y])
    w_0, got_wx, got_wy, kv_0, got_kx, got_ky, term_own, dl_y = sync(
        w_0, got_wx, got_wy, kv_0, got_kx, got_ky, term_own, dl_y + from_l
    )
    kv_near = kv_0 + got_kx + got_ky
    kv_sum = scatter_z(
        kv_near.reshape(2, 4, k_in, width).swapaxes(0, 1).reshape(8 * k_in, width)
    )
    w_near = w_0 + got_wx + got_wy
    w_sum = scatter_z(w_near)
    got_ly = swap(dl_y, "y")
    tokens_grad, gain1_sum = norm_return(
        tokens, resid_grad, term_own, normed1_there, norm1_gain, (f32,), [kv_near, w_near]
    )
    gain1_part, gain2_part = gain1_sum[0], gain2_sum[0]
    mixed_own = to_model([act_lo, act_hi], [dlo, dhi], order, 0, rows, [gain1_sum])
    mixed_there = swap(mixed_term, "c")
    output = (
        valid * (resid + mixed_own.astype(f32) + mixed_there.astype(f32))
    ).astype(bf16)
    dlo_sum = dl_0 + got_lx + got_ly

    gains = jnp.concatenate([gain1_part, gain2_part, q_gains[0], k_gains[0]])[None, :]
    for axis in ("c", "x", "y"):
        gains = gains + swap(gains, axis)
    for step in (1, 2):
        gains = gains + lax.ppermute(gains, "z", [(i, i ^ step) for i in range(4)])
    gains = gains[0]

    gate_sum, up_sum, down_sum = (
        jnp.concatenate(pair, axis=0)
        for pair in ((glo_sum, ghi_sum), (ulo_sum, uhi_sum), (dlo_sum, dhi_sum))
    )
    gate_sum, up_sum, down_sum = from_core(
        [(a[:, :eighth], a[:, eighth:]) for a in (gate_sum, up_sum, down_sum)], core
    )
    return (
        output,
        tokens_grad,
        gains[:width],
        w_sum.astype(f32).T,
        kv_sum[:k_in].astype(f32).T,
        kv_sum[k_in:].astype(f32).T,
        gains[2 * width : 2 * width + HEAD_SIZE],
        gains[2 * width + HEAD_SIZE :],
        o_sum.astype(f32),
        gains[width : 2 * width],
        gate_sum.astype(f32).T,
        up_sum.astype(f32).T,
        down_sum.astype(f32),
    )


def chip_solution(mesh):
    fine = Mesh(mesh.devices.reshape(2, 2, 2, 4), ("x", "c", "y", "z"))
    row_spec = P(("x", "c", "y", "z"), None)
    group_spec = P(("x", "c", "z"), None)
    head_cols = P(None, ("y", "x", "c", "z"))
    head_rows = P(("y", "x", "c", "z"), None)
    up_spec, down_spec = P(("x", "c", "y"), "z"), P("z", ("x", "c", "y"))
    return jax.shard_map(
        chip_layer,
        mesh=fine,
        in_specs=(
            row_spec,
            row_spec,
            group_spec,
            group_spec,
            P(),
            head_cols,
            head_cols,
            head_cols,
            P(),
            P(),
            head_rows,
            P(),
            up_spec,
            up_spec,
            down_spec,
        ),
        out_specs=(
            row_spec,
            row_spec,
            P(),
            head_cols,
            head_cols,
            head_cols,
            P(),
            P(),
            head_rows,
            P(),
            up_spec,
            up_spec,
            down_spec,
        ),
        check_vma=False,
    )


def solution(mesh):
    sizes = dict(mesh.shape)
    if sizes == {"fsdp": 4, "heads": 2, "tensor": 4}:
        return chip_solution(mesh)
    return plain_solution(mesh)
```

```python
import functools
import math

import jax
import jax.numpy as jnp
from jax import lax
from jax.experimental import pallas as pl
from jax.experimental.pallas import tpu as pltpu
from jax.sharding import Mesh
from jax.sharding import PartitionSpec as P

QUERY_HEADS = 16
KEY_VALUE_HEADS = 8
HEAD_SIZE = 128
BLK = 128


EPS_NORM = 1e-06
ROPE_BASE = 1000000.0
NEG_FILL = -1e30


def row_info(lengths, positions):
    block_count = (lengths + BLK - 1) // BLK
    ends = jnp.cumsum(block_count)
    starts = ends - block_count
    used = ends[-1]
    column = positions[:, None]
    inside = (column >= starts[None, :]) & (column < ends[None, :])
    past = positions >= used
    seq_block = jnp.sum((column >= ends[None, :]).astype(jnp.int32), axis=1)
    first_block = jnp.sum(jnp.where(inside, starts[None, :], 0), axis=1) + jnp.where(past, used, 0)
    limit = jnp.sum(jnp.where(inside, lengths[None, :], 0), axis=1)
    offsets = jnp.arange(BLK, dtype=jnp.int32)[None, :]
    pos_rows = (positions - first_block)[:, None] * BLK + offsets
    seq_rows = jnp.broadcast_to(seq_block[:, None], pos_rows.shape)
    valid_rows = jnp.logical_not(past)[:, None] & (pos_rows < limit[:, None])
    return (seq_rows.reshape(-1), pos_rows.reshape(-1), valid_rows.reshape(-1))


def rope_tables(pos_rows):
    half_dim = HEAD_SIZE // 2
    freq = jnp.exp(
        jnp.arange(half_dim, dtype=jnp.float32) * (-2.0 * math.log(ROPE_BASE) / HEAD_SIZE)
    )
    angles = pos_rows.astype(jnp.float32)[:, None] * freq[None, :]
    return (jnp.cos(angles)[:, None, :], jnp.sin(angles)[:, None, :])


def rotate(value_rows, cos_tab, sin_tab):
    half_dim = value_rows.shape[-1] // 2
    first_half, second_half = (value_rows[..., :half_dim], value_rows[..., half_dim:])
    return jnp.concatenate(
        [
            first_half * cos_tab - second_half * sin_tab,
            second_half * cos_tab + first_half * sin_tab,
        ],
        axis=-1,
    )


def unrotate(upstream, cos_tab, sin_tab):
    half_dim = upstream.shape[-1] // 2
    first_half, second_half = (upstream[..., :half_dim], upstream[..., half_dim:])
    return jnp.concatenate(
        [
            first_half * cos_tab + second_half * sin_tab,
            second_half * cos_tab - first_half * sin_tab,
        ],
        axis=-1,
    )


def rms_parts(value_rows, gain_vec):
    scales = lax.rsqrt(jnp.mean(value_rows * value_rows, axis=-1, keepdims=True) + EPS_NORM)
    return (value_rows * scales * gain_vec, scales)


def norm_back(value_rows, scales, gain_vec, upstream):
    weighted = upstream * gain_vec
    inner = jnp.sum(value_rows * weighted, axis=-1, keepdims=True) / value_rows.shape[-1]
    return scales * weighted - value_rows * scales * scales * scales * inner


def matrix_product(left, right):
    return jnp.dot(left, right, preferred_element_type=jnp.float32)


def dot_rows(left, right):
    return lax.dot_general(
        left, right, (((0,), (0,)), ((), ())), preferred_element_type=jnp.float32
    )


def dot_cols(left, right):
    return lax.dot_general(
        left, right, (((1,), (1,)), ((), ())), preferred_element_type=jnp.float32
    )


def swap_cols(array, outer, inner):
    lead = array.shape[0]
    return jnp.swapaxes(array.reshape(lead, outer, inner, -1), 1, 2).reshape(lead, -1)


def swap_rows(array, outer, inner):
    width = array.shape[1]
    return jnp.swapaxes(array.reshape(outer, inner, -1, width), 0, 1).reshape(-1, width)


def spread_rows(local_rows):
    return lax.all_gather(local_rows, "tensor", axis=0, tiled=True)


def to_heads(packed):
    return lax.all_to_all(packed, "heads", split_axis=1, concat_axis=0, tiled=True)


def to_rows(packed):
    return lax.all_to_all(packed, "heads", split_axis=0, concat_axis=1, tiled=True)


def tensor_sum(term, row_count):
    total = lax.psum(
        term(0, row_count * lax.axis_size("tensor")).astype(jnp.bfloat16), "tensor"
    ).astype(jnp.float32)
    return lax.dynamic_slice_in_dim(total, lax.axis_index("tensor") * row_count, row_count)


def block_scores(query_blk, key_all, seq_blk, pos_blk, seq_all, pos_all):
    scores = jnp.einsum(
        "qkgd,pkd->kgqp", query_blk, key_all, preferred_element_type=jnp.float32
    ) * HEAD_SIZE ** (-0.5)
    allowed = (seq_blk[:, None] == seq_all[None, :]) & (pos_all[None, :] <= pos_blk[:, None])
    return jnp.where(allowed[None, None], scores, NEG_FILL)


def attend_forward(query_grp, key_grp, value_grp, seq_all, pos_all):
    group_factor = QUERY_HEADS // KEY_VALUE_HEADS
    group_len = query_grp.shape[0]
    kv_local = key_grp.shape[1] // HEAD_SIZE
    query_four = query_grp.reshape(group_len, kv_local, group_factor, HEAD_SIZE)
    key_three = key_grp.reshape(group_len, kv_local, HEAD_SIZE)
    value_three = value_grp.reshape(group_len, kv_local, HEAD_SIZE)
    block_rows = min(512, group_len)

    def forward_block(block_idx):
        first_row = block_idx * block_rows
        query_blk = lax.dynamic_slice_in_dim(query_four, first_row, block_rows)
        seq_blk = lax.dynamic_slice_in_dim(seq_all, first_row, block_rows)
        pos_blk = lax.dynamic_slice_in_dim(pos_all, first_row, block_rows)
        scores = block_scores(query_blk, key_three, seq_blk, pos_blk, seq_all, pos_all)
        peak = jnp.max(scores, axis=-1, keepdims=True)
        expo = jnp.exp(scores - peak)
        total = jnp.sum(expo, axis=-1, keepdims=True)
        probs_b = (expo / total).astype(jnp.bfloat16)
        attended = jnp.einsum(
            "kgqp,pkd->qkgd", probs_b, value_three, preferred_element_type=jnp.float32
        )
        return (attended, (peak + jnp.log(total))[..., 0])

    attended, log_sums = lax.map(forward_block, jnp.arange(group_len // block_rows))
    return (
        attended.reshape(group_len, kv_local * group_factor * HEAD_SIZE).astype(jnp.bfloat16),
        log_sums,
    )


def attend_backward(query_grp, key_grp, value_grp, grad_grp, log_sums, seq_all, pos_all):
    group_factor = QUERY_HEADS // KEY_VALUE_HEADS
    scale = HEAD_SIZE ** (-0.5)
    group_len = query_grp.shape[0]
    kv_local = key_grp.shape[1] // HEAD_SIZE
    query_four = query_grp.reshape(group_len, kv_local, group_factor, HEAD_SIZE)
    key_three = key_grp.reshape(group_len, kv_local, HEAD_SIZE)
    value_three = value_grp.reshape(group_len, kv_local, HEAD_SIZE)
    grad_four = grad_grp.reshape(group_len, kv_local, group_factor, HEAD_SIZE)
    block_rows = min(512, group_len)

    def backward_block(carry, block_idx):
        key_acc, value_acc = carry
        first_row = block_idx * block_rows
        query_blk = lax.dynamic_slice_in_dim(query_four, first_row, block_rows)
        grad_blk = lax.dynamic_slice_in_dim(grad_four, first_row, block_rows)
        seq_blk = lax.dynamic_slice_in_dim(seq_all, first_row, block_rows)
        pos_blk = lax.dynamic_slice_in_dim(pos_all, first_row, block_rows)
        scores = block_scores(query_blk, key_three, seq_blk, pos_blk, seq_all, pos_all)
        probs = jnp.exp(scores - log_sums[block_idx][..., None])
        probs_b = probs.astype(jnp.bfloat16)
        prob_grad = jnp.einsum(
            "qkgd,pkd->kgqp", grad_blk, value_three, preferred_element_type=jnp.float32
        )
        score_grad_b = (
            probs * (prob_grad - jnp.sum(probs * prob_grad, axis=-1, keepdims=True))
        ).astype(jnp.bfloat16)
        query_grad = (
            jnp.einsum(
                "kgqp,pkd->qkgd", score_grad_b, key_three, preferred_element_type=jnp.float32
            )
            * scale
        )
        key_acc = (
            key_acc
            + jnp.einsum(
                "kgqp,qkgd->pkd", score_grad_b, query_blk, preferred_element_type=jnp.float32
            )
            * scale
        )
        value_acc = value_acc + jnp.einsum(
            "kgqp,qkgd->pkd", probs_b, grad_blk, preferred_element_type=jnp.float32
        )
        return ((key_acc, value_acc), query_grad)

    empty = jnp.zeros((group_len, kv_local, HEAD_SIZE), jnp.float32)
    (key_acc, value_acc), query_blocks = lax.scan(
        backward_block, (empty, empty), jnp.arange(group_len // block_rows)
    )
    query_grad_b = query_blocks.reshape(group_len, kv_local * group_factor * HEAD_SIZE).astype(
        jnp.bfloat16
    )
    key_grad_b = key_acc.reshape(group_len, kv_local * HEAD_SIZE).astype(jnp.bfloat16)
    value_grad_b = value_acc.reshape(group_len, kv_local * HEAD_SIZE).astype(jnp.bfloat16)
    return (query_grad_b, key_grad_b, value_grad_b)


def project_heads(normed_b, query_w, key_w, value_w, query_gain, key_gain, pos_rows):
    lines = normed_b.shape[0]
    q_raw = matrix_product(normed_b, query_w).reshape(lines, -1, HEAD_SIZE)
    key_unnormed = matrix_product(normed_b, key_w).reshape(lines, -1, HEAD_SIZE)
    value_b = matrix_product(normed_b, value_w).astype(jnp.bfloat16)
    cos_tab, sin_tab = rope_tables(pos_rows)
    q_normed, q_scale = rms_parts(q_raw, query_gain)
    k_normed, k_scale = rms_parts(key_unnormed, key_gain)
    query_b = rotate(q_normed, cos_tab, sin_tab).astype(jnp.bfloat16).reshape(lines, -1)
    key_b = rotate(k_normed, cos_tab, sin_tab).astype(jnp.bfloat16).reshape(lines, -1)
    return (query_b, key_b, value_b, (q_raw, q_scale, key_unnormed, k_scale, cos_tab, sin_tab))


def heads_back(query_back, key_back, kept, query_gain, key_gain):
    q_raw, q_scale, key_unnormed, k_scale, cos_tab, sin_tab = kept
    lines = q_raw.shape[0]
    q_turned = unrotate(query_back.astype(jnp.float32).reshape(q_raw.shape), cos_tab, sin_tab)
    k_turned = unrotate(key_back.astype(jnp.float32).reshape(key_unnormed.shape), cos_tab, sin_tab)
    q_raw_grad = (
        norm_back(q_raw, q_scale, query_gain, q_turned).reshape(lines, -1).astype(jnp.bfloat16)
    )
    k_raw_grad = (
        norm_back(key_unnormed, k_scale, key_gain, k_turned).reshape(lines, -1).astype(jnp.bfloat16)
    )
    qgain_part = jnp.sum(q_turned * q_raw * q_scale, axis=(0, 1))
    kgain_part = jnp.sum(k_turned * key_unnormed * k_scale, axis=(0, 1))
    return (q_raw_grad, k_raw_grad, qgain_part, kgain_part)


def plain_layer(
    tokens,
    cotangent,
    seq_lens,
    block_pos,
    norm1_gain,
    w_query,
    key_matrix,
    value_matrix,
    query_gain,
    key_gain,
    w_out,
    norm2_gain,
    w_gate,
    w_up,
    w_down,
):
    row_count = tokens.shape[0]
    fsdp_count = lax.axis_size("fsdp")
    heads_count = lax.axis_size("heads")
    gate_full, up_full, down_full = (
        lax.all_gather(w_gate, ("fsdp", "heads"), axis=0, tiled=True),
        lax.all_gather(w_up, ("fsdp", "heads"), axis=0, tiled=True),
        lax.all_gather(w_down, ("fsdp", "heads"), axis=1, tiled=True),
    )
    seq_all, pos_all, valid_all = row_info(seq_lens[0], block_pos[0])
    own_first = lax.axis_index("heads") * row_count
    pos_own = lax.dynamic_slice_in_dim(pos_all, own_first, row_count)
    valid_own = lax.dynamic_slice_in_dim(valid_all, own_first, row_count).astype(jnp.float32)[
        :, None
    ]
    inputs = tokens.astype(jnp.float32)
    first_normed, scale1 = rms_parts(inputs, norm1_gain)
    normed1_b = first_normed.astype(jnp.bfloat16)
    query_all, key_all, value_all, out_all = (
        lax.all_gather(w_query, ("fsdp", "heads", "tensor"), axis=1, tiled=True),
        lax.all_gather(key_matrix, ("fsdp", "heads", "tensor"), axis=1, tiled=True),
        lax.all_gather(value_matrix, ("fsdp", "heads", "tensor"), axis=1, tiled=True),
        lax.all_gather(w_out, ("fsdp", "heads", "tensor"), axis=0, tiled=True),
    )
    query_full = swap_cols(query_all, fsdp_count, heads_count)
    key_full = swap_cols(key_all, fsdp_count, heads_count)
    value_full = swap_cols(value_all, fsdp_count, heads_count)
    out_full = swap_rows(out_all, fsdp_count, heads_count)
    query_b, key_b, value_b, kept = project_heads(
        normed1_b, query_full, key_full, value_full, query_gain, key_gain, pos_own
    )
    q_width = query_b.shape[1] // heads_count
    k_width = key_b.shape[1] // heads_count
    packed = jnp.concatenate(
        [
            query_b.reshape(row_count, heads_count, q_width),
            key_b.reshape(row_count, heads_count, k_width),
            value_b.reshape(row_count, heads_count, k_width),
        ],
        axis=2,
    )
    grouped = to_heads(packed.reshape(row_count, -1))
    query_grp = grouped[:, :q_width]
    key_grp = grouped[:, q_width : q_width + k_width]
    value_grp = grouped[:, q_width + k_width :]
    attended_b, log_sums = attend_forward(query_grp, key_grp, value_grp, seq_all, pos_all)
    attn_tok = to_rows(attended_b)
    resid = inputs + matrix_product(attn_tok, out_full)
    normed2, scale2 = rms_parts(resid, norm2_gain)
    normed2_b = normed2.astype(jnp.bfloat16)
    wide_in = spread_rows(normed2_b)
    gate_pre = matrix_product(wide_in, gate_full)
    up_pre = matrix_product(wide_in, up_full)
    sigmoid_gate = jax.nn.sigmoid(gate_pre)
    silu_gate = gate_pre * sigmoid_gate
    act_b = (silu_gate * up_pre).astype(jnp.bfloat16)

    def forward_term(first_row, span):
        return matrix_product(act_b, down_full)

    mixed = tensor_sum(forward_term, row_count)
    output = (valid_own * (resid + mixed)).astype(jnp.bfloat16)
    grad_out = valid_own * cotangent.astype(jnp.float32)
    wide_grad = spread_rows(grad_out.astype(jnp.bfloat16))
    act_grad = dot_cols(wide_grad, down_full)
    down_grad = dot_rows(act_b, wide_grad)
    gate_grad_b = (
        act_grad * up_pre * sigmoid_gate * (1.0 + gate_pre * (1.0 - sigmoid_gate))
    ).astype(jnp.bfloat16)
    up_grad_b = (act_grad * silu_gate).astype(jnp.bfloat16)
    gate_wgrad = dot_rows(wide_in, gate_grad_b)
    up_wgrad = dot_rows(wide_in, up_grad_b)

    def backward_term(first_row, span):
        return dot_cols(gate_grad_b, gate_full) + dot_cols(up_grad_b, up_full)

    normed2_grad = tensor_sum(backward_term, row_count)
    gate_sum, up_sum, down_sum = (
        lax.psum_scatter(
            gate_wgrad.astype(jnp.bfloat16), ("fsdp", "heads"), scatter_dimension=0, tiled=True
        ).astype(jnp.float32),
        lax.psum_scatter(
            up_wgrad.astype(jnp.bfloat16), ("fsdp", "heads"), scatter_dimension=0, tiled=True
        ).astype(jnp.float32),
        lax.psum_scatter(
            down_grad.astype(jnp.bfloat16), ("fsdp", "heads"), scatter_dimension=1, tiled=True
        ).astype(jnp.float32),
    )
    resid_grad = grad_out + norm_back(resid, scale2, norm2_gain, normed2_grad)
    gain2_part = jnp.sum(normed2_grad * resid * scale2, axis=0)
    resid_grad_b = resid_grad.astype(jnp.bfloat16)
    out_wgrad = dot_rows(attn_tok, resid_grad_b)
    attn_grad_b = dot_cols(resid_grad_b, out_full).astype(jnp.bfloat16)
    attn_grad_grp = to_heads(attn_grad_b)
    query_grad_b, key_grad_b, value_grad_b = attend_backward(
        query_grp, key_grp, value_grp, attn_grad_grp, log_sums, seq_all, pos_all
    )
    back_packed = to_rows(jnp.concatenate([query_grad_b, key_grad_b, value_grad_b], axis=1))
    back_three = back_packed.reshape(row_count, heads_count, -1)
    query_back = back_three[:, :, :q_width].reshape(row_count, -1)
    key_back = back_three[:, :, q_width : q_width + k_width].reshape(row_count, -1)
    value_back = back_three[:, :, q_width + k_width :].reshape(row_count, -1)
    q_raw_grad, k_raw_grad, qgain_part, kgain_part = heads_back(
        query_back, key_back, kept, query_gain, key_gain
    )
    query_wgrad = swap_cols(dot_rows(normed1_b, q_raw_grad), heads_count, fsdp_count)
    key_wgrad = swap_cols(dot_rows(normed1_b, k_raw_grad), heads_count, fsdp_count)
    value_wgrad = swap_cols(dot_rows(normed1_b, value_back), heads_count, fsdp_count)
    out_wgrad = swap_rows(out_wgrad, heads_count, fsdp_count)
    normed1_grad = (
        dot_cols(q_raw_grad, query_full)
        + dot_cols(k_raw_grad, key_full)
        + dot_cols(value_back, value_full)
    )
    query_sum, key_sum, value_sum, out_sum = (
        lax.psum_scatter(query_wgrad, ("fsdp", "heads", "tensor"), scatter_dimension=1, tiled=True),
        lax.psum_scatter(key_wgrad, ("fsdp", "heads", "tensor"), scatter_dimension=1, tiled=True),
        lax.psum_scatter(value_wgrad, ("fsdp", "heads", "tensor"), scatter_dimension=1, tiled=True),
        lax.psum_scatter(out_wgrad, ("fsdp", "heads", "tensor"), scatter_dimension=0, tiled=True),
    )
    tokens_grad = resid_grad + norm_back(inputs, scale1, norm1_gain, normed1_grad)
    gain1_part = jnp.sum(normed1_grad * inputs * scale1, axis=0)
    gain1_sum, qgain_sum, kgain_sum, gain2_sum = lax.psum(
        (gain1_part, qgain_part, kgain_part, gain2_part), ("fsdp", "heads", "tensor")
    )
    return (
        output,
        tokens_grad,
        gain1_sum,
        query_sum,
        key_sum,
        value_sum,
        qgain_sum,
        kgain_sum,
        out_sum,
        gain2_sum,
        gate_sum,
        up_sum,
        down_sum,
    )


def plain_solution(mesh):
    return jax.shard_map(
        plain_layer,
        mesh=mesh,
        in_specs=(
            P(("fsdp", "heads", "tensor"), None),
            P(("fsdp", "heads", "tensor"), None),
            P(("fsdp", "tensor"), None),
            P(("fsdp", "tensor"), None),
            P(),
            P(None, ("heads", "fsdp", "tensor")),
            P(None, ("heads", "fsdp", "tensor")),
            P(None, ("heads", "fsdp", "tensor")),
            P(),
            P(),
            P(("heads", "fsdp", "tensor"), None),
            P(),
            P(("fsdp", "heads"), "tensor"),
            P(("fsdp", "heads"), "tensor"),
            P("tensor", ("fsdp", "heads")),
        ),
        out_specs=(
            P(("fsdp", "heads", "tensor"), None),
            P(("fsdp", "heads", "tensor"), None),
            P(),
            P(None, ("heads", "fsdp", "tensor")),
            P(None, ("heads", "fsdp", "tensor")),
            P(None, ("heads", "fsdp", "tensor")),
            P(),
            P(),
            P(("heads", "fsdp", "tensor"), None),
            P(),
            P(("fsdp", "heads"), "tensor"),
            P(("fsdp", "heads"), "tensor"),
            P("tensor", ("fsdp", "heads")),
        ),
        check_vma=False,
    )


VMEM_LIMIT = 56 * 1024 * 1024
LOG2_E = 1.4426950408889634
SWAP = ((0, 1), (1, 0))
ROW_TILE = 1024
SCALE = HEAD_SIZE ** (-0.5)


def dot_t(left, right):
    return lax.dot_general(
        left, right, (((1,), (1,)), ((), ())), preferred_element_type=jnp.float32
    )


def swap(array, axis):
    return lax.ppermute(array, axis, SWAP)


def pick(first, second, index):
    return jnp.where(index == 0, first, second)


def join(mine, other, index, axis):
    return pick(
        jnp.concatenate([mine, other], axis=axis),
        jnp.concatenate([other, mine], axis=axis),
        index,
    )


def gather_z(array):
    return lax.all_gather(array, "z", axis=0, tiled=True)


def scatter_z(array):
    return lax.psum_scatter(array, "z", scatter_dimension=0, tiled=True)


def after(array, *done):
    return lax.optimization_barrier((array, *done))[0]


def sync(*arrays):
    return lax.optimization_barrier(arrays)


def to_core(array, core):
    half = array.shape[0] // 2
    first, second = array[:half], array[half:]
    other = swap(pick(second, first, core), "c")
    mine = pick(first, second, core)
    return join(mine, other, core, 1)


def from_core(pairs, core):
    mine = [pick(a, b, core) for a, b in pairs]
    send = jnp.concatenate([pick(b, a, core) for a, b in pairs], axis=0)
    others = jnp.split(swap(send, "c"), len(pairs))
    return [join(m, o, core, 0) for m, o in zip(mine, others)]


def call(kernel, inputs, in_specs, out_specs, out_shape, grid, after=(), prefetch=None, **more):
    lead = 0 if prefetch is None else 1
    count, extra = lead + len(inputs), len(after)

    def body(*refs):
        kernel(*refs[:count], *refs[count + extra :])

    if prefetch is not None:
        prefetched, inputs = [prefetch], list(inputs)
    else:
        prefetched, inputs = [], list(inputs)
    scratch = more.pop("scratch_shapes", ())
    return pl.pallas_call(
        body,
        grid_spec=pltpu.PrefetchScalarGridSpec(
            num_scalar_prefetch=lead,
            grid=grid,
            in_specs=list(in_specs) + [pl.BlockSpec(memory_space=pl.ANY)] * extra,
            out_specs=out_specs,
            scratch_shapes=scratch,
        ),
        out_shape=out_shape,
        compiler_params=pltpu.CompilerParams(vmem_limit_bytes=VMEM_LIMIT),
        cost_estimate=pl.CostEstimate(flops=1000, bytes_accessed=1000, transcendentals=0),
        **more,
    )(*prefetched, *inputs, *after)


def reorder_kernel(order_ref, in_ref, out_ref):
    out_ref[...] = in_ref[...]


def reorder(array, order, after=()):
    rows, width = array.shape
    parts = order.shape[0]
    return call(
        reorder_kernel,
        [array],
        [pl.BlockSpec((rows, width // parts), lambda i, o: (0, o[i]))],
        pl.BlockSpec((rows, width // parts), lambda i, o: (0, i)),
        jax.ShapeDtypeStruct(array.shape, array.dtype),
        (parts,),
        after,
        order,
        name="reorder",
    )


def lane_mean(value):
    ones = jnp.full((2 * HEAD_SIZE, HEAD_SIZE), 1.0 / HEAD_SIZE, jnp.bfloat16)
    high = value.astype(jnp.bfloat16)
    low = (value - high.astype(jnp.float32)).astype(jnp.bfloat16)
    return matrix_product(jnp.concatenate([high, low], axis=1), ones)


def heads_kernel(count, raw_ref, cos_ref, sin_ref, gain_ref, out_ref):
    raw = raw_ref[:, :HEAD_SIZE]
    value = raw * lax.rsqrt(lane_mean(raw * raw) + EPS_NORM) * gain_ref[...]
    out_ref[:, :HEAD_SIZE] = (
        value * cos_ref[...] + pltpu.roll(value, HEAD_SIZE // 2, 1) * sin_ref[...]
    ).astype(jnp.bfloat16)
    if count == 2:
        out_ref[:, HEAD_SIZE:] = raw_ref[:, HEAD_SIZE:].astype(jnp.bfloat16)


def make_heads(group, raw, cos_tab, sin_tab, gain, count, after=()):
    rows, width = raw.shape
    skip = group * (rows // ROW_TILE)
    table = pl.BlockSpec((ROW_TILE, HEAD_SIZE), lambda i, r: (i + skip, 0))
    return call(
        functools.partial(heads_kernel, count),
        [raw, cos_tab, sin_tab, gain[None, :]],
        [
            pl.BlockSpec((ROW_TILE, count * HEAD_SIZE), lambda i, r: (i, r)),
            table,
            table,
            pl.BlockSpec((1, HEAD_SIZE), lambda i, r: (0, 0)),
        ],
        pl.BlockSpec((ROW_TILE, count * HEAD_SIZE), lambda i, r: (i, r)),
        jax.ShapeDtypeStruct((rows, width), jnp.bfloat16),
        (rows // ROW_TILE, width // (count * HEAD_SIZE)),
        after,
        name="make_heads",
    )


def heads_back_kernel(count, raw_ref, cos_ref, sin_ref, gain_ref, *rest):
    *up_refs, out_ref, sum_ref = rest

    @pl.when((pl.program_id(0) == 0) & (pl.program_id(1) == 0))
    def _():
        sum_ref[...] = jnp.zeros_like(sum_ref)

    raw = raw_ref[:, :HEAD_SIZE]
    upstream = up_refs[0][...].astype(jnp.float32)
    for ref in up_refs[1:]:
        upstream = upstream + ref[...].astype(jnp.float32)
    if count == 2:
        out_ref[:, HEAD_SIZE:] = upstream[:, HEAD_SIZE:].astype(jnp.bfloat16)
        upstream = upstream[:, :HEAD_SIZE]
    turned = upstream * cos_ref[...] - pltpu.roll(upstream, HEAD_SIZE // 2, 1) * sin_ref[...]
    scale = lax.rsqrt(lane_mean(raw * raw) + EPS_NORM)
    hat = raw * scale
    weighted = turned * gain_ref[...]
    out_ref[:, :HEAD_SIZE] = (scale * (weighted - hat * lane_mean(hat * weighted))).astype(
        jnp.bfloat16
    )
    sum_ref[0:1, :] += jnp.sum(turned * hat, axis=0, keepdims=True)


def heads_return(group, raw, upstream, far, cos_tab, sin_tab, gain, count, after=()):
    rows, width = raw.shape
    heads = width // (count * HEAD_SIZE)
    skip = group * (rows // ROW_TILE)
    table = pl.BlockSpec((ROW_TILE, HEAD_SIZE), lambda i, r: (i + skip, 0))
    one = pl.BlockSpec((ROW_TILE, count * HEAD_SIZE), lambda i, r: (i, r))
    across = pl.BlockSpec(
        (ROW_TILE, count * HEAD_SIZE), lambda i, r: (i, (r + heads // 2) % heads)
    )
    return call(
        functools.partial(heads_back_kernel, count),
        [raw, cos_tab, sin_tab, gain[None, :], upstream] + far,
        [one, table, table, pl.BlockSpec((1, HEAD_SIZE), lambda i, r: (0, 0)), one]
        + [across] * len(far),
        [one, pl.BlockSpec((8, HEAD_SIZE), lambda i, r: (0, 0))],
        [
            jax.ShapeDtypeStruct((rows, width), jnp.bfloat16),
            jax.ShapeDtypeStruct((8, HEAD_SIZE), jnp.float32),
        ],
        (rows // ROW_TILE, heads),
        after,
        name="heads_return",
    )


GROUP_WIDTH = 2 * HEAD_SIZE
TOGETHER = 2


def stack_heads(block):
    return jnp.concatenate([block[:, :HEAD_SIZE], block[:, HEAD_SIZE:]], axis=0)


def key_bias(first_key, pair, parity, queries=0):
    shape = (1, 2 * BLK) if queries == 0 else (2 * BLK, 1)
    cols = lax.broadcasted_iota(jnp.int32, shape, 1 - queries)
    block = 2 * pair + jnp.where(cols < BLK, parity, 1 - parity)
    return jnp.where(block >= first_key, 0.0, NEG_FILL)


def last_bias(first_key, pair, parity, queries=0):
    rows = lax.broadcasted_iota(jnp.int32, (2 * BLK, 2 * BLK), queries)
    cols = lax.broadcasted_iota(jnp.int32, (2 * BLK, 2 * BLK), 1 - queries)
    far = (parity == 1) & (2 * pair >= first_key)
    own = lax.rem(cols, BLK) <= lax.rem(rows, BLK)
    far_bias = jnp.where(far, 0.0, NEG_FILL)
    return jnp.where(cols < BLK, jnp.where(own, 0.0, NEG_FILL), far_bias)


def pair_of(own_ref, far_ref, m, first):
    at = pl.ds(pl.multiple_of(m * BLK, BLK), BLK)
    lanes = slice(first, first + HEAD_SIZE)
    return jnp.concatenate([own_ref[at, lanes], far_ref[at, lanes]], axis=0)


def head_lanes(head):
    return slice(head * GROUP_WIDTH, (head + 1) * GROUP_WIDTH)


def attend_kernel(group, info_ref, q_ref, own_ref, far_ref, o_ref, l_ref):
    blocks = q_ref.shape[0] // BLK
    parity = info_ref[group, blocks]

    def one_block(j, _):
        first_key = info_ref[group, j]
        rows = pl.ds(pl.multiple_of(j * BLK, BLK), BLK)
        queries = [stack_heads(q_ref[rows, head_lanes(h)]) for h in range(TOGETHER)]

        def step(m, bias, carry):
            out = []
            for h in range(TOGETHER):
                total, acc = carry[h]
                score = dot_t(queries[h], pair_of(own_ref, far_ref, m, h * GROUP_WIDTH))
                expo = jnp.exp2(score * (SCALE * LOG2_E) + bias)
                total = total + jnp.sum(expo, axis=1, keepdims=True)
                value = pair_of(own_ref, far_ref, m, h * GROUP_WIDTH + HEAD_SIZE)
                acc = acc + matrix_product(expo.astype(jnp.bfloat16), value)
                out.append((total, acc))
            return tuple(out)

        empty = (
            jnp.zeros((2 * BLK, 1), jnp.float32),
            jnp.zeros((2 * BLK, HEAD_SIZE), jnp.float32),
        )
        carry = step(j, last_bias(first_key, j, parity), (empty,) * TOGETHER)
        carry = lax.fori_loop(
            lax.div(first_key, 2),
            j,
            lambda m, c: step(m, key_bias(first_key, m, parity), c),
            carry,
        )
        lane = lax.broadcasted_iota(jnp.int32, (BLK, HEAD_SIZE), 1)
        for h, (total, acc) in enumerate(carry):
            out = (acc / total).astype(jnp.bfloat16)
            o_ref[rows, head_lanes(h)] = jnp.concatenate([out[:BLK], out[BLK:]], axis=1)
            l_ref[rows, h * HEAD_SIZE : (h + 1) * HEAD_SIZE] = jnp.where(
                lane == 0, total[:BLK], total[BLK:]
            )
        return 0

    lax.fori_loop(0, blocks, one_block, 0)


def attend(group, info, query, own, far, after=()):
    rows, width = query.shape
    span = TOGETHER * GROUP_WIDTH
    here = pl.BlockSpec((rows, span), lambda r, s: (0, r))
    there = pl.BlockSpec((rows, span), lambda r, s: (0, (r + 1) % 2))
    return call(
        functools.partial(attend_kernel, group),
        [query, own, far],
        [here, here, there],
        [here, pl.BlockSpec((rows, span // 2), lambda r, s: (0, r))],
        [
            jax.ShapeDtypeStruct((rows, width), jnp.bfloat16),
            jax.ShapeDtypeStruct((rows, width // 2), jnp.float32),
        ],
        (width // span,),
        after,
        info,
        name="attend",
    )


def row_sums(value):
    ones = jnp.ones((8, 2 * HEAD_SIZE), jnp.bfloat16)
    high = value.astype(jnp.bfloat16)
    low = (value - high.astype(jnp.float32)).astype(jnp.bfloat16)
    return dot_t(ones, jnp.concatenate([high, low], axis=1))[:1]


def attend_back_kernel(
    group,
    info_ref,
    q_ref,
    do_ref,
    o_ref,
    l_ref,
    own_ref,
    far_ref,
    dq_ref,
    down_ref,
    dfar_ref,
    kacc_ref,
    vacc_ref,
):
    blocks = q_ref.shape[0] // BLK
    parity = info_ref[group, blocks]
    kacc_ref[...] = jnp.zeros_like(kacc_ref)
    vacc_ref[...] = jnp.zeros_like(vacc_ref)

    def one_block(j, _):
        first_key = info_ref[group, j]
        rows = pl.ds(pl.multiple_of(j * BLK, BLK), BLK)
        held = []
        for h in range(TOGETHER):
            query = stack_heads(q_ref[rows, head_lanes(h)])
            attn = stack_heads(o_ref[rows, head_lanes(h)]).astype(jnp.float32)
            grad = stack_heads(do_ref[rows, head_lanes(h)]).astype(jnp.float32)
            at = h * HEAD_SIZE
            total = jnp.concatenate(
                [l_ref[rows, at : at + 1], l_ref[rows, at + 1 : at + 2]], axis=0
            )
            grad_b = (grad / total).astype(jnp.bfloat16)
            inner = row_sums(grad_b.astype(jnp.float32) * attn)
            held.append((query, grad_b, inner))

        def step(m, bias, carry):
            at = pl.ds(pl.multiple_of(m * BLK, BLK), BLK)
            out = []
            for h in range(TOGETHER):
                query, grad_b, inner = held[h]
                key = pair_of(own_ref, far_ref, m, h * GROUP_WIDTH)
                value = pair_of(own_ref, far_ref, m, h * GROUP_WIDTH + HEAD_SIZE)
                expo = jnp.exp2(dot_t(key, query) * (SCALE * LOG2_E) + bias)
                d_score = (expo * (dot_t(value, grad_b) - inner)).astype(jnp.bfloat16)
                d_key = matrix_product(d_score, query)
                d_value = matrix_product(expo.astype(jnp.bfloat16), grad_b)
                kacc_ref[h, 0, at, :] += d_key[:BLK]
                kacc_ref[h, 1, at, :] += d_key[BLK:]
                vacc_ref[h, 0, at, :] += d_value[:BLK]
                vacc_ref[h, 1, at, :] += d_value[BLK:]
                out.append(carry[h] + dot_rows(d_score, key))
            return tuple(out)

        empty = jnp.zeros((2 * BLK, HEAD_SIZE), jnp.float32)
        carry = step(j, last_bias(first_key, j, parity, 1), (empty,) * TOGETHER)
        carry = lax.fori_loop(
            lax.div(first_key, 2),
            j,
            lambda m, c: step(m, key_bias(first_key, m, parity, 1), c),
            carry,
        )
        for h, dq in enumerate(carry):
            dq = (dq * SCALE).astype(jnp.bfloat16)
            dq_ref[rows, head_lanes(h)] = jnp.concatenate([dq[:BLK], dq[BLK:]], axis=1)
        return 0

    lax.fori_loop(0, blocks, one_block, 0)
    for h in range(TOGETHER):
        for half, ref in enumerate((down_ref, dfar_ref)):
            first = h * GROUP_WIDTH
            ref[:, first : first + HEAD_SIZE] = (kacc_ref[h, half] * SCALE).astype(jnp.bfloat16)
            ref[:, first + HEAD_SIZE : first + GROUP_WIDTH] = vacc_ref[h, half].astype(
                jnp.bfloat16
            )


def attend_back(group, info, query, d_attn, attn, total, own, far, after=()):
    rows, width = query.shape
    span = TOGETHER * GROUP_WIDTH
    here = pl.BlockSpec((rows, span), lambda r, s: (0, r))
    there = pl.BlockSpec((rows, span), lambda r, s: (0, (r + 1) % 2))
    shape = jax.ShapeDtypeStruct((rows, width), jnp.bfloat16)
    return call(
        functools.partial(attend_back_kernel, group),
        [query, d_attn, attn, total, own, far],
        [here, here, here, pl.BlockSpec((rows, span // 2), lambda r, s: (0, r)), here, there],
        [here] * 3,
        [shape] * 3,
        (width // span,),
        after,
        info,
        scratch_shapes=[
            pltpu.VMEM((TOGETHER, 2, rows, HEAD_SIZE), jnp.float32),
            pltpu.VMEM((TOGETHER, 2, rows, HEAD_SIZE), jnp.float32),
        ],
        name="attend_back",
    )


HIDDEN_TILE = 512
ROW_STEP = 1024


def row_steps(*refs):
    for first_ref in range(len(refs)):
        for first in range(0, refs[first_ref].shape[0], ROW_STEP):
            begin = first_ref * refs[first_ref].shape[0] + first
            yield refs[first_ref][first : first + ROW_STEP, :], slice(begin, begin + ROW_STEP)


def joined(refs):
    return jnp.concatenate([ref[...] for ref in refs], axis=1)


def ffn_kernel(pieces, xa_ref, xb_ref, *refs):
    gate_w = joined(refs[:pieces]).T
    up_w, d_act_ref = refs[pieces][...].T, refs[pieces + 1]
    act_ref, gate_ref, up_ref = refs[pieces + 2 :]
    for x, rows in row_steps(xa_ref, xb_ref):
        gate = matrix_product(x, gate_w)
        upper = matrix_product(x, up_w)
        d_act = d_act_ref[rows, :].astype(jnp.float32)
        sig = 0.5 * jnp.tanh(0.5 * gate) + 0.5
        silu = gate * sig
        act_ref[rows, :] = (silu * upper).astype(jnp.bfloat16)
        gate_ref[rows, :] = (d_act * upper * (sig + silu * (1.0 - sig))).astype(jnp.bfloat16)
        up_ref[rows, :] = (d_act * silu).astype(jnp.bfloat16)


def ffn(xs, gates, up, d_act, after=()):
    rows, width = xs[0].shape
    hidden = up.shape[0]
    out = pl.BlockSpec((2 * rows, HIDDEN_TILE), lambda j: (0, j))
    shape = jax.ShapeDtypeStruct((2 * rows, hidden), jnp.bfloat16)
    return call(
        functools.partial(ffn_kernel, len(gates)),
        [*xs, *gates, up, d_act],
        [pl.BlockSpec((rows, width), lambda j: (0, 0))] * 2
        + [pl.BlockSpec((HIDDEN_TILE, w.shape[1]), lambda j: (j, 0)) for w in (*gates, up)]
        + [out],
        [out] * 3,
        [shape] * 3,
        (hidden // HIDDEN_TILE,),
        after,
        name="ffn",
    )


def to_hidden_kernel(xs, *refs):
    weight = joined(refs[xs:-1]).T
    for x, rows in row_steps(*refs[:xs]):
        refs[-1][rows, :] = matrix_product(x, weight).astype(refs[-1].dtype)


def to_hidden(xs, weights, dtype=jnp.bfloat16, after=()):
    rows, width = xs[0].shape
    hidden = weights[0].shape[0]
    return call(
        functools.partial(to_hidden_kernel, len(xs)),
        [*xs, *weights],
        [pl.BlockSpec((rows, width), lambda j: (0, 0))] * len(xs)
        + [pl.BlockSpec((HIDDEN_TILE, w.shape[1]), lambda j: (j, 0)) for w in weights],
        pl.BlockSpec((len(xs) * rows, HIDDEN_TILE), lambda j: (0, j)),
        jax.ShapeDtypeStruct((len(xs) * rows, hidden), dtype),
        (hidden // HIDDEN_TILE,),
        after,
        name="to_hidden",
    )


MODEL_STEP = 512
ROWS_STEP = 512


def left_parts(left_refs, rights):
    if len(left_refs) == rights:
        return [ref[...].T for ref in left_refs]
    rows = left_refs[0].shape[0] // rights
    return [left_refs[0][k * rows : (k + 1) * rows, :].T for k in range(rights)]


def weight_cols_step(left_ref, right_refs, out_refs):
    parts = left_parts([left_ref], len(right_refs))
    for first in range(0, right_refs[0].shape[1], MODEL_STEP):
        cols = slice(first, first + MODEL_STEP)
        term = matrix_product(parts[0], right_refs[0][:, cols])
        for part, ref in zip(parts[1:], right_refs[1:]):
            term = term + matrix_product(part, ref[:, cols])
        term = term.astype(jnp.bfloat16)
        begin = 0
        for out_ref in out_refs:
            end = begin + out_ref.shape[1]
            low, high = max(begin, first), min(end, first + MODEL_STEP)
            if low < high:
                out_ref[:, low - begin : high - begin] = term[:, low - first : high - first]
            begin = end


def weight_cols_kernel(steps, counts, *refs):
    ins, outs = refs[: 3 * len(counts)], refs[3 * len(counts) :]
    begin = 0
    for i, count in enumerate(counts):
        out_refs = outs[begin : begin + count]
        begin += count

        @pl.when(pl.program_id(0) // steps == i)
        def _():
            weight_cols_step(ins[3 * i], ins[3 * i + 1 : 3 * i + 3], out_refs)


def weight_cols(*jobs, after=()):
    rows, hidden = jobs[0][0].shape
    steps = hidden // HIDDEN_TILE
    inputs, in_specs, out_specs, out_shape = [], [], [], []
    for i, (left, rights, widths) in enumerate(jobs):

        def at(j, i=i):
            return jnp.clip(j - i * steps, 0, steps - 1)

        inputs += [left, *rights]
        in_specs += [pl.BlockSpec((rows, HIDDEN_TILE), lambda j, at=at: (0, at(j)))]
        in_specs += [
            pl.BlockSpec(r.shape, lambda j: (0, 0), pipeline_mode=pl.Buffered(1)) for r in rights
        ]
        out_specs += [pl.BlockSpec((HIDDEN_TILE, w), lambda j, at=at: (at(j), 0)) for w in widths]
        out_shape += [jax.ShapeDtypeStruct((hidden, w), jnp.bfloat16) for w in widths]
    return call(
        functools.partial(weight_cols_kernel, steps, tuple(len(job[2]) for job in jobs)),
        inputs,
        in_specs,
        out_specs,
        out_shape,
        (steps * len(jobs),),
        after,
        name="weight_cols",
    )


def add_halves_kernel(x_ref, y_ref, a_ref, b_ref, x_out, y_out):
    x_out[...] = x_ref[...] + b_ref[...]
    y_out[...] = y_ref[...] + a_ref[...]


def add_halves(along_x, along_y, from_a, from_b):
    rows, width = along_x.shape
    tile = rows // 2
    half = width // 2
    left = pl.BlockSpec((tile, half), lambda i: (i, 0))
    right = pl.BlockSpec((tile, half), lambda i: (i, 1))
    shape = jax.ShapeDtypeStruct((rows, width), along_x.dtype)
    return call(
        add_halves_kernel,
        [along_x, along_y, from_a, from_b],
        [right, left, left, left],
        [right, left],
        [shape, shape],
        (rows // tile,),
        input_output_aliases={0: 0, 1: 1},
        name="add_halves",
    )


def weight_rows_kernel(lefts, rights, *refs):
    left_refs, right_refs = refs[:lefts], refs[lefts : lefts + rights]
    out_refs, turned_ref = refs[lefts + rights : -1], refs[-1]
    rows = right_refs[0].shape[0]

    @pl.when(pl.program_id(0) == 0)
    def _():
        for k, ref in enumerate(left_refs):
            turned_ref[:, k * rows : (k + 1) * rows] = ref[...].T

    span = out_refs[0].shape[0]
    term = matrix_product(turned_ref[:, :rows], right_refs[0][...])
    for k in range(1, rights):
        term = term + matrix_product(turned_ref[:, k * rows : (k + 1) * rows], right_refs[k][...])
    term = term.astype(jnp.bfloat16)
    for i, out_ref in enumerate(out_refs):
        out_ref[...] = term[i * span : (i + 1) * span]


def weight_rows(lefts, rights, count, after=()):
    rows, hidden = lefts[0].shape
    width = rights[0].shape[1]
    shape = jax.ShapeDtypeStruct((hidden // count, width), jnp.bfloat16)
    return call(
        functools.partial(weight_rows_kernel, len(lefts), len(rights)),
        [*lefts, *rights],
        [
            pl.BlockSpec((rows, hidden), lambda j: (0, 0), pipeline_mode=pl.Buffered(1))
        ] * len(lefts)
        + [pl.BlockSpec((rows, ROWS_STEP), lambda j: (0, j))] * len(rights),
        [pl.BlockSpec((hidden // count, ROWS_STEP), lambda j: (0, j))] * count,
        [shape] * count,
        (width // ROWS_STEP,),
        after,
        scratch_shapes=[pltpu.VMEM((hidden, len(lefts) * rows), jnp.bfloat16)],
        name="weight_rows",
    )


def to_model_kernel(counts, order_ref, *refs):
    left_refs, weight_refs = refs[: len(counts)], refs[len(counts) : -2]
    out_ref, acc_ref = refs[-2:]

    @pl.when(pl.program_id(0) == 0)
    def _():
        acc_ref[...] = jnp.zeros_like(acc_ref)

    left = joined(left_refs)
    terms, begin = [], 0
    for count in counts:
        terms.append(joined(weight_refs[begin : begin + count]))
        begin += count
    weight = jnp.concatenate(terms, axis=0)
    for first in range(0, weight.shape[1], MODEL_STEP):
        cols = slice(first, first + MODEL_STEP)
        acc_ref[:, cols] += matrix_product(left, weight[:, cols])

    @pl.when(pl.program_id(0) == pl.num_programs(0) - 1)
    def _():
        block = acc_ref.shape[1] // order_ref.shape[0]
        for i in range(order_ref.shape[0]):
            at = pl.ds(pl.multiple_of(order_ref[i] * block, block), block)
            out_ref[:, at] = acc_ref[:, i * block : (i + 1) * block].astype(jnp.bfloat16)


def to_model(lefts, weights, order, half, rows, after=()):
    hidden = lefts[0].shape[1]
    flat = [w for pieces in weights for w in pieces]
    width = sum(w.shape[1] for w in weights[0])
    tile = HIDDEN_TILE // 2
    return call(
        functools.partial(to_model_kernel, tuple(len(pieces) for pieces in weights)),
        [*lefts, *flat],
        [pl.BlockSpec((rows, tile), lambda j, o: (half, j))] * len(lefts)
        + [pl.BlockSpec((tile, w.shape[1]), lambda j, o: (j, 0)) for w in flat],
        pl.BlockSpec((rows, width), lambda j, o: (0, 0)),
        jax.ShapeDtypeStruct((rows, width), jnp.bfloat16),
        (hidden // tile,),
        after,
        order,
        scratch_shapes=[pltpu.VMEM((rows, width), jnp.float32)],
        name="to_model",
    )


NORM_TILE = 128


def resid_kernel(order_ref, tokens_ref, own_ref, there_ref, gain_ref, resid_ref, normed_ref):
    resid = (
        tokens_ref[...].astype(jnp.float32)
        + own_ref[...].astype(jnp.float32)
        + there_ref[...].astype(jnp.float32)
    )
    resid_ref[...] = resid.astype(jnp.bfloat16)
    scale = lax.rsqrt(jnp.mean(resid * resid, axis=-1, keepdims=True) + EPS_NORM)
    normed = (resid * scale * gain_ref[...]).astype(jnp.bfloat16)
    block = normed.shape[1] // order_ref.shape[0]
    for i in range(order_ref.shape[0]):
        at = pl.ds(pl.multiple_of(order_ref[i] * block, block), block)
        normed_ref[:, at] = normed[:, i * block : (i + 1) * block]


def resid_norm(tokens, own, there, gain, order, after=()):
    rows, width = tokens.shape
    tile = pl.BlockSpec((NORM_TILE, width), lambda i, o: (i, 0))
    return call(
        resid_kernel,
        [tokens, own, there, gain[None, :]],
        [tile, tile, tile, pl.BlockSpec((1, width), lambda i, o: (0, 0))],
        [tile, tile],
        [
            jax.ShapeDtypeStruct((rows, width), jnp.bfloat16),
            jax.ShapeDtypeStruct((rows, width), jnp.bfloat16),
        ],
        (rows // NORM_TILE,),
        after,
        order,
        name="resid_norm",
    )


def norm_back_kernel(value_ref, base_ref, own_ref, there_ref, gain_ref, *out_refs):
    *grad_refs, sum_ref = out_refs

    @pl.when(pl.program_id(0) == 0)
    def _():
        sum_ref[...] = jnp.zeros_like(sum_ref)

    value = value_ref[...].astype(jnp.float32)
    upstream = own_ref[...].astype(jnp.float32) + there_ref[...].astype(jnp.float32)
    scale = lax.rsqrt(jnp.mean(value * value, axis=-1, keepdims=True) + EPS_NORM)
    hat = value * scale
    weighted = upstream * gain_ref[...]
    inner = jnp.mean(hat * weighted, axis=-1, keepdims=True)
    grad = base_ref[...].astype(jnp.float32) + scale * (weighted - hat * inner)
    for ref in grad_refs:
        ref[...] = grad.astype(ref.dtype)
    sum_ref[0:1, :] += jnp.sum(upstream * hat, axis=0, keepdims=True)


def norm_return(value, base, own, there, gain, dtypes, after=()):
    rows, width = value.shape
    tile = pl.BlockSpec((NORM_TILE, width), lambda i: (i, 0))
    return call(
        norm_back_kernel,
        [value, base, own, there, gain[None, :]],
        [tile, tile, tile, tile, pl.BlockSpec((1, width), lambda i: (0, 0))],
        [tile] * len(dtypes) + [pl.BlockSpec((8, width), lambda i: (0, 0))],
        [jax.ShapeDtypeStruct((rows, width), d) for d in dtypes]
        + [jax.ShapeDtypeStruct((8, width), jnp.float32)],
        (rows // NORM_TILE,),
        after,
        name="norm_return",
    )


def block_info(lengths, positions, first):
    count = (lengths + BLK - 1) // BLK
    ends = jnp.cumsum(count)
    starts = jnp.concatenate([jnp.zeros((1,), jnp.int32), ends])
    own = lax.dynamic_slice_in_dim(positions, first, 8)
    first_keys = jnp.max(jnp.where(starts[None, :] <= own[:, None], starts[None, :], 0), axis=1)
    limits = jnp.concatenate([lengths, jnp.zeros((1,), jnp.int32)])
    seq = jnp.sum((own[:, None] >= ends[None, :]).astype(jnp.int32), axis=1)
    limit = jnp.sum(jnp.where(seq[:, None] == jnp.arange(4)[None, :], limits[None, :], 0), axis=1)
    pos = ((own - first_keys)[:, None] * BLK + jnp.arange(BLK)[None, :]).astype(jnp.int32)
    valid = pos < limit[:, None]
    return first_keys, own, pos.reshape(-1), valid.reshape(-1)


def chip_layer(
    tokens,
    cotangent,
    seq_lens,
    block_pos,
    norm1_gain,
    w_query,
    key_matrix,
    value_matrix,
    query_gain,
    key_gain,
    w_out,
    norm2_gain,
    w_gate,
    w_up,
    w_down,
):
    xi, core, yi = lax.axis_index("x"), lax.axis_index("c"), lax.axis_index("y")
    rows, width = tokens.shape
    bf16, f32 = jnp.bfloat16, jnp.float32
    half, fourth = width // 2, width // 4

    q_in, k_in = w_query.shape[1], key_matrix.shape[1]
    fourth, eighth = width // 4, width // 8
    kvw_0 = gather_z(jnp.concatenate([key_matrix.T, value_matrix.T], axis=0))
    qw_0 = gather_z(w_query.T)
    up_0 = to_core(w_up.T, core)
    up_x, up_y = swap(up_0, "x"), swap(up_0, "y")
    down_0 = to_core(after(w_down, up_0), core)
    gate_0 = to_core(after(w_gate, up_0).T, core)
    low = up_0.shape[0] // 2
    out_0 = gather_z(w_out)
    dlo_0 = gather_z(down_0[:low])
    kvw_x, kvw_y = swap(kvw_0, "x"), swap(kvw_0, "y")
    middle = kvw_0.shape[0] // 2
    kvw_x, kvw_y, qw_0, up_x, up_y = sync(kvw_x, kvw_y, qw_0, up_x, up_y)
    kvw_ca, kvw_cb = swap(kvw_y[:middle], "x"), swap(kvw_x[middle:], "y")
    qw_x, qw_y = swap(qw_0, "x"), swap(qw_0, "y")
    kvw_ca, kvw_cb, qw_x, qw_y, out_0 = sync(kvw_ca, kvw_cb, qw_x, qw_y, out_0)
    qw_ca, qw_cb = swap(qw_y[:middle], "x"), swap(qw_x[middle:], "y")
    out_x, out_y = swap(out_0, "x"), swap(out_0, "y")
    kvw = [
        a.reshape(4, 2 * k_in, width)
        for a in (kvw_0, kvw_x, kvw_y, jnp.concatenate([kvw_ca, kvw_cb], axis=0))
    ]
    kv_w = jnp.concatenate(
        [part.reshape(-1, width) for a in kvw for part in (a[:, :k_in], a[:, k_in:])], axis=0
    )

    lengths_here = jnp.concatenate([seq_lens[0], block_pos[0]]).astype(f32)
    lengths_there = swap(lengths_here[None, :], "c")[0].astype(jnp.int32)
    first_own = yi * 8
    keys_here, at_here, pos_here, valid_here = block_info(seq_lens[0], block_pos[0], first_own)
    keys_there, at_there, pos_there, _ = block_info(
        lengths_there[:3], lengths_there[3:], first_own
    )
    info = jnp.stack(
        [
            jnp.concatenate([keys_here, at_here[:1]]),
            jnp.concatenate([keys_there, at_there[:1]]),
        ]
    ).astype(jnp.int32)
    freq = jnp.exp(
        jnp.arange(HEAD_SIZE // 2, dtype=f32) * (-2.0 * math.log(ROPE_BASE) / HEAD_SIZE)
    )
    angles = jnp.concatenate([pos_here, pos_there]).astype(f32)[:, None] * freq[None, :]
    cos_half, sin_half = jnp.cos(angles), jnp.sin(angles)
    cos_tab = jnp.concatenate([cos_half, cos_half], axis=1)
    sin_tab = jnp.concatenate([-sin_half, sin_half], axis=1)
    valid = valid_here.astype(f32)[:, None]

    blocks = jnp.arange(8)
    ry, rx, rc = blocks // 4, (blocks // 2) % 2, blocks % 2
    order = ((rx ^ xi) * 4 + rc * 2 + (ry ^ yi)).astype(jnp.int32)
    nx, nc, ny = blocks // 4, (blocks // 2) % 2, blocks % 2
    order_back = ((ny ^ yi) * 4 + (nx ^ xi) * 2 + nc).astype(jnp.int32)

    def stacked(first, second):
        return jnp.concatenate([first, second], axis=0)

    inputs = after(tokens, up_0).astype(f32)
    normed1 = rms_parts(inputs, norm1_gain)[0].astype(bf16)
    normed1 = [normed1, swap(normed1, "c")]
    dy_own = (valid * cotangent.astype(f32)).astype(bf16)

    def project(group, rows_in, weight, gain, count, wait=()):
        raw = to_hidden([rows_in], [weight], f32, wait)
        return raw, make_heads(group, raw, cos_tab, sin_tab, gain, count)

    normed1[0], kv_w = sync(normed1[0], kv_w)
    kv_raw0, kv0 = project(0, normed1[0], kv_w, key_gain, 2)
    kv0, qw_ca, qw_cb, out_x, out_y, up_y, normed1[0], gate_0, glo_in = sync(
        kv0, qw_ca, qw_cb, out_x, out_y, up_y, normed1[0], gate_0, gate_0[:low]
    )
    kv_far0, out_c, up_c = swap(kv0, "y"), swap(out_y, "x"), swap(up_y, "x")
    glo_0 = gather_z(glo_in)
    dhi_0, ghi_0 = gather_z(down_0[low:]), gather_z(gate_0[low:])
    q_w = jnp.concatenate([qw_0, qw_x, qw_y, qw_ca, qw_cb], axis=0)
    q_raw0, query0 = project(0, normed1[0], q_w, query_gain, 1)
    kv_raw1, kv1 = project(1, normed1[1], kv_w, key_gain, 2, [query0])
    kv_far0, out_c, up_c, dlo_0, kv1, normed1[1], dy_own = sync(
        kv_far0, out_c, up_c, dlo_0, kv1, normed1[1], dy_own
    )
    dlo_x, dlo_y = swap(dlo_0, "x"), swap(dlo_0, "y")
    up_in = jnp.concatenate([up_0, up_x, up_y, up_c], axis=1)
    ulo, uhi = gather_z(up_in[:low]), gather_z(up_in[low:])
    attn0, totals0 = attend(0, info, query0, kv0, kv_far0)
    out_w = jnp.concatenate([out_0, out_x, out_y, out_c], axis=0)
    attn0, out_w, dlo_x, dlo_y, kv_1, normed1[1] = sync(
        attn0, out_w, dlo_x, dlo_y, kv1, normed1[1]
    )
    q_raw1, query1 = project(1, normed1[1], q_w, query_gain, 1)
    dy = [reorder(dy_own, order, [query1])]
    dy.append(swap(dy[0], "c"))
    query, q_raw = [query0, query1], [q_raw0, q_raw1]
    kv, kv_raw = [kv0, kv1], [kv_raw0, kv_raw1]
    kv_far1, dlo_c = swap(kv_1, "y"), swap(dlo_y, "x")
    kv_far1, dlo_c, glo_0, query[1], dy[0] = sync(kv_far1, dlo_c, glo_0, query[1], dy[0])
    glo_x, glo_y = swap(glo_0, "x"), swap(glo_0, "y")
    attn1, totals1 = attend(1, info, query[1], kv[1], kv_far1)
    attn1, glo_x, glo_y, glo_0, dhi_0 = sync(attn1, glo_x, glo_y, glo_0, dhi_0)
    glo_ca, glo_cb = swap(glo_y[:, :eighth], "x"), swap(glo_x[:, eighth:], "y")
    dhi_x, dhi_y = swap(dhi_0, "x"), swap(dhi_0, "y")
    same = jnp.arange(8, dtype=jnp.int32)
    out_term = to_model([attn1], [[out_w]], same, 0, rows)
    out_there = swap(out_term, "c")
    out_here = to_model([attn0], [[out_w]], same, 0, rows, [out_term])
    dlo = [dlo_0, dlo_x, dlo_y, dlo_c]
    d_act_lo = to_hidden(dy, dlo, bf16, [out_here])
    resid, normed2_own = resid_norm(
        tokens, out_here, out_there, norm2_gain, order_back, [d_act_lo]
    )
    normed2_own, glo_ca, glo_cb, dhi_x, dhi_y, ghi_0 = sync(
        normed2_own, glo_ca, glo_cb, dhi_x, dhi_y, ghi_0
    )
    normed2 = [normed2_own, swap(normed2_own, "c")]
    ghi_x, ghi_y = swap(ghi_0, "x"), swap(ghi_0, "y")
    glo = [glo_0, glo_x, glo_y, glo_ca, glo_cb]
    act_lo, gg_lo, ug_lo = ffn(normed2, glo, ulo, d_act_lo)
    act_lo, dhi_y, ghi_x, ghi_y = sync(act_lo, dhi_y, ghi_x, ghi_y)
    dhi_c, ghi_c = swap(dhi_y, "x"), swap(ghi_x, "y")

    widths = [fourth, fourth, fourth, eighth, eighth]
    dlo_grad, gl_0, gl_x, gl_y, gl_ca, gl_cb = weight_cols(
        (act_lo, dy, [width]), (gg_lo, normed2, widths)
    )
    dlo_grad, gl_ca, gl_cb, dhi_c, ghi_c, ug_lo = sync(
        dlo_grad, gl_ca, gl_cb, dhi_c, ghi_c, ug_lo
    )
    dlo_sum = scatter_z(dlo_grad)
    from_a, from_b = swap(gl_ca, "x"), swap(gl_cb, "y")
    ul_0, ul_x, ul_y, ul_ca, ul_cb = weight_cols((ug_lo, normed2, widths))
    dhi, ghi = [dhi_0, dhi_x, dhi_y, dhi_c], [ghi_0, ghi_x, ghi_y, ghi_c]
    gl_x, gl_y, from_a, from_b, ul_ca, ul_cb, dhi[3] = sync(
        gl_x, gl_y, from_a, from_b, ul_ca, ul_cb, dhi[3]
    )
    from_ua, from_ub = swap(ul_ca, "x"), swap(ul_cb, "y")
    gl_x, gl_y = add_halves(gl_x, gl_y, from_a, from_b)
    d_act_hi = to_hidden(dy, dhi)
    gl_x, gl_y, ul_x, ul_y, from_ua, from_ub, d_act_hi = sync(
        gl_x, gl_y, ul_x, ul_y, from_ua, from_ub, d_act_hi
    )
    got_x, got_y = swap(gl_x, "x"), swap(gl_y, "y")
    ul_x, ul_y = add_halves(ul_x, ul_y, from_ua, from_ub)
    act_hi, gg_hi, ug_hi = ffn(normed2, ghi, uhi, d_act_hi)
    gl_0, got_x, got_y, ul_x, ul_y, act_hi, gg_hi, ug_hi = sync(
        gl_0, got_x, got_y, ul_x, ul_y, act_hi, gg_hi, ug_hi
    )
    got_ux, got_uy = swap(ul_x, "x"), swap(ul_y, "y")
    glo_near = gl_0 + got_x + got_y
    glo_sum = scatter_z(glo_near)
    dh_0, dh_x, dh_y, dh_ca, dh_cb, gh_0, gh_x, gh_y, gh_ca, gh_cb = weight_cols(
        (act_hi, dy, widths), (gg_hi, normed2, widths), after=[glo_near]
    )
    ul_0, got_ux, got_uy, dh_ca, dh_cb, ug_hi = sync(ul_0, got_ux, got_uy, dh_ca, dh_cb, ug_hi)
    from_a, from_b = swap(dh_ca, "x"), swap(dh_cb, "y")
    ulo_near = ul_0 + got_ux + got_uy
    ulo_sum = scatter_z(ulo_near)
    uh_0, uh_x, uh_y, uh_ca, uh_cb = weight_cols((ug_hi, normed2, widths), after=[ulo_near])
    dh_x, dh_y, from_a, from_b, gg_hi, uh_0 = sync(dh_x, dh_y, from_a, from_b, gg_hi, uh_0)
    dh_x, dh_y = add_halves(dh_x, dh_y, from_a, from_b)
    dh_x, dh_y, gg_hi = sync(dh_x, dh_y, gg_hi)
    got_x, got_y = swap(dh_x, "x"), swap(dh_y, "y")
    grads = [gg_lo, ug_lo, gg_hi, ug_hi]
    both_w = [glo, [ulo], ghi, [uhi]]
    there = to_model(grads, both_w, order, 1, rows)
    dh_0, got_x, got_y, gh_ca, gh_cb, uh_ca, uh_cb, there, gg_hi = sync(
        dh_0, got_x, got_y, gh_ca, gh_cb, uh_ca, uh_cb, there, gg_hi
    )
    normed2_there = swap(there, "c")
    from_ga, from_gb = swap(gh_ca, "x"), swap(gh_cb, "y")
    from_ua, from_ub = swap(uh_ca, "x"), swap(uh_cb, "y")
    dhi_near = dh_0 + got_x + got_y
    dhi_sum = scatter_z(dhi_near)
    grads = [gg_lo, ug_lo, gg_hi, ug_hi]
    grad_own = to_model(grads, both_w, order, 0, rows, [dhi_near])
    gh_x, gh_y, from_ga, from_gb, uh_x, uh_y, from_ua, from_ub, grad_own = sync(
        gh_x, gh_y, from_ga, from_gb, uh_x, uh_y, from_ua, from_ub, grad_own
    )
    gh_x, gh_y = add_halves(gh_x, gh_y, from_ga, from_gb)
    uh_x, uh_y = add_halves(uh_x, uh_y, from_ua, from_ub)
    gh_x, gh_y, uh_x, uh_y, grad_own = sync(gh_x, gh_y, uh_x, uh_y, grad_own)
    got_x, got_y = swap(gh_x, "x"), swap(gh_y, "y")
    got_ux, got_uy = swap(uh_x, "x"), swap(uh_y, "y")
    resid_here, gain2_sum = norm_return(
        resid, dy_own, grad_own, normed2_there, norm2_gain, (bf16,)
    )
    resid_first = resid_here
    resid_there = swap(resid_here, "c")

    d_attn0 = to_hidden([resid_here], [out_w])
    dq0, dkv0, dkv0_far = attend_back(0, info, query[0], d_attn0, attn0, totals0, kv[0], kv_far0)
    gh_0, got_x, got_y, uh_0, got_ux, got_uy, resid_there, dkv0_far, dlo_sum = sync(
        gh_0, got_x, got_y, uh_0, got_ux, got_uy, resid_there, dkv0_far, dlo_sum
    )
    dkv0_back = swap(dkv0_far, "y")
    dl_0, dl_x, dl_y, dl_c = (dlo_sum[:, i * fourth : (i + 1) * fourth] for i in range(4))
    from_l = swap(dl_c, "x")
    ghi_near, uhi_near = gh_0 + got_x + got_y, uh_0 + got_ux + got_uy
    ghi_sum, uhi_sum = scatter_z(ghi_near), scatter_z(uhi_near)
    o_0, o_x, o_y, o_c = weight_rows(
        [attn0, attn1], [resid_here, resid_there], 4, [ghi_near, uhi_near]
    )
    d_attn1 = to_hidden([resid_there], [out_w], bf16, [o_0])
    dq1, dkv1, dkv1_far = attend_back(1, info, query[1], d_attn1, attn1, totals1, kv[1], kv_far1)
    dkv1_far, dkv0_back, o_c, dl_x, dl_y, from_l, dq1 = sync(
        dkv1_far, dkv0_back, o_c, dl_x, dl_y, from_l, dq1
    )
    dkv1_back = swap(dkv1_far, "y")
    from_o = swap(o_c, "x")
    got_lx = swap(dl_x, "x")
    back = (cos_tab, sin_tab)
    q_grad = [
        heads_return(g, q_raw[g], d, [], *back, query_gain, 1, [dq1])
        for g, d in enumerate((dq0, dq1))
    ]
    q_gains = q_grad[0][1] + q_grad[1][1]
    q_grad = [q_grad[0][0], q_grad[1][0]]
    w_0, w_x, w_y, w_c = weight_rows(q_grad, normed1, 4)
    mixed_term = to_model([act_lo, act_hi], [dlo, dhi], order, 1, rows, [w_0])
    dkv1_back, from_o, w_c, mixed_term, o_x, o_y, dl_y, got_lx, gate_sum, up_sum = sync(
        dkv1_back, from_o, w_c, mixed_term, o_x, o_y, dl_y, got_lx, glo_sum, ulo_sum
    )
    glo_sum, ulo_sum = gate_sum, up_sum
    got_ly = swap(dl_y + from_l, "y")

    def halves(array):
        span = array.shape[0] // 2
        return array[:span], array[span:]

    def corner_rows(along_x, along_y, from_a, from_b):
        (x_a, x_b), (y_a, y_b) = halves(along_x), halves(along_y)
        return stacked(x_a, x_b + from_b), stacked(y_a + from_a, y_b)

    w_a, w_b = halves(w_c)
    from_wa, from_wb = swap(w_a, "x"), swap(w_b, "y")
    got_ox, got_oy = swap(o_x, "x"), swap(o_y + from_o, "y")
    kv_grad = [
        heads_return(g, kv_raw[g], d, [e], *back, key_gain, 2)
        for g, (d, e) in enumerate(((dkv0, dkv0_back), (dkv1, dkv1_back)))
    ]
    k_gains = kv_grad[0][1] + kv_grad[1][1]
    kv_grad = [kv_grad[0][0], kv_grad[1][0]]
    kv_0, kv_x, kv_y, kv_c = weight_rows(kv_grad, normed1, 4)
    kv_c, from_wa, from_wb, got_ox, got_oy, w_x, w_y, kv_grad[1], got_ly = sync(
        kv_c, from_wa, from_wb, got_ox, got_oy, w_x, w_y, kv_grad[1], got_ly
    )
    kv_a, kv_b = halves(kv_c)
    from_a, from_b = swap(kv_a, "x"), swap(kv_b, "y")
    w_x, w_y = corner_rows(w_x, w_y, from_wa, from_wb)
    got_wx, got_wy = swap(w_x, "x"), swap(w_y, "y")
    o_near = o_0 + got_ox + got_oy
    o_sum = scatter_z(o_near)
    term_there = to_model([q_grad[1], kv_grad[1]], [[q_w], [kv_w]], same, 0, rows, [o_near])
    kv_x, kv_y, from_a, from_b, term_there = sync(kv_x, kv_y, from_a, from_b, term_there)
    normed1_there = swap(term_there, "c")
    kv_x, kv_y = corner_rows(kv_x, kv_y, from_a, from_b)
    got_kx, got_ky = swap(kv_x, "x"), swap(kv_y, "y")
    term_own = to_model([q_grad[0], kv_grad[0]], [[q_w], [kv_w]], same, 0, rows, [kv_x, kv_y])
    w_0, got_wx, got_wy, kv_0, got_kx, got_ky, term_own = sync(
        w_0, got_wx, got_wy, kv_0, got_kx, got_ky, term_own
    )
    kv_near = kv_0 + got_kx + got_ky
    kv_sum = scatter_z(
        kv_near.reshape(2, 4, k_in, width).swapaxes(0, 1).reshape(8 * k_in, width)
    )
    w_near = w_0 + got_wx + got_wy
    w_sum = scatter_z(w_near)
    tokens_grad, gain1_sum = norm_return(
        tokens, resid_first, term_own, normed1_there, norm1_gain, (f32,), [kv_near, w_near]
    )
    gain1_part, gain2_part = gain1_sum[0], gain2_sum[0]
    gains = jnp.concatenate([gain1_part, gain2_part, q_gains[0], k_gains[0]])[None, :]
    gains = gains + swap(gains, "c")
    gains, act_hi = sync(gains, act_hi)
    gains_x = swap(gains, "x")
    mixed_own = to_model([act_lo, act_hi], [dlo, dhi], order, 0, rows, [gain1_sum])
    mixed_there = swap(mixed_term, "c")
    gains, gains_x, mixed_own = sync(gains, gains_x, mixed_own)
    gains = gains + gains_x
    gains = gains + swap(gains, "y")
    gains, mixed_own, kv_sum, w_sum, o_sum = sync(gains, mixed_own, kv_sum, w_sum, o_sum)
    gains_z = lax.ppermute(gains, "z", [(i, i ^ 1) for i in range(4)])
    output = (
        valid * (resid.astype(f32) + mixed_own.astype(f32) + mixed_there.astype(f32))
    ).astype(bf16)
    gains, gains_z, output = sync(gains, gains_z, output)
    gains = gains + gains_z
    gains = (gains + lax.ppermute(gains, "z", [(i, i ^ 2) for i in range(4)]))[0]
    dlo_sum = dl_0 + got_lx + got_ly

    gate_sum, up_sum, down_sum = (
        jnp.concatenate(pair, axis=0)
        for pair in ((glo_sum, ghi_sum), (ulo_sum, uhi_sum), (dlo_sum, dhi_sum))
    )
    gate_sum, up_sum, down_sum = from_core(
        [(a[:, :eighth], a[:, eighth:]) for a in (gate_sum, up_sum, down_sum)], core
    )
    return (
        output,
        tokens_grad,
        gains[:width],
        w_sum.astype(f32).T,
        kv_sum[:k_in].astype(f32).T,
        kv_sum[k_in:].astype(f32).T,
        gains[2 * width : 2 * width + HEAD_SIZE],
        gains[2 * width + HEAD_SIZE :],
        o_sum.astype(f32),
        gains[width : 2 * width],
        gate_sum.astype(f32).T,
        up_sum.astype(f32).T,
        down_sum.astype(f32),
    )


def chip_solution(mesh):
    fine = Mesh(mesh.devices.reshape(2, 2, 2, 4), ("x", "c", "y", "z"))
    row_spec = P(("x", "c", "y", "z"), None)
    group_spec = P(("x", "c", "z"), None)
    head_cols = P(None, ("y", "x", "c", "z"))
    head_rows = P(("y", "x", "c", "z"), None)
    up_spec, down_spec = P(("x", "c", "y"), "z"), P("z", ("x", "c", "y"))
    return jax.shard_map(
        chip_layer,
        mesh=fine,
        in_specs=(
            row_spec,
            row_spec,
            group_spec,
            group_spec,
            P(),
            head_cols,
            head_cols,
            head_cols,
            P(),
            P(),
            head_rows,
            P(),
            up_spec,
            up_spec,
            down_spec,
        ),
        out_specs=(
            row_spec,
            row_spec,
            P(),
            head_cols,
            head_cols,
            head_cols,
            P(),
            P(),
            head_rows,
            P(),
            up_spec,
            up_spec,
            down_spec,
        ),
        check_vma=False,
    )


def solution(mesh):
    sizes = dict(mesh.shape)
    if sizes == {"fsdp": 4, "heads": 2, "tensor": 4}:
        return chip_solution(mesh)
    return plain_solution(mesh)
```

```python
import functools
import math

import jax
import jax.numpy as jnp
from jax import lax
from jax.experimental import pallas as pl
from jax.experimental.pallas import tpu as pltpu
from jax.sharding import Mesh
from jax.sharding import PartitionSpec as P

QUERY_HEADS = 16
KEY_VALUE_HEADS = 8
HEAD_SIZE = 128
BLK = 128


EPS_NORM = 1e-06
ROPE_BASE = 1000000.0
NEG_FILL = -1e30


def row_info(lengths, positions):
    block_count = (lengths + BLK - 1) // BLK
    ends = jnp.cumsum(block_count)
    starts = ends - block_count
    used = ends[-1]
    column = positions[:, None]
    inside = (column >= starts[None, :]) & (column < ends[None, :])
    past = positions >= used
    seq_block = jnp.sum((column >= ends[None, :]).astype(jnp.int32), axis=1)
    first_block = jnp.sum(jnp.where(inside, starts[None, :], 0), axis=1) + jnp.where(past, used, 0)
    limit = jnp.sum(jnp.where(inside, lengths[None, :], 0), axis=1)
    offsets = jnp.arange(BLK, dtype=jnp.int32)[None, :]
    pos_rows = (positions - first_block)[:, None] * BLK + offsets
    seq_rows = jnp.broadcast_to(seq_block[:, None], pos_rows.shape)
    valid_rows = jnp.logical_not(past)[:, None] & (pos_rows < limit[:, None])
    return (seq_rows.reshape(-1), pos_rows.reshape(-1), valid_rows.reshape(-1))


def rope_tables(pos_rows):
    half_dim = HEAD_SIZE // 2
    freq = jnp.exp(
        jnp.arange(half_dim, dtype=jnp.float32) * (-2.0 * math.log(ROPE_BASE) / HEAD_SIZE)
    )
    angles = pos_rows.astype(jnp.float32)[:, None] * freq[None, :]
    return (jnp.cos(angles)[:, None, :], jnp.sin(angles)[:, None, :])


def rotate(value_rows, cos_tab, sin_tab):
    half_dim = value_rows.shape[-1] // 2
    first_half, second_half = (value_rows[..., :half_dim], value_rows[..., half_dim:])
    return jnp.concatenate(
        [
            first_half * cos_tab - second_half * sin_tab,
            second_half * cos_tab + first_half * sin_tab,
        ],
        axis=-1,
    )


def unrotate(upstream, cos_tab, sin_tab):
    half_dim = upstream.shape[-1] // 2
    first_half, second_half = (upstream[..., :half_dim], upstream[..., half_dim:])
    return jnp.concatenate(
        [
            first_half * cos_tab + second_half * sin_tab,
            second_half * cos_tab - first_half * sin_tab,
        ],
        axis=-1,
    )


def rms_parts(value_rows, gain_vec):
    scales = lax.rsqrt(jnp.mean(value_rows * value_rows, axis=-1, keepdims=True) + EPS_NORM)
    return (value_rows * scales * gain_vec, scales)


def norm_back(value_rows, scales, gain_vec, upstream):
    weighted = upstream * gain_vec
    inner = jnp.sum(value_rows * weighted, axis=-1, keepdims=True) / value_rows.shape[-1]
    return scales * weighted - value_rows * scales * scales * scales * inner


def matrix_product(left, right):
    return jnp.dot(left, right, preferred_element_type=jnp.float32)


def dot_rows(left, right):
    return lax.dot_general(
        left, right, (((0,), (0,)), ((), ())), preferred_element_type=jnp.float32
    )


def dot_cols(left, right):
    return lax.dot_general(
        left, right, (((1,), (1,)), ((), ())), preferred_element_type=jnp.float32
    )


def swap_cols(array, outer, inner):
    lead = array.shape[0]
    return jnp.swapaxes(array.reshape(lead, outer, inner, -1), 1, 2).reshape(lead, -1)


def swap_rows(array, outer, inner):
    width = array.shape[1]
    return jnp.swapaxes(array.reshape(outer, inner, -1, width), 0, 1).reshape(-1, width)


def spread_rows(local_rows):
    return lax.all_gather(local_rows, "tensor", axis=0, tiled=True)


def to_heads(packed):
    return lax.all_to_all(packed, "heads", split_axis=1, concat_axis=0, tiled=True)


def to_rows(packed):
    return lax.all_to_all(packed, "heads", split_axis=0, concat_axis=1, tiled=True)


def tensor_sum(term, row_count):
    total = lax.psum(
        term(0, row_count * lax.axis_size("tensor")).astype(jnp.bfloat16), "tensor"
    ).astype(jnp.float32)
    return lax.dynamic_slice_in_dim(total, lax.axis_index("tensor") * row_count, row_count)


def block_scores(query_blk, key_all, seq_blk, pos_blk, seq_all, pos_all):
    scores = jnp.einsum(
        "qkgd,pkd->kgqp", query_blk, key_all, preferred_element_type=jnp.float32
    ) * HEAD_SIZE ** (-0.5)
    allowed = (seq_blk[:, None] == seq_all[None, :]) & (pos_all[None, :] <= pos_blk[:, None])
    return jnp.where(allowed[None, None], scores, NEG_FILL)


def attend_forward(query_grp, key_grp, value_grp, seq_all, pos_all):
    group_factor = QUERY_HEADS // KEY_VALUE_HEADS
    group_len = query_grp.shape[0]
    kv_local = key_grp.shape[1] // HEAD_SIZE
    query_four = query_grp.reshape(group_len, kv_local, group_factor, HEAD_SIZE)
    key_three = key_grp.reshape(group_len, kv_local, HEAD_SIZE)
    value_three = value_grp.reshape(group_len, kv_local, HEAD_SIZE)
    block_rows = min(512, group_len)

    def forward_block(block_idx):
        first_row = block_idx * block_rows
        query_blk = lax.dynamic_slice_in_dim(query_four, first_row, block_rows)
        seq_blk = lax.dynamic_slice_in_dim(seq_all, first_row, block_rows)
        pos_blk = lax.dynamic_slice_in_dim(pos_all, first_row, block_rows)
        scores = block_scores(query_blk, key_three, seq_blk, pos_blk, seq_all, pos_all)
        peak = jnp.max(scores, axis=-1, keepdims=True)
        expo = jnp.exp(scores - peak)
        total = jnp.sum(expo, axis=-1, keepdims=True)
        probs_b = (expo / total).astype(jnp.bfloat16)
        attended = jnp.einsum(
            "kgqp,pkd->qkgd", probs_b, value_three, preferred_element_type=jnp.float32
        )
        return (attended, (peak + jnp.log(total))[..., 0])

    attended, log_sums = lax.map(forward_block, jnp.arange(group_len // block_rows))
    return (
        attended.reshape(group_len, kv_local * group_factor * HEAD_SIZE).astype(jnp.bfloat16),
        log_sums,
    )


def attend_backward(query_grp, key_grp, value_grp, grad_grp, log_sums, seq_all, pos_all):
    group_factor = QUERY_HEADS // KEY_VALUE_HEADS
    scale = HEAD_SIZE ** (-0.5)
    group_len = query_grp.shape[0]
    kv_local = key_grp.shape[1] // HEAD_SIZE
    query_four = query_grp.reshape(group_len, kv_local, group_factor, HEAD_SIZE)
    key_three = key_grp.reshape(group_len, kv_local, HEAD_SIZE)
    value_three = value_grp.reshape(group_len, kv_local, HEAD_SIZE)
    grad_four = grad_grp.reshape(group_len, kv_local, group_factor, HEAD_SIZE)
    block_rows = min(512, group_len)

    def backward_block(carry, block_idx):
        key_acc, value_acc = carry
        first_row = block_idx * block_rows
        query_blk = lax.dynamic_slice_in_dim(query_four, first_row, block_rows)
        grad_blk = lax.dynamic_slice_in_dim(grad_four, first_row, block_rows)
        seq_blk = lax.dynamic_slice_in_dim(seq_all, first_row, block_rows)
        pos_blk = lax.dynamic_slice_in_dim(pos_all, first_row, block_rows)
        scores = block_scores(query_blk, key_three, seq_blk, pos_blk, seq_all, pos_all)
        probs = jnp.exp(scores - log_sums[block_idx][..., None])
        probs_b = probs.astype(jnp.bfloat16)
        prob_grad = jnp.einsum(
            "qkgd,pkd->kgqp", grad_blk, value_three, preferred_element_type=jnp.float32
        )
        score_grad_b = (
            probs * (prob_grad - jnp.sum(probs * prob_grad, axis=-1, keepdims=True))
        ).astype(jnp.bfloat16)
        query_grad = (
            jnp.einsum(
                "kgqp,pkd->qkgd", score_grad_b, key_three, preferred_element_type=jnp.float32
            )
            * scale
        )
        key_acc = (
            key_acc
            + jnp.einsum(
                "kgqp,qkgd->pkd", score_grad_b, query_blk, preferred_element_type=jnp.float32
            )
            * scale
        )
        value_acc = value_acc + jnp.einsum(
            "kgqp,qkgd->pkd", probs_b, grad_blk, preferred_element_type=jnp.float32
        )
        return ((key_acc, value_acc), query_grad)

    empty = jnp.zeros((group_len, kv_local, HEAD_SIZE), jnp.float32)
    (key_acc, value_acc), query_blocks = lax.scan(
        backward_block, (empty, empty), jnp.arange(group_len // block_rows)
    )
    query_grad_b = query_blocks.reshape(group_len, kv_local * group_factor * HEAD_SIZE).astype(
        jnp.bfloat16
    )
    key_grad_b = key_acc.reshape(group_len, kv_local * HEAD_SIZE).astype(jnp.bfloat16)
    value_grad_b = value_acc.reshape(group_len, kv_local * HEAD_SIZE).astype(jnp.bfloat16)
    return (query_grad_b, key_grad_b, value_grad_b)


def project_heads(normed_b, query_w, key_w, value_w, query_gain, key_gain, pos_rows):
    lines = normed_b.shape[0]
    q_raw = matrix_product(normed_b, query_w).reshape(lines, -1, HEAD_SIZE)
    key_unnormed = matrix_product(normed_b, key_w).reshape(lines, -1, HEAD_SIZE)
    value_b = matrix_product(normed_b, value_w).astype(jnp.bfloat16)
    cos_tab, sin_tab = rope_tables(pos_rows)
    q_normed, q_scale = rms_parts(q_raw, query_gain)
    k_normed, k_scale = rms_parts(key_unnormed, key_gain)
    query_b = rotate(q_normed, cos_tab, sin_tab).astype(jnp.bfloat16).reshape(lines, -1)
    key_b = rotate(k_normed, cos_tab, sin_tab).astype(jnp.bfloat16).reshape(lines, -1)
    return (query_b, key_b, value_b, (q_raw, q_scale, key_unnormed, k_scale, cos_tab, sin_tab))


def heads_back(query_back, key_back, kept, query_gain, key_gain):
    q_raw, q_scale, key_unnormed, k_scale, cos_tab, sin_tab = kept
    lines = q_raw.shape[0]
    q_turned = unrotate(query_back.astype(jnp.float32).reshape(q_raw.shape), cos_tab, sin_tab)
    k_turned = unrotate(key_back.astype(jnp.float32).reshape(key_unnormed.shape), cos_tab, sin_tab)
    q_raw_grad = (
        norm_back(q_raw, q_scale, query_gain, q_turned).reshape(lines, -1).astype(jnp.bfloat16)
    )
    k_raw_grad = (
        norm_back(key_unnormed, k_scale, key_gain, k_turned).reshape(lines, -1).astype(jnp.bfloat16)
    )
    qgain_part = jnp.sum(q_turned * q_raw * q_scale, axis=(0, 1))
    kgain_part = jnp.sum(k_turned * key_unnormed * k_scale, axis=(0, 1))
    return (q_raw_grad, k_raw_grad, qgain_part, kgain_part)


def plain_layer(
    tokens,
    cotangent,
    seq_lens,
    block_pos,
    norm1_gain,
    w_query,
    key_matrix,
    value_matrix,
    query_gain,
    key_gain,
    w_out,
    norm2_gain,
    w_gate,
    w_up,
    w_down,
):
    row_count = tokens.shape[0]
    fsdp_count = lax.axis_size("fsdp")
    heads_count = lax.axis_size("heads")
    gate_full, up_full, down_full = (
        lax.all_gather(w_gate, ("fsdp", "heads"), axis=0, tiled=True),
        lax.all_gather(w_up, ("fsdp", "heads"), axis=0, tiled=True),
        lax.all_gather(w_down, ("fsdp", "heads"), axis=1, tiled=True),
    )
    seq_all, pos_all, valid_all = row_info(seq_lens[0], block_pos[0])
    own_first = lax.axis_index("heads") * row_count
    pos_own = lax.dynamic_slice_in_dim(pos_all, own_first, row_count)
    valid_own = lax.dynamic_slice_in_dim(valid_all, own_first, row_count).astype(jnp.float32)[
        :, None
    ]
    inputs = tokens.astype(jnp.float32)
    first_normed, scale1 = rms_parts(inputs, norm1_gain)
    normed1_b = first_normed.astype(jnp.bfloat16)
    query_all, key_all, value_all, out_all = (
        lax.all_gather(w_query, ("fsdp", "heads", "tensor"), axis=1, tiled=True),
        lax.all_gather(key_matrix, ("fsdp", "heads", "tensor"), axis=1, tiled=True),
        lax.all_gather(value_matrix, ("fsdp", "heads", "tensor"), axis=1, tiled=True),
        lax.all_gather(w_out, ("fsdp", "heads", "tensor"), axis=0, tiled=True),
    )
    query_full = swap_cols(query_all, fsdp_count, heads_count)
    key_full = swap_cols(key_all, fsdp_count, heads_count)
    value_full = swap_cols(value_all, fsdp_count, heads_count)
    out_full = swap_rows(out_all, fsdp_count, heads_count)
    query_b, key_b, value_b, kept = project_heads(
        normed1_b, query_full, key_full, value_full, query_gain, key_gain, pos_own
    )
    q_width = query_b.shape[1] // heads_count
    k_width = key_b.shape[1] // heads_count
    packed = jnp.concatenate(
        [
            query_b.reshape(row_count, heads_count, q_width),
            key_b.reshape(row_count, heads_count, k_width),
            value_b.reshape(row_count, heads_count, k_width),
        ],
        axis=2,
    )
    grouped = to_heads(packed.reshape(row_count, -1))
    query_grp = grouped[:, :q_width]
    key_grp = grouped[:, q_width : q_width + k_width]
    value_grp = grouped[:, q_width + k_width :]
    attended_b, log_sums = attend_forward(query_grp, key_grp, value_grp, seq_all, pos_all)
    attn_tok = to_rows(attended_b)
    resid = inputs + matrix_product(attn_tok, out_full)
    normed2, scale2 = rms_parts(resid, norm2_gain)
    normed2_b = normed2.astype(jnp.bfloat16)
    wide_in = spread_rows(normed2_b)
    gate_pre = matrix_product(wide_in, gate_full)
    up_pre = matrix_product(wide_in, up_full)
    sigmoid_gate = jax.nn.sigmoid(gate_pre)
    silu_gate = gate_pre * sigmoid_gate
    act_b = (silu_gate * up_pre).astype(jnp.bfloat16)

    def forward_term(first_row, span):
        return matrix_product(act_b, down_full)

    mixed = tensor_sum(forward_term, row_count)
    output = (valid_own * (resid + mixed)).astype(jnp.bfloat16)
    grad_out = valid_own * cotangent.astype(jnp.float32)
    wide_grad = spread_rows(grad_out.astype(jnp.bfloat16))
    act_grad = dot_cols(wide_grad, down_full)
    down_grad = dot_rows(act_b, wide_grad)
    gate_grad_b = (
        act_grad * up_pre * sigmoid_gate * (1.0 + gate_pre * (1.0 - sigmoid_gate))
    ).astype(jnp.bfloat16)
    up_grad_b = (act_grad * silu_gate).astype(jnp.bfloat16)
    gate_wgrad = dot_rows(wide_in, gate_grad_b)
    up_wgrad = dot_rows(wide_in, up_grad_b)

    def backward_term(first_row, span):
        return dot_cols(gate_grad_b, gate_full) + dot_cols(up_grad_b, up_full)

    normed2_grad = tensor_sum(backward_term, row_count)
    gate_sum, up_sum, down_sum = (
        lax.psum_scatter(
            gate_wgrad.astype(jnp.bfloat16), ("fsdp", "heads"), scatter_dimension=0, tiled=True
        ).astype(jnp.float32),
        lax.psum_scatter(
            up_wgrad.astype(jnp.bfloat16), ("fsdp", "heads"), scatter_dimension=0, tiled=True
        ).astype(jnp.float32),
        lax.psum_scatter(
            down_grad.astype(jnp.bfloat16), ("fsdp", "heads"), scatter_dimension=1, tiled=True
        ).astype(jnp.float32),
    )
    resid_grad = grad_out + norm_back(resid, scale2, norm2_gain, normed2_grad)
    gain2_part = jnp.sum(normed2_grad * resid * scale2, axis=0)
    resid_grad_b = resid_grad.astype(jnp.bfloat16)
    out_wgrad = dot_rows(attn_tok, resid_grad_b)
    attn_grad_b = dot_cols(resid_grad_b, out_full).astype(jnp.bfloat16)
    attn_grad_grp = to_heads(attn_grad_b)
    query_grad_b, key_grad_b, value_grad_b = attend_backward(
        query_grp, key_grp, value_grp, attn_grad_grp, log_sums, seq_all, pos_all
    )
    back_packed = to_rows(jnp.concatenate([query_grad_b, key_grad_b, value_grad_b], axis=1))
    back_three = back_packed.reshape(row_count, heads_count, -1)
    query_back = back_three[:, :, :q_width].reshape(row_count, -1)
    key_back = back_three[:, :, q_width : q_width + k_width].reshape(row_count, -1)
    value_back = back_three[:, :, q_width + k_width :].reshape(row_count, -1)
    q_raw_grad, k_raw_grad, qgain_part, kgain_part = heads_back(
        query_back, key_back, kept, query_gain, key_gain
    )
    query_wgrad = swap_cols(dot_rows(normed1_b, q_raw_grad), heads_count, fsdp_count)
    key_wgrad = swap_cols(dot_rows(normed1_b, k_raw_grad), heads_count, fsdp_count)
    value_wgrad = swap_cols(dot_rows(normed1_b, value_back), heads_count, fsdp_count)
    out_wgrad = swap_rows(out_wgrad, heads_count, fsdp_count)
    normed1_grad = (
        dot_cols(q_raw_grad, query_full)
        + dot_cols(k_raw_grad, key_full)
        + dot_cols(value_back, value_full)
    )
    query_sum, key_sum, value_sum, out_sum = (
        lax.psum_scatter(query_wgrad, ("fsdp", "heads", "tensor"), scatter_dimension=1, tiled=True),
        lax.psum_scatter(key_wgrad, ("fsdp", "heads", "tensor"), scatter_dimension=1, tiled=True),
        lax.psum_scatter(value_wgrad, ("fsdp", "heads", "tensor"), scatter_dimension=1, tiled=True),
        lax.psum_scatter(out_wgrad, ("fsdp", "heads", "tensor"), scatter_dimension=0, tiled=True),
    )
    tokens_grad = resid_grad + norm_back(inputs, scale1, norm1_gain, normed1_grad)
    gain1_part = jnp.sum(normed1_grad * inputs * scale1, axis=0)
    gain1_sum, qgain_sum, kgain_sum, gain2_sum = lax.psum(
        (gain1_part, qgain_part, kgain_part, gain2_part), ("fsdp", "heads", "tensor")
    )
    return (
        output,
        tokens_grad,
        gain1_sum,
        query_sum,
        key_sum,
        value_sum,
        qgain_sum,
        kgain_sum,
        out_sum,
        gain2_sum,
        gate_sum,
        up_sum,
        down_sum,
    )


def plain_solution(mesh):
    return jax.shard_map(
        plain_layer,
        mesh=mesh,
        in_specs=(
            P(("fsdp", "heads", "tensor"), None),
            P(("fsdp", "heads", "tensor"), None),
            P(("fsdp", "tensor"), None),
            P(("fsdp", "tensor"), None),
            P(),
            P(None, ("heads", "fsdp", "tensor")),
            P(None, ("heads", "fsdp", "tensor")),
            P(None, ("heads", "fsdp", "tensor")),
            P(),
            P(),
            P(("heads", "fsdp", "tensor"), None),
            P(),
            P(("fsdp", "heads"), "tensor"),
            P(("fsdp", "heads"), "tensor"),
            P("tensor", ("fsdp", "heads")),
        ),
        out_specs=(
            P(("fsdp", "heads", "tensor"), None),
            P(("fsdp", "heads", "tensor"), None),
            P(),
            P(None, ("heads", "fsdp", "tensor")),
            P(None, ("heads", "fsdp", "tensor")),
            P(None, ("heads", "fsdp", "tensor")),
            P(),
            P(),
            P(("heads", "fsdp", "tensor"), None),
            P(),
            P(("fsdp", "heads"), "tensor"),
            P(("fsdp", "heads"), "tensor"),
            P("tensor", ("fsdp", "heads")),
        ),
        check_vma=False,
    )


VMEM_LIMIT = 56 * 1024 * 1024
LOG2_E = 1.4426950408889634
SWAP = ((0, 1), (1, 0))
ROW_TILE = 1024
SCALE = HEAD_SIZE ** (-0.5)


def dot_t(left, right):
    return lax.dot_general(
        left, right, (((1,), (1,)), ((), ())), preferred_element_type=jnp.float32
    )


def swap(array, axis):
    return lax.ppermute(array, axis, SWAP)


def pick(first, second, index):
    return jnp.where(index == 0, first, second)


def join(mine, other, index, axis):
    return pick(
        jnp.concatenate([mine, other], axis=axis),
        jnp.concatenate([other, mine], axis=axis),
        index,
    )


def gather_z(array):
    return lax.all_gather(array, "z", axis=0, tiled=True)


def scatter_z(array):
    return lax.psum_scatter(array, "z", scatter_dimension=0, tiled=True)


def after(array, *done):
    return lax.optimization_barrier((array, *done))[0]


def sync(*arrays):
    return lax.optimization_barrier(arrays)


def to_core(array, core):
    half = array.shape[0] // 2
    first, second = array[:half], array[half:]
    other = swap(pick(second, first, core), "c")
    mine = pick(first, second, core)
    return join(mine, other, core, 1)


def from_core(pairs, core):
    mine = [pick(a, b, core) for a, b in pairs]
    send = jnp.concatenate([pick(b, a, core) for a, b in pairs], axis=0)
    others = jnp.split(swap(send, "c"), len(pairs))
    return [join(m, o, core, 0) for m, o in zip(mine, others)]


def call(kernel, inputs, in_specs, out_specs, out_shape, grid, after=(), prefetch=None, **more):
    lead = 0 if prefetch is None else 1
    count, extra = lead + len(inputs), len(after)

    def body(*refs):
        kernel(*refs[:count], *refs[count + extra :])

    if prefetch is not None:
        prefetched, inputs = [prefetch], list(inputs)
    else:
        prefetched, inputs = [], list(inputs)
    scratch = more.pop("scratch_shapes", ())
    return pl.pallas_call(
        body,
        grid_spec=pltpu.PrefetchScalarGridSpec(
            num_scalar_prefetch=lead,
            grid=grid,
            in_specs=list(in_specs) + [pl.BlockSpec(memory_space=pl.ANY)] * extra,
            out_specs=out_specs,
            scratch_shapes=scratch,
        ),
        out_shape=out_shape,
        compiler_params=pltpu.CompilerParams(vmem_limit_bytes=VMEM_LIMIT),
        cost_estimate=pl.CostEstimate(flops=1000, bytes_accessed=1000, transcendentals=0),
        **more,
    )(*prefetched, *inputs, *after)


def reorder_kernel(order_ref, in_ref, out_ref):
    out_ref[...] = in_ref[...]


def reorder(array, order, after=()):
    rows, width = array.shape
    parts = order.shape[0]
    return call(
        reorder_kernel,
        [array],
        [pl.BlockSpec((rows, width // parts), lambda i, o: (0, o[i]))],
        pl.BlockSpec((rows, width // parts), lambda i, o: (0, i)),
        jax.ShapeDtypeStruct(array.shape, array.dtype),
        (parts,),
        after,
        order,
        name="reorder",
    )


def lane_mean(value):
    ones = jnp.full((2 * HEAD_SIZE, HEAD_SIZE), 1.0 / HEAD_SIZE, jnp.bfloat16)
    high = value.astype(jnp.bfloat16)
    low = (value - high.astype(jnp.float32)).astype(jnp.bfloat16)
    return matrix_product(jnp.concatenate([high, low], axis=1), ones)


HEADS_STEP = 4


def heads_kernel(count, raw_ref, cos_ref, sin_ref, gain_ref, out_ref):
    for first in range(0, raw_ref.shape[1], count * HEAD_SIZE):
        lanes = slice(first, first + HEAD_SIZE)
        raw = raw_ref[:, lanes]
        value = raw * lax.rsqrt(lane_mean(raw * raw) + EPS_NORM) * gain_ref[...]
        out_ref[:, lanes] = (
            value * cos_ref[...] + pltpu.roll(value, HEAD_SIZE // 2, 1) * sin_ref[...]
        ).astype(jnp.bfloat16)
        if count == 2:
            lanes = slice(first + HEAD_SIZE, first + 2 * HEAD_SIZE)
            out_ref[:, lanes] = raw_ref[:, lanes].astype(jnp.bfloat16)


def make_heads(group, raw, cos_tab, sin_tab, gain, count, after=()):
    rows, width = raw.shape
    skip = group * (rows // ROW_TILE)
    table = pl.BlockSpec((ROW_TILE, HEAD_SIZE), lambda i, r: (i + skip, 0))
    one = pl.BlockSpec((ROW_TILE, HEADS_STEP * HEAD_SIZE), lambda i, r: (i, r))
    return call(
        functools.partial(heads_kernel, count),
        [raw, cos_tab, sin_tab, gain[None, :]],
        [one, table, table, pl.BlockSpec((1, HEAD_SIZE), lambda i, r: (0, 0))],
        one,
        jax.ShapeDtypeStruct((rows, width), jnp.bfloat16),
        (rows // ROW_TILE, width // (HEADS_STEP * HEAD_SIZE)),
        after,
        name="make_heads",
    )


def heads_back_kernel(count, raw_ref, cos_ref, sin_ref, gain_ref, *rest):
    *up_refs, out_ref, sum_ref = rest

    @pl.when((pl.program_id(0) == 0) & (pl.program_id(1) == 0))
    def _():
        sum_ref[...] = jnp.zeros_like(sum_ref)

    total = jnp.zeros((1, HEAD_SIZE), jnp.float32)
    for first in range(0, raw_ref.shape[1], count * HEAD_SIZE):
        lanes = slice(first, first + HEAD_SIZE)
        raw = raw_ref[:, lanes]
        upstream = up_refs[0][:, lanes].astype(jnp.float32)
        for ref in up_refs[1:]:
            upstream = upstream + ref[:, lanes].astype(jnp.float32)
        turned = upstream * cos_ref[...] - pltpu.roll(upstream, HEAD_SIZE // 2, 1) * sin_ref[...]
        scale = lax.rsqrt(lane_mean(raw * raw) + EPS_NORM)
        hat = raw * scale
        weighted = turned * gain_ref[...]
        out_ref[:, lanes] = (scale * (weighted - hat * lane_mean(hat * weighted))).astype(
            jnp.bfloat16
        )
        total = total + jnp.sum(turned * hat, axis=0, keepdims=True)
        if count == 2:
            lanes = slice(first + HEAD_SIZE, first + 2 * HEAD_SIZE)
            value_up = up_refs[0][:, lanes].astype(jnp.float32)
            for ref in up_refs[1:]:
                value_up = value_up + ref[:, lanes].astype(jnp.float32)
            out_ref[:, lanes] = value_up.astype(jnp.bfloat16)
    sum_ref[0:1, :] += total


def heads_return(group, raw, upstream, far, cos_tab, sin_tab, gain, count, after=()):
    rows, width = raw.shape
    skip = group * (rows // ROW_TILE)
    span = HEADS_STEP * HEAD_SIZE
    table = pl.BlockSpec((ROW_TILE, HEAD_SIZE), lambda i, r: (i + skip, 0))
    one = pl.BlockSpec((ROW_TILE, span), lambda i, r: (i, r))
    across = pl.BlockSpec((ROW_TILE, span), lambda i, r: (i, (r + 1) % 2))
    return call(
        functools.partial(heads_back_kernel, count),
        [raw, cos_tab, sin_tab, gain[None, :], upstream] + far,
        [one, table, table, pl.BlockSpec((1, HEAD_SIZE), lambda i, r: (0, 0)), one]
        + [across] * len(far),
        [one, pl.BlockSpec((8, HEAD_SIZE), lambda i, r: (0, 0))],
        [
            jax.ShapeDtypeStruct((rows, width), jnp.bfloat16),
            jax.ShapeDtypeStruct((8, HEAD_SIZE), jnp.float32),
        ],
        (rows // ROW_TILE, width // span),
        after,
        name="heads_return",
    )


GROUP_WIDTH = 2 * HEAD_SIZE
TOGETHER = 2


def stack_heads(block):
    return jnp.concatenate([block[:, :HEAD_SIZE], block[:, HEAD_SIZE:]], axis=0)


def key_bias(first_key, pair, parity, queries=0):
    shape = (1, 2 * BLK) if queries == 0 else (2 * BLK, 1)
    cols = lax.broadcasted_iota(jnp.int32, shape, 1 - queries)
    block = 2 * pair + jnp.where(cols < BLK, parity, 1 - parity)
    return jnp.where(block >= first_key, 0.0, NEG_FILL)


def last_bias(first_key, pair, parity, queries=0):
    rows = lax.broadcasted_iota(jnp.int32, (2 * BLK, 2 * BLK), queries)
    cols = lax.broadcasted_iota(jnp.int32, (2 * BLK, 2 * BLK), 1 - queries)
    far = (parity == 1) & (2 * pair >= first_key)
    own = lax.rem(cols, BLK) <= lax.rem(rows, BLK)
    far_bias = jnp.where(far, 0.0, NEG_FILL)
    return jnp.where(cols < BLK, jnp.where(own, 0.0, NEG_FILL), far_bias)


def pair_of(own_ref, far_ref, m, first):
    at = pl.ds(pl.multiple_of(m * BLK, BLK), BLK)
    lanes = slice(first, first + HEAD_SIZE)
    return jnp.concatenate([own_ref[at, lanes], far_ref[at, lanes]], axis=0)


def head_lanes(head):
    return slice(head * GROUP_WIDTH, (head + 1) * GROUP_WIDTH)


def attend_kernel(group, info_ref, q_ref, own_ref, far_ref, o_ref, l_ref):
    blocks = q_ref.shape[0] // BLK
    parity = info_ref[group, blocks]

    def one_block(j, _):
        first_key = info_ref[group, j]
        rows = pl.ds(pl.multiple_of(j * BLK, BLK), BLK)
        queries = [stack_heads(q_ref[rows, head_lanes(h)]) for h in range(TOGETHER)]

        def step(m, bias, carry):
            out = []
            for h in range(TOGETHER):
                total, acc = carry[h]
                score = dot_t(queries[h], pair_of(own_ref, far_ref, m, h * GROUP_WIDTH))
                expo = jnp.exp2(score * (SCALE * LOG2_E) + bias)
                total = total + jnp.sum(expo, axis=1, keepdims=True)
                value = pair_of(own_ref, far_ref, m, h * GROUP_WIDTH + HEAD_SIZE)
                acc = acc + matrix_product(expo.astype(jnp.bfloat16), value)
                out.append((total, acc))
            return tuple(out)

        empty = (
            jnp.zeros((2 * BLK, 1), jnp.float32),
            jnp.zeros((2 * BLK, HEAD_SIZE), jnp.float32),
        )
        carry = step(j, last_bias(first_key, j, parity), (empty,) * TOGETHER)
        carry = lax.fori_loop(
            lax.div(first_key, 2),
            j,
            lambda m, c: step(m, key_bias(first_key, m, parity), c),
            carry,
        )
        lane = lax.broadcasted_iota(jnp.int32, (BLK, HEAD_SIZE), 1)
        for h, (total, acc) in enumerate(carry):
            out = (acc / total).astype(jnp.bfloat16)
            o_ref[rows, head_lanes(h)] = jnp.concatenate([out[:BLK], out[BLK:]], axis=1)
            l_ref[rows, h * HEAD_SIZE : (h + 1) * HEAD_SIZE] = jnp.where(
                lane == 0, total[:BLK], total[BLK:]
            )
        return 0

    lax.fori_loop(0, blocks, one_block, 0)


def attend(group, info, query, own, far, after=()):
    rows, width = query.shape
    span = TOGETHER * GROUP_WIDTH
    here = pl.BlockSpec((rows, span), lambda r, s: (0, r))
    there = pl.BlockSpec((rows, span), lambda r, s: (0, (r + 1) % 2))
    return call(
        functools.partial(attend_kernel, group),
        [query, own, far],
        [here, here, there],
        [here, pl.BlockSpec((rows, span // 2), lambda r, s: (0, r))],
        [
            jax.ShapeDtypeStruct((rows, width), jnp.bfloat16),
            jax.ShapeDtypeStruct((rows, width // 2), jnp.float32),
        ],
        (width // span,),
        after,
        info,
        name="attend",
    )


def row_sums(value):
    ones = jnp.ones((8, 2 * HEAD_SIZE), jnp.bfloat16)
    high = value.astype(jnp.bfloat16)
    low = (value - high.astype(jnp.float32)).astype(jnp.bfloat16)
    return dot_t(ones, jnp.concatenate([high, low], axis=1))[:1]


def attend_back_kernel(
    group,
    info_ref,
    q_ref,
    do_ref,
    o_ref,
    l_ref,
    own_ref,
    far_ref,
    dq_ref,
    down_ref,
    dfar_ref,
    kacc_ref,
    vacc_ref,
):
    blocks = q_ref.shape[0] // BLK
    parity = info_ref[group, blocks]
    kacc_ref[...] = jnp.zeros_like(kacc_ref)
    vacc_ref[...] = jnp.zeros_like(vacc_ref)

    def one_block(j, _):
        first_key = info_ref[group, j]
        rows = pl.ds(pl.multiple_of(j * BLK, BLK), BLK)
        held = []
        for h in range(TOGETHER):
            query = stack_heads(q_ref[rows, head_lanes(h)])
            attn = stack_heads(o_ref[rows, head_lanes(h)]).astype(jnp.float32)
            grad = stack_heads(do_ref[rows, head_lanes(h)]).astype(jnp.float32)
            at = h * HEAD_SIZE
            total = jnp.concatenate(
                [l_ref[rows, at : at + 1], l_ref[rows, at + 1 : at + 2]], axis=0
            )
            grad_b = (grad / total).astype(jnp.bfloat16)
            inner = row_sums(grad_b.astype(jnp.float32) * attn)
            held.append((query, grad_b, inner))

        def step(m, bias, carry):
            at = pl.ds(pl.multiple_of(m * BLK, BLK), BLK)
            out = []
            for h in range(TOGETHER):
                query, grad_b, inner = held[h]
                key = pair_of(own_ref, far_ref, m, h * GROUP_WIDTH)
                value = pair_of(own_ref, far_ref, m, h * GROUP_WIDTH + HEAD_SIZE)
                expo = jnp.exp2(dot_t(key, query) * (SCALE * LOG2_E) + bias)
                d_score = (expo * (dot_t(value, grad_b) - inner)).astype(jnp.bfloat16)
                d_key = matrix_product(d_score, query)
                d_value = matrix_product(expo.astype(jnp.bfloat16), grad_b)
                kacc_ref[h, 0, at, :] += d_key[:BLK]
                kacc_ref[h, 1, at, :] += d_key[BLK:]
                vacc_ref[h, 0, at, :] += d_value[:BLK]
                vacc_ref[h, 1, at, :] += d_value[BLK:]
                out.append(carry[h] + dot_rows(d_score, key))
            return tuple(out)

        empty = jnp.zeros((2 * BLK, HEAD_SIZE), jnp.float32)
        carry = step(j, last_bias(first_key, j, parity, 1), (empty,) * TOGETHER)
        carry = lax.fori_loop(
            lax.div(first_key, 2),
            j,
            lambda m, c: step(m, key_bias(first_key, m, parity, 1), c),
            carry,
        )
        for h, dq in enumerate(carry):
            dq = (dq * SCALE).astype(jnp.bfloat16)
            dq_ref[rows, head_lanes(h)] = jnp.concatenate([dq[:BLK], dq[BLK:]], axis=1)
        return 0

    lax.fori_loop(0, blocks, one_block, 0)
    for h in range(TOGETHER):
        for half, ref in enumerate((down_ref, dfar_ref)):
            first = h * GROUP_WIDTH
            ref[:, first : first + HEAD_SIZE] = (kacc_ref[h, half] * SCALE).astype(jnp.bfloat16)
            ref[:, first + HEAD_SIZE : first + GROUP_WIDTH] = vacc_ref[h, half].astype(
                jnp.bfloat16
            )


def attend_back(group, info, query, d_attn, attn, total, own, far, after=()):
    rows, width = query.shape
    span = TOGETHER * GROUP_WIDTH
    here = pl.BlockSpec((rows, span), lambda r, s: (0, r))
    there = pl.BlockSpec((rows, span), lambda r, s: (0, (r + 1) % 2))
    shape = jax.ShapeDtypeStruct((rows, width), jnp.bfloat16)
    return call(
        functools.partial(attend_back_kernel, group),
        [query, d_attn, attn, total, own, far],
        [here, here, here, pl.BlockSpec((rows, span // 2), lambda r, s: (0, r)), here, there],
        [here] * 3,
        [shape] * 3,
        (width // span,),
        after,
        info,
        scratch_shapes=[
            pltpu.VMEM((TOGETHER, 2, rows, HEAD_SIZE), jnp.float32),
            pltpu.VMEM((TOGETHER, 2, rows, HEAD_SIZE), jnp.float32),
        ],
        name="attend_back",
    )


HIDDEN_TILE = 512
ROW_STEP = 1024


def row_steps(*refs):
    for first_ref in range(len(refs)):
        for first in range(0, refs[first_ref].shape[0], ROW_STEP):
            begin = first_ref * refs[first_ref].shape[0] + first
            yield refs[first_ref][first : first + ROW_STEP, :], slice(begin, begin + ROW_STEP)


def joined(refs):
    return jnp.concatenate([ref[...] for ref in refs], axis=1)


def ffn_kernel(pieces, xa_ref, xb_ref, *refs):
    gate_w = joined(refs[:pieces]).T
    up_w, d_act_ref = refs[pieces][...].T, refs[pieces + 1]
    act_ref, gate_ref, up_ref = refs[pieces + 2 :]
    for x, rows in row_steps(xa_ref, xb_ref):
        gate = matrix_product(x, gate_w)
        upper = matrix_product(x, up_w)
        d_act = d_act_ref[rows, :].astype(jnp.float32)
        sig = 0.5 * jnp.tanh(0.5 * gate) + 0.5
        silu = gate * sig
        act_ref[rows, :] = (silu * upper).astype(jnp.bfloat16)
        gate_ref[rows, :] = (d_act * upper * (sig + silu * (1.0 - sig))).astype(jnp.bfloat16)
        up_ref[rows, :] = (d_act * silu).astype(jnp.bfloat16)


def ffn(xs, gates, up, d_act, after=()):
    rows, width = xs[0].shape
    hidden = up.shape[0]
    out = pl.BlockSpec((2 * rows, HIDDEN_TILE), lambda j: (0, j))
    shape = jax.ShapeDtypeStruct((2 * rows, hidden), jnp.bfloat16)
    return call(
        functools.partial(ffn_kernel, len(gates)),
        [*xs, *gates, up, d_act],
        [pl.BlockSpec((rows, width), lambda j: (0, 0))] * 2
        + [pl.BlockSpec((HIDDEN_TILE, w.shape[1]), lambda j: (j, 0)) for w in (*gates, up)]
        + [out],
        [out] * 3,
        [shape] * 3,
        (hidden // HIDDEN_TILE,),
        after,
        name="ffn",
    )


def to_hidden_kernel(xs, *refs):
    weight = joined(refs[xs:-1]).T
    for x, rows in row_steps(*refs[:xs]):
        refs[-1][rows, :] = matrix_product(x, weight).astype(refs[-1].dtype)


def to_hidden(xs, weights, dtype=jnp.bfloat16, after=()):
    rows, width = xs[0].shape
    hidden = weights[0].shape[0]
    return call(
        functools.partial(to_hidden_kernel, len(xs)),
        [*xs, *weights],
        [pl.BlockSpec((rows, width), lambda j: (0, 0))] * len(xs)
        + [pl.BlockSpec((HIDDEN_TILE, w.shape[1]), lambda j: (j, 0)) for w in weights],
        pl.BlockSpec((len(xs) * rows, HIDDEN_TILE), lambda j: (0, j)),
        jax.ShapeDtypeStruct((len(xs) * rows, hidden), dtype),
        (hidden // HIDDEN_TILE,),
        after,
        name="to_hidden",
    )


MODEL_STEP = 512
ROWS_STEP = 512


def left_parts(left_refs, rights):
    if len(left_refs) == rights:
        return [ref[...].T for ref in left_refs]
    rows = left_refs[0].shape[0] // rights
    return [left_refs[0][k * rows : (k + 1) * rows, :].T for k in range(rights)]


def weight_cols_step(left_ref, right_refs, out_refs):
    parts = left_parts([left_ref], len(right_refs))
    for first in range(0, right_refs[0].shape[1], MODEL_STEP):
        cols = slice(first, first + MODEL_STEP)
        term = matrix_product(parts[0], right_refs[0][:, cols])
        for part, ref in zip(parts[1:], right_refs[1:]):
            term = term + matrix_product(part, ref[:, cols])
        term = term.astype(jnp.bfloat16)
        begin = 0
        for out_ref in out_refs:
            end = begin + out_ref.shape[1]
            low, high = max(begin, first), min(end, first + MODEL_STEP)
            if low < high:
                out_ref[:, low - begin : high - begin] = term[:, low - first : high - first]
            begin = end


def weight_cols_kernel(steps, counts, *refs):
    ins, outs = refs[: 3 * len(counts)], refs[3 * len(counts) :]
    begin = 0
    for i, count in enumerate(counts):
        out_refs = outs[begin : begin + count]
        begin += count

        @pl.when(pl.program_id(0) // steps == i)
        def _():
            weight_cols_step(ins[3 * i], ins[3 * i + 1 : 3 * i + 3], out_refs)


def weight_cols(*jobs, after=()):
    rows, hidden = jobs[0][0].shape
    steps = hidden // HIDDEN_TILE
    inputs, in_specs, out_specs, out_shape = [], [], [], []
    for i, (left, rights, widths) in enumerate(jobs):

        def at(j, i=i):
            return jnp.clip(j - i * steps, 0, steps - 1)

        inputs += [left, *rights]
        in_specs += [pl.BlockSpec((rows, HIDDEN_TILE), lambda j, at=at: (0, at(j)))]
        in_specs += [
            pl.BlockSpec(r.shape, lambda j: (0, 0), pipeline_mode=pl.Buffered(1)) for r in rights
        ]
        out_specs += [pl.BlockSpec((HIDDEN_TILE, w), lambda j, at=at: (at(j), 0)) for w in widths]
        out_shape += [jax.ShapeDtypeStruct((hidden, w), jnp.bfloat16) for w in widths]
    return call(
        functools.partial(weight_cols_kernel, steps, tuple(len(job[2]) for job in jobs)),
        inputs,
        in_specs,
        out_specs,
        out_shape,
        (steps * len(jobs),),
        after,
        name="weight_cols",
    )


def add_halves_kernel(x_ref, y_ref, a_ref, b_ref, x_out, y_out):
    x_out[...] = x_ref[...] + b_ref[...]
    y_out[...] = y_ref[...] + a_ref[...]


def add_halves(along_x, along_y, from_a, from_b):
    rows, width = along_x.shape
    tile = rows // 2
    half = width // 2
    left = pl.BlockSpec((tile, half), lambda i: (i, 0))
    right = pl.BlockSpec((tile, half), lambda i: (i, 1))
    shape = jax.ShapeDtypeStruct((rows, width), along_x.dtype)
    return call(
        add_halves_kernel,
        [along_x, along_y, from_a, from_b],
        [right, left, left, left],
        [right, left],
        [shape, shape],
        (rows // tile,),
        input_output_aliases={0: 0, 1: 1},
        name="add_halves",
    )


def weight_rows_kernel(lefts, rights, *refs):
    left_refs, right_refs = refs[:lefts], refs[lefts : lefts + rights]
    out_refs, turned_ref = refs[lefts + rights : -1], refs[-1]
    rows = right_refs[0].shape[0]

    @pl.when(pl.program_id(0) == 0)
    def _():
        for k, ref in enumerate(left_refs):
            turned_ref[:, k * rows : (k + 1) * rows] = ref[...].T

    span = out_refs[0].shape[0]
    term = matrix_product(turned_ref[:, :rows], right_refs[0][...])
    for k in range(1, rights):
        term = term + matrix_product(turned_ref[:, k * rows : (k + 1) * rows], right_refs[k][...])
    term = term.astype(jnp.bfloat16)
    for i, out_ref in enumerate(out_refs):
        out_ref[...] = term[i * span : (i + 1) * span]


def weight_rows(lefts, rights, count, after=()):
    rows, hidden = lefts[0].shape
    width = rights[0].shape[1]
    shape = jax.ShapeDtypeStruct((hidden // count, width), jnp.bfloat16)
    return call(
        functools.partial(weight_rows_kernel, len(lefts), len(rights)),
        [*lefts, *rights],
        [
            pl.BlockSpec((rows, hidden), lambda j: (0, 0), pipeline_mode=pl.Buffered(1))
        ] * len(lefts)
        + [pl.BlockSpec((rows, ROWS_STEP), lambda j: (0, j))] * len(rights),
        [pl.BlockSpec((hidden // count, ROWS_STEP), lambda j: (0, j))] * count,
        [shape] * count,
        (width // ROWS_STEP,),
        after,
        scratch_shapes=[pltpu.VMEM((hidden, len(lefts) * rows), jnp.bfloat16)],
        name="weight_rows",
    )


def to_model_kernel(counts, order_ref, *refs):
    left_refs, weight_refs = refs[: len(counts)], refs[len(counts) : -2]
    out_ref, acc_ref = refs[-2:]

    @pl.when(pl.program_id(0) == 0)
    def _():
        acc_ref[...] = jnp.zeros_like(acc_ref)

    left = joined(left_refs)
    terms, begin = [], 0
    for count in counts:
        terms.append(joined(weight_refs[begin : begin + count]))
        begin += count
    weight = jnp.concatenate(terms, axis=0)
    for first in range(0, weight.shape[1], MODEL_STEP):
        cols = slice(first, first + MODEL_STEP)
        acc_ref[:, cols] += matrix_product(left, weight[:, cols])

    @pl.when(pl.program_id(0) == pl.num_programs(0) - 1)
    def _():
        block = acc_ref.shape[1] // order_ref.shape[0]
        for i in range(order_ref.shape[0]):
            at = pl.ds(pl.multiple_of(order_ref[i] * block, block), block)
            out_ref[:, at] = acc_ref[:, i * block : (i + 1) * block].astype(jnp.bfloat16)


def to_model(lefts, weights, order, half, rows, after=()):
    hidden = lefts[0].shape[1]
    flat = [w for pieces in weights for w in pieces]
    width = sum(w.shape[1] for w in weights[0])
    tile = HIDDEN_TILE // 2
    return call(
        functools.partial(to_model_kernel, tuple(len(pieces) for pieces in weights)),
        [*lefts, *flat],
        [pl.BlockSpec((rows, tile), lambda j, o: (half, j))] * len(lefts)
        + [pl.BlockSpec((tile, w.shape[1]), lambda j, o: (j, 0)) for w in flat],
        pl.BlockSpec((rows, width), lambda j, o: (0, 0)),
        jax.ShapeDtypeStruct((rows, width), jnp.bfloat16),
        (hidden // tile,),
        after,
        order,
        scratch_shapes=[pltpu.VMEM((rows, width), jnp.float32)],
        name="to_model",
    )


NORM_TILE = 256


def resid_kernel(order_ref, tokens_ref, own_ref, there_ref, gain_ref, resid_ref, normed_ref):
    resid = (
        tokens_ref[...].astype(jnp.float32)
        + own_ref[...].astype(jnp.float32)
        + there_ref[...].astype(jnp.float32)
    )
    resid_ref[...] = resid.astype(jnp.bfloat16)
    scale = lax.rsqrt(jnp.mean(resid * resid, axis=-1, keepdims=True) + EPS_NORM)
    normed = (resid * scale * gain_ref[...]).astype(jnp.bfloat16)
    block = normed.shape[1] // order_ref.shape[0]
    for i in range(order_ref.shape[0]):
        at = pl.ds(pl.multiple_of(order_ref[i] * block, block), block)
        normed_ref[:, at] = normed[:, i * block : (i + 1) * block]


def resid_norm(tokens, own, there, gain, order, after=()):
    rows, width = tokens.shape
    tile = pl.BlockSpec((NORM_TILE, width), lambda i, o: (i, 0))
    return call(
        resid_kernel,
        [tokens, own, there, gain[None, :]],
        [tile, tile, tile, pl.BlockSpec((1, width), lambda i, o: (0, 0))],
        [tile, tile],
        [
            jax.ShapeDtypeStruct((rows, width), jnp.bfloat16),
            jax.ShapeDtypeStruct((rows, width), jnp.bfloat16),
        ],
        (rows // NORM_TILE,),
        after,
        order,
        name="resid_norm",
    )


def norm_back_kernel(value_ref, base_ref, own_ref, there_ref, gain_ref, *out_refs):
    *grad_refs, sum_ref = out_refs

    @pl.when(pl.program_id(0) == 0)
    def _():
        sum_ref[...] = jnp.zeros_like(sum_ref)

    value = value_ref[...].astype(jnp.float32)
    upstream = own_ref[...].astype(jnp.float32) + there_ref[...].astype(jnp.float32)
    scale = lax.rsqrt(jnp.mean(value * value, axis=-1, keepdims=True) + EPS_NORM)
    hat = value * scale
    weighted = upstream * gain_ref[...]
    inner = jnp.mean(hat * weighted, axis=-1, keepdims=True)
    grad = base_ref[...].astype(jnp.float32) + scale * (weighted - hat * inner)
    for ref in grad_refs:
        ref[...] = grad.astype(ref.dtype)
    sum_ref[0:1, :] += jnp.sum(upstream * hat, axis=0, keepdims=True)


def norm_return(value, base, own, there, gain, dtypes, after=()):
    rows, width = value.shape
    tile = pl.BlockSpec((NORM_TILE, width), lambda i: (i, 0))
    return call(
        norm_back_kernel,
        [value, base, own, there, gain[None, :]],
        [tile, tile, tile, tile, pl.BlockSpec((1, width), lambda i: (0, 0))],
        [tile] * len(dtypes) + [pl.BlockSpec((8, width), lambda i: (0, 0))],
        [jax.ShapeDtypeStruct((rows, width), d) for d in dtypes]
        + [jax.ShapeDtypeStruct((8, width), jnp.float32)],
        (rows // NORM_TILE,),
        after,
        name="norm_return",
    )


def block_info(lengths, positions, first):
    count = (lengths + BLK - 1) // BLK
    ends = jnp.cumsum(count)
    starts = jnp.concatenate([jnp.zeros((1,), jnp.int32), ends])
    own = lax.dynamic_slice_in_dim(positions, first, 8)
    first_keys = jnp.max(jnp.where(starts[None, :] <= own[:, None], starts[None, :], 0), axis=1)
    limits = jnp.concatenate([lengths, jnp.zeros((1,), jnp.int32)])
    seq = jnp.sum((own[:, None] >= ends[None, :]).astype(jnp.int32), axis=1)
    limit = jnp.sum(jnp.where(seq[:, None] == jnp.arange(4)[None, :], limits[None, :], 0), axis=1)
    pos = ((own - first_keys)[:, None] * BLK + jnp.arange(BLK)[None, :]).astype(jnp.int32)
    valid = pos < limit[:, None]
    return first_keys, own, pos.reshape(-1), valid.reshape(-1)


def chip_layer(
    tokens,
    cotangent,
    seq_lens,
    block_pos,
    norm1_gain,
    w_query,
    key_matrix,
    value_matrix,
    query_gain,
    key_gain,
    w_out,
    norm2_gain,
    w_gate,
    w_up,
    w_down,
):
    xi, core, yi = lax.axis_index("x"), lax.axis_index("c"), lax.axis_index("y")
    rows, width = tokens.shape
    bf16, f32 = jnp.bfloat16, jnp.float32
    half, fourth = width // 2, width // 4

    q_in, k_in = w_query.shape[1], key_matrix.shape[1]
    fourth, eighth = width // 4, width // 8
    kvw_0 = gather_z(jnp.concatenate([key_matrix.T, value_matrix.T], axis=0))
    qw_0 = gather_z(w_query.T)
    up_0 = to_core(w_up.T, core)
    up_x, up_y = swap(up_0, "x"), swap(up_0, "y")
    down_0 = to_core(after(w_down, up_0), core)
    gate_0 = to_core(after(w_gate, up_0).T, core)
    low = up_0.shape[0] // 2
    out_0 = gather_z(w_out)
    dlo_0 = gather_z(down_0[:low])
    kvw_x, kvw_y = swap(kvw_0, "x"), swap(kvw_0, "y")
    middle = kvw_0.shape[0] // 2
    kvw_x, kvw_y, qw_0, up_x, up_y = sync(kvw_x, kvw_y, qw_0, up_x, up_y)
    kvw_ca, kvw_cb = swap(kvw_y[:middle], "x"), swap(kvw_x[middle:], "y")
    qw_x, qw_y = swap(qw_0, "x"), swap(qw_0, "y")
    kvw_ca, kvw_cb, qw_x, qw_y, out_0 = sync(kvw_ca, kvw_cb, qw_x, qw_y, out_0)
    qw_ca, qw_cb = swap(qw_y[:middle], "x"), swap(qw_x[middle:], "y")
    out_x, out_y = swap(out_0, "x"), swap(out_0, "y")
    kvw = [
        a.reshape(4, 2 * k_in, width)
        for a in (kvw_0, kvw_x, kvw_y, jnp.concatenate([kvw_ca, kvw_cb], axis=0))
    ]
    kv_w = jnp.concatenate(
        [part.reshape(-1, width) for a in kvw for part in (a[:, :k_in], a[:, k_in:])], axis=0
    )

    lengths_here = jnp.concatenate([seq_lens[0], block_pos[0]]).astype(f32)
    lengths_there = swap(lengths_here[None, :], "c")[0].astype(jnp.int32)
    first_own = yi * 8
    keys_here, at_here, pos_here, valid_here = block_info(seq_lens[0], block_pos[0], first_own)
    keys_there, at_there, pos_there, _ = block_info(
        lengths_there[:3], lengths_there[3:], first_own
    )
    info = jnp.stack(
        [
            jnp.concatenate([keys_here, at_here[:1]]),
            jnp.concatenate([keys_there, at_there[:1]]),
        ]
    ).astype(jnp.int32)
    freq = jnp.exp(
        jnp.arange(HEAD_SIZE // 2, dtype=f32) * (-2.0 * math.log(ROPE_BASE) / HEAD_SIZE)
    )
    angles = jnp.concatenate([pos_here, pos_there]).astype(f32)[:, None] * freq[None, :]
    cos_half, sin_half = jnp.cos(angles), jnp.sin(angles)
    cos_tab = jnp.concatenate([cos_half, cos_half], axis=1)
    sin_tab = jnp.concatenate([-sin_half, sin_half], axis=1)
    valid = valid_here.astype(f32)[:, None]

    blocks = jnp.arange(8)
    ry, rx, rc = blocks // 4, (blocks // 2) % 2, blocks % 2
    order = ((rx ^ xi) * 4 + rc * 2 + (ry ^ yi)).astype(jnp.int32)
    nx, nc, ny = blocks // 4, (blocks // 2) % 2, blocks % 2
    order_back = ((ny ^ yi) * 4 + (nx ^ xi) * 2 + nc).astype(jnp.int32)

    def stacked(first, second):
        return jnp.concatenate([first, second], axis=0)

    inputs = after(tokens, up_0).astype(f32)
    normed1 = rms_parts(inputs, norm1_gain)[0].astype(bf16)
    normed1 = [normed1, swap(normed1, "c")]
    dy_own = (valid * cotangent.astype(f32)).astype(bf16)

    def project(group, rows_in, weight, gain, count, wait=()):
        raw = to_hidden([rows_in], [weight], f32, wait)
        return raw, make_heads(group, raw, cos_tab, sin_tab, gain, count)

    normed1[0], kv_w = sync(normed1[0], kv_w)
    kv_raw0, kv0 = project(0, normed1[0], kv_w, key_gain, 2)
    kv0, qw_ca, qw_cb, out_x, out_y, up_y, normed1[0], gate_0, glo_in = sync(
        kv0, qw_ca, qw_cb, out_x, out_y, up_y, normed1[0], gate_0, gate_0[:low]
    )
    kv_far0, out_c, up_c = swap(kv0, "y"), swap(out_y, "x"), swap(up_y, "x")
    glo_0 = gather_z(glo_in)
    dhi_0, ghi_0 = gather_z(down_0[low:]), gather_z(gate_0[low:])
    q_w = jnp.concatenate([qw_0, qw_x, qw_y, qw_ca, qw_cb], axis=0)
    q_raw0, query0 = project(0, normed1[0], q_w, query_gain, 1)
    kv_raw1, kv1 = project(1, normed1[1], kv_w, key_gain, 2, [query0])
    kv_far0, out_c, up_c, dlo_0, kv1, normed1[1], dy_own = sync(
        kv_far0, out_c, up_c, dlo_0, kv1, normed1[1], dy_own
    )
    dlo_x, dlo_y = swap(dlo_0, "x"), swap(dlo_0, "y")
    up_in = jnp.concatenate([up_0, up_x, up_y, up_c], axis=1)
    ulo, uhi = gather_z(up_in[:low]), gather_z(up_in[low:])
    attn0, totals0 = attend(0, info, query0, kv0, kv_far0)
    out_w = jnp.concatenate([out_0, out_x, out_y, out_c], axis=0)
    attn0, out_w, dlo_x, dlo_y, kv_1, normed1[1] = sync(
        attn0, out_w, dlo_x, dlo_y, kv1, normed1[1]
    )
    q_raw1, query1 = project(1, normed1[1], q_w, query_gain, 1)
    dy = [reorder(dy_own, order, [query1])]
    dy.append(swap(dy[0], "c"))
    query, q_raw = [query0, query1], [q_raw0, q_raw1]
    kv, kv_raw = [kv0, kv1], [kv_raw0, kv_raw1]
    kv_far1, dlo_c = swap(kv_1, "y"), swap(dlo_y, "x")
    kv_far1, dlo_c, glo_0, query[1], dy[0] = sync(kv_far1, dlo_c, glo_0, query[1], dy[0])
    glo_x, glo_y = swap(glo_0, "x"), swap(glo_0, "y")
    attn1, totals1 = attend(1, info, query[1], kv[1], kv_far1)
    attn1, glo_x, glo_y, glo_0 = sync(attn1, glo_x, glo_y, glo_0)
    glo_ca, glo_cb = swap(glo_y[:, :eighth], "x"), swap(glo_x[:, eighth:], "y")
    same = jnp.arange(8, dtype=jnp.int32)
    out_term = to_model([attn1], [[out_w]], same, 0, rows)
    out_there = swap(out_term, "c")
    out_here = to_model([attn0], [[out_w]], same, 0, rows, [out_term])
    dlo = [dlo_0, dlo_x, dlo_y, dlo_c]
    d_act_lo = to_hidden(dy, dlo, bf16, [out_here])
    resid, normed2_own = resid_norm(
        tokens, out_here, out_there, norm2_gain, order_back, [d_act_lo]
    )
    normed2_own, glo_ca, glo_cb, dhi_0 = sync(normed2_own, glo_ca, glo_cb, dhi_0)
    normed2 = [normed2_own, swap(normed2_own, "c")]
    dhi_x, dhi_y = swap(dhi_0, "x"), swap(dhi_0, "y")
    glo = [glo_0, glo_x, glo_y, glo_ca, glo_cb]
    act_lo, gg_lo, ug_lo = ffn(normed2, glo, ulo, d_act_lo)
    act_lo, gg_lo, dhi_x, dhi_y, ghi_0 = sync(act_lo, gg_lo, dhi_x, dhi_y, ghi_0)
    ghi_x, ghi_y = swap(ghi_0, "x"), swap(ghi_0, "y")

    widths = [fourth, fourth, fourth, eighth, eighth]
    dlo_grad, gl_0, gl_x, gl_y, gl_ca, gl_cb = weight_cols(
        (act_lo, dy, [width]), (gg_lo, normed2, widths)
    )
    dlo_grad, gl_ca, gl_cb, ghi_x, ghi_y, ug_lo, dhi_x, dhi_y = sync(
        dlo_grad, gl_ca, gl_cb, ghi_x, ghi_y, ug_lo, dhi_x, dhi_y
    )
    dlo_sum = scatter_z(dlo_grad)
    dhi_ca, dhi_cb = swap(dhi_y[:, :eighth], "x"), swap(dhi_x[:, eighth:], "y")
    ul_0, ul_x, ul_y, ul_ca, ul_cb = weight_cols((ug_lo, normed2, widths))
    dhi_ca, dhi_cb, ul_ca, ul_cb, ghi_x, ghi_y = sync(dhi_ca, dhi_cb, ul_ca, ul_cb, ghi_x, ghi_y)
    dhi = [dhi_0, dhi_x, dhi_y, dhi_ca, dhi_cb]
    ghi_ca, ghi_cb = swap(ghi_y[:, :eighth], "x"), swap(ghi_x[:, eighth:], "y")
    d_act_hi = to_hidden(dy, dhi)
    ghi_ca, ghi_cb, gl_ca, gl_cb, d_act_hi = sync(ghi_ca, ghi_cb, gl_ca, gl_cb, d_act_hi)
    ghi = [ghi_0, ghi_x, ghi_y, ghi_ca, ghi_cb]
    from_a, from_b = swap(gl_ca, "x"), swap(gl_cb, "y")
    from_ua, from_ub = swap(ul_ca, "x"), swap(ul_cb, "y")
    act_hi, gg_hi, ug_hi = ffn(normed2, ghi, uhi, d_act_hi)
    gl_x, gl_y, from_a, from_b, ul_x, ul_y, from_ua, from_ub, act_hi, gg_hi, ug_hi = sync(
        gl_x, gl_y, from_a, from_b, ul_x, ul_y, from_ua, from_ub, act_hi, gg_hi, ug_hi
    )
    gl_x, gl_y = add_halves(gl_x, gl_y, from_a, from_b)
    gl_x, gl_y, gg_hi = sync(gl_x, gl_y, gg_hi)
    got_x, got_y = swap(gl_x, "x"), swap(gl_y, "y")
    pieces = [fourth] * 4
    dh_0, dh_x, dh_y, dh_ca, dh_cb, gh_0, gh_x, gh_y, gh_c = weight_cols(
        (act_hi, dy, widths), (gg_hi, normed2, pieces)
    )
    gl_0, got_x, got_y, dh_ca, dh_cb, ug_hi, ul_x, ul_y = sync(
        gl_0, got_x, got_y, dh_ca, dh_cb, ug_hi, ul_x, ul_y
    )
    from_a, from_b = swap(dh_ca, "x"), swap(dh_cb, "y")
    glo_near = gl_0 + got_x + got_y
    glo_sum = scatter_z(glo_near)
    ul_x, ul_y = add_halves(ul_x, ul_y, from_ua, from_ub)
    uh_0, uh_x, uh_y, uh_c = weight_cols(
        (ug_hi, normed2, pieces), after=[glo_near, ul_x]
    )
    dh_x, dh_y, from_a, from_b, ul_x, ul_y, gg_hi, uh_0 = sync(
        dh_x, dh_y, from_a, from_b, ul_x, ul_y, gg_hi, uh_0
    )
    got_ux, got_uy = swap(ul_x, "x"), swap(ul_y, "y")
    dh_x, dh_y = add_halves(dh_x, dh_y, from_a, from_b)
    grads = [gg_lo, ug_lo, gg_hi, ug_hi]
    both_w = [glo, [ulo], ghi, [uhi]]
    there = to_model(grads, both_w, order, 1, rows, [dh_x, dh_y])
    ul_0, got_ux, got_uy, dh_x, dh_y, there, gg_hi = sync(
        ul_0, got_ux, got_uy, dh_x, dh_y, there, gg_hi
    )
    normed2_there = swap(there, "c")
    got_x, got_y = swap(dh_x, "x"), swap(dh_y, "y")
    ulo_near = ul_0 + got_ux + got_uy
    ulo_sum = scatter_z(ulo_near)
    grads = [gg_lo, ug_lo, gg_hi, ug_hi]
    grad_own = to_model(grads, both_w, order, 0, rows, [ulo_near])
    dh_0, got_x, got_y, gh_c, uh_c, grad_own = sync(dh_0, got_x, got_y, gh_c, uh_c, grad_own)
    from_g, from_u = swap(gh_c, "x"), swap(uh_c, "y")
    dhi_near = dh_0 + got_x + got_y
    dhi_sum = scatter_z(dhi_near)
    resid_here, gain2_sum = norm_return(
        resid, dy_own, grad_own, normed2_there, norm2_gain, (bf16,), [dhi_near]
    )
    resid_first = resid_here
    resid_there = swap(resid_here, "c")
    mixed_term = to_model([act_lo, act_hi], [dlo, dhi], order, 1, rows, [resid_here])
    d_attn0 = to_hidden([resid_here], [out_w], bf16, [mixed_term])
    gh_x, gh_y, from_g, uh_x, uh_y, from_u, mixed_term, d_attn0 = sync(
        gh_x, gh_y, from_g, uh_x, uh_y, from_u, mixed_term, d_attn0
    )
    gh_y, uh_x = gh_y + from_g, uh_x + from_u
    gh_x, gh_y, uh_x, uh_y, d_attn0 = sync(gh_x, gh_y, uh_x, uh_y, d_attn0)
    got_x, got_y = swap(gh_x, "x"), swap(gh_y, "y")
    got_ux, got_uy = swap(uh_x, "x"), swap(uh_y, "y")
    mixed_there = swap(mixed_term, "c")

    dq0, dkv0, dkv0_far = attend_back(0, info, query[0], d_attn0, attn0, totals0, kv[0], kv_far0)
    o_0, o_x, o_y, o_c = weight_rows([attn0, attn1], [resid_here, resid_there], 4, [dq0])
    gh_0, got_x, got_y, uh_0, got_ux, got_uy, resid_there, dkv0_far, dlo_sum, o_c = sync(
        gh_0, got_x, got_y, uh_0, got_ux, got_uy, resid_there, dkv0_far, dlo_sum, o_c
    )
    dkv0_back, from_o = swap(dkv0_far, "y"), swap(o_c, "x")
    dl_0, dl_x, dl_y, dl_c = (dlo_sum[:, i * fourth : (i + 1) * fourth] for i in range(4))
    from_l, got_lx = swap(dl_c, "x"), swap(dl_x, "x")
    ghi_near, uhi_near = gh_0 + got_x + got_y, uh_0 + got_ux + got_uy
    ghi_sum, uhi_sum = scatter_z(ghi_near), scatter_z(uhi_near)
    back = (cos_tab, sin_tab)
    d_attn1 = to_hidden([resid_there], [out_w], bf16, [ghi_near, uhi_near])
    dq1, dkv1, dkv1_far = attend_back(1, info, query[1], d_attn1, attn1, totals1, kv[1], kv_far1)
    q_grad0, q_gain0 = heads_return(0, q_raw[0], dq0, [], *back, query_gain, 1, [dq1])
    dkv1_far, dkv0_back, o_x, o_y, from_o, got_lx, dl_y, from_l, q_grad0 = sync(
        dkv1_far, dkv0_back, o_x, o_y, from_o, got_lx, dl_y, from_l, q_grad0
    )
    dkv1_back, got_ox = swap(dkv1_far, "y"), swap(o_x, "x")
    q_grad1, q_gain1 = heads_return(1, q_raw[1], dq1, [], *back, query_gain, 1, [q_grad0])
    q_grad, q_gains = [q_grad0, q_grad1], q_gain0 + q_gain1
    w_0, w_x, w_y, w_c = weight_rows(q_grad, normed1, 4)
    w_c, act_hi = sync(w_c, act_hi)
    from_w = swap(w_c, "x")
    mixed_own = to_model([act_lo, act_hi], [dlo, dhi], order, 0, rows)
    dkv1_back, got_ox, from_w, mixed_own, o_y, dl_y, w_x, w_y = sync(
        dkv1_back, got_ox, from_w, mixed_own, o_y + from_o, dl_y + from_l, w_x, w_y
    )
    got_oy, got_wx = swap(o_y, "y"), swap(w_x, "x")
    got_wy = swap(w_y + from_w, "y")

    def halves(array):
        span = array.shape[0] // 2
        return array[:span], array[span:]

    def corner_rows(along_x, along_y, from_a, from_b):
        (x_a, x_b), (y_a, y_b) = halves(along_x), halves(along_y)
        return stacked(x_a, x_b + from_b), stacked(y_a + from_a, y_b)

    kv_grad = [
        heads_return(g, kv_raw[g], d, [e], *back, key_gain, 2, [mixed_own, w_y])
        for g, (d, e) in enumerate(((dkv0, dkv0_back), (dkv1, dkv1_back)))
    ]
    k_gains = kv_grad[0][1] + kv_grad[1][1]
    kv_grad = [kv_grad[0][0], kv_grad[1][0]]
    kv_0, kv_x, kv_y, kv_c = weight_rows(kv_grad, normed1, 4)
    kv_c, kv_grad[1], got_oy, got_wx = sync(kv_c, kv_grad[1], got_oy, got_wx)
    kv_a, kv_b = halves(kv_c)
    from_a, from_b = swap(kv_a, "x"), swap(kv_b, "y")
    term_there = to_model([q_grad[1], kv_grad[1]], [[q_w], [kv_w]], same, 0, rows)
    o_0, got_oy, w_0, got_wx, got_wy, kv_x, kv_y, from_a, from_b, term_there, dl_y = sync(
        o_0, got_oy, w_0, got_wx, got_wy, kv_x, kv_y, from_a, from_b, term_there, dl_y
    )
    normed1_there = swap(term_there, "c")
    kv_x, kv_y = corner_rows(kv_x, kv_y, from_a, from_b)
    got_kx, got_ky, got_ly = swap(kv_x, "x"), swap(kv_y, "y"), swap(dl_y, "y")
    o_near, w_near = o_0 + got_ox + got_oy, w_0 + got_wx + got_wy
    ow_near = jnp.concatenate(
        [o_near.reshape(4, q_in, width), w_near.reshape(4, q_in, width)], axis=1
    ).reshape(8 * q_in, width)
    ow_sum = scatter_z(ow_near)
    term_own = to_model(
        [q_grad[0], kv_grad[0]], [[q_w], [kv_w]], same, 0, rows, [kv_x, kv_y, ow_near]
    )
    kv_0, got_kx, got_ky, got_ly, term_own = sync(kv_0, got_kx, got_ky, got_ly, term_own)
    kv_near = kv_0 + got_kx + got_ky
    kv_sum = scatter_z(
        kv_near.reshape(2, 4, k_in, width).swapaxes(0, 1).reshape(8 * k_in, width)
    )
    tokens_grad, gain1_sum = norm_return(
        tokens, resid_first, term_own, normed1_there, norm1_gain, (f32,), [kv_near]
    )
    gain1_part = gain1_sum[0]
    gain2_part = gain2_sum[0]
    gains = jnp.concatenate([gain1_part, gain2_part, q_gains[0], k_gains[0]])[None, :]
    gains = gains + swap(gains, "c")
    gains_xy = lax.ppermute(gains, ("x", "y"), [(i, i ^ 3) for i in range(4)])
    gains_x, gains_y = swap(gains, "x"), swap(gains, "y")
    gains = (gains + gains_x) + (gains_y + gains_xy)
    gains, mixed_own, ow_sum = sync(gains, mixed_own, ow_sum)
    gains_z = [lax.ppermute(gains, "z", [(i, i ^ k) for i in range(4)]) for k in (1, 2, 3)]
    output = (
        valid * (resid.astype(f32) + mixed_own.astype(f32) + mixed_there.astype(f32))
    ).astype(bf16)
    gains, output, kv_sum, *gains_z = sync(gains, output, kv_sum, *gains_z)
    o_sum, w_sum = ow_sum[:q_in], ow_sum[q_in:]
    gains = ((gains + gains_z[0]) + (gains_z[1] + gains_z[2]))[0]
    dlo_sum = dl_0 + got_lx + got_ly

    gate_sum, up_sum, down_sum = (
        jnp.concatenate(pair, axis=0)
        for pair in ((glo_sum, ghi_sum), (ulo_sum, uhi_sum), (dlo_sum, dhi_sum))
    )
    gate_sum, up_sum, down_sum = from_core(
        [(a[:, :eighth], a[:, eighth:]) for a in (gate_sum, up_sum, down_sum)], core
    )
    return (
        output,
        tokens_grad,
        gains[:width],
        w_sum.astype(f32).T,
        kv_sum[:k_in].astype(f32).T,
        kv_sum[k_in:].astype(f32).T,
        gains[2 * width : 2 * width + HEAD_SIZE],
        gains[2 * width + HEAD_SIZE :],
        o_sum.astype(f32),
        gains[width : 2 * width],
        gate_sum.astype(f32).T,
        up_sum.astype(f32).T,
        down_sum.astype(f32),
    )


def chip_solution(mesh):
    fine = Mesh(mesh.devices.reshape(2, 2, 2, 4), ("x", "c", "y", "z"))
    row_spec = P(("x", "c", "y", "z"), None)
    group_spec = P(("x", "c", "z"), None)
    head_cols = P(None, ("y", "x", "c", "z"))
    head_rows = P(("y", "x", "c", "z"), None)
    up_spec, down_spec = P(("x", "c", "y"), "z"), P("z", ("x", "c", "y"))
    return jax.shard_map(
        chip_layer,
        mesh=fine,
        in_specs=(
            row_spec,
            row_spec,
            group_spec,
            group_spec,
            P(),
            head_cols,
            head_cols,
            head_cols,
            P(),
            P(),
            head_rows,
            P(),
            up_spec,
            up_spec,
            down_spec,
        ),
        out_specs=(
            row_spec,
            row_spec,
            P(),
            head_cols,
            head_cols,
            head_cols,
            P(),
            P(),
            head_rows,
            P(),
            up_spec,
            up_spec,
            down_spec,
        ),
        check_vma=False,
    )


def solution(mesh):
    sizes = dict(mesh.shape)
    if sizes == {"fsdp": 4, "heads": 2, "tensor": 4}:
        return chip_solution(mesh)
    return plain_solution(mesh)
```

```python
import functools
import math

import jax
import jax.numpy as jnp
from jax import lax
from jax.experimental import pallas as pl
from jax.experimental.pallas import tpu as pltpu
from jax.sharding import Mesh
from jax.sharding import PartitionSpec as P

QUERY_HEADS = 16
KEY_VALUE_HEADS = 8
HEAD_SIZE = 128
BLK = 128


EPS_NORM = 1e-06
ROPE_BASE = 1000000.0
NEG_FILL = -1e30


def row_info(lengths, positions):
    block_count = (lengths + BLK - 1) // BLK
    ends = jnp.cumsum(block_count)
    starts = ends - block_count
    used = ends[-1]
    column = positions[:, None]
    inside = (column >= starts[None, :]) & (column < ends[None, :])
    past = positions >= used
    seq_block = jnp.sum((column >= ends[None, :]).astype(jnp.int32), axis=1)
    first_block = jnp.sum(jnp.where(inside, starts[None, :], 0), axis=1) + jnp.where(past, used, 0)
    limit = jnp.sum(jnp.where(inside, lengths[None, :], 0), axis=1)
    offsets = jnp.arange(BLK, dtype=jnp.int32)[None, :]
    pos_rows = (positions - first_block)[:, None] * BLK + offsets
    seq_rows = jnp.broadcast_to(seq_block[:, None], pos_rows.shape)
    valid_rows = jnp.logical_not(past)[:, None] & (pos_rows < limit[:, None])
    return (seq_rows.reshape(-1), pos_rows.reshape(-1), valid_rows.reshape(-1))


def rope_tables(pos_rows):
    half_dim = HEAD_SIZE // 2
    freq = jnp.exp(
        jnp.arange(half_dim, dtype=jnp.float32) * (-2.0 * math.log(ROPE_BASE) / HEAD_SIZE)
    )
    angles = pos_rows.astype(jnp.float32)[:, None] * freq[None, :]
    return (jnp.cos(angles)[:, None, :], jnp.sin(angles)[:, None, :])


def rotate(value_rows, cos_tab, sin_tab):
    half_dim = value_rows.shape[-1] // 2
    first_half, second_half = (value_rows[..., :half_dim], value_rows[..., half_dim:])
    return jnp.concatenate(
        [
            first_half * cos_tab - second_half * sin_tab,
            second_half * cos_tab + first_half * sin_tab,
        ],
        axis=-1,
    )


def unrotate(upstream, cos_tab, sin_tab):
    half_dim = upstream.shape[-1] // 2
    first_half, second_half = (upstream[..., :half_dim], upstream[..., half_dim:])
    return jnp.concatenate(
        [
            first_half * cos_tab + second_half * sin_tab,
            second_half * cos_tab - first_half * sin_tab,
        ],
        axis=-1,
    )


def rms_parts(value_rows, gain_vec):
    scales = lax.rsqrt(jnp.mean(value_rows * value_rows, axis=-1, keepdims=True) + EPS_NORM)
    return (value_rows * scales * gain_vec, scales)


def norm_back(value_rows, scales, gain_vec, upstream):
    weighted = upstream * gain_vec
    inner = jnp.sum(value_rows * weighted, axis=-1, keepdims=True) / value_rows.shape[-1]
    return scales * weighted - value_rows * scales * scales * scales * inner


def matrix_product(left, right):
    return jnp.dot(left, right, preferred_element_type=jnp.float32)


def dot_rows(left, right):
    return lax.dot_general(
        left, right, (((0,), (0,)), ((), ())), preferred_element_type=jnp.float32
    )


def dot_cols(left, right):
    return lax.dot_general(
        left, right, (((1,), (1,)), ((), ())), preferred_element_type=jnp.float32
    )


def swap_cols(array, outer, inner):
    lead = array.shape[0]
    return jnp.swapaxes(array.reshape(lead, outer, inner, -1), 1, 2).reshape(lead, -1)


def swap_rows(array, outer, inner):
    width = array.shape[1]
    return jnp.swapaxes(array.reshape(outer, inner, -1, width), 0, 1).reshape(-1, width)


def spread_rows(local_rows):
    return lax.all_gather(local_rows, "tensor", axis=0, tiled=True)


def to_heads(packed):
    return lax.all_to_all(packed, "heads", split_axis=1, concat_axis=0, tiled=True)


def to_rows(packed):
    return lax.all_to_all(packed, "heads", split_axis=0, concat_axis=1, tiled=True)


def tensor_sum(term, row_count):
    total = lax.psum(
        term(0, row_count * lax.axis_size("tensor")).astype(jnp.bfloat16), "tensor"
    ).astype(jnp.float32)
    return lax.dynamic_slice_in_dim(total, lax.axis_index("tensor") * row_count, row_count)


def block_scores(query_blk, key_all, seq_blk, pos_blk, seq_all, pos_all):
    scores = jnp.einsum(
        "qkgd,pkd->kgqp", query_blk, key_all, preferred_element_type=jnp.float32
    ) * HEAD_SIZE ** (-0.5)
    allowed = (seq_blk[:, None] == seq_all[None, :]) & (pos_all[None, :] <= pos_blk[:, None])
    return jnp.where(allowed[None, None], scores, NEG_FILL)


def attend_forward(query_grp, key_grp, value_grp, seq_all, pos_all):
    group_factor = QUERY_HEADS // KEY_VALUE_HEADS
    group_len = query_grp.shape[0]
    kv_local = key_grp.shape[1] // HEAD_SIZE
    query_four = query_grp.reshape(group_len, kv_local, group_factor, HEAD_SIZE)
    key_three = key_grp.reshape(group_len, kv_local, HEAD_SIZE)
    value_three = value_grp.reshape(group_len, kv_local, HEAD_SIZE)
    block_rows = min(512, group_len)

    def forward_block(block_idx):
        first_row = block_idx * block_rows
        query_blk = lax.dynamic_slice_in_dim(query_four, first_row, block_rows)
        seq_blk = lax.dynamic_slice_in_dim(seq_all, first_row, block_rows)
        pos_blk = lax.dynamic_slice_in_dim(pos_all, first_row, block_rows)
        scores = block_scores(query_blk, key_three, seq_blk, pos_blk, seq_all, pos_all)
        peak = jnp.max(scores, axis=-1, keepdims=True)
        expo = jnp.exp(scores - peak)
        total = jnp.sum(expo, axis=-1, keepdims=True)
        probs_b = (expo / total).astype(jnp.bfloat16)
        attended = jnp.einsum(
            "kgqp,pkd->qkgd", probs_b, value_three, preferred_element_type=jnp.float32
        )
        return (attended, (peak + jnp.log(total))[..., 0])

    attended, log_sums = lax.map(forward_block, jnp.arange(group_len // block_rows))
    return (
        attended.reshape(group_len, kv_local * group_factor * HEAD_SIZE).astype(jnp.bfloat16),
        log_sums,
    )


def attend_backward(query_grp, key_grp, value_grp, grad_grp, log_sums, seq_all, pos_all):
    group_factor = QUERY_HEADS // KEY_VALUE_HEADS
    scale = HEAD_SIZE ** (-0.5)
    group_len = query_grp.shape[0]
    kv_local = key_grp.shape[1] // HEAD_SIZE
    query_four = query_grp.reshape(group_len, kv_local, group_factor, HEAD_SIZE)
    key_three = key_grp.reshape(group_len, kv_local, HEAD_SIZE)
    value_three = value_grp.reshape(group_len, kv_local, HEAD_SIZE)
    grad_four = grad_grp.reshape(group_len, kv_local, group_factor, HEAD_SIZE)
    block_rows = min(512, group_len)

    def backward_block(carry, block_idx):
        key_acc, value_acc = carry
        first_row = block_idx * block_rows
        query_blk = lax.dynamic_slice_in_dim(query_four, first_row, block_rows)
        grad_blk = lax.dynamic_slice_in_dim(grad_four, first_row, block_rows)
        seq_blk = lax.dynamic_slice_in_dim(seq_all, first_row, block_rows)
        pos_blk = lax.dynamic_slice_in_dim(pos_all, first_row, block_rows)
        scores = block_scores(query_blk, key_three, seq_blk, pos_blk, seq_all, pos_all)
        probs = jnp.exp(scores - log_sums[block_idx][..., None])
        probs_b = probs.astype(jnp.bfloat16)
        prob_grad = jnp.einsum(
            "qkgd,pkd->kgqp", grad_blk, value_three, preferred_element_type=jnp.float32
        )
        score_grad_b = (
            probs * (prob_grad - jnp.sum(probs * prob_grad, axis=-1, keepdims=True))
        ).astype(jnp.bfloat16)
        query_grad = (
            jnp.einsum(
                "kgqp,pkd->qkgd", score_grad_b, key_three, preferred_element_type=jnp.float32
            )
            * scale
        )
        key_acc = (
            key_acc
            + jnp.einsum(
                "kgqp,qkgd->pkd", score_grad_b, query_blk, preferred_element_type=jnp.float32
            )
            * scale
        )
        value_acc = value_acc + jnp.einsum(
            "kgqp,qkgd->pkd", probs_b, grad_blk, preferred_element_type=jnp.float32
        )
        return ((key_acc, value_acc), query_grad)

    empty = jnp.zeros((group_len, kv_local, HEAD_SIZE), jnp.float32)
    (key_acc, value_acc), query_blocks = lax.scan(
        backward_block, (empty, empty), jnp.arange(group_len // block_rows)
    )
    query_grad_b = query_blocks.reshape(group_len, kv_local * group_factor * HEAD_SIZE).astype(
        jnp.bfloat16
    )
    key_grad_b = key_acc.reshape(group_len, kv_local * HEAD_SIZE).astype(jnp.bfloat16)
    value_grad_b = value_acc.reshape(group_len, kv_local * HEAD_SIZE).astype(jnp.bfloat16)
    return (query_grad_b, key_grad_b, value_grad_b)


def project_heads(normed_b, query_w, key_w, value_w, query_gain, key_gain, pos_rows):
    lines = normed_b.shape[0]
    q_raw = matrix_product(normed_b, query_w).reshape(lines, -1, HEAD_SIZE)
    key_unnormed = matrix_product(normed_b, key_w).reshape(lines, -1, HEAD_SIZE)
    value_b = matrix_product(normed_b, value_w).astype(jnp.bfloat16)
    cos_tab, sin_tab = rope_tables(pos_rows)
    q_normed, q_scale = rms_parts(q_raw, query_gain)
    k_normed, k_scale = rms_parts(key_unnormed, key_gain)
    query_b = rotate(q_normed, cos_tab, sin_tab).astype(jnp.bfloat16).reshape(lines, -1)
    key_b = rotate(k_normed, cos_tab, sin_tab).astype(jnp.bfloat16).reshape(lines, -1)
    return (query_b, key_b, value_b, (q_raw, q_scale, key_unnormed, k_scale, cos_tab, sin_tab))


def heads_back(query_back, key_back, kept, query_gain, key_gain):
    q_raw, q_scale, key_unnormed, k_scale, cos_tab, sin_tab = kept
    lines = q_raw.shape[0]
    q_turned = unrotate(query_back.astype(jnp.float32).reshape(q_raw.shape), cos_tab, sin_tab)
    k_turned = unrotate(key_back.astype(jnp.float32).reshape(key_unnormed.shape), cos_tab, sin_tab)
    q_raw_grad = (
        norm_back(q_raw, q_scale, query_gain, q_turned).reshape(lines, -1).astype(jnp.bfloat16)
    )
    k_raw_grad = (
        norm_back(key_unnormed, k_scale, key_gain, k_turned).reshape(lines, -1).astype(jnp.bfloat16)
    )
    qgain_part = jnp.sum(q_turned * q_raw * q_scale, axis=(0, 1))
    kgain_part = jnp.sum(k_turned * key_unnormed * k_scale, axis=(0, 1))
    return (q_raw_grad, k_raw_grad, qgain_part, kgain_part)


def plain_layer(
    tokens,
    cotangent,
    seq_lens,
    block_pos,
    norm1_gain,
    w_query,
    key_matrix,
    value_matrix,
    query_gain,
    key_gain,
    w_out,
    norm2_gain,
    w_gate,
    w_up,
    w_down,
):
    row_count = tokens.shape[0]
    fsdp_count = lax.axis_size("fsdp")
    heads_count = lax.axis_size("heads")
    gate_full, up_full, down_full = (
        lax.all_gather(w_gate, ("fsdp", "heads"), axis=0, tiled=True),
        lax.all_gather(w_up, ("fsdp", "heads"), axis=0, tiled=True),
        lax.all_gather(w_down, ("fsdp", "heads"), axis=1, tiled=True),
    )
    seq_all, pos_all, valid_all = row_info(seq_lens[0], block_pos[0])
    own_first = lax.axis_index("heads") * row_count
    pos_own = lax.dynamic_slice_in_dim(pos_all, own_first, row_count)
    valid_own = lax.dynamic_slice_in_dim(valid_all, own_first, row_count).astype(jnp.float32)[
        :, None
    ]
    inputs = tokens.astype(jnp.float32)
    first_normed, scale1 = rms_parts(inputs, norm1_gain)
    normed1_b = first_normed.astype(jnp.bfloat16)
    query_all, key_all, value_all, out_all = (
        lax.all_gather(w_query, ("fsdp", "heads", "tensor"), axis=1, tiled=True),
        lax.all_gather(key_matrix, ("fsdp", "heads", "tensor"), axis=1, tiled=True),
        lax.all_gather(value_matrix, ("fsdp", "heads", "tensor"), axis=1, tiled=True),
        lax.all_gather(w_out, ("fsdp", "heads", "tensor"), axis=0, tiled=True),
    )
    query_full = swap_cols(query_all, fsdp_count, heads_count)
    key_full = swap_cols(key_all, fsdp_count, heads_count)
    value_full = swap_cols(value_all, fsdp_count, heads_count)
    out_full = swap_rows(out_all, fsdp_count, heads_count)
    query_b, key_b, value_b, kept = project_heads(
        normed1_b, query_full, key_full, value_full, query_gain, key_gain, pos_own
    )
    q_width = query_b.shape[1] // heads_count
    k_width = key_b.shape[1] // heads_count
    packed = jnp.concatenate(
        [
            query_b.reshape(row_count, heads_count, q_width),
            key_b.reshape(row_count, heads_count, k_width),
            value_b.reshape(row_count, heads_count, k_width),
        ],
        axis=2,
    )
    grouped = to_heads(packed.reshape(row_count, -1))
    query_grp = grouped[:, :q_width]
    key_grp = grouped[:, q_width : q_width + k_width]
    value_grp = grouped[:, q_width + k_width :]
    attended_b, log_sums = attend_forward(query_grp, key_grp, value_grp, seq_all, pos_all)
    attn_tok = to_rows(attended_b)
    resid = inputs + matrix_product(attn_tok, out_full)
    normed2, scale2 = rms_parts(resid, norm2_gain)
    normed2_b = normed2.astype(jnp.bfloat16)
    wide_in = spread_rows(normed2_b)
    gate_pre = matrix_product(wide_in, gate_full)
    up_pre = matrix_product(wide_in, up_full)
    sigmoid_gate = jax.nn.sigmoid(gate_pre)
    silu_gate = gate_pre * sigmoid_gate
    act_b = (silu_gate * up_pre).astype(jnp.bfloat16)

    def forward_term(first_row, span):
        return matrix_product(act_b, down_full)

    mixed = tensor_sum(forward_term, row_count)
    output = (valid_own * (resid + mixed)).astype(jnp.bfloat16)
    grad_out = valid_own * cotangent.astype(jnp.float32)
    wide_grad = spread_rows(grad_out.astype(jnp.bfloat16))
    act_grad = dot_cols(wide_grad, down_full)
    down_grad = dot_rows(act_b, wide_grad)
    gate_grad_b = (
        act_grad * up_pre * sigmoid_gate * (1.0 + gate_pre * (1.0 - sigmoid_gate))
    ).astype(jnp.bfloat16)
    up_grad_b = (act_grad * silu_gate).astype(jnp.bfloat16)
    gate_wgrad = dot_rows(wide_in, gate_grad_b)
    up_wgrad = dot_rows(wide_in, up_grad_b)

    def backward_term(first_row, span):
        return dot_cols(gate_grad_b, gate_full) + dot_cols(up_grad_b, up_full)

    normed2_grad = tensor_sum(backward_term, row_count)
    gate_sum, up_sum, down_sum = (
        lax.psum_scatter(
            gate_wgrad.astype(jnp.bfloat16), ("fsdp", "heads"), scatter_dimension=0, tiled=True
        ).astype(jnp.float32),
        lax.psum_scatter(
            up_wgrad.astype(jnp.bfloat16), ("fsdp", "heads"), scatter_dimension=0, tiled=True
        ).astype(jnp.float32),
        lax.psum_scatter(
            down_grad.astype(jnp.bfloat16), ("fsdp", "heads"), scatter_dimension=1, tiled=True
        ).astype(jnp.float32),
    )
    resid_grad = grad_out + norm_back(resid, scale2, norm2_gain, normed2_grad)
    gain2_part = jnp.sum(normed2_grad * resid * scale2, axis=0)
    resid_grad_b = resid_grad.astype(jnp.bfloat16)
    out_wgrad = dot_rows(attn_tok, resid_grad_b)
    attn_grad_b = dot_cols(resid_grad_b, out_full).astype(jnp.bfloat16)
    attn_grad_grp = to_heads(attn_grad_b)
    query_grad_b, key_grad_b, value_grad_b = attend_backward(
        query_grp, key_grp, value_grp, attn_grad_grp, log_sums, seq_all, pos_all
    )
    back_packed = to_rows(jnp.concatenate([query_grad_b, key_grad_b, value_grad_b], axis=1))
    back_three = back_packed.reshape(row_count, heads_count, -1)
    query_back = back_three[:, :, :q_width].reshape(row_count, -1)
    key_back = back_three[:, :, q_width : q_width + k_width].reshape(row_count, -1)
    value_back = back_three[:, :, q_width + k_width :].reshape(row_count, -1)
    q_raw_grad, k_raw_grad, qgain_part, kgain_part = heads_back(
        query_back, key_back, kept, query_gain, key_gain
    )
    query_wgrad = swap_cols(dot_rows(normed1_b, q_raw_grad), heads_count, fsdp_count)
    key_wgrad = swap_cols(dot_rows(normed1_b, k_raw_grad), heads_count, fsdp_count)
    value_wgrad = swap_cols(dot_rows(normed1_b, value_back), heads_count, fsdp_count)
    out_wgrad = swap_rows(out_wgrad, heads_count, fsdp_count)
    normed1_grad = (
        dot_cols(q_raw_grad, query_full)
        + dot_cols(k_raw_grad, key_full)
        + dot_cols(value_back, value_full)
    )
    query_sum, key_sum, value_sum, out_sum = (
        lax.psum_scatter(query_wgrad, ("fsdp", "heads", "tensor"), scatter_dimension=1, tiled=True),
        lax.psum_scatter(key_wgrad, ("fsdp", "heads", "tensor"), scatter_dimension=1, tiled=True),
        lax.psum_scatter(value_wgrad, ("fsdp", "heads", "tensor"), scatter_dimension=1, tiled=True),
        lax.psum_scatter(out_wgrad, ("fsdp", "heads", "tensor"), scatter_dimension=0, tiled=True),
    )
    tokens_grad = resid_grad + norm_back(inputs, scale1, norm1_gain, normed1_grad)
    gain1_part = jnp.sum(normed1_grad * inputs * scale1, axis=0)
    gain1_sum, qgain_sum, kgain_sum, gain2_sum = lax.psum(
        (gain1_part, qgain_part, kgain_part, gain2_part), ("fsdp", "heads", "tensor")
    )
    return (
        output,
        tokens_grad,
        gain1_sum,
        query_sum,
        key_sum,
        value_sum,
        qgain_sum,
        kgain_sum,
        out_sum,
        gain2_sum,
        gate_sum,
        up_sum,
        down_sum,
    )


def plain_solution(mesh):
    return jax.shard_map(
        plain_layer,
        mesh=mesh,
        in_specs=(
            P(("fsdp", "heads", "tensor"), None),
            P(("fsdp", "heads", "tensor"), None),
            P(("fsdp", "tensor"), None),
            P(("fsdp", "tensor"), None),
            P(),
            P(None, ("heads", "fsdp", "tensor")),
            P(None, ("heads", "fsdp", "tensor")),
            P(None, ("heads", "fsdp", "tensor")),
            P(),
            P(),
            P(("heads", "fsdp", "tensor"), None),
            P(),
            P(("fsdp", "heads"), "tensor"),
            P(("fsdp", "heads"), "tensor"),
            P("tensor", ("fsdp", "heads")),
        ),
        out_specs=(
            P(("fsdp", "heads", "tensor"), None),
            P(("fsdp", "heads", "tensor"), None),
            P(),
            P(None, ("heads", "fsdp", "tensor")),
            P(None, ("heads", "fsdp", "tensor")),
            P(None, ("heads", "fsdp", "tensor")),
            P(),
            P(),
            P(("heads", "fsdp", "tensor"), None),
            P(),
            P(("fsdp", "heads"), "tensor"),
            P(("fsdp", "heads"), "tensor"),
            P("tensor", ("fsdp", "heads")),
        ),
        check_vma=False,
    )


VMEM_LIMIT = 56 * 1024 * 1024
LOG2_E = 1.4426950408889634
SWAP = ((0, 1), (1, 0))
ROW_TILE = 1024
SCALE = HEAD_SIZE ** (-0.5)


def dot_t(left, right):
    return lax.dot_general(
        left, right, (((1,), (1,)), ((), ())), preferred_element_type=jnp.float32
    )


def swap(array, axis):
    return lax.ppermute(array, axis, SWAP)


def pick(first, second, index):
    return jnp.where(index == 0, first, second)


def join(mine, other, index, axis):
    return pick(
        jnp.concatenate([mine, other], axis=axis),
        jnp.concatenate([other, mine], axis=axis),
        index,
    )


def gather_z(array):
    return lax.all_gather(array, "z", axis=0, tiled=True)


def scatter_z(array):
    return lax.psum_scatter(array, "z", scatter_dimension=0, tiled=True)


def after(array, *done):
    return lax.optimization_barrier((array, *done))[0]


def sync(*arrays):
    return lax.optimization_barrier(arrays)


def to_core(array, core):
    half = array.shape[0] // 2
    first, second = array[:half], array[half:]
    other = swap(pick(second, first, core), "c")
    mine = pick(first, second, core)
    return join(mine, other, core, 1)


def from_core(pairs, core):
    mine = [pick(a, b, core) for a, b in pairs]
    send = jnp.concatenate([pick(b, a, core) for a, b in pairs], axis=0)
    others = jnp.split(swap(send, "c"), len(pairs))
    return [join(m, o, core, 0) for m, o in zip(mine, others)]


def call(kernel, inputs, in_specs, out_specs, out_shape, grid, after=(), prefetch=None, **more):
    lead = 0 if prefetch is None else 1
    count, extra = lead + len(inputs), len(after)

    def body(*refs):
        kernel(*refs[:count], *refs[count + extra :])

    if prefetch is not None:
        prefetched, inputs = [prefetch], list(inputs)
    else:
        prefetched, inputs = [], list(inputs)
    scratch = more.pop("scratch_shapes", ())
    return pl.pallas_call(
        body,
        grid_spec=pltpu.PrefetchScalarGridSpec(
            num_scalar_prefetch=lead,
            grid=grid,
            in_specs=list(in_specs) + [pl.BlockSpec(memory_space=pl.ANY)] * extra,
            out_specs=out_specs,
            scratch_shapes=scratch,
        ),
        out_shape=out_shape,
        compiler_params=pltpu.CompilerParams(vmem_limit_bytes=VMEM_LIMIT),
        cost_estimate=pl.CostEstimate(flops=1000, bytes_accessed=1000, transcendentals=0),
        **more,
    )(*prefetched, *inputs, *after)


def reorder_kernel(order_ref, in_ref, out_ref):
    out_ref[...] = in_ref[...]


def reorder(array, order, after=()):
    rows, width = array.shape
    parts = order.shape[0]
    return call(
        reorder_kernel,
        [array],
        [pl.BlockSpec((rows, width // parts), lambda i, o: (0, o[i]))],
        pl.BlockSpec((rows, width // parts), lambda i, o: (0, i)),
        jax.ShapeDtypeStruct(array.shape, array.dtype),
        (parts,),
        after,
        order,
        name="reorder",
    )


def lane_mean(value):
    ones = jnp.full((2 * HEAD_SIZE, HEAD_SIZE), 1.0 / HEAD_SIZE, jnp.bfloat16)
    high = value.astype(jnp.bfloat16)
    low = (value - high.astype(jnp.float32)).astype(jnp.bfloat16)
    return matrix_product(jnp.concatenate([high, low], axis=1), ones)


HEADS_STEP = 4


def heads_kernel(count, raw_ref, cos_ref, sin_ref, gain_ref, out_ref):
    for first in range(0, raw_ref.shape[1], count * HEAD_SIZE):
        lanes = slice(first, first + HEAD_SIZE)
        raw = raw_ref[:, lanes]
        value = raw * lax.rsqrt(lane_mean(raw * raw) + EPS_NORM) * gain_ref[...]
        out_ref[:, lanes] = (
            value * cos_ref[...] + pltpu.roll(value, HEAD_SIZE // 2, 1) * sin_ref[...]
        ).astype(jnp.bfloat16)
        if count == 2:
            lanes = slice(first + HEAD_SIZE, first + 2 * HEAD_SIZE)
            out_ref[:, lanes] = raw_ref[:, lanes].astype(jnp.bfloat16)


def make_heads(group, raw, cos_tab, sin_tab, gain, count, after=()):
    rows, width = raw.shape
    skip = group * (rows // ROW_TILE)
    table = pl.BlockSpec((ROW_TILE, HEAD_SIZE), lambda i, r: (i + skip, 0))
    one = pl.BlockSpec((ROW_TILE, HEADS_STEP * HEAD_SIZE), lambda i, r: (i, r))
    return call(
        functools.partial(heads_kernel, count),
        [raw, cos_tab, sin_tab, gain[None, :]],
        [one, table, table, pl.BlockSpec((1, HEAD_SIZE), lambda i, r: (0, 0))],
        one,
        jax.ShapeDtypeStruct((rows, width), jnp.bfloat16),
        (rows // ROW_TILE, width // (HEADS_STEP * HEAD_SIZE)),
        after,
        name="make_heads",
    )


def heads_back_kernel(count, raw_ref, cos_ref, sin_ref, gain_ref, *rest):
    *up_refs, out_ref, sum_ref = rest

    @pl.when((pl.program_id(0) == 0) & (pl.program_id(1) == 0))
    def _():
        sum_ref[...] = jnp.zeros_like(sum_ref)

    total = jnp.zeros((1, HEAD_SIZE), jnp.float32)
    for first in range(0, raw_ref.shape[1], count * HEAD_SIZE):
        lanes = slice(first, first + HEAD_SIZE)
        raw = raw_ref[:, lanes]
        upstream = up_refs[0][:, lanes].astype(jnp.float32)
        for ref in up_refs[1:]:
            upstream = upstream + ref[:, lanes].astype(jnp.float32)
        turned = upstream * cos_ref[...] - pltpu.roll(upstream, HEAD_SIZE // 2, 1) * sin_ref[...]
        scale = lax.rsqrt(lane_mean(raw * raw) + EPS_NORM)
        hat = raw * scale
        weighted = turned * gain_ref[...]
        out_ref[:, lanes] = (scale * (weighted - hat * lane_mean(hat * weighted))).astype(
            jnp.bfloat16
        )
        total = total + jnp.sum(turned * hat, axis=0, keepdims=True)
        if count == 2:
            lanes = slice(first + HEAD_SIZE, first + 2 * HEAD_SIZE)
            value_up = up_refs[0][:, lanes].astype(jnp.float32)
            for ref in up_refs[1:]:
                value_up = value_up + ref[:, lanes].astype(jnp.float32)
            out_ref[:, lanes] = value_up.astype(jnp.bfloat16)
    sum_ref[0:1, :] += total


def heads_return(group, raw, upstream, far, cos_tab, sin_tab, gain, count, after=()):
    rows, width = raw.shape
    skip = group * (rows // ROW_TILE)
    span = HEADS_STEP * HEAD_SIZE
    table = pl.BlockSpec((ROW_TILE, HEAD_SIZE), lambda i, r: (i + skip, 0))
    one = pl.BlockSpec((ROW_TILE, span), lambda i, r: (i, r))
    across = pl.BlockSpec((ROW_TILE, span), lambda i, r: (i, (r + 1) % 2))
    return call(
        functools.partial(heads_back_kernel, count),
        [raw, cos_tab, sin_tab, gain[None, :], upstream] + far,
        [one, table, table, pl.BlockSpec((1, HEAD_SIZE), lambda i, r: (0, 0)), one]
        + [across] * len(far),
        [one, pl.BlockSpec((8, HEAD_SIZE), lambda i, r: (0, 0))],
        [
            jax.ShapeDtypeStruct((rows, width), jnp.bfloat16),
            jax.ShapeDtypeStruct((8, HEAD_SIZE), jnp.float32),
        ],
        (rows // ROW_TILE, width // span),
        after,
        name="heads_return",
    )


GROUP_WIDTH = 2 * HEAD_SIZE
TOGETHER = 2


def stack_heads(block):
    return jnp.concatenate([block[:, :HEAD_SIZE], block[:, HEAD_SIZE:]], axis=0)


def key_bias(first_key, pair, parity, queries=0):
    shape = (1, 2 * BLK) if queries == 0 else (2 * BLK, 1)
    cols = lax.broadcasted_iota(jnp.int32, shape, 1 - queries)
    block = 2 * pair + jnp.where(cols < BLK, parity, 1 - parity)
    return jnp.where(block >= first_key, 0.0, NEG_FILL)


def last_bias(first_key, pair, parity, queries=0):
    rows = lax.broadcasted_iota(jnp.int32, (2 * BLK, 2 * BLK), queries)
    cols = lax.broadcasted_iota(jnp.int32, (2 * BLK, 2 * BLK), 1 - queries)
    far = (parity == 1) & (2 * pair >= first_key)
    own = lax.rem(cols, BLK) <= lax.rem(rows, BLK)
    far_bias = jnp.where(far, 0.0, NEG_FILL)
    return jnp.where(cols < BLK, jnp.where(own, 0.0, NEG_FILL), far_bias)


def pair_of(own_ref, far_ref, m, first):
    at = pl.ds(pl.multiple_of(m * BLK, BLK), BLK)
    lanes = slice(first, first + HEAD_SIZE)
    return jnp.concatenate([own_ref[at, lanes], far_ref[at, lanes]], axis=0)


def head_lanes(head):
    return slice(head * GROUP_WIDTH, (head + 1) * GROUP_WIDTH)


def attend_kernel(group, info_ref, q_ref, own_ref, far_ref, o_ref, l_ref):
    blocks = q_ref.shape[0] // BLK
    parity = info_ref[group, blocks]

    def one_block(j, _):
        first_key = info_ref[group, j]
        rows = pl.ds(pl.multiple_of(j * BLK, BLK), BLK)
        queries = [stack_heads(q_ref[rows, head_lanes(h)]) for h in range(TOGETHER)]

        def step(m, bias, carry):
            out = []
            for h in range(TOGETHER):
                total, acc = carry[h]
                score = dot_t(queries[h], pair_of(own_ref, far_ref, m, h * GROUP_WIDTH))
                expo = jnp.exp2(score * (SCALE * LOG2_E) + bias)
                total = total + jnp.sum(expo, axis=1, keepdims=True)
                value = pair_of(own_ref, far_ref, m, h * GROUP_WIDTH + HEAD_SIZE)
                acc = acc + matrix_product(expo.astype(jnp.bfloat16), value)
                out.append((total, acc))
            return tuple(out)

        empty = (
            jnp.zeros((2 * BLK, 1), jnp.float32),
            jnp.zeros((2 * BLK, HEAD_SIZE), jnp.float32),
        )
        carry = step(j, last_bias(first_key, j, parity), (empty,) * TOGETHER)
        carry = lax.fori_loop(
            lax.div(first_key, 2),
            j,
            lambda m, c: step(m, key_bias(first_key, m, parity), c),
            carry,
        )
        lane = lax.broadcasted_iota(jnp.int32, (BLK, HEAD_SIZE), 1)
        for h, (total, acc) in enumerate(carry):
            out = (acc / total).astype(jnp.bfloat16)
            o_ref[rows, head_lanes(h)] = jnp.concatenate([out[:BLK], out[BLK:]], axis=1)
            l_ref[rows, h * HEAD_SIZE : (h + 1) * HEAD_SIZE] = jnp.where(
                lane == 0, total[:BLK], total[BLK:]
            )
        return 0

    lax.fori_loop(0, blocks, one_block, 0)


def attend(group, info, query, own, far, after=()):
    rows, width = query.shape
    span = TOGETHER * GROUP_WIDTH
    here = pl.BlockSpec((rows, span), lambda r, s: (0, r))
    there = pl.BlockSpec((rows, span), lambda r, s: (0, (r + 1) % 2))
    return call(
        functools.partial(attend_kernel, group),
        [query, own, far],
        [here, here, there],
        [here, pl.BlockSpec((rows, span // 2), lambda r, s: (0, r))],
        [
            jax.ShapeDtypeStruct((rows, width), jnp.bfloat16),
            jax.ShapeDtypeStruct((rows, width // 2), jnp.float32),
        ],
        (width // span,),
        after,
        info,
        name="attend",
    )


def row_sums(value):
    ones = jnp.ones((8, 2 * HEAD_SIZE), jnp.bfloat16)
    high = value.astype(jnp.bfloat16)
    low = (value - high.astype(jnp.float32)).astype(jnp.bfloat16)
    return dot_t(ones, jnp.concatenate([high, low], axis=1))[:1]


def attend_back_kernel(
    group,
    info_ref,
    q_ref,
    do_ref,
    o_ref,
    l_ref,
    own_ref,
    far_ref,
    dq_ref,
    down_ref,
    dfar_ref,
    kacc_ref,
    vacc_ref,
):
    blocks = q_ref.shape[0] // BLK
    parity = info_ref[group, blocks]
    kacc_ref[...] = jnp.zeros_like(kacc_ref)
    vacc_ref[...] = jnp.zeros_like(vacc_ref)

    def one_block(j, _):
        first_key = info_ref[group, j]
        rows = pl.ds(pl.multiple_of(j * BLK, BLK), BLK)
        held = []
        for h in range(TOGETHER):
            query = stack_heads(q_ref[rows, head_lanes(h)])
            attn = stack_heads(o_ref[rows, head_lanes(h)]).astype(jnp.float32)
            grad = stack_heads(do_ref[rows, head_lanes(h)]).astype(jnp.float32)
            at = h * HEAD_SIZE
            total = jnp.concatenate(
                [l_ref[rows, at : at + 1], l_ref[rows, at + 1 : at + 2]], axis=0
            )
            grad_b = (grad / total).astype(jnp.bfloat16)
            inner = row_sums(grad_b.astype(jnp.float32) * attn)
            held.append((query, grad_b, inner))

        def step(m, bias, carry):
            at = pl.ds(pl.multiple_of(m * BLK, BLK), BLK)
            out = []
            for h in range(TOGETHER):
                query, grad_b, inner = held[h]
                key = pair_of(own_ref, far_ref, m, h * GROUP_WIDTH)
                value = pair_of(own_ref, far_ref, m, h * GROUP_WIDTH + HEAD_SIZE)
                expo = jnp.exp2(dot_t(key, query) * (SCALE * LOG2_E) + bias)
                d_score = (expo * (dot_t(value, grad_b) - inner)).astype(jnp.bfloat16)
                d_key = matrix_product(d_score, query)
                d_value = matrix_product(expo.astype(jnp.bfloat16), grad_b)
                kacc_ref[h, 0, at, :] += d_key[:BLK]
                kacc_ref[h, 1, at, :] += d_key[BLK:]
                vacc_ref[h, 0, at, :] += d_value[:BLK]
                vacc_ref[h, 1, at, :] += d_value[BLK:]
                out.append(carry[h] + dot_rows(d_score, key))
            return tuple(out)

        empty = jnp.zeros((2 * BLK, HEAD_SIZE), jnp.float32)
        carry = step(j, last_bias(first_key, j, parity, 1), (empty,) * TOGETHER)
        carry = lax.fori_loop(
            lax.div(first_key, 2),
            j,
            lambda m, c: step(m, key_bias(first_key, m, parity, 1), c),
            carry,
        )
        for h, dq in enumerate(carry):
            dq = (dq * SCALE).astype(jnp.bfloat16)
            dq_ref[rows, head_lanes(h)] = jnp.concatenate([dq[:BLK], dq[BLK:]], axis=1)
        return 0

    lax.fori_loop(0, blocks, one_block, 0)
    for h in range(TOGETHER):
        for half, ref in enumerate((down_ref, dfar_ref)):
            first = h * GROUP_WIDTH
            ref[:, first : first + HEAD_SIZE] = (kacc_ref[h, half] * SCALE).astype(jnp.bfloat16)
            ref[:, first + HEAD_SIZE : first + GROUP_WIDTH] = vacc_ref[h, half].astype(
                jnp.bfloat16
            )


def attend_back(group, info, query, d_attn, attn, total, own, far, after=()):
    rows, width = query.shape
    span = TOGETHER * GROUP_WIDTH
    here = pl.BlockSpec((rows, span), lambda r, s: (0, r))
    there = pl.BlockSpec((rows, span), lambda r, s: (0, (r + 1) % 2))
    shape = jax.ShapeDtypeStruct((rows, width), jnp.bfloat16)
    return call(
        functools.partial(attend_back_kernel, group),
        [query, d_attn, attn, total, own, far],
        [here, here, here, pl.BlockSpec((rows, span // 2), lambda r, s: (0, r)), here, there],
        [here] * 3,
        [shape] * 3,
        (width // span,),
        after,
        info,
        scratch_shapes=[
            pltpu.VMEM((TOGETHER, 2, rows, HEAD_SIZE), jnp.float32),
            pltpu.VMEM((TOGETHER, 2, rows, HEAD_SIZE), jnp.float32),
        ],
        name="attend_back",
    )


HIDDEN_TILE = 512
ROW_STEP = 1024


def row_steps(*refs):
    for first_ref in range(len(refs)):
        for first in range(0, refs[first_ref].shape[0], ROW_STEP):
            begin = first_ref * refs[first_ref].shape[0] + first
            yield refs[first_ref][first : first + ROW_STEP, :], slice(begin, begin + ROW_STEP)


def joined(refs):
    return jnp.concatenate([ref[...] for ref in refs], axis=1)


def ffn_kernel(pieces, xa_ref, xb_ref, *refs):
    gate_w = joined(refs[:pieces]).T
    up_w, d_act_ref = refs[pieces][...].T, refs[pieces + 1]
    act_ref, gate_ref, up_ref = refs[pieces + 2 :]
    for x, rows in row_steps(xa_ref, xb_ref):
        gate = matrix_product(x, gate_w)
        upper = matrix_product(x, up_w)
        d_act = d_act_ref[rows, :].astype(jnp.float32)
        sig = 0.5 * jnp.tanh(0.5 * gate) + 0.5
        silu = gate * sig
        act_ref[rows, :] = (silu * upper).astype(jnp.bfloat16)
        gate_ref[rows, :] = (d_act * upper * (sig + silu * (1.0 - sig))).astype(jnp.bfloat16)
        up_ref[rows, :] = (d_act * silu).astype(jnp.bfloat16)


def ffn(xs, gates, up, d_act, after=()):
    rows, width = xs[0].shape
    hidden = up.shape[0]
    out = pl.BlockSpec((2 * rows, HIDDEN_TILE), lambda j: (0, j))
    shape = jax.ShapeDtypeStruct((2 * rows, hidden), jnp.bfloat16)
    return call(
        functools.partial(ffn_kernel, len(gates)),
        [*xs, *gates, up, d_act],
        [pl.BlockSpec((rows, width), lambda j: (0, 0))] * 2
        + [pl.BlockSpec((HIDDEN_TILE, w.shape[1]), lambda j: (j, 0)) for w in (*gates, up)]
        + [out],
        [out] * 3,
        [shape] * 3,
        (hidden // HIDDEN_TILE,),
        after,
        name="ffn",
    )


def to_hidden_kernel(xs, *refs):
    weight = joined(refs[xs:-1]).T
    for x, rows in row_steps(*refs[:xs]):
        refs[-1][rows, :] = matrix_product(x, weight).astype(refs[-1].dtype)


def to_hidden(xs, weights, dtype=jnp.bfloat16, after=()):
    rows, width = xs[0].shape
    hidden = weights[0].shape[0]
    return call(
        functools.partial(to_hidden_kernel, len(xs)),
        [*xs, *weights],
        [pl.BlockSpec((rows, width), lambda j: (0, 0))] * len(xs)
        + [pl.BlockSpec((HIDDEN_TILE, w.shape[1]), lambda j: (j, 0)) for w in weights],
        pl.BlockSpec((len(xs) * rows, HIDDEN_TILE), lambda j: (0, j)),
        jax.ShapeDtypeStruct((len(xs) * rows, hidden), dtype),
        (hidden // HIDDEN_TILE,),
        after,
        name="to_hidden",
    )


MODEL_STEP = 512
ROWS_STEP = 512


def left_parts(left_refs, rights):
    if len(left_refs) == rights:
        return [ref[...].T for ref in left_refs]
    rows = left_refs[0].shape[0] // rights
    return [left_refs[0][k * rows : (k + 1) * rows, :].T for k in range(rights)]


def weight_cols_step(left_ref, right_refs, out_refs):
    parts = left_parts([left_ref], len(right_refs))
    for first in range(0, right_refs[0].shape[1], MODEL_STEP):
        cols = slice(first, first + MODEL_STEP)
        term = matrix_product(parts[0], right_refs[0][:, cols])
        for part, ref in zip(parts[1:], right_refs[1:]):
            term = term + matrix_product(part, ref[:, cols])
        term = term.astype(jnp.bfloat16)
        begin = 0
        for out_ref in out_refs:
            end = begin + out_ref.shape[1]
            low, high = max(begin, first), min(end, first + MODEL_STEP)
            if low < high:
                out_ref[:, low - begin : high - begin] = term[:, low - first : high - first]
            begin = end


def weight_cols_kernel(steps, counts, *refs):
    ins, outs = refs[: 3 * len(counts)], refs[3 * len(counts) :]
    begin = 0
    for i, count in enumerate(counts):
        out_refs = outs[begin : begin + count]
        begin += count

        @pl.when(pl.program_id(0) // steps == i)
        def _():
            weight_cols_step(ins[3 * i], ins[3 * i + 1 : 3 * i + 3], out_refs)


def weight_cols(*jobs, after=()):
    rows, hidden = jobs[0][0].shape
    steps = hidden // HIDDEN_TILE
    inputs, in_specs, out_specs, out_shape = [], [], [], []
    for i, (left, rights, widths) in enumerate(jobs):

        def at(j, i=i):
            return jnp.clip(j - i * steps, 0, steps - 1)

        inputs += [left, *rights]
        in_specs += [pl.BlockSpec((rows, HIDDEN_TILE), lambda j, at=at: (0, at(j)))]
        in_specs += [
            pl.BlockSpec(r.shape, lambda j: (0, 0), pipeline_mode=pl.Buffered(1)) for r in rights
        ]
        out_specs += [pl.BlockSpec((HIDDEN_TILE, w), lambda j, at=at: (at(j), 0)) for w in widths]
        out_shape += [jax.ShapeDtypeStruct((hidden, w), jnp.bfloat16) for w in widths]
    return call(
        functools.partial(weight_cols_kernel, steps, tuple(len(job[2]) for job in jobs)),
        inputs,
        in_specs,
        out_specs,
        out_shape,
        (steps * len(jobs),),
        after,
        name="weight_cols",
    )


def add_halves_kernel(x_ref, y_ref, a_ref, b_ref, x_out, y_out):
    x_out[...] = x_ref[...] + b_ref[...]
    y_out[...] = y_ref[...] + a_ref[...]


def add_halves(along_x, along_y, from_a, from_b):
    rows, width = along_x.shape
    tile = rows // 2
    half = width // 2
    left = pl.BlockSpec((tile, half), lambda i: (i, 0))
    right = pl.BlockSpec((tile, half), lambda i: (i, 1))
    shape = jax.ShapeDtypeStruct((rows, width), along_x.dtype)
    return call(
        add_halves_kernel,
        [along_x, along_y, from_a, from_b],
        [right, left, left, left],
        [right, left],
        [shape, shape],
        (rows // tile,),
        input_output_aliases={0: 0, 1: 1},
        name="add_halves",
    )


def weight_rows_kernel(lefts, rights, *refs):
    left_refs, right_refs = refs[:lefts], refs[lefts : lefts + rights]
    out_refs, turned_ref = refs[lefts + rights : -1], refs[-1]
    rows = right_refs[0].shape[0]

    @pl.when(pl.program_id(0) == 0)
    def _():
        for k, ref in enumerate(left_refs):
            turned_ref[:, k * rows : (k + 1) * rows] = ref[...].T

    span = out_refs[0].shape[0]
    term = matrix_product(turned_ref[:, :rows], right_refs[0][...])
    for k in range(1, rights):
        term = term + matrix_product(turned_ref[:, k * rows : (k + 1) * rows], right_refs[k][...])
    term = term.astype(jnp.bfloat16)
    for i, out_ref in enumerate(out_refs):
        out_ref[...] = term[i * span : (i + 1) * span]


def weight_rows(lefts, rights, count, after=()):
    rows, hidden = lefts[0].shape
    width = rights[0].shape[1]
    shape = jax.ShapeDtypeStruct((hidden // count, width), jnp.bfloat16)
    return call(
        functools.partial(weight_rows_kernel, len(lefts), len(rights)),
        [*lefts, *rights],
        [
            pl.BlockSpec((rows, hidden), lambda j: (0, 0), pipeline_mode=pl.Buffered(1))
        ] * len(lefts)
        + [pl.BlockSpec((rows, ROWS_STEP), lambda j: (0, j))] * len(rights),
        [pl.BlockSpec((hidden // count, ROWS_STEP), lambda j: (0, j))] * count,
        [shape] * count,
        (width // ROWS_STEP,),
        after,
        scratch_shapes=[pltpu.VMEM((hidden, len(lefts) * rows), jnp.bfloat16)],
        name="weight_rows",
    )


def to_model_kernel(counts, order_ref, *refs):
    left_refs, weight_refs = refs[: len(counts)], refs[len(counts) : -2]
    out_ref, acc_ref = refs[-2:]

    @pl.when(pl.program_id(0) == 0)
    def _():
        acc_ref[...] = jnp.zeros_like(acc_ref)

    left = joined(left_refs)
    terms, begin = [], 0
    for count in counts:
        terms.append(joined(weight_refs[begin : begin + count]))
        begin += count
    weight = jnp.concatenate(terms, axis=0)
    for first in range(0, weight.shape[1], MODEL_STEP):
        cols = slice(first, first + MODEL_STEP)
        acc_ref[:, cols] += matrix_product(left, weight[:, cols])

    @pl.when(pl.program_id(0) == pl.num_programs(0) - 1)
    def _():
        block = acc_ref.shape[1] // order_ref.shape[0]
        for i in range(order_ref.shape[0]):
            at = pl.ds(pl.multiple_of(order_ref[i] * block, block), block)
            out_ref[:, at] = acc_ref[:, i * block : (i + 1) * block].astype(jnp.bfloat16)


def to_model(lefts, weights, order, half, rows, after=()):
    hidden = lefts[0].shape[1]
    flat = [w for pieces in weights for w in pieces]
    width = sum(w.shape[1] for w in weights[0])
    tile = HIDDEN_TILE // 2
    return call(
        functools.partial(to_model_kernel, tuple(len(pieces) for pieces in weights)),
        [*lefts, *flat],
        [pl.BlockSpec((rows, tile), lambda j, o: (half, j))] * len(lefts)
        + [pl.BlockSpec((tile, w.shape[1]), lambda j, o: (j, 0)) for w in flat],
        pl.BlockSpec((rows, width), lambda j, o: (0, 0)),
        jax.ShapeDtypeStruct((rows, width), jnp.bfloat16),
        (hidden // tile,),
        after,
        order,
        scratch_shapes=[pltpu.VMEM((rows, width), jnp.float32)],
        name="to_model",
    )


NORM_TILE = 256


def resid_kernel(order_ref, tokens_ref, own_ref, there_ref, gain_ref, resid_ref, normed_ref):
    resid = (
        tokens_ref[...].astype(jnp.float32)
        + own_ref[...].astype(jnp.float32)
        + there_ref[...].astype(jnp.float32)
    )
    resid_ref[...] = resid.astype(jnp.bfloat16)
    scale = lax.rsqrt(jnp.mean(resid * resid, axis=-1, keepdims=True) + EPS_NORM)
    normed = (resid * scale * gain_ref[...]).astype(jnp.bfloat16)
    block = normed.shape[1] // order_ref.shape[0]
    for i in range(order_ref.shape[0]):
        at = pl.ds(pl.multiple_of(order_ref[i] * block, block), block)
        normed_ref[:, at] = normed[:, i * block : (i + 1) * block]


def resid_norm(tokens, own, there, gain, order, after=()):
    rows, width = tokens.shape
    tile = pl.BlockSpec((NORM_TILE, width), lambda i, o: (i, 0))
    return call(
        resid_kernel,
        [tokens, own, there, gain[None, :]],
        [tile, tile, tile, pl.BlockSpec((1, width), lambda i, o: (0, 0))],
        [tile, tile],
        [
            jax.ShapeDtypeStruct((rows, width), jnp.bfloat16),
            jax.ShapeDtypeStruct((rows, width), jnp.bfloat16),
        ],
        (rows // NORM_TILE,),
        after,
        order,
        name="resid_norm",
    )


def norm_back_kernel(value_ref, base_ref, own_ref, there_ref, gain_ref, *out_refs):
    *grad_refs, sum_ref = out_refs

    @pl.when(pl.program_id(0) == 0)
    def _():
        sum_ref[...] = jnp.zeros_like(sum_ref)

    value = value_ref[...].astype(jnp.float32)
    upstream = own_ref[...].astype(jnp.float32) + there_ref[...].astype(jnp.float32)
    scale = lax.rsqrt(jnp.mean(value * value, axis=-1, keepdims=True) + EPS_NORM)
    hat = value * scale
    weighted = upstream * gain_ref[...]
    inner = jnp.mean(hat * weighted, axis=-1, keepdims=True)
    grad = base_ref[...].astype(jnp.float32) + scale * (weighted - hat * inner)
    for ref in grad_refs:
        ref[...] = grad.astype(ref.dtype)
    sum_ref[0:1, :] += jnp.sum(upstream * hat, axis=0, keepdims=True)


def norm_return(value, base, own, there, gain, dtypes, after=()):
    rows, width = value.shape
    tile = pl.BlockSpec((NORM_TILE, width), lambda i: (i, 0))
    return call(
        norm_back_kernel,
        [value, base, own, there, gain[None, :]],
        [tile, tile, tile, tile, pl.BlockSpec((1, width), lambda i: (0, 0))],
        [tile] * len(dtypes) + [pl.BlockSpec((8, width), lambda i: (0, 0))],
        [jax.ShapeDtypeStruct((rows, width), d) for d in dtypes]
        + [jax.ShapeDtypeStruct((8, width), jnp.float32)],
        (rows // NORM_TILE,),
        after,
        name="norm_return",
    )


def block_info(lengths, positions, first):
    count = (lengths + BLK - 1) // BLK
    ends = jnp.cumsum(count)
    starts = jnp.concatenate([jnp.zeros((1,), jnp.int32), ends])
    own = lax.dynamic_slice_in_dim(positions, first, 8)
    first_keys = jnp.max(jnp.where(starts[None, :] <= own[:, None], starts[None, :], 0), axis=1)
    limits = jnp.concatenate([lengths, jnp.zeros((1,), jnp.int32)])
    seq = jnp.sum((own[:, None] >= ends[None, :]).astype(jnp.int32), axis=1)
    limit = jnp.sum(jnp.where(seq[:, None] == jnp.arange(4)[None, :], limits[None, :], 0), axis=1)
    pos = ((own - first_keys)[:, None] * BLK + jnp.arange(BLK)[None, :]).astype(jnp.int32)
    valid = pos < limit[:, None]
    return first_keys, own, pos.reshape(-1), valid.reshape(-1)


def chip_layer(
    tokens,
    cotangent,
    seq_lens,
    block_pos,
    norm1_gain,
    w_query,
    key_matrix,
    value_matrix,
    query_gain,
    key_gain,
    w_out,
    norm2_gain,
    w_gate,
    w_up,
    w_down,
):
    xi, core, yi = lax.axis_index("x"), lax.axis_index("c"), lax.axis_index("y")
    rows, width = tokens.shape
    bf16, f32 = jnp.bfloat16, jnp.float32
    half, fourth = width // 2, width // 4

    q_in, k_in = w_query.shape[1], key_matrix.shape[1]
    fourth, eighth = width // 4, width // 8
    kvw_0 = gather_z(jnp.concatenate([key_matrix.T, value_matrix.T], axis=0))
    qw_0 = gather_z(w_query.T)
    up_0 = to_core(w_up.T, core)
    up_x, up_y = swap(up_0, "x"), swap(up_0, "y")
    down_0 = to_core(after(w_down, up_0), core)
    gate_0 = to_core(after(w_gate, up_0).T, core)
    low = up_0.shape[0] // 2
    out_0 = gather_z(w_out)
    dlo_0 = gather_z(down_0[:low])
    kvw_x, kvw_y = swap(kvw_0, "x"), swap(kvw_0, "y")
    middle = kvw_0.shape[0] // 2
    kvw_x, kvw_y, qw_0, up_x, up_y = sync(kvw_x, kvw_y, qw_0, up_x, up_y)
    kvw_ca, kvw_cb = swap(kvw_y[:middle], "x"), swap(kvw_x[middle:], "y")
    qw_x, qw_y = swap(qw_0, "x"), swap(qw_0, "y")
    kvw_ca, kvw_cb, qw_x, qw_y, out_0 = sync(kvw_ca, kvw_cb, qw_x, qw_y, out_0)
    qw_ca, qw_cb = swap(qw_y[:middle], "x"), swap(qw_x[middle:], "y")
    out_x, out_y = swap(out_0, "x"), swap(out_0, "y")
    kvw = [
        a.reshape(4, 2 * k_in, width)
        for a in (kvw_0, kvw_x, kvw_y, jnp.concatenate([kvw_ca, kvw_cb], axis=0))
    ]
    kv_w = jnp.concatenate(
        [part.reshape(-1, width) for a in kvw for part in (a[:, :k_in], a[:, k_in:])], axis=0
    )

    lengths_here = jnp.concatenate([seq_lens[0], block_pos[0]]).astype(f32)
    lengths_there = swap(lengths_here[None, :], "c")[0].astype(jnp.int32)
    first_own = yi * 8
    keys_here, at_here, pos_here, valid_here = block_info(seq_lens[0], block_pos[0], first_own)
    keys_there, at_there, pos_there, _ = block_info(
        lengths_there[:3], lengths_there[3:], first_own
    )
    info = jnp.stack(
        [
            jnp.concatenate([keys_here, at_here[:1]]),
            jnp.concatenate([keys_there, at_there[:1]]),
        ]
    ).astype(jnp.int32)
    freq = jnp.exp(
        jnp.arange(HEAD_SIZE // 2, dtype=f32) * (-2.0 * math.log(ROPE_BASE) / HEAD_SIZE)
    )
    angles = jnp.concatenate([pos_here, pos_there]).astype(f32)[:, None] * freq[None, :]
    cos_half, sin_half = jnp.cos(angles), jnp.sin(angles)
    cos_tab = jnp.concatenate([cos_half, cos_half], axis=1)
    sin_tab = jnp.concatenate([-sin_half, sin_half], axis=1)
    valid = valid_here.astype(f32)[:, None]

    blocks = jnp.arange(8)
    ry, rx, rc = blocks // 4, (blocks // 2) % 2, blocks % 2
    order = ((rx ^ xi) * 4 + rc * 2 + (ry ^ yi)).astype(jnp.int32)
    nx, nc, ny = blocks // 4, (blocks // 2) % 2, blocks % 2
    order_back = ((ny ^ yi) * 4 + (nx ^ xi) * 2 + nc).astype(jnp.int32)

    def stacked(first, second):
        return jnp.concatenate([first, second], axis=0)

    inputs = after(tokens, up_0).astype(f32)
    normed1 = rms_parts(inputs, norm1_gain)[0].astype(bf16)
    normed1 = [normed1, swap(normed1, "c")]
    dy_own = (valid * cotangent.astype(f32)).astype(bf16)

    def project(group, rows_in, weight, gain, count, wait=()):
        raw = to_hidden([rows_in], [weight], f32, wait)
        return raw, make_heads(group, raw, cos_tab, sin_tab, gain, count)

    normed1[0], kv_w = sync(normed1[0], kv_w)
    kv_raw0, kv0 = project(0, normed1[0], kv_w, key_gain, 2)
    kv0, qw_ca, qw_cb, out_x, out_y, up_y, normed1[0], gate_0, glo_in = sync(
        kv0, qw_ca, qw_cb, out_x, out_y, up_y, normed1[0], gate_0, gate_0[:low]
    )
    kv_far0, out_c, up_c = swap(kv0, "y"), swap(out_y, "x"), swap(up_y, "x")
    glo_0 = gather_z(glo_in)
    dhi_0, ghi_0 = gather_z(down_0[low:]), gather_z(gate_0[low:])
    q_w = jnp.concatenate([qw_0, qw_x, qw_y, qw_ca, qw_cb], axis=0)
    q_raw0, query0 = project(0, normed1[0], q_w, query_gain, 1)
    kv_raw1, kv1 = project(1, normed1[1], kv_w, key_gain, 2, [query0])
    kv_far0, out_c, up_c, dlo_0, kv1, normed1[1], dy_own = sync(
        kv_far0, out_c, up_c, dlo_0, kv1, normed1[1], dy_own
    )
    dlo_x, dlo_y = swap(dlo_0, "x"), swap(dlo_0, "y")
    up_in = jnp.concatenate([up_0, up_x, up_y, up_c], axis=1)
    ulo, uhi = gather_z(up_in[:low]), gather_z(up_in[low:])
    attn0, totals0 = attend(0, info, query0, kv0, kv_far0)
    out_w = jnp.concatenate([out_0, out_x, out_y, out_c], axis=0)
    attn0, out_w, dlo_x, dlo_y, kv_1, normed1[1] = sync(
        attn0, out_w, dlo_x, dlo_y, kv1, normed1[1]
    )
    q_raw1, query1 = project(1, normed1[1], q_w, query_gain, 1)
    dy = [reorder(dy_own, order, [query1])]
    dy.append(swap(dy[0], "c"))
    query, q_raw = [query0, query1], [q_raw0, q_raw1]
    kv, kv_raw = [kv0, kv1], [kv_raw0, kv_raw1]
    kv_far1, dlo_c = swap(kv_1, "y"), swap(dlo_y, "x")
    kv_far1, dlo_c, glo_0, query[1], dy[0] = sync(kv_far1, dlo_c, glo_0, query[1], dy[0])
    glo_x, glo_y = swap(glo_0, "x"), swap(glo_0, "y")
    attn1, totals1 = attend(1, info, query[1], kv[1], kv_far1)
    attn1, glo_x, glo_y, glo_0 = sync(attn1, glo_x, glo_y, glo_0)
    glo_ca, glo_cb = swap(glo_y[:, :eighth], "x"), swap(glo_x[:, eighth:], "y")
    same = jnp.arange(8, dtype=jnp.int32)
    out_term = to_model([attn1], [[out_w]], same, 0, rows)
    out_there = swap(out_term, "c")
    out_here = to_model([attn0], [[out_w]], same, 0, rows, [out_term])
    dlo = [dlo_0, dlo_x, dlo_y, dlo_c]
    d_act_lo = to_hidden(dy, dlo, bf16, [out_here])
    resid, normed2_own = resid_norm(
        tokens, out_here, out_there, norm2_gain, order_back, [d_act_lo]
    )
    normed2_own, glo_ca, glo_cb, dhi_0 = sync(normed2_own, glo_ca, glo_cb, dhi_0)
    normed2 = [normed2_own, swap(normed2_own, "c")]
    dhi_x, dhi_y = swap(dhi_0, "x"), swap(dhi_0, "y")
    glo = [glo_0, glo_x, glo_y, glo_ca, glo_cb]
    act_lo, gg_lo, ug_lo = ffn(normed2, glo, ulo, d_act_lo)
    act_lo, gg_lo, dhi_x, dhi_y, ghi_0 = sync(act_lo, gg_lo, dhi_x, dhi_y, ghi_0)
    ghi_x, ghi_y = swap(ghi_0, "x"), swap(ghi_0, "y")

    widths = [fourth, fourth, fourth, eighth, eighth]
    pieces = [fourth] * 4
    dlo_grad, gl_0, gl_x, gl_y, gl_c = weight_cols(
        (act_lo, dy, [width]), (gg_lo, normed2, pieces)
    )
    dlo_grad, gl_c, ghi_x, ghi_y, ug_lo, dhi_x, dhi_y = sync(
        dlo_grad, gl_c, ghi_x, ghi_y, ug_lo, dhi_x, dhi_y
    )
    dlo_sum = scatter_z(dlo_grad)
    dhi_ca, dhi_cb = swap(dhi_y[:, :eighth], "x"), swap(dhi_x[:, eighth:], "y")
    ul_0, ul_x, ul_y, ul_c = weight_cols((ug_lo, normed2, pieces))
    dhi_ca, dhi_cb, ul_c, ghi_x, ghi_y = sync(dhi_ca, dhi_cb, ul_c, ghi_x, ghi_y)
    dhi = [dhi_0, dhi_x, dhi_y, dhi_ca, dhi_cb]
    ghi_ca, ghi_cb = swap(ghi_y[:, :eighth], "x"), swap(ghi_x[:, eighth:], "y")
    d_act_hi = to_hidden(dy, dhi)
    ghi_ca, ghi_cb, gl_c, ul_c, d_act_hi = sync(ghi_ca, ghi_cb, gl_c, ul_c, d_act_hi)
    ghi = [ghi_0, ghi_x, ghi_y, ghi_ca, ghi_cb]
    from_g, from_u = swap(gl_c, "x"), swap(ul_c, "y")
    act_hi, gg_hi, ug_hi = ffn(normed2, ghi, uhi, d_act_hi)
    gl_x, gl_y, from_g, ul_x, ul_y, from_u, act_hi, gg_hi, ug_hi = sync(
        gl_x, gl_y, from_g, ul_x, ul_y, from_u, act_hi, gg_hi, ug_hi
    )
    gl_y = gl_y + from_g
    gl_x, gl_y, gg_hi = sync(gl_x, gl_y, gg_hi)
    got_x, got_y = swap(gl_x, "x"), swap(gl_y, "y")
    dh_0, dh_x, dh_y, dh_ca, dh_cb, gh_0, gh_x, gh_y, gh_c = weight_cols(
        (act_hi, dy, widths), (gg_hi, normed2, pieces)
    )
    gl_0, got_x, got_y, dh_ca, dh_cb, ug_hi, ul_x, ul_y = sync(
        gl_0, got_x, got_y, dh_ca, dh_cb, ug_hi, ul_x, ul_y
    )
    from_a, from_b = swap(dh_ca, "x"), swap(dh_cb, "y")
    glo_near = gl_0 + got_x + got_y
    glo_sum = scatter_z(glo_near)
    ul_x = ul_x + from_u
    uh_0, uh_x, uh_y, uh_c = weight_cols(
        (ug_hi, normed2, pieces), after=[glo_near, ul_x]
    )
    dh_x, dh_y, from_a, from_b, ul_x, ul_y, gg_hi, uh_0 = sync(
        dh_x, dh_y, from_a, from_b, ul_x, ul_y, gg_hi, uh_0
    )
    got_ux, got_uy = swap(ul_x, "x"), swap(ul_y, "y")
    dh_x, dh_y = add_halves(dh_x, dh_y, from_a, from_b)
    grads = [gg_lo, ug_lo, gg_hi, ug_hi]
    both_w = [glo, [ulo], ghi, [uhi]]
    there = to_model(grads, both_w, order, 1, rows, [dh_x, dh_y])
    ul_0, got_ux, got_uy, dh_x, dh_y, there, gg_hi = sync(
        ul_0, got_ux, got_uy, dh_x, dh_y, there, gg_hi
    )
    normed2_there = swap(there, "c")
    got_x, got_y = swap(dh_x, "x"), swap(dh_y, "y")
    ulo_near = ul_0 + got_ux + got_uy
    ulo_sum = scatter_z(ulo_near)
    grads = [gg_lo, ug_lo, gg_hi, ug_hi]
    grad_own = to_model(grads, both_w, order, 0, rows, [ulo_near])
    dh_0, got_x, got_y, gh_c, uh_c, grad_own = sync(dh_0, got_x, got_y, gh_c, uh_c, grad_own)
    from_g, from_u = swap(gh_c, "x"), swap(uh_c, "y")
    dhi_near = dh_0 + got_x + got_y
    dhi_sum = scatter_z(dhi_near)
    resid_here, gain2_sum = norm_return(
        resid, dy_own, grad_own, normed2_there, norm2_gain, (bf16,), [dhi_near]
    )
    resid_first = resid_here
    resid_there = swap(resid_here, "c")
    mixed_term = to_model([act_lo, act_hi], [dlo, dhi], order, 1, rows, [resid_here])
    d_attn0 = to_hidden([resid_here], [out_w], bf16, [mixed_term])
    gh_x, gh_y, from_g, uh_x, uh_y, from_u, mixed_term, d_attn0 = sync(
        gh_x, gh_y, from_g, uh_x, uh_y, from_u, mixed_term, d_attn0
    )
    gh_y, uh_x = gh_y + from_g, uh_x + from_u
    gh_x, gh_y, uh_x, uh_y, d_attn0 = sync(gh_x, gh_y, uh_x, uh_y, d_attn0)
    got_x, got_y = swap(gh_x, "x"), swap(gh_y, "y")
    got_ux, got_uy = swap(uh_x, "x"), swap(uh_y, "y")
    mixed_there = swap(mixed_term, "c")

    dq0, dkv0, dkv0_far = attend_back(0, info, query[0], d_attn0, attn0, totals0, kv[0], kv_far0)
    o_0, o_x, o_y, o_c = weight_rows([attn0, attn1], [resid_here, resid_there], 4, [dq0])
    d_attn1 = to_hidden([resid_there], [out_w], bf16, [o_0])
    gh_0, got_x, got_y, uh_0, got_ux, got_uy, d_attn1, dkv0_far, dlo_sum, o_c = sync(
        gh_0, got_x, got_y, uh_0, got_ux, got_uy, d_attn1, dkv0_far, dlo_sum, o_c
    )
    dkv0_back, from_o = swap(dkv0_far, "y"), swap(o_c, "x")
    dl_0, dl_x, dl_y, dl_c = (dlo_sum[:, i * fourth : (i + 1) * fourth] for i in range(4))
    from_l, got_lx = swap(dl_c, "x"), swap(dl_x, "x")
    ghi_near, uhi_near = gh_0 + got_x + got_y, uh_0 + got_ux + got_uy
    ghi_sum, uhi_sum = scatter_z(ghi_near), scatter_z(uhi_near)
    back = (cos_tab, sin_tab)
    dq1, dkv1, dkv1_far = attend_back(
        1, info, query[1], d_attn1, attn1, totals1, kv[1], kv_far1, [ghi_near, uhi_near]
    )
    q_grad0, q_gain0 = heads_return(0, q_raw[0], dq0, [], *back, query_gain, 1, [dq1])
    dkv1_far, dkv0_back, o_x, o_y, from_o, got_lx, dl_y, from_l, q_grad0 = sync(
        dkv1_far, dkv0_back, o_x, o_y, from_o, got_lx, dl_y, from_l, q_grad0
    )
    dkv1_back, got_ox = swap(dkv1_far, "y"), swap(o_x, "x")
    q_grad1, q_gain1 = heads_return(1, q_raw[1], dq1, [], *back, query_gain, 1, [q_grad0])
    q_grad, q_gains = [q_grad0, q_grad1], q_gain0 + q_gain1
    w_0, w_x, w_y, w_c = weight_rows(q_grad, normed1, 4)
    w_c, act_hi = sync(w_c, act_hi)
    from_w = swap(w_c, "x")
    mixed_own = to_model([act_lo, act_hi], [dlo, dhi], order, 0, rows)
    dkv1_back, got_ox, from_w, mixed_own, o_y, dl_y, w_x, w_y = sync(
        dkv1_back, got_ox, from_w, mixed_own, o_y + from_o, dl_y + from_l, w_x, w_y
    )
    got_oy, got_wx = swap(o_y, "y"), swap(w_x, "x")
    got_wy = swap(w_y + from_w, "y")

    def halves(array):
        span = array.shape[0] // 2
        return array[:span], array[span:]

    def corner_rows(along_x, along_y, from_a, from_b):
        (x_a, x_b), (y_a, y_b) = halves(along_x), halves(along_y)
        return stacked(x_a, x_b + from_b), stacked(y_a + from_a, y_b)

    kv_grad = [
        heads_return(g, kv_raw[g], d, [e], *back, key_gain, 2, [mixed_own, w_y])
        for g, (d, e) in enumerate(((dkv0, dkv0_back), (dkv1, dkv1_back)))
    ]
    k_gains = kv_grad[0][1] + kv_grad[1][1]
    kv_grad = [kv_grad[0][0], kv_grad[1][0]]
    kv_0, kv_x, kv_y, kv_c = weight_rows(kv_grad, normed1, 4)
    kv_c, kv_grad[1], got_oy, got_wx = sync(kv_c, kv_grad[1], got_oy, got_wx)
    kv_a, kv_b = halves(kv_c)
    from_a, from_b = swap(kv_a, "x"), swap(kv_b, "y")
    term_there = to_model([q_grad[1], kv_grad[1]], [[q_w], [kv_w]], same, 0, rows)
    o_0, got_oy, w_0, got_wx, got_wy, kv_x, kv_y, from_a, from_b, term_there, dl_y = sync(
        o_0, got_oy, w_0, got_wx, got_wy, kv_x, kv_y, from_a, from_b, term_there, dl_y
    )
    normed1_there = swap(term_there, "c")
    kv_x, kv_y = corner_rows(kv_x, kv_y, from_a, from_b)
    got_kx, got_ky, got_ly = swap(kv_x, "x"), swap(kv_y, "y"), swap(dl_y, "y")
    o_near, w_near = o_0 + got_ox + got_oy, w_0 + got_wx + got_wy
    ow_near = jnp.concatenate(
        [o_near.reshape(4, q_in, width), w_near.reshape(4, q_in, width)], axis=1
    ).reshape(8 * q_in, width)
    ow_sum = scatter_z(ow_near)
    term_own = to_model(
        [q_grad[0], kv_grad[0]], [[q_w], [kv_w]], same, 0, rows, [kv_x, kv_y, ow_near]
    )
    kv_0, got_kx, got_ky, got_ly, term_own = sync(kv_0, got_kx, got_ky, got_ly, term_own)
    kv_near = kv_0 + got_kx + got_ky
    kv_sum = scatter_z(
        kv_near.reshape(2, 4, k_in, width).swapaxes(0, 1).reshape(8 * k_in, width)
    )
    tokens_grad, gain1_sum = norm_return(
        tokens, resid_first, term_own, normed1_there, norm1_gain, (f32,), [kv_near]
    )
    gain1_part = gain1_sum[0]
    gain2_part = gain2_sum[0]
    gains = jnp.concatenate([gain1_part, gain2_part, q_gains[0], k_gains[0]])[None, :]
    gains = gains + swap(gains, "c")
    gains_xy = lax.ppermute(gains, ("x", "y"), [(i, i ^ 3) for i in range(4)])
    gains_x, gains_y = swap(gains, "x"), swap(gains, "y")
    gains = (gains + gains_x) + (gains_y + gains_xy)
    gains, mixed_own, ow_sum = sync(gains, mixed_own, ow_sum)
    gains_z = [lax.ppermute(gains, "z", [(i, i ^ k) for i in range(4)]) for k in (1, 2, 3)]
    output = (
        valid * (resid.astype(f32) + mixed_own.astype(f32) + mixed_there.astype(f32))
    ).astype(bf16)
    gains, output, kv_sum, *gains_z = sync(gains, output, kv_sum, *gains_z)
    o_sum, w_sum = ow_sum[:q_in], ow_sum[q_in:]
    gains = ((gains + gains_z[0]) + (gains_z[1] + gains_z[2]))[0]
    dlo_sum = dl_0 + got_lx + got_ly

    gate_sum, up_sum, down_sum = (
        jnp.concatenate(pair, axis=0)
        for pair in ((glo_sum, ghi_sum), (ulo_sum, uhi_sum), (dlo_sum, dhi_sum))
    )
    gate_sum, up_sum, down_sum = from_core(
        [(a[:, :eighth], a[:, eighth:]) for a in (gate_sum, up_sum, down_sum)], core
    )
    return (
        output,
        tokens_grad,
        gains[:width],
        w_sum.astype(f32).T,
        kv_sum[:k_in].astype(f32).T,
        kv_sum[k_in:].astype(f32).T,
        gains[2 * width : 2 * width + HEAD_SIZE],
        gains[2 * width + HEAD_SIZE :],
        o_sum.astype(f32),
        gains[width : 2 * width],
        gate_sum.astype(f32).T,
        up_sum.astype(f32).T,
        down_sum.astype(f32),
    )


def chip_solution(mesh):
    fine = Mesh(mesh.devices.reshape(2, 2, 2, 4), ("x", "c", "y", "z"))
    row_spec = P(("x", "c", "y", "z"), None)
    group_spec = P(("x", "c", "z"), None)
    head_cols = P(None, ("y", "x", "c", "z"))
    head_rows = P(("y", "x", "c", "z"), None)
    up_spec, down_spec = P(("x", "c", "y"), "z"), P("z", ("x", "c", "y"))
    return jax.shard_map(
        chip_layer,
        mesh=fine,
        in_specs=(
            row_spec,
            row_spec,
            group_spec,
            group_spec,
            P(),
            head_cols,
            head_cols,
            head_cols,
            P(),
            P(),
            head_rows,
            P(),
            up_spec,
            up_spec,
            down_spec,
        ),
        out_specs=(
            row_spec,
            row_spec,
            P(),
            head_cols,
            head_cols,
            head_cols,
            P(),
            P(),
            head_rows,
            P(),
            up_spec,
            up_spec,
            down_spec,
        ),
        check_vma=False,
    )


def solution(mesh):
    sizes = dict(mesh.shape)
    if sizes == {"fsdp": 4, "heads": 2, "tensor": 4}:
        return chip_solution(mesh)
    return plain_solution(mesh)
```

```python
import functools
import math

import jax
import jax.numpy as jnp
from jax import lax
from jax.experimental import pallas as pl
from jax.experimental.pallas import tpu as pltpu
from jax.sharding import Mesh
from jax.sharding import PartitionSpec as P

QUERY_HEADS = 16
KEY_VALUE_HEADS = 8
HEAD_SIZE = 128
BLK = 128


EPS_NORM = 1e-06
ROPE_BASE = 1000000.0
NEG_FILL = -1e30


def row_info(lengths, positions):
    block_count = (lengths + BLK - 1) // BLK
    ends = jnp.cumsum(block_count)
    starts = ends - block_count
    used = ends[-1]
    column = positions[:, None]
    inside = (column >= starts[None, :]) & (column < ends[None, :])
    past = positions >= used
    seq_block = jnp.sum((column >= ends[None, :]).astype(jnp.int32), axis=1)
    first_block = jnp.sum(jnp.where(inside, starts[None, :], 0), axis=1) + jnp.where(past, used, 0)
    limit = jnp.sum(jnp.where(inside, lengths[None, :], 0), axis=1)
    offsets = jnp.arange(BLK, dtype=jnp.int32)[None, :]
    pos_rows = (positions - first_block)[:, None] * BLK + offsets
    seq_rows = jnp.broadcast_to(seq_block[:, None], pos_rows.shape)
    valid_rows = jnp.logical_not(past)[:, None] & (pos_rows < limit[:, None])
    return (seq_rows.reshape(-1), pos_rows.reshape(-1), valid_rows.reshape(-1))


def rope_tables(pos_rows):
    half_dim = HEAD_SIZE // 2
    freq = jnp.exp(
        jnp.arange(half_dim, dtype=jnp.float32) * (-2.0 * math.log(ROPE_BASE) / HEAD_SIZE)
    )
    angles = pos_rows.astype(jnp.float32)[:, None] * freq[None, :]
    return (jnp.cos(angles)[:, None, :], jnp.sin(angles)[:, None, :])


def rotate(value_rows, cos_tab, sin_tab):
    half_dim = value_rows.shape[-1] // 2
    first_half, second_half = (value_rows[..., :half_dim], value_rows[..., half_dim:])
    return jnp.concatenate(
        [
            first_half * cos_tab - second_half * sin_tab,
            second_half * cos_tab + first_half * sin_tab,
        ],
        axis=-1,
    )


def unrotate(upstream, cos_tab, sin_tab):
    half_dim = upstream.shape[-1] // 2
    first_half, second_half = (upstream[..., :half_dim], upstream[..., half_dim:])
    return jnp.concatenate(
        [
            first_half * cos_tab + second_half * sin_tab,
            second_half * cos_tab - first_half * sin_tab,
        ],
        axis=-1,
    )


def rms_parts(value_rows, gain_vec):
    scales = lax.rsqrt(jnp.mean(value_rows * value_rows, axis=-1, keepdims=True) + EPS_NORM)
    return (value_rows * scales * gain_vec, scales)


def norm_back(value_rows, scales, gain_vec, upstream):
    weighted = upstream * gain_vec
    inner = jnp.sum(value_rows * weighted, axis=-1, keepdims=True) / value_rows.shape[-1]
    return scales * weighted - value_rows * scales * scales * scales * inner


def matrix_product(left, right):
    return jnp.dot(left, right, preferred_element_type=jnp.float32)


def dot_rows(left, right):
    return lax.dot_general(
        left, right, (((0,), (0,)), ((), ())), preferred_element_type=jnp.float32
    )


def dot_cols(left, right):
    return lax.dot_general(
        left, right, (((1,), (1,)), ((), ())), preferred_element_type=jnp.float32
    )


def swap_cols(array, outer, inner):
    lead = array.shape[0]
    return jnp.swapaxes(array.reshape(lead, outer, inner, -1), 1, 2).reshape(lead, -1)


def swap_rows(array, outer, inner):
    width = array.shape[1]
    return jnp.swapaxes(array.reshape(outer, inner, -1, width), 0, 1).reshape(-1, width)


def spread_rows(local_rows):
    return lax.all_gather(local_rows, "tensor", axis=0, tiled=True)


def to_heads(packed):
    return lax.all_to_all(packed, "heads", split_axis=1, concat_axis=0, tiled=True)


def to_rows(packed):
    return lax.all_to_all(packed, "heads", split_axis=0, concat_axis=1, tiled=True)


def tensor_sum(term, row_count):
    total = lax.psum(
        term(0, row_count * lax.axis_size("tensor")).astype(jnp.bfloat16), "tensor"
    ).astype(jnp.float32)
    return lax.dynamic_slice_in_dim(total, lax.axis_index("tensor") * row_count, row_count)


def block_scores(query_blk, key_all, seq_blk, pos_blk, seq_all, pos_all):
    scores = jnp.einsum(
        "qkgd,pkd->kgqp", query_blk, key_all, preferred_element_type=jnp.float32
    ) * HEAD_SIZE ** (-0.5)
    allowed = (seq_blk[:, None] == seq_all[None, :]) & (pos_all[None, :] <= pos_blk[:, None])
    return jnp.where(allowed[None, None], scores, NEG_FILL)


def attend_forward(query_grp, key_grp, value_grp, seq_all, pos_all):
    group_factor = QUERY_HEADS // KEY_VALUE_HEADS
    group_len = query_grp.shape[0]
    kv_local = key_grp.shape[1] // HEAD_SIZE
    query_four = query_grp.reshape(group_len, kv_local, group_factor, HEAD_SIZE)
    key_three = key_grp.reshape(group_len, kv_local, HEAD_SIZE)
    value_three = value_grp.reshape(group_len, kv_local, HEAD_SIZE)
    block_rows = min(512, group_len)

    def forward_block(block_idx):
        first_row = block_idx * block_rows
        query_blk = lax.dynamic_slice_in_dim(query_four, first_row, block_rows)
        seq_blk = lax.dynamic_slice_in_dim(seq_all, first_row, block_rows)
        pos_blk = lax.dynamic_slice_in_dim(pos_all, first_row, block_rows)
        scores = block_scores(query_blk, key_three, seq_blk, pos_blk, seq_all, pos_all)
        peak = jnp.max(scores, axis=-1, keepdims=True)
        expo = jnp.exp(scores - peak)
        total = jnp.sum(expo, axis=-1, keepdims=True)
        probs_b = (expo / total).astype(jnp.bfloat16)
        attended = jnp.einsum(
            "kgqp,pkd->qkgd", probs_b, value_three, preferred_element_type=jnp.float32
        )
        return (attended, (peak + jnp.log(total))[..., 0])

    attended, log_sums = lax.map(forward_block, jnp.arange(group_len // block_rows))
    return (
        attended.reshape(group_len, kv_local * group_factor * HEAD_SIZE).astype(jnp.bfloat16),
        log_sums,
    )


def attend_backward(query_grp, key_grp, value_grp, grad_grp, log_sums, seq_all, pos_all):
    group_factor = QUERY_HEADS // KEY_VALUE_HEADS
    scale = HEAD_SIZE ** (-0.5)
    group_len = query_grp.shape[0]
    kv_local = key_grp.shape[1] // HEAD_SIZE
    query_four = query_grp.reshape(group_len, kv_local, group_factor, HEAD_SIZE)
    key_three = key_grp.reshape(group_len, kv_local, HEAD_SIZE)
    value_three = value_grp.reshape(group_len, kv_local, HEAD_SIZE)
    grad_four = grad_grp.reshape(group_len, kv_local, group_factor, HEAD_SIZE)
    block_rows = min(512, group_len)

    def backward_block(carry, block_idx):
        key_acc, value_acc = carry
        first_row = block_idx * block_rows
        query_blk = lax.dynamic_slice_in_dim(query_four, first_row, block_rows)
        grad_blk = lax.dynamic_slice_in_dim(grad_four, first_row, block_rows)
        seq_blk = lax.dynamic_slice_in_dim(seq_all, first_row, block_rows)
        pos_blk = lax.dynamic_slice_in_dim(pos_all, first_row, block_rows)
        scores = block_scores(query_blk, key_three, seq_blk, pos_blk, seq_all, pos_all)
        probs = jnp.exp(scores - log_sums[block_idx][..., None])
        probs_b = probs.astype(jnp.bfloat16)
        prob_grad = jnp.einsum(
            "qkgd,pkd->kgqp", grad_blk, value_three, preferred_element_type=jnp.float32
        )
        score_grad_b = (
            probs * (prob_grad - jnp.sum(probs * prob_grad, axis=-1, keepdims=True))
        ).astype(jnp.bfloat16)
        query_grad = (
            jnp.einsum(
                "kgqp,pkd->qkgd", score_grad_b, key_three, preferred_element_type=jnp.float32
            )
            * scale
        )
        key_acc = (
            key_acc
            + jnp.einsum(
                "kgqp,qkgd->pkd", score_grad_b, query_blk, preferred_element_type=jnp.float32
            )
            * scale
        )
        value_acc = value_acc + jnp.einsum(
            "kgqp,qkgd->pkd", probs_b, grad_blk, preferred_element_type=jnp.float32
        )
        return ((key_acc, value_acc), query_grad)

    empty = jnp.zeros((group_len, kv_local, HEAD_SIZE), jnp.float32)
    (key_acc, value_acc), query_blocks = lax.scan(
        backward_block, (empty, empty), jnp.arange(group_len // block_rows)
    )
    query_grad_b = query_blocks.reshape(group_len, kv_local * group_factor * HEAD_SIZE).astype(
        jnp.bfloat16
    )
    key_grad_b = key_acc.reshape(group_len, kv_local * HEAD_SIZE).astype(jnp.bfloat16)
    value_grad_b = value_acc.reshape(group_len, kv_local * HEAD_SIZE).astype(jnp.bfloat16)
    return (query_grad_b, key_grad_b, value_grad_b)


def project_heads(normed_b, query_w, key_w, value_w, query_gain, key_gain, pos_rows):
    lines = normed_b.shape[0]
    q_raw = matrix_product(normed_b, query_w).reshape(lines, -1, HEAD_SIZE)
    key_unnormed = matrix_product(normed_b, key_w).reshape(lines, -1, HEAD_SIZE)
    value_b = matrix_product(normed_b, value_w).astype(jnp.bfloat16)
    cos_tab, sin_tab = rope_tables(pos_rows)
    q_normed, q_scale = rms_parts(q_raw, query_gain)
    k_normed, k_scale = rms_parts(key_unnormed, key_gain)
    query_b = rotate(q_normed, cos_tab, sin_tab).astype(jnp.bfloat16).reshape(lines, -1)
    key_b = rotate(k_normed, cos_tab, sin_tab).astype(jnp.bfloat16).reshape(lines, -1)
    return (query_b, key_b, value_b, (q_raw, q_scale, key_unnormed, k_scale, cos_tab, sin_tab))


def heads_back(query_back, key_back, kept, query_gain, key_gain):
    q_raw, q_scale, key_unnormed, k_scale, cos_tab, sin_tab = kept
    lines = q_raw.shape[0]
    q_turned = unrotate(query_back.astype(jnp.float32).reshape(q_raw.shape), cos_tab, sin_tab)
    k_turned = unrotate(key_back.astype(jnp.float32).reshape(key_unnormed.shape), cos_tab, sin_tab)
    q_raw_grad = (
        norm_back(q_raw, q_scale, query_gain, q_turned).reshape(lines, -1).astype(jnp.bfloat16)
    )
    k_raw_grad = (
        norm_back(key_unnormed, k_scale, key_gain, k_turned).reshape(lines, -1).astype(jnp.bfloat16)
    )
    qgain_part = jnp.sum(q_turned * q_raw * q_scale, axis=(0, 1))
    kgain_part = jnp.sum(k_turned * key_unnormed * k_scale, axis=(0, 1))
    return (q_raw_grad, k_raw_grad, qgain_part, kgain_part)


def plain_layer(
    tokens,
    cotangent,
    seq_lens,
    block_pos,
    norm1_gain,
    w_query,
    key_matrix,
    value_matrix,
    query_gain,
    key_gain,
    w_out,
    norm2_gain,
    w_gate,
    w_up,
    w_down,
):
    row_count = tokens.shape[0]
    fsdp_count = lax.axis_size("fsdp")
    heads_count = lax.axis_size("heads")
    gate_full, up_full, down_full = (
        lax.all_gather(w_gate, ("fsdp", "heads"), axis=0, tiled=True),
        lax.all_gather(w_up, ("fsdp", "heads"), axis=0, tiled=True),
        lax.all_gather(w_down, ("fsdp", "heads"), axis=1, tiled=True),
    )
    seq_all, pos_all, valid_all = row_info(seq_lens[0], block_pos[0])
    own_first = lax.axis_index("heads") * row_count
    pos_own = lax.dynamic_slice_in_dim(pos_all, own_first, row_count)
    valid_own = lax.dynamic_slice_in_dim(valid_all, own_first, row_count).astype(jnp.float32)[
        :, None
    ]
    inputs = tokens.astype(jnp.float32)
    first_normed, scale1 = rms_parts(inputs, norm1_gain)
    normed1_b = first_normed.astype(jnp.bfloat16)
    query_all, key_all, value_all, out_all = (
        lax.all_gather(w_query, ("fsdp", "heads", "tensor"), axis=1, tiled=True),
        lax.all_gather(key_matrix, ("fsdp", "heads", "tensor"), axis=1, tiled=True),
        lax.all_gather(value_matrix, ("fsdp", "heads", "tensor"), axis=1, tiled=True),
        lax.all_gather(w_out, ("fsdp", "heads", "tensor"), axis=0, tiled=True),
    )
    query_full = swap_cols(query_all, fsdp_count, heads_count)
    key_full = swap_cols(key_all, fsdp_count, heads_count)
    value_full = swap_cols(value_all, fsdp_count, heads_count)
    out_full = swap_rows(out_all, fsdp_count, heads_count)
    query_b, key_b, value_b, kept = project_heads(
        normed1_b, query_full, key_full, value_full, query_gain, key_gain, pos_own
    )
    q_width = query_b.shape[1] // heads_count
    k_width = key_b.shape[1] // heads_count
    packed = jnp.concatenate(
        [
            query_b.reshape(row_count, heads_count, q_width),
            key_b.reshape(row_count, heads_count, k_width),
            value_b.reshape(row_count, heads_count, k_width),
        ],
        axis=2,
    )
    grouped = to_heads(packed.reshape(row_count, -1))
    query_grp = grouped[:, :q_width]
    key_grp = grouped[:, q_width : q_width + k_width]
    value_grp = grouped[:, q_width + k_width :]
    attended_b, log_sums = attend_forward(query_grp, key_grp, value_grp, seq_all, pos_all)
    attn_tok = to_rows(attended_b)
    resid = inputs + matrix_product(attn_tok, out_full)
    normed2, scale2 = rms_parts(resid, norm2_gain)
    normed2_b = normed2.astype(jnp.bfloat16)
    wide_in = spread_rows(normed2_b)
    gate_pre = matrix_product(wide_in, gate_full)
    up_pre = matrix_product(wide_in, up_full)
    sigmoid_gate = jax.nn.sigmoid(gate_pre)
    silu_gate = gate_pre * sigmoid_gate
    act_b = (silu_gate * up_pre).astype(jnp.bfloat16)

    def forward_term(first_row, span):
        return matrix_product(act_b, down_full)

    mixed = tensor_sum(forward_term, row_count)
    output = (valid_own * (resid + mixed)).astype(jnp.bfloat16)
    grad_out = valid_own * cotangent.astype(jnp.float32)
    wide_grad = spread_rows(grad_out.astype(jnp.bfloat16))
    act_grad = dot_cols(wide_grad, down_full)
    down_grad = dot_rows(act_b, wide_grad)
    gate_grad_b = (
        act_grad * up_pre * sigmoid_gate * (1.0 + gate_pre * (1.0 - sigmoid_gate))
    ).astype(jnp.bfloat16)
    up_grad_b = (act_grad * silu_gate).astype(jnp.bfloat16)
    gate_wgrad = dot_rows(wide_in, gate_grad_b)
    up_wgrad = dot_rows(wide_in, up_grad_b)

    def backward_term(first_row, span):
        return dot_cols(gate_grad_b, gate_full) + dot_cols(up_grad_b, up_full)

    normed2_grad = tensor_sum(backward_term, row_count)
    gate_sum, up_sum, down_sum = (
        lax.psum_scatter(
            gate_wgrad.astype(jnp.bfloat16), ("fsdp", "heads"), scatter_dimension=0, tiled=True
        ).astype(jnp.float32),
        lax.psum_scatter(
            up_wgrad.astype(jnp.bfloat16), ("fsdp", "heads"), scatter_dimension=0, tiled=True
        ).astype(jnp.float32),
        lax.psum_scatter(
            down_grad.astype(jnp.bfloat16), ("fsdp", "heads"), scatter_dimension=1, tiled=True
        ).astype(jnp.float32),
    )
    resid_grad = grad_out + norm_back(resid, scale2, norm2_gain, normed2_grad)
    gain2_part = jnp.sum(normed2_grad * resid * scale2, axis=0)
    resid_grad_b = resid_grad.astype(jnp.bfloat16)
    out_wgrad = dot_rows(attn_tok, resid_grad_b)
    attn_grad_b = dot_cols(resid_grad_b, out_full).astype(jnp.bfloat16)
    attn_grad_grp = to_heads(attn_grad_b)
    query_grad_b, key_grad_b, value_grad_b = attend_backward(
        query_grp, key_grp, value_grp, attn_grad_grp, log_sums, seq_all, pos_all
    )
    back_packed = to_rows(jnp.concatenate([query_grad_b, key_grad_b, value_grad_b], axis=1))
    back_three = back_packed.reshape(row_count, heads_count, -1)
    query_back = back_three[:, :, :q_width].reshape(row_count, -1)
    key_back = back_three[:, :, q_width : q_width + k_width].reshape(row_count, -1)
    value_back = back_three[:, :, q_width + k_width :].reshape(row_count, -1)
    q_raw_grad, k_raw_grad, qgain_part, kgain_part = heads_back(
        query_back, key_back, kept, query_gain, key_gain
    )
    query_wgrad = swap_cols(dot_rows(normed1_b, q_raw_grad), heads_count, fsdp_count)
    key_wgrad = swap_cols(dot_rows(normed1_b, k_raw_grad), heads_count, fsdp_count)
    value_wgrad = swap_cols(dot_rows(normed1_b, value_back), heads_count, fsdp_count)
    out_wgrad = swap_rows(out_wgrad, heads_count, fsdp_count)
    normed1_grad = (
        dot_cols(q_raw_grad, query_full)
        + dot_cols(k_raw_grad, key_full)
        + dot_cols(value_back, value_full)
    )
    query_sum, key_sum, value_sum, out_sum = (
        lax.psum_scatter(query_wgrad, ("fsdp", "heads", "tensor"), scatter_dimension=1, tiled=True),
        lax.psum_scatter(key_wgrad, ("fsdp", "heads", "tensor"), scatter_dimension=1, tiled=True),
        lax.psum_scatter(value_wgrad, ("fsdp", "heads", "tensor"), scatter_dimension=1, tiled=True),
        lax.psum_scatter(out_wgrad, ("fsdp", "heads", "tensor"), scatter_dimension=0, tiled=True),
    )
    tokens_grad = resid_grad + norm_back(inputs, scale1, norm1_gain, normed1_grad)
    gain1_part = jnp.sum(normed1_grad * inputs * scale1, axis=0)
    gain1_sum, qgain_sum, kgain_sum, gain2_sum = lax.psum(
        (gain1_part, qgain_part, kgain_part, gain2_part), ("fsdp", "heads", "tensor")
    )
    return (
        output,
        tokens_grad,
        gain1_sum,
        query_sum,
        key_sum,
        value_sum,
        qgain_sum,
        kgain_sum,
        out_sum,
        gain2_sum,
        gate_sum,
        up_sum,
        down_sum,
    )


def plain_solution(mesh):
    return jax.shard_map(
        plain_layer,
        mesh=mesh,
        in_specs=(
            P(("fsdp", "heads", "tensor"), None),
            P(("fsdp", "heads", "tensor"), None),
            P(("fsdp", "tensor"), None),
            P(("fsdp", "tensor"), None),
            P(),
            P(None, ("heads", "fsdp", "tensor")),
            P(None, ("heads", "fsdp", "tensor")),
            P(None, ("heads", "fsdp", "tensor")),
            P(),
            P(),
            P(("heads", "fsdp", "tensor"), None),
            P(),
            P(("fsdp", "heads"), "tensor"),
            P(("fsdp", "heads"), "tensor"),
            P("tensor", ("fsdp", "heads")),
        ),
        out_specs=(
            P(("fsdp", "heads", "tensor"), None),
            P(("fsdp", "heads", "tensor"), None),
            P(),
            P(None, ("heads", "fsdp", "tensor")),
            P(None, ("heads", "fsdp", "tensor")),
            P(None, ("heads", "fsdp", "tensor")),
            P(),
            P(),
            P(("heads", "fsdp", "tensor"), None),
            P(),
            P(("fsdp", "heads"), "tensor"),
            P(("fsdp", "heads"), "tensor"),
            P("tensor", ("fsdp", "heads")),
        ),
        check_vma=False,
    )


VMEM_LIMIT = 56 * 1024 * 1024
LOG2_E = 1.4426950408889634
SWAP = ((0, 1), (1, 0))
ROW_TILE = 1024
SCALE = HEAD_SIZE ** (-0.5)


def dot_t(left, right):
    return lax.dot_general(
        left, right, (((1,), (1,)), ((), ())), preferred_element_type=jnp.float32
    )


def swap(array, axis):
    return lax.ppermute(array, axis, SWAP)


def pick(first, second, index):
    return jnp.where(index == 0, first, second)


def join(mine, other, index, axis):
    return pick(
        jnp.concatenate([mine, other], axis=axis),
        jnp.concatenate([other, mine], axis=axis),
        index,
    )


def gather_z(array):
    return lax.all_gather(array, "z", axis=0, tiled=True)


def scatter_z(array):
    return lax.psum_scatter(array, "z", scatter_dimension=0, tiled=True)


def after(array, *done):
    return lax.optimization_barrier((array, *done))[0]


def sync(*arrays):
    return lax.optimization_barrier(arrays)


def to_core(array, core):
    half = array.shape[0] // 2
    first, second = array[:half], array[half:]
    other = swap(pick(second, first, core), "c")
    mine = pick(first, second, core)
    return join(mine, other, core, 1)


def from_core(pairs, core):
    mine = [pick(a, b, core) for a, b in pairs]
    send = jnp.concatenate([pick(b, a, core) for a, b in pairs], axis=0)
    others = jnp.split(swap(send, "c"), len(pairs))
    return [join(m, o, core, 0) for m, o in zip(mine, others)]


def call(kernel, inputs, in_specs, out_specs, out_shape, grid, after=(), prefetch=None, **more):
    lead = 0 if prefetch is None else 1
    count, extra = lead + len(inputs), len(after)

    def body(*refs):
        kernel(*refs[:count], *refs[count + extra :])

    if prefetch is not None:
        prefetched, inputs = [prefetch], list(inputs)
    else:
        prefetched, inputs = [], list(inputs)
    scratch = more.pop("scratch_shapes", ())
    return pl.pallas_call(
        body,
        grid_spec=pltpu.PrefetchScalarGridSpec(
            num_scalar_prefetch=lead,
            grid=grid,
            in_specs=list(in_specs) + [pl.BlockSpec(memory_space=pl.ANY)] * extra,
            out_specs=out_specs,
            scratch_shapes=scratch,
        ),
        out_shape=out_shape,
        compiler_params=pltpu.CompilerParams(vmem_limit_bytes=VMEM_LIMIT),
        cost_estimate=pl.CostEstimate(flops=1000, bytes_accessed=1000, transcendentals=0),
        **more,
    )(*prefetched, *inputs, *after)


def reorder_kernel(order_ref, in_ref, out_ref):
    out_ref[...] = in_ref[...]


def reorder(array, order, after=()):
    rows, width = array.shape
    parts = order.shape[0]
    return call(
        reorder_kernel,
        [array],
        [pl.BlockSpec((rows, width // parts), lambda i, o: (0, o[i]))],
        pl.BlockSpec((rows, width // parts), lambda i, o: (0, i)),
        jax.ShapeDtypeStruct(array.shape, array.dtype),
        (parts,),
        after,
        order,
        name="reorder",
    )


def lane_mean(value):
    ones = jnp.full((2 * HEAD_SIZE, HEAD_SIZE), 1.0 / HEAD_SIZE, jnp.bfloat16)
    high = value.astype(jnp.bfloat16)
    low = (value - high.astype(jnp.float32)).astype(jnp.bfloat16)
    return matrix_product(jnp.concatenate([high, low], axis=1), ones)


HEADS_STEP = 4


def heads_kernel(count, raw_ref, cos_ref, sin_ref, gain_ref, out_ref):
    for first in range(0, raw_ref.shape[1], count * HEAD_SIZE):
        lanes = slice(first, first + HEAD_SIZE)
        raw = raw_ref[:, lanes]
        value = raw * lax.rsqrt(lane_mean(raw * raw) + EPS_NORM) * gain_ref[...]
        out_ref[:, lanes] = (
            value * cos_ref[...] + pltpu.roll(value, HEAD_SIZE // 2, 1) * sin_ref[...]
        ).astype(jnp.bfloat16)
        if count == 2:
            lanes = slice(first + HEAD_SIZE, first + 2 * HEAD_SIZE)
            out_ref[:, lanes] = raw_ref[:, lanes].astype(jnp.bfloat16)


def make_heads(group, raw, cos_tab, sin_tab, gain, count, after=()):
    rows, width = raw.shape
    skip = group * (rows // ROW_TILE)
    table = pl.BlockSpec((ROW_TILE, HEAD_SIZE), lambda i, r: (i + skip, 0))
    one = pl.BlockSpec((ROW_TILE, HEADS_STEP * HEAD_SIZE), lambda i, r: (i, r))
    return call(
        functools.partial(heads_kernel, count),
        [raw, cos_tab, sin_tab, gain[None, :]],
        [one, table, table, pl.BlockSpec((1, HEAD_SIZE), lambda i, r: (0, 0))],
        one,
        jax.ShapeDtypeStruct((rows, width), jnp.bfloat16),
        (rows // ROW_TILE, width // (HEADS_STEP * HEAD_SIZE)),
        after,
        name="make_heads",
    )


def heads_back_kernel(count, raw_ref, cos_ref, sin_ref, gain_ref, *rest):
    *up_refs, out_ref, sum_ref = rest

    @pl.when((pl.program_id(0) == 0) & (pl.program_id(1) == 0))
    def _():
        sum_ref[...] = jnp.zeros_like(sum_ref)

    total = jnp.zeros((1, HEAD_SIZE), jnp.float32)
    for first in range(0, raw_ref.shape[1], count * HEAD_SIZE):
        lanes = slice(first, first + HEAD_SIZE)
        raw = raw_ref[:, lanes]
        upstream = up_refs[0][:, lanes].astype(jnp.float32)
        for ref in up_refs[1:]:
            upstream = upstream + ref[:, lanes].astype(jnp.float32)
        turned = upstream * cos_ref[...] - pltpu.roll(upstream, HEAD_SIZE // 2, 1) * sin_ref[...]
        scale = lax.rsqrt(lane_mean(raw * raw) + EPS_NORM)
        hat = raw * scale
        weighted = turned * gain_ref[...]
        out_ref[:, lanes] = (scale * (weighted - hat * lane_mean(hat * weighted))).astype(
            jnp.bfloat16
        )
        total = total + jnp.sum(turned * hat, axis=0, keepdims=True)
        if count == 2:
            lanes = slice(first + HEAD_SIZE, first + 2 * HEAD_SIZE)
            value_up = up_refs[0][:, lanes].astype(jnp.float32)
            for ref in up_refs[1:]:
                value_up = value_up + ref[:, lanes].astype(jnp.float32)
            out_ref[:, lanes] = value_up.astype(jnp.bfloat16)
    sum_ref[0:1, :] += total


def heads_return(group, raw, upstream, far, cos_tab, sin_tab, gain, count, after=()):
    rows, width = raw.shape
    skip = group * (rows // ROW_TILE)
    span = HEADS_STEP * HEAD_SIZE
    table = pl.BlockSpec((ROW_TILE, HEAD_SIZE), lambda i, r: (i + skip, 0))
    one = pl.BlockSpec((ROW_TILE, span), lambda i, r: (i, r))
    across = pl.BlockSpec((ROW_TILE, span), lambda i, r: (i, (r + 1) % 2))
    return call(
        functools.partial(heads_back_kernel, count),
        [raw, cos_tab, sin_tab, gain[None, :], upstream] + far,
        [one, table, table, pl.BlockSpec((1, HEAD_SIZE), lambda i, r: (0, 0)), one]
        + [across] * len(far),
        [one, pl.BlockSpec((8, HEAD_SIZE), lambda i, r: (0, 0))],
        [
            jax.ShapeDtypeStruct((rows, width), jnp.bfloat16),
            jax.ShapeDtypeStruct((8, HEAD_SIZE), jnp.float32),
        ],
        (rows // ROW_TILE, width // span),
        after,
        name="heads_return",
    )


GROUP_WIDTH = 2 * HEAD_SIZE
TOGETHER = 2


def stack_heads(block):
    return jnp.concatenate([block[:, :HEAD_SIZE], block[:, HEAD_SIZE:]], axis=0)


def key_bias(first_key, pair, parity, queries=0):
    shape = (1, 2 * BLK) if queries == 0 else (2 * BLK, 1)
    cols = lax.broadcasted_iota(jnp.int32, shape, 1 - queries)
    block = 2 * pair + jnp.where(cols < BLK, parity, 1 - parity)
    return jnp.where(block >= first_key, 0.0, NEG_FILL)


def last_bias(first_key, pair, parity, queries=0):
    rows = lax.broadcasted_iota(jnp.int32, (2 * BLK, 2 * BLK), queries)
    cols = lax.broadcasted_iota(jnp.int32, (2 * BLK, 2 * BLK), 1 - queries)
    far = (parity == 1) & (2 * pair >= first_key)
    own = lax.rem(cols, BLK) <= lax.rem(rows, BLK)
    far_bias = jnp.where(far, 0.0, NEG_FILL)
    return jnp.where(cols < BLK, jnp.where(own, 0.0, NEG_FILL), far_bias)


def pair_of(own_ref, far_ref, m, first):
    at = pl.ds(pl.multiple_of(m * BLK, BLK), BLK)
    lanes = slice(first, first + HEAD_SIZE)
    return jnp.concatenate([own_ref[at, lanes], far_ref[at, lanes]], axis=0)


def head_lanes(head):
    return slice(head * GROUP_WIDTH, (head + 1) * GROUP_WIDTH)


def attend_kernel(group, info_ref, q_ref, own_ref, far_ref, o_ref, l_ref):
    blocks = q_ref.shape[0] // BLK
    parity = info_ref[group, blocks]

    def one_block(j, _):
        first_key = info_ref[group, j]
        rows = pl.ds(pl.multiple_of(j * BLK, BLK), BLK)
        queries = [stack_heads(q_ref[rows, head_lanes(h)]) for h in range(TOGETHER)]

        def step(m, bias, carry):
            out = []
            for h in range(TOGETHER):
                total, acc = carry[h]
                score = dot_t(queries[h], pair_of(own_ref, far_ref, m, h * GROUP_WIDTH))
                expo = jnp.exp2(score * (SCALE * LOG2_E) + bias)
                total = total + jnp.sum(expo, axis=1, keepdims=True)
                value = pair_of(own_ref, far_ref, m, h * GROUP_WIDTH + HEAD_SIZE)
                acc = acc + matrix_product(expo.astype(jnp.bfloat16), value)
                out.append((total, acc))
            return tuple(out)

        empty = (
            jnp.zeros((2 * BLK, 1), jnp.float32),
            jnp.zeros((2 * BLK, HEAD_SIZE), jnp.float32),
        )
        carry = step(j, last_bias(first_key, j, parity), (empty,) * TOGETHER)
        carry = lax.fori_loop(
            lax.div(first_key, 2),
            j,
            lambda m, c: step(m, key_bias(first_key, m, parity), c),
            carry,
        )
        lane = lax.broadcasted_iota(jnp.int32, (BLK, HEAD_SIZE), 1)
        for h, (total, acc) in enumerate(carry):
            out = (acc / total).astype(jnp.bfloat16)
            o_ref[rows, head_lanes(h)] = jnp.concatenate([out[:BLK], out[BLK:]], axis=1)
            l_ref[rows, h * HEAD_SIZE : (h + 1) * HEAD_SIZE] = jnp.where(
                lane == 0, total[:BLK], total[BLK:]
            )
        return 0

    lax.fori_loop(0, blocks, one_block, 0)


def attend(group, info, query, own, far, after=()):
    rows, width = query.shape
    span = TOGETHER * GROUP_WIDTH
    here = pl.BlockSpec((rows, span), lambda r, s: (0, r))
    there = pl.BlockSpec((rows, span), lambda r, s: (0, (r + 1) % 2))
    return call(
        functools.partial(attend_kernel, group),
        [query, own, far],
        [here, here, there],
        [here, pl.BlockSpec((rows, span // 2), lambda r, s: (0, r))],
        [
            jax.ShapeDtypeStruct((rows, width), jnp.bfloat16),
            jax.ShapeDtypeStruct((rows, width // 2), jnp.float32),
        ],
        (width // span,),
        after,
        info,
        name="attend",
    )


def row_sums(value):
    ones = jnp.ones((8, 2 * HEAD_SIZE), jnp.bfloat16)
    high = value.astype(jnp.bfloat16)
    low = (value - high.astype(jnp.float32)).astype(jnp.bfloat16)
    return dot_t(ones, jnp.concatenate([high, low], axis=1))[:1]


def attend_back_kernel(
    group,
    info_ref,
    q_ref,
    do_ref,
    o_ref,
    l_ref,
    own_ref,
    far_ref,
    dq_ref,
    down_ref,
    dfar_ref,
    kacc_ref,
    vacc_ref,
):
    blocks = q_ref.shape[0] // BLK
    parity = info_ref[group, blocks]
    kacc_ref[...] = jnp.zeros_like(kacc_ref)
    vacc_ref[...] = jnp.zeros_like(vacc_ref)

    def one_block(j, _):
        first_key = info_ref[group, j]
        rows = pl.ds(pl.multiple_of(j * BLK, BLK), BLK)
        held = []
        for h in range(TOGETHER):
            query = stack_heads(q_ref[rows, head_lanes(h)])
            attn = stack_heads(o_ref[rows, head_lanes(h)]).astype(jnp.float32)
            grad = stack_heads(do_ref[rows, head_lanes(h)]).astype(jnp.float32)
            at = h * HEAD_SIZE
            total = jnp.concatenate(
                [l_ref[rows, at : at + 1], l_ref[rows, at + 1 : at + 2]], axis=0
            )
            grad_b = (grad / total).astype(jnp.bfloat16)
            inner = row_sums(grad_b.astype(jnp.float32) * attn)
            held.append((query, grad_b, inner))

        def step(m, bias, carry):
            at = pl.ds(pl.multiple_of(m * BLK, BLK), BLK)
            out = []
            for h in range(TOGETHER):
                query, grad_b, inner = held[h]
                key = pair_of(own_ref, far_ref, m, h * GROUP_WIDTH)
                value = pair_of(own_ref, far_ref, m, h * GROUP_WIDTH + HEAD_SIZE)
                expo = jnp.exp2(dot_t(key, query) * (SCALE * LOG2_E) + bias)
                d_score = (expo * (dot_t(value, grad_b) - inner)).astype(jnp.bfloat16)
                d_key = matrix_product(d_score, query)
                d_value = matrix_product(expo.astype(jnp.bfloat16), grad_b)
                kacc_ref[h, 0, at, :] += d_key[:BLK]
                kacc_ref[h, 1, at, :] += d_key[BLK:]
                vacc_ref[h, 0, at, :] += d_value[:BLK]
                vacc_ref[h, 1, at, :] += d_value[BLK:]
                out.append(carry[h] + dot_rows(d_score, key))
            return tuple(out)

        empty = jnp.zeros((2 * BLK, HEAD_SIZE), jnp.float32)
        carry = step(j, last_bias(first_key, j, parity, 1), (empty,) * TOGETHER)
        carry = lax.fori_loop(
            lax.div(first_key, 2),
            j,
            lambda m, c: step(m, key_bias(first_key, m, parity, 1), c),
            carry,
        )
        for h, dq in enumerate(carry):
            dq = (dq * SCALE).astype(jnp.bfloat16)
            dq_ref[rows, head_lanes(h)] = jnp.concatenate([dq[:BLK], dq[BLK:]], axis=1)
        return 0

    lax.fori_loop(0, blocks, one_block, 0)
    for h in range(TOGETHER):
        for half, ref in enumerate((down_ref, dfar_ref)):
            first = h * GROUP_WIDTH
            ref[:, first : first + HEAD_SIZE] = (kacc_ref[h, half] * SCALE).astype(jnp.bfloat16)
            ref[:, first + HEAD_SIZE : first + GROUP_WIDTH] = vacc_ref[h, half].astype(
                jnp.bfloat16
            )


def attend_back(group, info, query, d_attn, attn, total, own, far, after=()):
    rows, width = query.shape
    span = TOGETHER * GROUP_WIDTH
    here = pl.BlockSpec((rows, span), lambda r, s: (0, r))
    there = pl.BlockSpec((rows, span), lambda r, s: (0, (r + 1) % 2))
    shape = jax.ShapeDtypeStruct((rows, width), jnp.bfloat16)
    return call(
        functools.partial(attend_back_kernel, group),
        [query, d_attn, attn, total, own, far],
        [here, here, here, pl.BlockSpec((rows, span // 2), lambda r, s: (0, r)), here, there],
        [here] * 3,
        [shape] * 3,
        (width // span,),
        after,
        info,
        scratch_shapes=[
            pltpu.VMEM((TOGETHER, 2, rows, HEAD_SIZE), jnp.float32),
            pltpu.VMEM((TOGETHER, 2, rows, HEAD_SIZE), jnp.float32),
        ],
        name="attend_back",
    )


HIDDEN_TILE = 512
ROW_STEP = 1024


def row_steps(*refs):
    for first_ref in range(len(refs)):
        for first in range(0, refs[first_ref].shape[0], ROW_STEP):
            begin = first_ref * refs[first_ref].shape[0] + first
            yield refs[first_ref][first : first + ROW_STEP, :], slice(begin, begin + ROW_STEP)


def joined(refs):
    return jnp.concatenate([ref[...] for ref in refs], axis=1)


def ffn_kernel(pieces, xa_ref, xb_ref, *refs):
    gate_w = joined(refs[:pieces]).T
    up_w, d_act_ref = refs[pieces][...].T, refs[pieces + 1]
    act_ref, gate_ref, up_ref = refs[pieces + 2 :]
    for x, rows in row_steps(xa_ref, xb_ref):
        gate = matrix_product(x, gate_w)
        upper = matrix_product(x, up_w)
        d_act = d_act_ref[rows, :].astype(jnp.float32)
        sig = 0.5 * jnp.tanh(0.5 * gate) + 0.5
        silu = gate * sig
        act_ref[rows, :] = (silu * upper).astype(jnp.bfloat16)
        gate_ref[rows, :] = (d_act * upper * (sig + silu * (1.0 - sig))).astype(jnp.bfloat16)
        up_ref[rows, :] = (d_act * silu).astype(jnp.bfloat16)


def ffn(xs, gates, up, d_act, after=()):
    rows, width = xs[0].shape
    hidden = up.shape[0]
    out = pl.BlockSpec((2 * rows, HIDDEN_TILE), lambda j: (0, j))
    shape = jax.ShapeDtypeStruct((2 * rows, hidden), jnp.bfloat16)
    return call(
        functools.partial(ffn_kernel, len(gates)),
        [*xs, *gates, up, d_act],
        [pl.BlockSpec((rows, width), lambda j: (0, 0))] * 2
        + [pl.BlockSpec((HIDDEN_TILE, w.shape[1]), lambda j: (j, 0)) for w in (*gates, up)]
        + [out],
        [out] * 3,
        [shape] * 3,
        (hidden // HIDDEN_TILE,),
        after,
        name="ffn",
    )


def to_hidden_kernel(xs, *refs):
    weight = joined(refs[xs:-1]).T
    for x, rows in row_steps(*refs[:xs]):
        refs[-1][rows, :] = matrix_product(x, weight).astype(refs[-1].dtype)


def to_hidden(xs, weights, dtype=jnp.bfloat16, after=()):
    rows, width = xs[0].shape
    hidden = weights[0].shape[0]
    return call(
        functools.partial(to_hidden_kernel, len(xs)),
        [*xs, *weights],
        [pl.BlockSpec((rows, width), lambda j: (0, 0))] * len(xs)
        + [pl.BlockSpec((HIDDEN_TILE, w.shape[1]), lambda j: (j, 0)) for w in weights],
        pl.BlockSpec((len(xs) * rows, HIDDEN_TILE), lambda j: (0, j)),
        jax.ShapeDtypeStruct((len(xs) * rows, hidden), dtype),
        (hidden // HIDDEN_TILE,),
        after,
        name="to_hidden",
    )


MODEL_STEP = 512
ROWS_STEP = 512


def left_parts(left_refs, rights):
    if len(left_refs) == rights:
        return [ref[...].T for ref in left_refs]
    rows = left_refs[0].shape[0] // rights
    return [left_refs[0][k * rows : (k + 1) * rows, :].T for k in range(rights)]


def weight_cols_step(left_ref, right_refs, out_refs):
    parts = left_parts([left_ref], len(right_refs))
    for first in range(0, right_refs[0].shape[1], MODEL_STEP):
        cols = slice(first, first + MODEL_STEP)
        term = matrix_product(parts[0], right_refs[0][:, cols])
        for part, ref in zip(parts[1:], right_refs[1:]):
            term = term + matrix_product(part, ref[:, cols])
        term = term.astype(jnp.bfloat16)
        begin = 0
        for out_ref in out_refs:
            end = begin + out_ref.shape[1]
            low, high = max(begin, first), min(end, first + MODEL_STEP)
            if low < high:
                out_ref[:, low - begin : high - begin] = term[:, low - first : high - first]
            begin = end


def weight_cols_kernel(steps, counts, *refs):
    ins, outs = refs[: 3 * len(counts)], refs[3 * len(counts) :]
    begin = 0
    for i, count in enumerate(counts):
        out_refs = outs[begin : begin + count]
        begin += count

        @pl.when(pl.program_id(0) // steps == i)
        def _():
            weight_cols_step(ins[3 * i], ins[3 * i + 1 : 3 * i + 3], out_refs)


def weight_cols(*jobs, after=()):
    rows, hidden = jobs[0][0].shape
    steps = hidden // HIDDEN_TILE
    inputs, in_specs, out_specs, out_shape = [], [], [], []
    for i, (left, rights, widths) in enumerate(jobs):

        def at(j, i=i):
            return jnp.clip(j - i * steps, 0, steps - 1)

        inputs += [left, *rights]
        in_specs += [pl.BlockSpec((rows, HIDDEN_TILE), lambda j, at=at: (0, at(j)))]
        in_specs += [
            pl.BlockSpec(r.shape, lambda j: (0, 0), pipeline_mode=pl.Buffered(1)) for r in rights
        ]
        out_specs += [pl.BlockSpec((HIDDEN_TILE, w), lambda j, at=at: (at(j), 0)) for w in widths]
        out_shape += [jax.ShapeDtypeStruct((hidden, w), jnp.bfloat16) for w in widths]
    return call(
        functools.partial(weight_cols_kernel, steps, tuple(len(job[2]) for job in jobs)),
        inputs,
        in_specs,
        out_specs,
        out_shape,
        (steps * len(jobs),),
        after,
        name="weight_cols",
    )


def add_halves_kernel(x_ref, y_ref, a_ref, b_ref, x_out, y_out):
    x_out[...] = x_ref[...] + b_ref[...]
    y_out[...] = y_ref[...] + a_ref[...]


def add_halves(along_x, along_y, from_a, from_b):
    rows, width = along_x.shape
    tile = rows // 2
    half = width // 2
    left = pl.BlockSpec((tile, half), lambda i: (i, 0))
    right = pl.BlockSpec((tile, half), lambda i: (i, 1))
    shape = jax.ShapeDtypeStruct((rows, width), along_x.dtype)
    return call(
        add_halves_kernel,
        [along_x, along_y, from_a, from_b],
        [right, left, left, left],
        [right, left],
        [shape, shape],
        (rows // tile,),
        input_output_aliases={0: 0, 1: 1},
        name="add_halves",
    )


def weight_rows_kernel(lefts, rights, *refs):
    left_refs, right_refs = refs[:lefts], refs[lefts : lefts + rights]
    out_refs, turned_ref = refs[lefts + rights : -1], refs[-1]
    rows = right_refs[0].shape[0]

    @pl.when(pl.program_id(0) == 0)
    def _():
        for k, ref in enumerate(left_refs):
            turned_ref[:, k * rows : (k + 1) * rows] = ref[...].T

    span = out_refs[0].shape[0]
    term = matrix_product(turned_ref[:, :rows], right_refs[0][...])
    for k in range(1, rights):
        term = term + matrix_product(turned_ref[:, k * rows : (k + 1) * rows], right_refs[k][...])
    term = term.astype(jnp.bfloat16)
    for i, out_ref in enumerate(out_refs):
        out_ref[...] = term[i * span : (i + 1) * span]


def weight_rows(lefts, rights, count, after=()):
    rows, hidden = lefts[0].shape
    width = rights[0].shape[1]
    shape = jax.ShapeDtypeStruct((hidden // count, width), jnp.bfloat16)
    return call(
        functools.partial(weight_rows_kernel, len(lefts), len(rights)),
        [*lefts, *rights],
        [
            pl.BlockSpec((rows, hidden), lambda j: (0, 0), pipeline_mode=pl.Buffered(1))
        ] * len(lefts)
        + [pl.BlockSpec((rows, ROWS_STEP), lambda j: (0, j))] * len(rights),
        [pl.BlockSpec((hidden // count, ROWS_STEP), lambda j: (0, j))] * count,
        [shape] * count,
        (width // ROWS_STEP,),
        after,
        scratch_shapes=[pltpu.VMEM((hidden, len(lefts) * rows), jnp.bfloat16)],
        name="weight_rows",
    )


def to_model_kernel(counts, order_ref, *refs):
    left_refs, weight_refs = refs[: len(counts)], refs[len(counts) : -2]
    out_ref, acc_ref = refs[-2:]

    @pl.when(pl.program_id(0) == 0)
    def _():
        acc_ref[...] = jnp.zeros_like(acc_ref)

    left = joined(left_refs)
    terms, begin = [], 0
    for count in counts:
        terms.append(joined(weight_refs[begin : begin + count]))
        begin += count
    weight = jnp.concatenate(terms, axis=0)
    for first in range(0, weight.shape[1], MODEL_STEP):
        cols = slice(first, first + MODEL_STEP)
        acc_ref[:, cols] += matrix_product(left, weight[:, cols])

    @pl.when(pl.program_id(0) == pl.num_programs(0) - 1)
    def _():
        block = acc_ref.shape[1] // order_ref.shape[0]
        for i in range(order_ref.shape[0]):
            at = pl.ds(pl.multiple_of(order_ref[i] * block, block), block)
            out_ref[:, at] = acc_ref[:, i * block : (i + 1) * block].astype(jnp.bfloat16)


def to_model(lefts, weights, order, half, rows, after=()):
    hidden = lefts[0].shape[1]
    flat = [w for pieces in weights for w in pieces]
    width = sum(w.shape[1] for w in weights[0])
    tile = HIDDEN_TILE // 2
    return call(
        functools.partial(to_model_kernel, tuple(len(pieces) for pieces in weights)),
        [*lefts, *flat],
        [pl.BlockSpec((rows, tile), lambda j, o: (half, j))] * len(lefts)
        + [pl.BlockSpec((tile, w.shape[1]), lambda j, o: (j, 0)) for w in flat],
        pl.BlockSpec((rows, width), lambda j, o: (0, 0)),
        jax.ShapeDtypeStruct((rows, width), jnp.bfloat16),
        (hidden // tile,),
        after,
        order,
        scratch_shapes=[pltpu.VMEM((rows, width), jnp.float32)],
        name="to_model",
    )


NORM_TILE = 256


def resid_kernel(order_ref, tokens_ref, own_ref, there_ref, gain_ref, resid_ref, normed_ref):
    resid = (
        tokens_ref[...].astype(jnp.float32)
        + own_ref[...].astype(jnp.float32)
        + there_ref[...].astype(jnp.float32)
    )
    resid_ref[...] = resid.astype(jnp.bfloat16)
    scale = lax.rsqrt(jnp.mean(resid * resid, axis=-1, keepdims=True) + EPS_NORM)
    normed = (resid * scale * gain_ref[...]).astype(jnp.bfloat16)
    block = normed.shape[1] // order_ref.shape[0]
    for i in range(order_ref.shape[0]):
        at = pl.ds(pl.multiple_of(order_ref[i] * block, block), block)
        normed_ref[:, at] = normed[:, i * block : (i + 1) * block]


def resid_norm(tokens, own, there, gain, order, after=()):
    rows, width = tokens.shape
    tile = pl.BlockSpec((NORM_TILE, width), lambda i, o: (i, 0))
    return call(
        resid_kernel,
        [tokens, own, there, gain[None, :]],
        [tile, tile, tile, pl.BlockSpec((1, width), lambda i, o: (0, 0))],
        [tile, tile],
        [
            jax.ShapeDtypeStruct((rows, width), jnp.bfloat16),
            jax.ShapeDtypeStruct((rows, width), jnp.bfloat16),
        ],
        (rows // NORM_TILE,),
        after,
        order,
        name="resid_norm",
    )


def norm_back_kernel(value_ref, base_ref, own_ref, there_ref, gain_ref, *out_refs):
    *grad_refs, sum_ref = out_refs

    @pl.when(pl.program_id(0) == 0)
    def _():
        sum_ref[...] = jnp.zeros_like(sum_ref)

    value = value_ref[...].astype(jnp.float32)
    upstream = own_ref[...].astype(jnp.float32) + there_ref[...].astype(jnp.float32)
    scale = lax.rsqrt(jnp.mean(value * value, axis=-1, keepdims=True) + EPS_NORM)
    hat = value * scale
    weighted = upstream * gain_ref[...]
    inner = jnp.mean(hat * weighted, axis=-1, keepdims=True)
    grad = base_ref[...].astype(jnp.float32) + scale * (weighted - hat * inner)
    for ref in grad_refs:
        ref[...] = grad.astype(ref.dtype)
    sum_ref[0:1, :] += jnp.sum(upstream * hat, axis=0, keepdims=True)


def norm_return(value, base, own, there, gain, dtypes, after=()):
    rows, width = value.shape
    tile = pl.BlockSpec((NORM_TILE, width), lambda i: (i, 0))
    return call(
        norm_back_kernel,
        [value, base, own, there, gain[None, :]],
        [tile, tile, tile, tile, pl.BlockSpec((1, width), lambda i: (0, 0))],
        [tile] * len(dtypes) + [pl.BlockSpec((8, width), lambda i: (0, 0))],
        [jax.ShapeDtypeStruct((rows, width), d) for d in dtypes]
        + [jax.ShapeDtypeStruct((8, width), jnp.float32)],
        (rows // NORM_TILE,),
        after,
        name="norm_return",
    )


def block_info(lengths, positions, first):
    count = (lengths + BLK - 1) // BLK
    ends = jnp.cumsum(count)
    starts = jnp.concatenate([jnp.zeros((1,), jnp.int32), ends])
    own = lax.dynamic_slice_in_dim(positions, first, 8)
    first_keys = jnp.max(jnp.where(starts[None, :] <= own[:, None], starts[None, :], 0), axis=1)
    limits = jnp.concatenate([lengths, jnp.zeros((1,), jnp.int32)])
    seq = jnp.sum((own[:, None] >= ends[None, :]).astype(jnp.int32), axis=1)
    limit = jnp.sum(jnp.where(seq[:, None] == jnp.arange(4)[None, :], limits[None, :], 0), axis=1)
    pos = ((own - first_keys)[:, None] * BLK + jnp.arange(BLK)[None, :]).astype(jnp.int32)
    valid = pos < limit[:, None]
    return first_keys, own, pos.reshape(-1), valid.reshape(-1)


def chip_layer(
    tokens,
    cotangent,
    seq_lens,
    block_pos,
    norm1_gain,
    w_query,
    key_matrix,
    value_matrix,
    query_gain,
    key_gain,
    w_out,
    norm2_gain,
    w_gate,
    w_up,
    w_down,
):
    xi, core, yi = lax.axis_index("x"), lax.axis_index("c"), lax.axis_index("y")
    rows, width = tokens.shape
    bf16, f32 = jnp.bfloat16, jnp.float32
    half, fourth = width // 2, width // 4

    q_in, k_in = w_query.shape[1], key_matrix.shape[1]
    fourth, eighth = width // 4, width // 8
    kvw_0 = gather_z(jnp.concatenate([key_matrix.T, value_matrix.T], axis=0))
    qw_0 = gather_z(w_query.T)
    up_0 = to_core(w_up.T, core)
    up_x, up_y = swap(up_0, "x"), swap(up_0, "y")
    down_0 = to_core(after(w_down, up_0), core)
    gate_0 = to_core(after(w_gate, up_0).T, core)
    low = up_0.shape[0] // 2
    out_0 = gather_z(w_out)
    dlo_0 = gather_z(down_0[:low])
    kvw_x, kvw_y = swap(kvw_0, "x"), swap(kvw_0, "y")
    middle = kvw_0.shape[0] // 2
    kvw_x, kvw_y, qw_0, up_x, up_y = sync(kvw_x, kvw_y, qw_0, up_x, up_y)
    kvw_ca, kvw_cb = swap(kvw_y[:middle], "x"), swap(kvw_x[middle:], "y")
    qw_x, qw_y = swap(qw_0, "x"), swap(qw_0, "y")
    kvw_ca, kvw_cb, qw_x, qw_y, out_0 = sync(kvw_ca, kvw_cb, qw_x, qw_y, out_0)
    qw_ca, qw_cb = swap(qw_y[:middle], "x"), swap(qw_x[middle:], "y")
    out_x, out_y = swap(out_0, "x"), swap(out_0, "y")
    kvw = [
        a.reshape(4, 2 * k_in, width)
        for a in (kvw_0, kvw_x, kvw_y, jnp.concatenate([kvw_ca, kvw_cb], axis=0))
    ]
    kv_w = jnp.concatenate(
        [part.reshape(-1, width) for a in kvw for part in (a[:, :k_in], a[:, k_in:])], axis=0
    )

    lengths_here = jnp.concatenate([seq_lens[0], block_pos[0]]).astype(f32)
    lengths_there = swap(lengths_here[None, :], "c")[0].astype(jnp.int32)
    first_own = yi * 8
    keys_here, at_here, pos_here, valid_here = block_info(seq_lens[0], block_pos[0], first_own)
    keys_there, at_there, pos_there, _ = block_info(
        lengths_there[:3], lengths_there[3:], first_own
    )
    info = jnp.stack(
        [
            jnp.concatenate([keys_here, at_here[:1]]),
            jnp.concatenate([keys_there, at_there[:1]]),
        ]
    ).astype(jnp.int32)
    freq = jnp.exp(
        jnp.arange(HEAD_SIZE // 2, dtype=f32) * (-2.0 * math.log(ROPE_BASE) / HEAD_SIZE)
    )
    angles = jnp.concatenate([pos_here, pos_there]).astype(f32)[:, None] * freq[None, :]
    cos_half, sin_half = jnp.cos(angles), jnp.sin(angles)
    cos_tab = jnp.concatenate([cos_half, cos_half], axis=1)
    sin_tab = jnp.concatenate([-sin_half, sin_half], axis=1)
    valid = valid_here.astype(f32)[:, None]

    blocks = jnp.arange(8)
    ry, rx, rc = blocks // 4, (blocks // 2) % 2, blocks % 2
    order = ((rx ^ xi) * 4 + rc * 2 + (ry ^ yi)).astype(jnp.int32)
    nx, nc, ny = blocks // 4, (blocks // 2) % 2, blocks % 2
    order_back = ((ny ^ yi) * 4 + (nx ^ xi) * 2 + nc).astype(jnp.int32)

    def stacked(first, second):
        return jnp.concatenate([first, second], axis=0)

    inputs = after(tokens, up_0).astype(f32)
    normed1 = rms_parts(inputs, norm1_gain)[0].astype(bf16)
    normed1 = [normed1, swap(normed1, "c")]
    dy_own = (valid * cotangent.astype(f32)).astype(bf16)

    def project(group, rows_in, weight, gain, count, wait=()):
        raw = to_hidden([rows_in], [weight], f32, wait)
        return raw, make_heads(group, raw, cos_tab, sin_tab, gain, count)

    normed1[0], kv_w = sync(normed1[0], kv_w)
    kv_raw0, kv0 = project(0, normed1[0], kv_w, key_gain, 2)
    kv0, qw_ca, qw_cb, out_x, out_y, up_y, normed1[0], gate_0, glo_in = sync(
        kv0, qw_ca, qw_cb, out_x, out_y, up_y, normed1[0], gate_0, gate_0[:low]
    )
    kv_far0, out_c, up_c = swap(kv0, "y"), swap(out_y, "x"), swap(up_y, "x")
    glo_0 = gather_z(glo_in)
    dhi_0, ghi_0 = gather_z(down_0[low:]), gather_z(gate_0[low:])
    q_w = jnp.concatenate([qw_0, qw_x, qw_y, qw_ca, qw_cb], axis=0)
    q_raw0, query0 = project(0, normed1[0], q_w, query_gain, 1)
    kv_raw1, kv1 = project(1, normed1[1], kv_w, key_gain, 2, [query0])
    kv_far0, out_c, up_c, dlo_0, kv1, normed1[1], dy_own = sync(
        kv_far0, out_c, up_c, dlo_0, kv1, normed1[1], dy_own
    )
    dlo_x, dlo_y = swap(dlo_0, "x"), swap(dlo_0, "y")
    up_in = jnp.concatenate([up_0, up_x, up_y, up_c], axis=1)
    ulo, uhi = gather_z(up_in[:low]), gather_z(up_in[low:])
    attn0, totals0 = attend(0, info, query0, kv0, kv_far0)
    out_w = jnp.concatenate([out_0, out_x, out_y, out_c], axis=0)
    attn0, out_w, dlo_x, dlo_y, kv_1, normed1[1] = sync(
        attn0, out_w, dlo_x, dlo_y, kv1, normed1[1]
    )
    q_raw1, query1 = project(1, normed1[1], q_w, query_gain, 1)
    dy = [reorder(dy_own, order, [query1])]
    dy.append(swap(dy[0], "c"))
    query, q_raw = [query0, query1], [q_raw0, q_raw1]
    kv, kv_raw = [kv0, kv1], [kv_raw0, kv_raw1]
    kv_far1, dlo_c = swap(kv_1, "y"), swap(dlo_y, "x")
    kv_far1, dlo_c, glo_0, query[1], dy[0] = sync(kv_far1, dlo_c, glo_0, query[1], dy[0])
    glo_x, glo_y = swap(glo_0, "x"), swap(glo_0, "y")
    attn1, totals1 = attend(1, info, query[1], kv[1], kv_far1)
    attn1, glo_x, glo_y, glo_0 = sync(attn1, glo_x, glo_y, glo_0)
    glo_ca, glo_cb = swap(glo_y[:, :eighth], "x"), swap(glo_x[:, eighth:], "y")
    same = jnp.arange(8, dtype=jnp.int32)
    out_term = to_model([attn1], [[out_w]], same, 0, rows)
    out_there = swap(out_term, "c")
    out_here = to_model([attn0], [[out_w]], same, 0, rows, [out_term])
    dlo = [dlo_0, dlo_x, dlo_y, dlo_c]
    d_act_lo = to_hidden(dy, dlo, bf16, [out_here])
    resid, normed2_own = resid_norm(
        tokens, out_here, out_there, norm2_gain, order_back, [d_act_lo]
    )
    normed2_own, glo_ca, glo_cb, dhi_0 = sync(normed2_own, glo_ca, glo_cb, dhi_0)
    normed2 = [normed2_own, swap(normed2_own, "c")]
    dhi_x, dhi_y = swap(dhi_0, "x"), swap(dhi_0, "y")
    glo = [glo_0, glo_x, glo_y, glo_ca, glo_cb]
    act_lo, gg_lo, ug_lo = ffn(normed2, glo, ulo, d_act_lo)
    act_lo, gg_lo, dhi_x, dhi_y, ghi_0 = sync(act_lo, gg_lo, dhi_x, dhi_y, ghi_0)
    ghi_x, ghi_y = swap(ghi_0, "x"), swap(ghi_0, "y")

    widths = [fourth, fourth, fourth, eighth, eighth]
    pieces = [fourth] * 4
    dlo_grad, gl_0, gl_x, gl_y, gl_c = weight_cols(
        (act_lo, dy, [width]), (gg_lo, normed2, pieces)
    )
    dlo_grad, gl_c, ghi_x, ghi_y, ug_lo, dhi_x, dhi_y = sync(
        dlo_grad, gl_c, ghi_x, ghi_y, ug_lo, dhi_x, dhi_y
    )
    dlo_sum = scatter_z(dlo_grad)
    dhi_ca, dhi_cb = swap(dhi_y[:, :eighth], "x"), swap(dhi_x[:, eighth:], "y")
    ul_0, ul_x, ul_y, ul_c = weight_cols((ug_lo, normed2, pieces))
    dhi_ca, dhi_cb, ul_c, ghi_x, ghi_y = sync(dhi_ca, dhi_cb, ul_c, ghi_x, ghi_y)
    dhi = [dhi_0, dhi_x, dhi_y, dhi_ca, dhi_cb]
    ghi_ca, ghi_cb = swap(ghi_y[:, :eighth], "x"), swap(ghi_x[:, eighth:], "y")
    d_act_hi = to_hidden(dy, dhi)
    ghi_ca, ghi_cb, gl_c, ul_c, d_act_hi = sync(ghi_ca, ghi_cb, gl_c, ul_c, d_act_hi)
    ghi = [ghi_0, ghi_x, ghi_y, ghi_ca, ghi_cb]
    from_g, from_u = swap(gl_c, "x"), swap(ul_c, "y")
    act_hi, gg_hi, ug_hi = ffn(normed2, ghi, uhi, d_act_hi)
    gl_x, gl_y, from_g, ul_x, ul_y, from_u, act_hi, gg_hi, ug_hi = sync(
        gl_x, gl_y, from_g, ul_x, ul_y, from_u, act_hi, gg_hi, ug_hi
    )
    gl_y = gl_y + from_g
    gl_x, gl_y, gg_hi = sync(gl_x, gl_y, gg_hi)
    got_x, got_y = swap(gl_x, "x"), swap(gl_y, "y")
    dh_0, dh_x, dh_y, dh_ca, dh_cb, gh_0, gh_x, gh_y, gh_c = weight_cols(
        (act_hi, dy, widths), (gg_hi, normed2, pieces)
    )
    gl_0, got_x, got_y, dh_ca, dh_cb, ug_hi, ul_x, ul_y = sync(
        gl_0, got_x, got_y, dh_ca, dh_cb, ug_hi, ul_x, ul_y
    )
    from_a, from_b = swap(dh_ca, "x"), swap(dh_cb, "y")
    glo_near = gl_0 + got_x + got_y
    glo_sum = scatter_z(glo_near)
    ul_x = ul_x + from_u
    uh_0, uh_x, uh_y, uh_c = weight_cols(
        (ug_hi, normed2, pieces), after=[glo_near, ul_x]
    )
    dh_x, dh_y, from_a, from_b, ul_x, ul_y, gg_hi, uh_0 = sync(
        dh_x, dh_y, from_a, from_b, ul_x, ul_y, gg_hi, uh_0
    )
    got_ux, got_uy = swap(ul_x, "x"), swap(ul_y, "y")
    dh_x, dh_y = add_halves(dh_x, dh_y, from_a, from_b)
    grads = [gg_lo, ug_lo, gg_hi, ug_hi]
    both_w = [glo, [ulo], ghi, [uhi]]
    there = to_model(grads, both_w, order, 1, rows, [dh_x, dh_y])
    ul_0, got_ux, got_uy, dh_x, dh_y, there, gg_hi = sync(
        ul_0, got_ux, got_uy, dh_x, dh_y, there, gg_hi
    )
    normed2_there = swap(there, "c")
    got_x, got_y = swap(dh_x, "x"), swap(dh_y, "y")
    ulo_near = ul_0 + got_ux + got_uy
    ulo_sum = scatter_z(ulo_near)
    grads = [gg_lo, ug_lo, gg_hi, ug_hi]
    grad_own = to_model(grads, both_w, order, 0, rows, [ulo_near])
    dh_0, got_x, got_y, gh_c, uh_c, grad_own = sync(dh_0, got_x, got_y, gh_c, uh_c, grad_own)
    from_g, from_u = swap(gh_c, "x"), swap(uh_c, "y")
    dhi_near = dh_0 + got_x + got_y
    dhi_sum = scatter_z(dhi_near)
    resid_here, gain2_sum = norm_return(
        resid, dy_own, grad_own, normed2_there, norm2_gain, (bf16,), [dhi_near]
    )
    resid_first = resid_here
    resid_there = swap(resid_here, "c")
    mixed_term = to_model([act_lo, act_hi], [dlo, dhi], order, 1, rows, [resid_here])
    d_attn0 = to_hidden([resid_here], [out_w], bf16, [mixed_term])
    gh_x, gh_y, from_g, uh_x, uh_y, from_u, mixed_term, d_attn0 = sync(
        gh_x, gh_y, from_g, uh_x, uh_y, from_u, mixed_term, d_attn0
    )
    gh_y, uh_x = gh_y + from_g, uh_x + from_u
    gh_x, gh_y, uh_x, uh_y, d_attn0 = sync(gh_x, gh_y, uh_x, uh_y, d_attn0)
    got_x, got_y = swap(gh_x, "x"), swap(gh_y, "y")
    got_ux, got_uy = swap(uh_x, "x"), swap(uh_y, "y")
    mixed_there = swap(mixed_term, "c")

    dq0, dkv0, dkv0_far = attend_back(0, info, query[0], d_attn0, attn0, totals0, kv[0], kv_far0)
    o_0, o_x, o_y, o_c = weight_rows([attn0, attn1], [resid_here, resid_there], 4, [dq0])
    d_attn1 = to_hidden([resid_there], [out_w], bf16, [o_0])
    gh_0, got_x, got_y, uh_0, got_ux, got_uy, d_attn1, dkv0_far, dlo_sum, o_c = sync(
        gh_0, got_x, got_y, uh_0, got_ux, got_uy, d_attn1, dkv0_far, dlo_sum, o_c
    )
    dkv0_back, from_o = swap(dkv0_far, "y"), swap(o_c, "x")
    dl_0, dl_x, dl_y, dl_c = (dlo_sum[:, i * fourth : (i + 1) * fourth] for i in range(4))
    from_l, got_lx = swap(dl_c, "x"), swap(dl_x, "x")
    ghi_near, uhi_near = gh_0 + got_x + got_y, uh_0 + got_ux + got_uy
    ghi_sum, uhi_sum = scatter_z(ghi_near), scatter_z(uhi_near)
    back = (cos_tab, sin_tab)
    dq1, dkv1, dkv1_far = attend_back(
        1, info, query[1], d_attn1, attn1, totals1, kv[1], kv_far1, [ghi_near, uhi_near]
    )
    q_grad0, q_gain0 = heads_return(0, q_raw[0], dq0, [], *back, query_gain, 1, [dq1])
    dkv1_far, dkv0_back, o_x, o_y, from_o, got_lx, dl_y, from_l, q_grad0 = sync(
        dkv1_far, dkv0_back, o_x, o_y, from_o, got_lx, dl_y, from_l, q_grad0
    )
    dkv1_back, got_ox = swap(dkv1_far, "y"), swap(o_x, "x")
    q_grad1, q_gain1 = heads_return(1, q_raw[1], dq1, [], *back, query_gain, 1, [q_grad0])
    q_grad, q_gains = [q_grad0, q_grad1], q_gain0 + q_gain1
    w_0, w_x, w_y, w_c = weight_rows(q_grad, normed1, 4)
    w_c, act_hi = sync(w_c, act_hi)
    from_w = swap(w_c, "x")
    mixed_own = to_model([act_lo, act_hi], [dlo, dhi], order, 0, rows)
    dkv1_back, got_ox, mixed_own, o_y, dl_y, w_x = sync(
        dkv1_back, got_ox, mixed_own, o_y + from_o, dl_y + from_l, w_x
    )
    got_oy, got_wx = swap(o_y, "y"), swap(w_x, "x")

    def halves(array):
        span = array.shape[0] // 2
        return array[:span], array[span:]

    def corner_rows(along_x, along_y, from_a, from_b):
        (x_a, x_b), (y_a, y_b) = halves(along_x), halves(along_y)
        return stacked(x_a, x_b + from_b), stacked(y_a + from_a, y_b)

    kv_grad = [
        heads_return(g, kv_raw[g], d, [e], *back, key_gain, 2, [mixed_own, w_x])
        for g, (d, e) in enumerate(((dkv0, dkv0_back), (dkv1, dkv1_back)))
    ]
    k_gains = kv_grad[0][1] + kv_grad[1][1]
    *kv_grad, from_w, w_y = sync(kv_grad[0][0], kv_grad[1][0], from_w, w_y)
    got_wy = swap(w_y + from_w, "y")
    kv_0, kv_x, kv_y, kv_c = weight_rows(kv_grad, normed1, 4)
    kv_c, kv_grad[1], got_oy, got_wx = sync(kv_c, kv_grad[1], got_oy, got_wx)
    kv_a, kv_b = halves(kv_c)
    from_a, from_b = swap(kv_a, "x"), swap(kv_b, "y")
    term_there = to_model([q_grad[1], kv_grad[1]], [[q_w], [kv_w]], same, 0, rows)
    o_0, got_oy, w_0, got_wx, got_wy, kv_x, kv_y, from_a, from_b, term_there, dl_y = sync(
        o_0, got_oy, w_0, got_wx, got_wy, kv_x, kv_y, from_a, from_b, term_there, dl_y
    )
    normed1_there = swap(term_there, "c")
    kv_x, kv_y = corner_rows(kv_x, kv_y, from_a, from_b)
    got_kx, got_ky, got_ly = swap(kv_x, "x"), swap(kv_y, "y"), swap(dl_y, "y")
    o_near, w_near = o_0 + got_ox + got_oy, w_0 + got_wx + got_wy
    ow_near = jnp.concatenate(
        [o_near.reshape(4, q_in, width), w_near.reshape(4, q_in, width)], axis=1
    ).reshape(8 * q_in, width)
    ow_sum = scatter_z(ow_near)
    term_own = to_model(
        [q_grad[0], kv_grad[0]], [[q_w], [kv_w]], same, 0, rows, [kv_x, kv_y, ow_near]
    )
    kv_0, got_kx, got_ky, got_ly, term_own = sync(kv_0, got_kx, got_ky, got_ly, term_own)
    kv_near = kv_0 + got_kx + got_ky
    kv_sum = scatter_z(
        kv_near.reshape(2, 4, k_in, width).swapaxes(0, 1).reshape(8 * k_in, width)
    )
    tokens_grad, gain1_sum = norm_return(
        tokens, resid_first, term_own, normed1_there, norm1_gain, (f32,), [kv_near]
    )
    gain1_part = gain1_sum[0]
    gain2_part = gain2_sum[0]
    gains = jnp.concatenate([gain1_part, gain2_part, q_gains[0], k_gains[0]])[None, :]
    gains = gains + swap(gains, "c")
    gains_xy = lax.ppermute(gains, ("x", "y"), [(i, i ^ 3) for i in range(4)])
    gains_x, gains_y = swap(gains, "x"), swap(gains, "y")
    gains = (gains + gains_x) + (gains_y + gains_xy)
    gains, mixed_own, ow_sum = sync(gains, mixed_own, ow_sum)
    gains_z = [lax.ppermute(gains, "z", [(i, i ^ k) for i in range(4)]) for k in (1, 2, 3)]
    output = (
        valid * (resid.astype(f32) + mixed_own.astype(f32) + mixed_there.astype(f32))
    ).astype(bf16)
    gains, output, kv_sum, *gains_z = sync(gains, output, kv_sum, *gains_z)
    o_sum, w_sum = ow_sum[:q_in], ow_sum[q_in:]
    gains = ((gains + gains_z[0]) + (gains_z[1] + gains_z[2]))[0]
    dlo_sum = dl_0 + got_lx + got_ly

    gate_sum, up_sum, down_sum = (
        jnp.concatenate(pair, axis=0)
        for pair in ((glo_sum, ghi_sum), (ulo_sum, uhi_sum), (dlo_sum, dhi_sum))
    )
    gate_sum, up_sum, down_sum = from_core(
        [(a[:, :eighth], a[:, eighth:]) for a in (gate_sum, up_sum, down_sum)], core
    )
    return (
        output,
        tokens_grad,
        gains[:width],
        w_sum.astype(f32).T,
        kv_sum[:k_in].astype(f32).T,
        kv_sum[k_in:].astype(f32).T,
        gains[2 * width : 2 * width + HEAD_SIZE],
        gains[2 * width + HEAD_SIZE :],
        o_sum.astype(f32),
        gains[width : 2 * width],
        gate_sum.astype(f32).T,
        up_sum.astype(f32).T,
        down_sum.astype(f32),
    )


def chip_solution(mesh):
    fine = Mesh(mesh.devices.reshape(2, 2, 2, 4), ("x", "c", "y", "z"))
    row_spec = P(("x", "c", "y", "z"), None)
    group_spec = P(("x", "c", "z"), None)
    head_cols = P(None, ("y", "x", "c", "z"))
    head_rows = P(("y", "x", "c", "z"), None)
    up_spec, down_spec = P(("x", "c", "y"), "z"), P("z", ("x", "c", "y"))
    return jax.shard_map(
        chip_layer,
        mesh=fine,
        in_specs=(
            row_spec,
            row_spec,
            group_spec,
            group_spec,
            P(),
            head_cols,
            head_cols,
            head_cols,
            P(),
            P(),
            head_rows,
            P(),
            up_spec,
            up_spec,
            down_spec,
        ),
        out_specs=(
            row_spec,
            row_spec,
            P(),
            head_cols,
            head_cols,
            head_cols,
            P(),
            P(),
            head_rows,
            P(),
            up_spec,
            up_spec,
            down_spec,
        ),
        check_vma=False,
    )


def solution(mesh):
    sizes = dict(mesh.shape)
    if sizes == {"fsdp": 4, "heads": 2, "tensor": 4}:
        return chip_solution(mesh)
    return plain_solution(mesh)
```
